32 devices in a mesh: seq: 8 (over z, y), fsdp: 4 (over x, core).
Axes of the slice: x: 2, y: 2, z: 4, core: 2. Of those that a mesh axis runs over, the one named last changes fastest.
Arguments:
- queries: bfloat16 [2048, 4096], P('seq', 'fsdp'), may hold values from -6 to 6
- keys: bfloat16 [2048, 4096], P('seq', 'fsdp'), may hold values from -6 to 6
- values: bfloat16 [2048, 4096], P('seq', 'fsdp'), may hold values from -6 to 6
- filters: float32 [2048, 4096], P('seq', 'fsdp'), as said below
- skip_weight: float32 [4096], P('fsdp'), may hold values from -4 to 4
- out_weight: bfloat16 [4096, 4096], P('fsdp'), may hold values from -0.125 to 0.125
Outputs:
- mixed_out: bfloat16 [2048, 4096], P('seq', 'fsdp')
The draws below stay inside these ranges and needn't reach their ends.
Inputs may be any that keep to these rules, and one draw needn't show every extreme that they name: `filters`: real filter values of the 4096 channels at 2048 lags.
All inputs are finite; a program needn't handle non-finite values.
Results may differ from the reference program's by a relative error of at most 0.0049.
Values may be sent and summed in bfloat16 or wider, within the bound.
No kernel may reach another device: no remote copies, remote signals or barrier semaphores. Data moves between devices by JAX's collectives and lax.ppermute only.
A program may use at most 128 MiB of HBM per device.

```python
import math
import jax
import jax.numpy as jnp
from jax import lax

D = 4096
SEQ_LEN = 2048


def draw_filters(key, part):
    sampler_starting_states = jax.random.split(key, 6)
    kernel_span_size = SEQ_LEN
    shift_reach_coordinate = jnp.arange(kernel_span_size, dtype=jnp.float32)[:, None]
    slow_share = 0.5
    is_slow = jax.random.uniform(sampler_starting_states[0], (D,)) < slow_share
    slow_rate = jnp.exp(jax.random.uniform(sampler_starting_states[1], (D,), minval=math.log(0.3 / kernel_span_size), maxval=math.log(2.3 / kernel_span_size)))
    fast_rate = jnp.exp(jax.random.uniform(sampler_starting_states[2], (D,), minval=math.log(1.0 / 50.0), maxval=math.log(1.0 / 30.0)))
    damping_speed = jnp.where(is_slow, slow_rate, fast_rate)[None, :]
    gaussian_jitter = jnp.clip(jax.random.normal(sampler_starting_states[3], (kernel_span_size, D)), -6.0, 6.0)
    impulse_displacements = jax.random.randint(sampler_starting_states[4], (3,), 1, kernel_span_size).astype(jnp.float32)
    impulse_keepers = jax.random.uniform(sampler_starting_states[5], (3,), minval=0.5, maxval=0.8)
    impulse_happenings = jnp.ones((kernel_span_size, 1), jnp.float32)
    for element_number in range(3):
        impulse_happenings = impulse_happenings * jnp.where(shift_reach_coordinate >= impulse_displacements[element_number], impulse_keepers[element_number], 1.0)
    envelope_kernel = gaussian_jitter * jnp.sqrt(2.0 * damping_speed) * jnp.exp(-damping_speed * shift_reach_coordinate) * impulse_happenings
    return envelope_kernel.astype(jnp.float32)


def spiked(drawn, rng, source, target, parts, factor):
    owner, partner = [(jnp.arange(drawn.shape[position]) // (drawn.shape[position] // parts)).reshape([-1 if axis == position else 1 for axis in range(drawn.ndim)]) for position in (source, target)]
    chosen = jax.random.permutation(rng, parts)[partner]
    strong = (owner == chosen) | (owner == (partner + parts // 2) % parts)
    return jnp.where(strong, factor * drawn, drawn)


def level_of(key, shape, cuts, least, largest):
    def one(axis_at, blocks):
        heights = jax.random.uniform(jax.random.fold_in(jax.random.fold_in(key, 6), axis_at), (blocks,), jnp.float32, least / len(cuts), largest / len(cuts))
        return jnp.repeat(jnp.exp(heights), shape[axis_at] // blocks).reshape((-1,) + (1,) * (len(shape) - axis_at - 1))

    level = one(*cuts[0])
    for cut in cuts[1:]:
        level = level * one(*cut)
    return level


def noise(rng, dims, deviation, bound, cuts=(), held_as=jnp.bfloat16):
    entries = jax.random.normal(rng, dims, jnp.float32) * deviation
    if len(cuts) > 0:
        entries = level_of(rng, dims, cuts, -0.22, 0.18) * entries
    return jnp.clip(entries, min=-bound, max=bound).astype(held_as)


def noise_with(rng, dims, scale, bound, pieces, heavy, kind=jnp.bfloat16):
    drawn = scale * jax.random.normal(rng, dims, jnp.float32)
    if pieces:
        drawn = drawn * level_of(rng, dims, pieces, -0.22, 0.18)
    return jnp.clip(spiked(drawn, jax.random.fold_in(rng, 3), *heavy), -bound, bound).astype(kind)


def setup_inputs(seed: int = 0) -> dict:
    streams_of = jax.random.split(jax.random.key(seed), 7)
    return {
        "queries": noise(streams_of[0], (SEQ_LEN, D), 1.0, 6.0, ((0, 8), (1, 4))),
        "keys": noise(streams_of[1], (SEQ_LEN, D), 1.0, 6.0, ((0, 8), (1, 4))),
        "values": noise(streams_of[2], (SEQ_LEN, D), 1.0, 6.0, ((0, 8), (1, 4))),
        "filters": draw_filters(jax.random.fold_in(streams_of[6], 71), 0),
        "skip_weight": noise(streams_of[4], (D,), 1.0, 4.0, ((0, 4),), jnp.float32),
        "out_weight": noise_with(streams_of[5], (D, D), D ** -0.5, 0.125, ((0, 4),), (0, 1, 4, 2.0)),
    }


def convolve_block(block):
    signal, kernel = block
    kernel_span_size = signal.shape[0]
    spectrum = jnp.fft.rfft(signal, 2 * kernel_span_size, axis=0) * jnp.fft.rfft(kernel, 2 * kernel_span_size, axis=0)
    return jnp.fft.irfft(spectrum, 2 * kernel_span_size, axis=0)[:kernel_span_size].astype(signal.dtype)


def reference(queries, keys, values, filters, skip_weight, out_weight):
    product = keys.astype(jnp.float32) * values.astype(jnp.float32)
    width = product.shape[1]
    block_width = min(width, 256)
    block_tally = width // block_width
    kernel_span_size = product.shape[0]
    signal = product.reshape(kernel_span_size, block_tally, block_width).transpose(1, 0, 2)
    kernel = filters.reshape(kernel_span_size, block_tally, block_width).transpose(1, 0, 2)
    conv = lax.map(convolve_block, (signal, kernel))
    conv = conv.transpose(1, 0, 2).reshape(kernel_span_size, width)
    mixed = conv + skip_weight[None, :] * product
    gated = (queries.astype(jnp.float32) * mixed).astype(jnp.bfloat16)
    return jnp.dot(gated, out_weight, preferred_element_type=jnp.float32).astype(jnp.bfloat16)
```

```python
import functools

import numpy as np

import jax
import jax.numpy as jnp
from jax import lax
from jax.experimental import pallas as pl
from jax.experimental.pallas import tpu as pltpu
from jax.sharding import PartitionSpec as P

BF16 = jnp.bfloat16
F32 = jnp.float32
CONV_VMEM = 24 * 2**20
PROJECT_VMEM = 24 * 2**20
SMALL_VMEM = 12 * 2**20


def split_bf16(table):
    high = table.astype(BF16)
    low = (table - high.astype(np.float64)).astype(BF16)
    return np.concatenate([high, low], axis=0)


def make_tables(rows):
    order = np.concatenate([np.arange(0, rows, 2), np.arange(1, rows, 2)])
    times = np.arange(rows)
    angle = np.pi * (((2 * order[:, None] + 1) * times[None, :]) % (4 * rows)) / (2 * rows)
    forward = np.concatenate([np.cos(angle), -np.sin(angle)], axis=0)
    backward = forward.T / rows
    return split_bf16(forward), split_bf16(backward)


def peer_of(slot):
    return lax.bitwise_xor(lax.axis_index("seq"), slot)


def peer_block(slot, size):
    return pl.ds(pl.multiple_of(peer_of(slot) * size, size), size)


def pre_kernel(n_peers, keys_hbm, values_hbm, filters_hbm, fwd_hbm, bwd_hbm, *refs):
    out_refs = refs[:n_peers]
    fwd_ref, bwd_ref, keys, values, filters, sem = refs[n_peers:]
    chans = keys.shape[1] // n_peers
    copies = [
        pltpu.make_async_copy(src, dst, sem.at[i])
        for i, (src, dst) in enumerate(
            (
                (keys_hbm, keys),
                (values_hbm, values),
                (filters_hbm, filters),
                (fwd_hbm, fwd_ref),
                (bwd_hbm, bwd_ref),
            )
        )
    ]
    for copy in copies:
        copy.start()
    for copy in copies[:3]:
        copy.wait()
    for slot, out_ref in zip(slots_of(n_peers, False), out_refs):
        at = peer_block(slot, chans)
        product = keys[:, at].astype(F32) * values[:, at].astype(F32)
        out_ref[:, :chans] = product.astype(BF16)
        out_ref[:, chans:] = filters[:, at].astype(BF16)
    for copy in copies[3:]:
        copy.wait()


def pre(keys, values, filters, fwd, bwd, n_peers):
    rows, width = keys.shape
    chans = width // n_peers
    args = [
        pltpu.with_memory_space_constraint(a, pltpu.HBM) for a in (keys, values, filters, fwd, bwd)
    ]
    *blocks, fwd, bwd = pl.pallas_call(
        functools.partial(pre_kernel, n_peers),
        in_specs=[pl.BlockSpec(memory_space=pltpu.HBM)] * 5,
        out_specs=[pl.BlockSpec(memory_space=pltpu.VMEM)] * (n_peers + 2),
        out_shape=[jax.ShapeDtypeStruct((rows, 2 * chans), BF16)] * n_peers
        + [jax.ShapeDtypeStruct(t.shape, BF16) for t in (fwd, bwd)],
        scratch_shapes=[
            pltpu.VMEM((rows, width), BF16),
            pltpu.VMEM((rows, width), BF16),
            pltpu.VMEM((rows, width), F32),
            pltpu.SemaphoreType.DMA((5,)),
        ],
        compiler_params=pltpu.CompilerParams(vmem_limit_bytes=SMALL_VMEM),
        cost_estimate=pl.CostEstimate(
            flops=rows * width, bytes_accessed=12 * rows * width, transcendentals=0
        ),
    )(*args)
    return blocks, fwd, bwd


def slots_of(n_peers, back):
    half = n_peers // 2
    near, far = list(range(1, half)), list(range(half, n_peers))
    if back:
        return [0, near[0], far[0], near[1], far[1]] + near[2:] + far[2:]
    return [0, far[0], near[0], far[1], near[1]] + near[2:] + far[2:]


def exchange(blocks, n_peers, back):
    return [
        lax.ppermute(block, "seq", [(i, i ^ slot) for i in range(n_peers)]) if slot else block
        for slot, block in zip(slots_of(n_peers, back), blocks)
    ]


def conv_kernel(fwd_ref, bwd_ref, *refs):
    *refs, spec, turned = refs
    n_blocks = spec.shape[0]
    in_refs, out_refs = refs[:n_blocks], refs[n_blocks:]
    rows, chans = in_refs[0].shape[0], in_refs[0].shape[1] // 2
    step = 8

    for slot, in_ref in zip(slots_of(n_blocks, False), in_refs):
        j = peer_of(slot)
        block = in_ref[...]
        high = jnp.dot(fwd_ref[: 2 * rows], block, preferred_element_type=F32)
        low = jnp.dot(fwd_ref[2 * rows :], block, preferred_element_type=F32)
        spec[j] = high + low

    def mix(row, sign):
        re, im = pl.ds(row, step), pl.ds(row + rows, step)
        x_re = [spec[j, re, :chans] for j in range(n_blocks)]
        x_im = [spec[j, im, :chans] for j in range(n_blocks)]
        out_re, out_im = [None] * n_blocks, [None] * n_blocks
        last_re = last_im = None
        for d in range(n_blocks):
            f_re, f_im = spec[d, re, chans:], spec[d, im, chans:]
            g_re, g_im = f_re, f_im
            if d > 0:
                g_re, g_im = f_re - sign * last_im, f_im + sign * last_re
            last_re, last_im = f_re, f_im
            for i in range(d, n_blocks):
                a_re, a_im = x_re[i - d], x_im[i - d]
                t_re = g_re * a_re - g_im * a_im
                t_im = g_re * a_im + g_im * a_re
                out_re[i] = t_re if d == 0 else out_re[i] + t_re
                out_im[i] = t_im if d == 0 else out_im[i] + t_im
        for i in range(n_blocks):
            for where, value in ((re, out_re[i]), (im, out_im[i])):
                high = value.astype(BF16).astype(F32)
                turned[i, where, :chans] = high
                turned[i, where, chans:] = value - high

    half = rows // 2

    @pl.loop(0, half // step)
    def _(t):
        row = pl.multiple_of(t * step, step)
        mix(row, 1.0)

    @pl.loop(half // step, rows // step)
    def _(t):
        row = pl.multiple_of(t * step, step)
        mix(row, -1.0)

    for slot, out_ref in zip(slots_of(n_blocks, True), out_refs):
        i = peer_of(slot)
        both = jnp.dot(bwd_ref[...], turned[i].astype(BF16), preferred_element_type=F32)
        value = both[:rows, :chans] + both[:rows, chans:] + both[rows:, :chans]
        out_ref[...] = value.astype(BF16)


def conv_fast(received, fwd, bwd):
    n_blocks = len(received)
    rows, chans = received[0].shape[0], received[0].shape[1] // 2
    whole = pl.BlockSpec(memory_space=pltpu.VMEM)
    return pl.pallas_call(
        conv_kernel,
        in_specs=[whole] * (2 + n_blocks),
        out_specs=[whole] * n_blocks,
        out_shape=[jax.ShapeDtypeStruct((rows, chans), BF16)] * n_blocks,
        scratch_shapes=[
            pltpu.VMEM((n_blocks, 2 * rows, 2 * chans), F32),
            pltpu.VMEM((n_blocks, 2 * rows, 2 * chans), F32),
        ],
        compiler_params=pltpu.CompilerParams(vmem_limit_bytes=CONV_VMEM),
        cost_estimate=pl.CostEstimate(
            flops=16 * n_blocks * rows * rows * chans * 2, bytes_accessed=4 * 2**20, transcendentals=0
        ),
    )(fwd, bwd, *received)


def conv_plain(received, fwd, bwd):
    n_blocks, rows, chans = received.shape[0], received.shape[1], received.shape[2] // 2
    exact = lax.Precision.HIGHEST
    fwd32 = fwd[: 2 * rows].astype(F32) + fwd[2 * rows :].astype(F32)
    bwd32 = bwd[:rows].astype(F32) + bwd[rows:].astype(F32)
    sign = jnp.where(jnp.arange(rows) < rows // 2, 1.0, -1.0).astype(F32)[:, None]

    def spectrum(blocks):
        spec = jnp.einsum("kt,jtc->jkc", fwd32, blocks.astype(F32), precision=exact)
        return spec[:, :rows], spec[:, rows:]

    x_re, x_im = spectrum(received[:, :, :chans])
    f_re, f_im = spectrum(received[:, :, chans:])
    g_re = f_re.at[1:].add(-sign * f_im[:-1])
    g_im = f_im.at[1:].add(sign * f_re[:-1])

    def one(d, total):
        t_re, t_im = total
        later = (jnp.arange(n_blocks) >= d)[:, None, None]
        a_re = jnp.where(later, jnp.roll(x_re, d, axis=0), 0.0)
        a_im = jnp.where(later, jnp.roll(x_im, d, axis=0), 0.0)
        return (
            t_re + g_re[d] * a_re - g_im[d] * a_im,
            t_im + g_re[d] * a_im + g_im[d] * a_re,
        )

    zero = jnp.zeros_like(x_re)
    y_re, y_im = lax.fori_loop(0, n_blocks, one, (zero, zero))
    both = jnp.concatenate([y_re, y_im], axis=1)
    return jnp.einsum("tk,jkc->jtc", bwd32, both, precision=exact).astype(BF16)


def gate_kernel(queries_ref, keys_ref, values_ref, skip_ref, *refs):
    *conv_refs, out_ref = refs
    chans = conv_refs[0].shape[1]
    for slot, conv_ref in zip(slots_of(len(conv_refs), True), conv_refs):
        at = peer_block(slot, chans)
        product = keys_ref[:, at].astype(F32) * values_ref[:, at].astype(F32)
        mixed = conv_ref[...].astype(F32) + skip_ref[:, at] * product
        out_ref[:, at] = (queries_ref[:, at].astype(F32) * mixed).astype(BF16)


def gate(queries, keys, values, skip, conv):
    rows, width = queries.shape
    whole = pl.BlockSpec(memory_space=pltpu.VMEM)
    return pl.pallas_call(
        gate_kernel,
        in_specs=[whole] * (4 + len(conv)),
        out_specs=whole,
        out_shape=jax.ShapeDtypeStruct((rows, width), BF16),
        compiler_params=pltpu.CompilerParams(vmem_limit_bytes=SMALL_VMEM),
        cost_estimate=pl.CostEstimate(
            flops=4 * rows * width, bytes_accessed=10 * rows * width, transcendentals=0
        ),
    )(queries, keys, values, skip, *conv)


def side_columns(across, out_width):
    place = lax.axis_index("fsdp")
    core, side = lax.rem(place, 2), lax.div(place, 2)
    side = jnp.where(across, 1 - side, side)
    return pl.multiple_of((2 * side + core) * out_width, out_width)


def project_kernel(across, first, mine_ref, theirs_ref, own_w_ref, their_w_ref, out_ref):
    width = out_ref.shape[1]
    start = side_columns(across, own_w_ref.shape[1] // 4) + first
    at = pl.ds(pl.multiple_of(start, width), width)
    total = jnp.dot(mine_ref[...], own_w_ref[:, at], preferred_element_type=F32)
    total += jnp.dot(theirs_ref[...], their_w_ref[:, at], preferred_element_type=F32)
    out_ref[...] = total.astype(out_ref.dtype)


def project(mine, theirs, own_weight, their_weight, across, first, width, dtype):
    rows, depth = mine.shape
    return pl.pallas_call(
        functools.partial(project_kernel, across, first),
        in_specs=[pl.BlockSpec(memory_space=pltpu.VMEM)] * 4,
        out_specs=pl.BlockSpec(memory_space=pltpu.VMEM),
        out_shape=jax.ShapeDtypeStruct((rows, width), dtype),
        compiler_params=pltpu.CompilerParams(vmem_limit_bytes=PROJECT_VMEM),
        cost_estimate=pl.CostEstimate(
            flops=4 * rows * depth * width, bytes_accessed=4 * depth * width, transcendentals=0
        ),
    )(mine, theirs, own_weight, their_weight)


def finish_kernel(own_ref, *refs):
    *arrived_refs, out_ref = refs
    width = out_ref.shape[1] // len(arrived_refs)
    for c, arrived_ref in enumerate(arrived_refs):
        at = slice(c * width, (c + 1) * width)
        out_ref[:, at] = (own_ref[:, at] + arrived_ref[...].astype(F32)).astype(out_ref.dtype)


def finish(own, arrived):
    rows, width = own.shape
    whole = pl.BlockSpec(memory_space=pltpu.VMEM)
    return pl.pallas_call(
        finish_kernel,
        in_specs=[whole] * (1 + len(arrived)),
        out_specs=whole,
        out_shape=jax.ShapeDtypeStruct((rows, width), BF16),
        compiler_params=pltpu.CompilerParams(vmem_limit_bytes=SMALL_VMEM),
        cost_estimate=pl.CostEstimate(
            flops=rows * width, bytes_accessed=8 * rows * width, transcendentals=0
        ),
    )(own, *arrived)


def body(pieces, tables, queries, keys, values, filters, skip_weight, out_weight):
    rows, width = keys.shape
    n_peers = lax.axis_size("seq")
    chans = width // n_peers
    fwd, bwd = (jnp.asarray(t) for t in tables)
    skip = skip_weight[None, :]
    in_chip = [(0, 1), (1, 0), (2, 3), (3, 2)]
    across = [(0, 2), (2, 0), (1, 3), (3, 1)]

    if chans % 128 == 0 and n_peers in (8, 16):
        blocks, fwd, bwd = pre(keys, values, filters, fwd, bwd, n_peers)
        received = exchange(blocks, n_peers, False)
        out_weight, received = lax.optimization_barrier((out_weight, received))
        their_weight = lax.ppermute(out_weight, "fsdp", in_chip)
        back = exchange(conv_fast(received, fwd, bwd), n_peers, True)
        gated = gate(queries, keys, values, skip, back)
    else:
        their_weight = lax.ppermute(out_weight, "fsdp", in_chip)
        product = keys.astype(F32) * values.astype(F32)
        parts = [a.astype(BF16).reshape(rows, n_peers, chans) for a in (product, filters)]
        sent = jnp.concatenate(parts, axis=2).transpose(1, 0, 2)
        received = lax.all_to_all(sent, "seq", split_axis=0, concat_axis=0, tiled=True)
        conv = conv_plain(received, fwd, bwd)
        back = lax.all_to_all(conv, "seq", split_axis=0, concat_axis=0, tiled=True)
        mixed = back.transpose(1, 0, 2).reshape(rows, width).astype(F32) + skip * product
        gated = (queries.astype(F32) * mixed).astype(BF16)

    theirs = lax.ppermute(gated, "fsdp", in_chip)
    out_width = out_weight.shape[1] // 4
    piece = out_width // pieces
    arrived = []
    for c in range(pieces):
        remote = project(gated, theirs, out_weight, their_weight, True, c * piece, piece, BF16)
        arrived.append(lax.ppermute(remote, "fsdp", across))
    own = project(gated, theirs, out_weight, their_weight, False, 0, out_width, F32)
    return finish(own, arrived)


def solution(mesh):
    in_specs = (
        P("seq", "fsdp"),
        P("seq", "fsdp"),
        P("seq", "fsdp"),
        P("seq", "fsdp"),
        P("fsdp"),
        P("fsdp", None),
    )
    out_specs = P("seq", "fsdp")

    def run(queries, keys, values, filters, skip_weight, out_weight):
        rows = keys.shape[0] // mesh.shape["seq"]
        fn = functools.partial(body, 2, make_tables(rows))
        return jax.shard_map(fn, mesh=mesh, in_specs=in_specs, out_specs=out_specs, check_vma=False)(
            queries, keys, values, filters, skip_weight, out_weight
        )

    return run
```

```python
import functools

import numpy as np

import jax
import jax.numpy as jnp
from jax import lax
from jax.experimental import pallas as pl
from jax.experimental.pallas import tpu as pltpu
from jax.sharding import PartitionSpec as P

BF16 = jnp.bfloat16
F32 = jnp.float32
CONV_VMEM = 24 * 2**20
PROJECT_VMEM = 24 * 2**20
SMALL_VMEM = 12 * 2**20


def split_bf16(table):
    high = table.astype(BF16)
    return high, (table - high.astype(np.float64)).astype(BF16)


def make_tables(rows):
    order = np.concatenate([np.arange(0, rows, 2), np.arange(1, rows, 2)])
    times = np.arange(rows)
    angle = np.pi * (((2 * order[:, None] + 1) * times[None, :]) % (4 * rows)) / (2 * rows)
    forward = np.concatenate([np.cos(angle), -np.sin(angle)], axis=0)
    high, low = split_bf16(forward)
    back_high, back_low = split_bf16(forward.T / rows)
    return (
        np.concatenate([high, low], axis=1),
        np.concatenate([back_high, back_low, back_high], axis=1),
    )


def peer_of(slot):
    return lax.bitwise_xor(lax.axis_index("seq"), slot)


def peer_block(slot, size):
    return pl.ds(pl.multiple_of(peer_of(slot) * size, size), size)


def pre_kernel(n_peers, keys_hbm, values_hbm, filters_hbm, *refs):
    out_refs = refs[:n_peers]
    keys, values, filters, sem = refs[n_peers:]
    rows, width = keys.shape
    chans = width // n_peers
    steps = sem.shape[0]
    parts = [pl.ds(c * rows // steps, rows // steps) for c in range(steps)]
    pairs = ((keys_hbm, keys), (values_hbm, values), (filters_hbm, filters))
    copies = [
        [
            pltpu.make_async_copy(src.at[part], dst.at[part], sem.at[c, i])
            for i, (src, dst) in enumerate(pairs)
        ]
        for c, part in enumerate(parts)
    ]
    for group in copies:
        for copy in group:
            copy.start()
    for part, group in zip(parts, copies):
        for copy in group:
            copy.wait()
        for slot, out_ref in zip(slots_of(n_peers, False), out_refs):
            at = peer_block(slot, chans)
            product = keys[part, at].astype(F32) * values[part, at].astype(F32)
            out_ref[part, :chans] = product.astype(BF16)
            out_ref[part, chans:] = filters[part, at].astype(BF16)


def pre(keys, values, filters, n_peers):
    rows, width = keys.shape
    chans = width // n_peers
    args = [pltpu.with_memory_space_constraint(a, pltpu.HBM) for a in (keys, values, filters)]
    return pl.pallas_call(
        functools.partial(pre_kernel, n_peers),
        in_specs=[pl.BlockSpec(memory_space=pltpu.HBM)] * 3,
        out_specs=[pl.BlockSpec(memory_space=pltpu.VMEM)] * n_peers,
        out_shape=[jax.ShapeDtypeStruct((rows, 2 * chans), BF16)] * n_peers,
        scratch_shapes=[
            pltpu.VMEM((rows, width), BF16),
            pltpu.VMEM((rows, width), BF16),
            pltpu.VMEM((rows, width), F32),
            pltpu.SemaphoreType.DMA((2, 3)),
        ],
        compiler_params=pltpu.CompilerParams(vmem_limit_bytes=SMALL_VMEM),
        cost_estimate=pl.CostEstimate(
            flops=rows * width, bytes_accessed=12 * rows * width, transcendentals=0
        ),
    )(*args)


def slots_of(n_peers, back):
    half = n_peers // 2
    near, far = list(range(1, half)), list(range(half, n_peers))
    if back:
        return [0, near[0]] + far[:3] + [near[1]] + far[3:] + near[2:]
    return [0, near[0], far[0], near[1], far[1]] + near[2:] + far[2:]


def exchange(blocks, n_peers, back):
    return [
        lax.ppermute(block, "seq", [(i, i ^ slot) for i in range(n_peers)]) if slot else block
        for slot, block in zip(slots_of(n_peers, back), blocks)
    ]


def block_spectrum(table, block):
    return jnp.dot(table, jnp.concatenate([block, block], axis=0), preferred_element_type=F32)


def spectra_kernel(n_peers, fwd_hbm, bwd_hbm, *refs):
    *in_refs, fwd_ref, bwd_ref, spec_ref, sem = refs
    copies = [
        pltpu.make_async_copy(fwd_hbm, fwd_ref, sem.at[0]),
        pltpu.make_async_copy(bwd_hbm, bwd_ref, sem.at[1]),
    ]
    for copy in copies:
        copy.start()
    for copy in copies:
        copy.wait()
    for slot, in_ref in zip(slots_of(n_peers, False), in_refs):
        spec_ref[peer_of(slot)] = block_spectrum(fwd_ref[...], in_ref[...])


def spectra(received, fwd, bwd, n_peers):
    rows, width = received[0].shape
    whole = pl.BlockSpec(memory_space=pltpu.VMEM)
    args = [pltpu.with_memory_space_constraint(a, pltpu.HBM) for a in (fwd, bwd)]
    return pl.pallas_call(
        functools.partial(spectra_kernel, n_peers),
        in_specs=[pl.BlockSpec(memory_space=pltpu.HBM)] * 2 + [whole] * len(received),
        out_specs=[whole] * 3,
        out_shape=[
            jax.ShapeDtypeStruct(fwd.shape, BF16),
            jax.ShapeDtypeStruct(bwd.shape, BF16),
            jax.ShapeDtypeStruct((n_peers, 2 * rows, width), F32),
        ],
        scratch_shapes=[pltpu.SemaphoreType.DMA((2,))],
        compiler_params=pltpu.CompilerParams(vmem_limit_bytes=CONV_VMEM),
        cost_estimate=pl.CostEstimate(
            flops=8 * len(received) * rows * rows * width, bytes_accessed=4 * 2**20, transcendentals=0
        ),
    )(*args, *received)


def conv_kernel(fwd_ref, bwd_ref, early_ref, *refs):
    *refs, late, held, turned = refs
    n_blocks, step = early_ref.shape[0], held.shape[2]
    in_refs, out_refs = refs[:-n_blocks], refs[-n_blocks:]
    rows, chans = in_refs[0].shape[0], in_refs[0].shape[1] // 2
    late_slots = slots_of(n_blocks, False)[-2:]
    for slot, in_ref in zip(late_slots, in_refs):
        late[lax.bitwise_and(peer_of(slot), 1)] = block_spectrum(fwd_ref[...], in_ref[...])
    late_pair = lax.div(peer_of(late_slots[0]), 2)

    def spectrum(j, at, lanes):
        return jnp.where(late_pair == j // 2, late[j % 2, at, lanes], early_ref[j, at, lanes])

    def mix(row, sign):
        re, im = pl.ds(row, step), pl.ds(row + rows, step)
        x_at, f_at = slice(0, chans), slice(chans, 2 * chans)
        gains = []
        last_re = last_im = None
        for j in range(n_blocks):
            held[j, 0] = spectrum(j, re, x_at)
            held[j, 1] = spectrum(j, im, x_at)
            f_re, f_im = spectrum(j, re, f_at), spectrum(j, im, f_at)
            if j == 0:
                gains.append((f_re, f_im))
            else:
                gains.append((f_re - sign * last_im, f_im + sign * last_re))
            last_re, last_im = f_re, f_im
        for i in range(n_blocks):
            out_re = out_im = None
            for d in range(i + 1):
                (g_re, g_im), x_re, x_im = gains[d], held[i - d, 0], held[i - d, 1]
                t_re = g_re * x_re - g_im * x_im
                t_im = g_re * x_im + g_im * x_re
                out_re = t_re if d == 0 else out_re + t_re
                out_im = t_im if d == 0 else out_im + t_im
            lanes = slice(i % 2 * chans, (i % 2 + 1) * chans)
            for first, value in ((row, out_re), (row + rows, out_im)):
                high = value.astype(BF16)
                low = (value - high.astype(F32)).astype(BF16)
                for part, piece in enumerate((high, high, low)):
                    turned[i // 2, pl.ds(first + 2 * part * rows, step), lanes] = piece

    half = rows // 2

    @pl.loop(0, half // step)
    def _(t):
        mix(pl.multiple_of(t * step, step), 1.0)

    @pl.loop(half // step, rows // step)
    def _(t):
        mix(pl.multiple_of(t * step, step), -1.0)

    odd = lax.bitwise_and(lax.axis_index("seq"), 1) == 1
    by_slot = dict(zip(slots_of(n_blocks, True), out_refs))
    for slot in range(0, n_blocks, 2):
        pair = lax.div(peer_of(slot), 2)
        both = jnp.dot(bwd_ref[...], turned[pair], preferred_element_type=F32)
        left, right = both[:, :chans], both[:, chans:]
        by_slot[slot][...] = jnp.where(odd, right, left).astype(BF16)
        by_slot[slot + 1][...] = jnp.where(odd, left, right).astype(BF16)


def conv_fast(early, late, fwd, bwd):
    n_blocks = early.shape[0]
    rows, chans = late[0].shape[0], late[0].shape[1] // 2
    step = 16
    whole = pl.BlockSpec(memory_space=pltpu.VMEM)
    return pl.pallas_call(
        conv_kernel,
        in_specs=[whole] * 5,
        out_specs=[whole] * n_blocks,
        out_shape=[jax.ShapeDtypeStruct((rows, chans), BF16)] * n_blocks,
        scratch_shapes=[
            pltpu.VMEM((2, 2 * rows, 2 * chans), F32),
            pltpu.VMEM((n_blocks, 2, step, chans), F32),
            pltpu.VMEM((n_blocks // 2, 6 * rows, 2 * chans), BF16),
        ],
        compiler_params=pltpu.CompilerParams(vmem_limit_bytes=CONV_VMEM),
        cost_estimate=pl.CostEstimate(
            flops=16 * n_blocks * rows * rows * chans, bytes_accessed=4 * 2**20, transcendentals=0
        ),
    )(fwd, bwd, early, *late)


def conv_plain(received, fwd, bwd):
    n_blocks, rows, chans = received.shape[0], received.shape[1], received.shape[2] // 2
    exact = lax.Precision.HIGHEST
    fwd32 = fwd[:, :rows].astype(F32) + fwd[:, rows:].astype(F32)
    bwd32 = bwd[:, : 2 * rows].astype(F32) + bwd[:, 2 * rows : 4 * rows].astype(F32)
    sign = jnp.where(jnp.arange(rows) < rows // 2, 1.0, -1.0).astype(F32)[:, None]

    def spectrum(blocks):
        spec = jnp.einsum("kt,jtc->jkc", fwd32, blocks.astype(F32), precision=exact)
        return spec[:, :rows], spec[:, rows:]

    x_re, x_im = spectrum(received[:, :, :chans])
    f_re, f_im = spectrum(received[:, :, chans:])
    g_re = f_re.at[1:].add(-sign * f_im[:-1])
    g_im = f_im.at[1:].add(sign * f_re[:-1])

    def one(d, total):
        t_re, t_im = total
        later = (jnp.arange(n_blocks) >= d)[:, None, None]
        a_re = jnp.where(later, jnp.roll(x_re, d, axis=0), 0.0)
        a_im = jnp.where(later, jnp.roll(x_im, d, axis=0), 0.0)
        return (
            t_re + g_re[d] * a_re - g_im[d] * a_im,
            t_im + g_re[d] * a_im + g_im[d] * a_re,
        )

    zero = jnp.zeros_like(x_re)
    y_re, y_im = lax.fori_loop(0, n_blocks, one, (zero, zero))
    both = jnp.concatenate([y_re, y_im], axis=1)
    return jnp.einsum("tk,jkc->jtc", bwd32, both, precision=exact).astype(BF16)


def gate_kernel(queries_ref, keys_ref, values_ref, skip_ref, *refs):
    *conv_refs, out_ref = refs
    chans = conv_refs[0].shape[1]
    for slot, conv_ref in zip(slots_of(len(conv_refs), True), conv_refs):
        at = peer_block(slot, chans)
        product = keys_ref[:, at].astype(F32) * values_ref[:, at].astype(F32)
        mixed = conv_ref[...].astype(F32) + skip_ref[:, at] * product
        out_ref[:, at] = (queries_ref[:, at].astype(F32) * mixed).astype(BF16)


def gate(queries, keys, values, skip, conv):
    rows, width = queries.shape
    whole = pl.BlockSpec(memory_space=pltpu.VMEM)
    return pl.pallas_call(
        gate_kernel,
        in_specs=[whole] * (4 + len(conv)),
        out_specs=whole,
        out_shape=jax.ShapeDtypeStruct((rows, width), BF16),
        compiler_params=pltpu.CompilerParams(vmem_limit_bytes=SMALL_VMEM),
        cost_estimate=pl.CostEstimate(
            flops=4 * rows * width, bytes_accessed=10 * rows * width, transcendentals=0
        ),
    )(queries, keys, values, skip, *conv)


def side_columns(across, out_width):
    place = lax.axis_index("fsdp")
    core, side = lax.rem(place, 2), lax.div(place, 2)
    side = jnp.where(across, 1 - side, side)
    return pl.multiple_of((2 * side + core) * out_width, out_width)


def project_kernel(across, first, mine_ref, theirs_ref, own_w_ref, their_w_ref, out_ref):
    width = out_ref.shape[1]
    start = side_columns(across, own_w_ref.shape[1] // 4) + first
    at = pl.ds(pl.multiple_of(start, width), width)
    total = jnp.dot(mine_ref[...], own_w_ref[:, at], preferred_element_type=F32)
    total += jnp.dot(theirs_ref[...], their_w_ref[:, at], preferred_element_type=F32)
    out_ref[...] = total.astype(out_ref.dtype)


def project(mine, theirs, own_weight, their_weight, across, first, width, dtype):
    rows, depth = mine.shape
    return pl.pallas_call(
        functools.partial(project_kernel, across, first),
        in_specs=[pl.BlockSpec(memory_space=pltpu.VMEM)] * 4,
        out_specs=pl.BlockSpec(memory_space=pltpu.VMEM),
        out_shape=jax.ShapeDtypeStruct((rows, width), dtype),
        compiler_params=pltpu.CompilerParams(vmem_limit_bytes=PROJECT_VMEM),
        cost_estimate=pl.CostEstimate(
            flops=4 * rows * depth * width, bytes_accessed=4 * depth * width, transcendentals=0
        ),
    )(mine, theirs, own_weight, their_weight)


def finish_kernel(own_ref, *refs):
    *arrived_refs, out_ref = refs
    width = out_ref.shape[1] // len(arrived_refs)
    for c, arrived_ref in enumerate(arrived_refs):
        at = slice(c * width, (c + 1) * width)
        out_ref[:, at] = (own_ref[:, at] + arrived_ref[...].astype(F32)).astype(out_ref.dtype)


def finish(own, arrived):
    rows, width = own.shape
    whole = pl.BlockSpec(memory_space=pltpu.VMEM)
    return pl.pallas_call(
        finish_kernel,
        in_specs=[whole] * (1 + len(arrived)),
        out_specs=whole,
        out_shape=jax.ShapeDtypeStruct((rows, width), BF16),
        compiler_params=pltpu.CompilerParams(vmem_limit_bytes=SMALL_VMEM),
        cost_estimate=pl.CostEstimate(
            flops=rows * width, bytes_accessed=8 * rows * width, transcendentals=0
        ),
    )(own, *arrived)


def body(pieces, tables, queries, keys, values, filters, skip_weight, out_weight):
    rows, width = keys.shape
    n_peers = lax.axis_size("seq")
    chans = width // n_peers
    fwd, bwd = (jnp.asarray(t) for t in tables)
    skip = skip_weight[None, :]
    in_chip = [(0, 1), (1, 0), (2, 3), (3, 2)]
    across = [(0, 2), (2, 0), (1, 3), (3, 1)]

    their_weight = lax.ppermute(out_weight, "fsdp", in_chip)

    if chans % 128 == 0 and n_peers == 8:
        blocks = pre(keys, values, filters, n_peers)
        received = exchange(blocks, n_peers, False)
        fwd, bwd, early = spectra(received[:-2], fwd, bwd, n_peers)
        their_weight, early = lax.optimization_barrier((their_weight, early))
        back = exchange(conv_fast(early, received[-2:], fwd, bwd), n_peers, True)
        gated = gate(queries, keys, values, skip, back)
    else:
        product = keys.astype(F32) * values.astype(F32)
        parts = [a.astype(BF16).reshape(rows, n_peers, chans) for a in (product, filters)]
        sent = jnp.concatenate(parts, axis=2).transpose(1, 0, 2)
        received = lax.all_to_all(sent, "seq", split_axis=0, concat_axis=0, tiled=True)
        conv = conv_plain(received, fwd, bwd)
        back = lax.all_to_all(conv, "seq", split_axis=0, concat_axis=0, tiled=True)
        mixed = back.transpose(1, 0, 2).reshape(rows, width).astype(F32) + skip * product
        gated = (queries.astype(F32) * mixed).astype(BF16)

    theirs = lax.ppermute(gated, "fsdp", in_chip)
    out_width = out_weight.shape[1] // 4
    piece = out_width // pieces
    arrived = []
    for c in range(pieces):
        remote = project(gated, theirs, out_weight, their_weight, True, c * piece, piece, BF16)
        arrived.append(lax.ppermute(remote, "fsdp", across))
    own = project(gated, theirs, out_weight, their_weight, False, 0, out_width, F32)
    return finish(own, arrived)


def solution(mesh):
    in_specs = (
        P("seq", "fsdp"),
        P("seq", "fsdp"),
        P("seq", "fsdp"),
        P("seq", "fsdp"),
        P("fsdp"),
        P("fsdp", None),
    )
    out_specs = P("seq", "fsdp")

    def run(queries, keys, values, filters, skip_weight, out_weight):
        rows = keys.shape[0] // mesh.shape["seq"]
        fn = functools.partial(body, 2, make_tables(rows))
        return jax.shard_map(fn, mesh=mesh, in_specs=in_specs, out_specs=out_specs, check_vma=False)(
            queries, keys, values, filters, skip_weight, out_weight
        )

    return run
```

```python
import functools

import numpy as np

import jax
import jax.numpy as jnp
from jax import lax
from jax.experimental import pallas as pl
from jax.experimental.pallas import tpu as pltpu
from jax.sharding import PartitionSpec as P

BF16 = jnp.bfloat16
F32 = jnp.float32
CONV_VMEM = 24 * 2**20
PROJECT_VMEM = 24 * 2**20
SMALL_VMEM = 12 * 2**20


def split_bf16(table):
    high = table.astype(BF16)
    return high, (table - high.astype(np.float64)).astype(BF16)


def make_tables(rows):
    order = np.concatenate([np.arange(0, rows, 2), np.arange(1, rows, 2)])
    times = np.arange(rows)
    angle = np.pi * (((2 * order[:, None] + 1) * times[None, :]) % (4 * rows)) / (2 * rows)
    forward = np.concatenate([np.cos(angle), -np.sin(angle)], axis=0)
    high, low = split_bf16(forward)
    back_high, back_low = split_bf16(forward.T / rows)
    return (
        np.concatenate([high, low], axis=1),
        np.concatenate([back_high, back_low, back_high], axis=1),
    )


def peer_of(slot):
    return lax.bitwise_xor(lax.axis_index("seq"), slot)


def peer_block(slot, size):
    return pl.ds(pl.multiple_of(peer_of(slot) * size, size), size)


def pre_kernel(n_peers, keys_hbm, values_hbm, filters_hbm, *refs):
    out_refs = refs[:n_peers]
    keys, values, filters, sem = refs[n_peers:]
    rows, width = keys.shape
    chans = width // n_peers
    steps = sem.shape[0]
    parts = [pl.ds(c * rows // steps, rows // steps) for c in range(steps)]
    pairs = ((keys_hbm, keys), (values_hbm, values), (filters_hbm, filters))
    copies = [
        [
            pltpu.make_async_copy(src.at[part], dst.at[part], sem.at[c, i])
            for i, (src, dst) in enumerate(pairs)
        ]
        for c, part in enumerate(parts)
    ]
    for group in copies:
        for copy in group:
            copy.start()
    for part, group in zip(parts, copies):
        for copy in group:
            copy.wait()
        for slot, out_ref in zip(slots_of(n_peers, False), out_refs):
            at = peer_block(slot, chans)
            product = keys[part, at].astype(F32) * values[part, at].astype(F32)
            out_ref[part, :chans] = product.astype(BF16)
            out_ref[part, chans:] = filters[part, at].astype(BF16)


def pre(keys, values, filters, n_peers):
    rows, width = keys.shape
    chans = width // n_peers
    args = [pltpu.with_memory_space_constraint(a, pltpu.HBM) for a in (keys, values, filters)]
    return pl.pallas_call(
        functools.partial(pre_kernel, n_peers),
        in_specs=[pl.BlockSpec(memory_space=pltpu.HBM)] * 3,
        out_specs=[pl.BlockSpec(memory_space=pltpu.VMEM)] * n_peers,
        out_shape=[jax.ShapeDtypeStruct((rows, 2 * chans), BF16)] * n_peers,
        scratch_shapes=[
            pltpu.VMEM((rows, width), BF16),
            pltpu.VMEM((rows, width), BF16),
            pltpu.VMEM((rows, width), F32),
            pltpu.SemaphoreType.DMA((2, 3)),
        ],
        compiler_params=pltpu.CompilerParams(vmem_limit_bytes=SMALL_VMEM),
        cost_estimate=pl.CostEstimate(
            flops=rows * width, bytes_accessed=12 * rows * width, transcendentals=0
        ),
    )(*args)


def slots_of(n_peers, back):
    half = n_peers // 2
    near, far = list(range(1, half)), list(range(half, n_peers))
    if back:
        return [0, near[0]] + far[:3] + [near[1]] + far[3:] + near[2:]
    return [0, near[0], far[0], near[1], far[1]] + near[2:] + far[2:]


def exchange(blocks, n_peers, back):
    return [
        lax.ppermute(block, "seq", [(i, i ^ slot) for i in range(n_peers)]) if slot else block
        for slot, block in zip(slots_of(n_peers, back), blocks)
    ]


def block_spectrum(table, block):
    return jnp.dot(table, jnp.concatenate([block, block], axis=0), preferred_element_type=F32)


def spectra_kernel(n_peers, fwd_hbm, bwd_hbm, *refs):
    *in_refs, fwd_ref, bwd_ref, spec_ref, sem = refs
    copies = [
        pltpu.make_async_copy(fwd_hbm, fwd_ref, sem.at[0]),
        pltpu.make_async_copy(bwd_hbm, bwd_ref, sem.at[1]),
    ]
    for copy in copies:
        copy.start()
    for copy in copies:
        copy.wait()
    for slot, in_ref in zip(slots_of(n_peers, False), in_refs):
        spec_ref[peer_of(slot)] = block_spectrum(fwd_ref[...], in_ref[...])


def spectra(received, fwd, bwd, n_peers):
    rows, width = received[0].shape
    whole = pl.BlockSpec(memory_space=pltpu.VMEM)
    args = [pltpu.with_memory_space_constraint(a, pltpu.HBM) for a in (fwd, bwd)]
    return pl.pallas_call(
        functools.partial(spectra_kernel, n_peers),
        in_specs=[pl.BlockSpec(memory_space=pltpu.HBM)] * 2 + [whole] * len(received),
        out_specs=[whole] * 3,
        out_shape=[
            jax.ShapeDtypeStruct(fwd.shape, BF16),
            jax.ShapeDtypeStruct(bwd.shape, BF16),
            jax.ShapeDtypeStruct((n_peers, 2 * rows, width), F32),
        ],
        scratch_shapes=[pltpu.SemaphoreType.DMA((2,))],
        compiler_params=pltpu.CompilerParams(vmem_limit_bytes=CONV_VMEM),
        cost_estimate=pl.CostEstimate(
            flops=8 * len(received) * rows * rows * width, bytes_accessed=4 * 2**20, transcendentals=0
        ),
    )(*args, *received)


def conv_kernel(fwd_ref, bwd_ref, early_ref, *refs):
    *refs, late, held, turned = refs
    n_blocks, step = early_ref.shape[0], held.shape[2]
    in_refs, out_refs = refs[:-n_blocks], refs[-n_blocks:]
    rows, chans = in_refs[0].shape[0], in_refs[0].shape[1] // 2
    late_slots = slots_of(n_blocks, False)[-2:]
    for slot, in_ref in zip(late_slots, in_refs):
        late[lax.bitwise_and(peer_of(slot), 1)] = block_spectrum(fwd_ref[...], in_ref[...])
    late_pair = lax.div(peer_of(late_slots[0]), 2)

    def spectrum(j, at, lanes):
        return jnp.where(late_pair == j // 2, late[j % 2, at, lanes], early_ref[j, at, lanes])

    def mix(row, sign):
        re, im = pl.ds(row, step), pl.ds(row + rows, step)
        x_at, f_at = slice(0, chans), slice(chans, 2 * chans)
        gains = []
        last_re = last_im = None
        for j in range(n_blocks):
            held[j, 0] = spectrum(j, re, x_at)
            held[j, 1] = spectrum(j, im, x_at)
            f_re, f_im = spectrum(j, re, f_at), spectrum(j, im, f_at)
            if j == 0:
                gains.append((f_re, f_im))
            else:
                gains.append((f_re - sign * last_im, f_im + sign * last_re))
            last_re, last_im = f_re, f_im
        for i in range(n_blocks):
            out_re = out_im = None
            for d in range(i + 1):
                (g_re, g_im), x_re, x_im = gains[d], held[i - d, 0], held[i - d, 1]
                t_re = g_re * x_re - g_im * x_im
                t_im = g_re * x_im + g_im * x_re
                out_re = t_re if d == 0 else out_re + t_re
                out_im = t_im if d == 0 else out_im + t_im
            lanes = slice(i % 2 * chans, (i % 2 + 1) * chans)
            for first, value in ((row, out_re), (row + rows, out_im)):
                high = value.astype(BF16)
                low = (value - high.astype(F32)).astype(BF16)
                for part, piece in enumerate((high, high, low)):
                    turned[i // 2, pl.ds(first + 2 * part * rows, step), lanes] = piece

    half = rows // 2

    @pl.loop(0, half // step)
    def _(t):
        mix(pl.multiple_of(t * step, step), 1.0)

    @pl.loop(half // step, rows // step)
    def _(t):
        mix(pl.multiple_of(t * step, step), -1.0)

    odd = lax.bitwise_and(lax.axis_index("seq"), 1) == 1
    by_slot = dict(zip(slots_of(n_blocks, True), out_refs))
    for slot in range(0, n_blocks, 2):
        pair = lax.div(peer_of(slot), 2)
        both = jnp.dot(bwd_ref[...], turned[pair], preferred_element_type=F32)
        left, right = both[:, :chans], both[:, chans:]
        by_slot[slot][...] = jnp.where(odd, right, left).astype(BF16)
        by_slot[slot + 1][...] = jnp.where(odd, left, right).astype(BF16)


def conv_fast(early, late, fwd, bwd):
    n_blocks = early.shape[0]
    rows, chans = late[0].shape[0], late[0].shape[1] // 2
    step = 16
    whole = pl.BlockSpec(memory_space=pltpu.VMEM)
    return pl.pallas_call(
        conv_kernel,
        in_specs=[whole] * 5,
        out_specs=[whole] * n_blocks,
        out_shape=[jax.ShapeDtypeStruct((rows, chans), BF16)] * n_blocks,
        scratch_shapes=[
            pltpu.VMEM((2, 2 * rows, 2 * chans), F32),
            pltpu.VMEM((n_blocks, 2, step, chans), F32),
            pltpu.VMEM((n_blocks // 2, 6 * rows, 2 * chans), BF16),
        ],
        compiler_params=pltpu.CompilerParams(vmem_limit_bytes=CONV_VMEM),
        cost_estimate=pl.CostEstimate(
            flops=16 * n_blocks * rows * rows * chans, bytes_accessed=4 * 2**20, transcendentals=0
        ),
    )(fwd, bwd, early, *late)


def conv_plain(received, fwd, bwd):
    n_blocks, rows, chans = received.shape[0], received.shape[1], received.shape[2] // 2
    exact = lax.Precision.HIGHEST
    fwd32 = fwd[:, :rows].astype(F32) + fwd[:, rows:].astype(F32)
    bwd32 = bwd[:, : 2 * rows].astype(F32) + bwd[:, 2 * rows : 4 * rows].astype(F32)
    sign = jnp.where(jnp.arange(rows) < rows // 2, 1.0, -1.0).astype(F32)[:, None]

    def spectrum(blocks):
        spec = jnp.einsum("kt,jtc->jkc", fwd32, blocks.astype(F32), precision=exact)
        return spec[:, :rows], spec[:, rows:]

    x_re, x_im = spectrum(received[:, :, :chans])
    f_re, f_im = spectrum(received[:, :, chans:])
    g_re = f_re.at[1:].add(-sign * f_im[:-1])
    g_im = f_im.at[1:].add(sign * f_re[:-1])

    def one(d, total):
        t_re, t_im = total
        later = (jnp.arange(n_blocks) >= d)[:, None, None]
        a_re = jnp.where(later, jnp.roll(x_re, d, axis=0), 0.0)
        a_im = jnp.where(later, jnp.roll(x_im, d, axis=0), 0.0)
        return (
            t_re + g_re[d] * a_re - g_im[d] * a_im,
            t_im + g_re[d] * a_im + g_im[d] * a_re,
        )

    zero = jnp.zeros_like(x_re)
    y_re, y_im = lax.fori_loop(0, n_blocks, one, (zero, zero))
    both = jnp.concatenate([y_re, y_im], axis=1)
    return jnp.einsum("tk,jkc->jtc", bwd32, both, precision=exact).astype(BF16)


def gate_kernel(queries_ref, keys_ref, values_ref, skip_ref, *refs):
    *conv_refs, out_ref = refs
    chans = conv_refs[0].shape[1]
    for slot, conv_ref in zip(slots_of(len(conv_refs), True), conv_refs):
        at = peer_block(slot, chans)
        product = keys_ref[:, at].astype(F32) * values_ref[:, at].astype(F32)
        mixed = conv_ref[...].astype(F32) + skip_ref[:, at] * product
        out_ref[:, at] = (queries_ref[:, at].astype(F32) * mixed).astype(BF16)


def gate(queries, keys, values, skip, conv):
    rows, width = queries.shape
    whole = pl.BlockSpec(memory_space=pltpu.VMEM)
    return pl.pallas_call(
        gate_kernel,
        in_specs=[whole] * (4 + len(conv)),
        out_specs=whole,
        out_shape=jax.ShapeDtypeStruct((rows, width), BF16),
        compiler_params=pltpu.CompilerParams(vmem_limit_bytes=SMALL_VMEM),
        cost_estimate=pl.CostEstimate(
            flops=4 * rows * width, bytes_accessed=10 * rows * width, transcendentals=0
        ),
    )(queries, keys, values, skip, *conv)


def weight_block(weight_ref, other, across, piece, pieces):
    width = weight_ref.shape[1] // 4 // pieces
    place = lax.axis_index("fsdp")
    core, side = lax.rem(place, 2), lax.div(place, 2)
    block = 2 * (1 - side if across else side) + (1 - core if other else core)
    return weight_ref[:, pl.ds(pl.multiple_of((block * pieces + piece) * width, width), width)]


def project_kernel(blocks, gated_ref, weight_ref, *out_refs):
    for block, out_ref in zip(blocks, out_refs):
        columns = weight_block(weight_ref, *block)
        total = jnp.dot(gated_ref[...], columns, preferred_element_type=F32)
        out_ref[...] = total.astype(out_ref.dtype)


def project(gated, weight, blocks, dtypes):
    rows, depth = gated.shape
    widths = [weight.shape[1] // 4 // pieces for *_, pieces in blocks]
    whole = pl.BlockSpec(memory_space=pltpu.VMEM)
    return pl.pallas_call(
        functools.partial(project_kernel, blocks),
        in_specs=[whole] * 2,
        out_specs=[whole] * len(blocks),
        out_shape=[jax.ShapeDtypeStruct((rows, w), t) for w, t in zip(widths, dtypes)],
        compiler_params=pltpu.CompilerParams(vmem_limit_bytes=PROJECT_VMEM),
        cost_estimate=pl.CostEstimate(
            flops=2 * rows * depth * sum(widths), bytes_accessed=2 * depth * sum(widths), transcendentals=0
        ),
    )(gated, weight)


def add_kernel(own_ref, arrived_ref, out_ref):
    total = own_ref[...] + arrived_ref[...].astype(F32)
    out_ref[...] = total.astype(out_ref.dtype)


def add(own, arrived):
    whole = pl.BlockSpec(memory_space=pltpu.VMEM)
    return pl.pallas_call(
        add_kernel,
        in_specs=[whole] * 2,
        out_specs=whole,
        out_shape=jax.ShapeDtypeStruct(arrived.shape, BF16),
        compiler_params=pltpu.CompilerParams(vmem_limit_bytes=SMALL_VMEM),
        cost_estimate=pl.CostEstimate(
            flops=arrived.size, bytes_accessed=8 * arrived.size, transcendentals=0
        ),
    )(own, arrived)


def mark_kernel(*refs):
    refs[-1][...] = jnp.zeros_like(refs[-1])


def mark(arrays):
    return pl.pallas_call(
        mark_kernel,
        in_specs=[pl.BlockSpec(memory_space=pl.ANY)] * len(arrays),
        out_specs=pl.BlockSpec(memory_space=pltpu.VMEM),
        out_shape=jax.ShapeDtypeStruct((8, 128), F32),
        compiler_params=pltpu.CompilerParams(vmem_limit_bytes=SMALL_VMEM),
        cost_estimate=pl.CostEstimate(flops=2 * 10**10, bytes_accessed=2**20, transcendentals=0),
    )(*arrays)


def finish_kernel(own_ref, near_ref, *refs):
    *arrived_refs, _, out_ref = refs
    width = out_ref.shape[1] // len(arrived_refs)
    for c, arrived_ref in enumerate(arrived_refs):
        at = slice(c * width, (c + 1) * width)
        total = own_ref[:, at] + near_ref[:, at].astype(F32) + arrived_ref[...].astype(F32)
        out_ref[:, at] = total.astype(out_ref.dtype)


def finish(own, near, arrived):
    rows, width = own.shape
    whole = pl.BlockSpec(memory_space=pltpu.VMEM)
    return pl.pallas_call(
        finish_kernel,
        in_specs=[whole] * (2 + len(arrived)) + [pl.BlockSpec(memory_space=pl.ANY)],
        out_specs=whole,
        out_shape=jax.ShapeDtypeStruct((rows, width), BF16),
        compiler_params=pltpu.CompilerParams(vmem_limit_bytes=SMALL_VMEM),
        cost_estimate=pl.CostEstimate(
            flops=rows * width, bytes_accessed=8 * rows * width, transcendentals=0
        ),
    )(own, near, *arrived, mark(arrived))


def body(pieces, tables, queries, keys, values, filters, skip_weight, out_weight):
    rows, width = keys.shape
    n_peers = lax.axis_size("seq")
    chans = width // n_peers
    fwd, bwd = (jnp.asarray(t) for t in tables)
    skip = skip_weight[None, :]
    in_chip = [(0, 1), (1, 0), (2, 3), (3, 2)]
    across = [(0, 2), (2, 0), (1, 3), (3, 1)]

    if chans % 128 == 0 and n_peers == 8:
        blocks = pre(keys, values, filters, n_peers)
        received = exchange(blocks, n_peers, False)
        fwd, bwd, early = spectra(received[:-2], fwd, bwd, n_peers)
        back = exchange(conv_fast(early, received[-2:], fwd, bwd), n_peers, True)
        gated = gate(queries, keys, values, skip, back)
    else:
        product = keys.astype(F32) * values.astype(F32)
        parts = [a.astype(BF16).reshape(rows, n_peers, chans) for a in (product, filters)]
        sent = jnp.concatenate(parts, axis=2).transpose(1, 0, 2)
        received = lax.all_to_all(sent, "seq", split_axis=0, concat_axis=0, tiled=True)
        conv = conv_plain(received, fwd, bwd)
        back = lax.all_to_all(conv, "seq", split_axis=0, concat_axis=0, tiled=True)
        mixed = back.transpose(1, 0, 2).reshape(rows, width).astype(F32) + skip * product
        gated = (queries.astype(F32) * mixed).astype(BF16)

    theirs = []
    for c in range(pieces):
        (sent,) = project(gated, out_weight, [(True, True, c, pieces)], [BF16])
        theirs.append(lax.ppermute(sent, "fsdp", in_chip))
    blocks = [(False, True, c, pieces) for c in range(pieces)]
    ours = project(gated, out_weight, blocks, [F32] * pieces)
    arrived = [lax.ppermute(add(*pair), "fsdp", across) for pair in zip(ours, theirs)]
    blocks = [(True, False, 0, 1), (False, False, 0, 1)]
    sent, own = project(gated, out_weight, blocks, [BF16, F32])
    near = lax.ppermute(sent, "fsdp", in_chip)
    return finish(own, near, arrived)


def solution(mesh):
    in_specs = (
        P("seq", "fsdp"),
        P("seq", "fsdp"),
        P("seq", "fsdp"),
        P("seq", "fsdp"),
        P("fsdp"),
        P("fsdp", None),
    )
    out_specs = P("seq", "fsdp")

    def run(queries, keys, values, filters, skip_weight, out_weight):
        rows = keys.shape[0] // mesh.shape["seq"]
        fn = functools.partial(body, 2, make_tables(rows))
        return jax.shard_map(fn, mesh=mesh, in_specs=in_specs, out_specs=out_specs, check_vma=False)(
            queries, keys, values, filters, skip_weight, out_weight
        )

    return run
```

```python
import functools

import numpy as np

import jax
import jax.numpy as jnp
from jax import lax
from jax.experimental import pallas as pl
from jax.experimental.pallas import tpu as pltpu
from jax.sharding import PartitionSpec as P

BF16 = jnp.bfloat16
F32 = jnp.float32
CONV_VMEM = 24 * 2**20
PROJECT_VMEM = 24 * 2**20
SMALL_VMEM = 12 * 2**20


def split_bf16(table):
    high = table.astype(BF16)
    return high, (table - high.astype(np.float64)).astype(BF16)


def make_tables(rows):
    order = np.concatenate([np.arange(0, rows, 2), np.arange(1, rows, 2)])
    times = np.arange(rows)
    angle = np.pi * (((2 * order[:, None] + 1) * times[None, :]) % (4 * rows)) / (2 * rows)
    forward = np.concatenate([np.cos(angle), -np.sin(angle)], axis=0)
    high, low = split_bf16(forward)
    back_high, back_low = split_bf16(forward.T / rows)
    return (
        np.concatenate([high, low], axis=1),
        np.concatenate([back_high, back_low, back_high], axis=1),
    )


def peer_of(slot):
    return lax.bitwise_xor(lax.axis_index("seq"), slot)


def peer_block(slot, size):
    return pl.ds(pl.multiple_of(peer_of(slot) * size, size), size)


def pre_kernel(slots, keys_hbm, values_hbm, filters_hbm, *refs):
    out_refs, (keys, values, filters, sem) = refs[: len(slots)], refs[len(slots) :]
    chans = keys.shape[2]
    pairs = ((keys_hbm, keys), (values_hbm, values), (filters_hbm, filters))
    copies = [
        [
            pltpu.make_async_copy(src.at[:, peer_block(slot, chans)], dst.at[s], sem.at[s, i])
            for i, (src, dst) in enumerate(pairs)
        ]
        for s, slot in enumerate(slots)
    ]
    for group in copies:
        for copy in group:
            copy.start()
    for s, (group, out_ref) in enumerate(zip(copies, out_refs)):
        for copy in group:
            copy.wait()
        product = keys[s].astype(F32) * values[s].astype(F32)
        out_ref[:, :chans] = product.astype(BF16)
        out_ref[:, chans:] = filters[s].astype(BF16)


def pre(keys, values, filters, slots, n_peers):
    rows, width = keys.shape
    chans = width // n_peers
    args = [pltpu.with_memory_space_constraint(a, pltpu.HBM) for a in (keys, values, filters)]
    return pl.pallas_call(
        functools.partial(pre_kernel, slots),
        in_specs=[pl.BlockSpec(memory_space=pltpu.HBM)] * 3,
        out_specs=[pl.BlockSpec(memory_space=pltpu.VMEM)] * len(slots),
        out_shape=[jax.ShapeDtypeStruct((rows, 2 * chans), BF16)] * len(slots),
        scratch_shapes=[
            pltpu.VMEM((len(slots), rows, chans), BF16),
            pltpu.VMEM((len(slots), rows, chans), BF16),
            pltpu.VMEM((len(slots), rows, chans), F32),
            pltpu.SemaphoreType.DMA((len(slots), 3)),
        ],
        compiler_params=pltpu.CompilerParams(vmem_limit_bytes=SMALL_VMEM),
        cost_estimate=pl.CostEstimate(
            flops=rows * chans * len(slots),
            bytes_accessed=12 * rows * chans * len(slots),
            transcendentals=0,
        ),
    )(*args)


def slots_of(n_peers, back):
    half = n_peers // 2
    near, far = list(range(1, half)), list(range(half, n_peers))
    if back:
        return [0, near[0]] + far[:3] + [near[1]] + far[3:] + near[2:]
    return [0] + far[:2] + near + far[2:]


def exchange(blocks, n_peers, back):
    return [
        lax.ppermute(block, "seq", [(i, i ^ slot) for i in range(n_peers)]) if slot else block
        for slot, block in zip(slots_of(n_peers, back), blocks)
    ]


def block_spectrum(table, block):
    return jnp.dot(table, jnp.concatenate([block, block], axis=0), preferred_element_type=F32)


def spectra_kernel(n_peers, fwd_hbm, bwd_hbm, *refs):
    *in_refs, fwd_ref, bwd_ref, spec_ref, sem = refs
    copies = [
        pltpu.make_async_copy(fwd_hbm, fwd_ref, sem.at[0]),
        pltpu.make_async_copy(bwd_hbm, bwd_ref, sem.at[1]),
    ]
    for copy in copies:
        copy.start()
    for copy in copies:
        copy.wait()
    for slot, in_ref in zip(slots_of(n_peers, False), in_refs):
        spec_ref[peer_of(slot)] = block_spectrum(fwd_ref[...], in_ref[...])


def spectra(received, fwd, bwd, n_peers):
    rows, width = received[0].shape
    whole = pl.BlockSpec(memory_space=pltpu.VMEM)
    args = [pltpu.with_memory_space_constraint(a, pltpu.HBM) for a in (fwd, bwd)]
    return pl.pallas_call(
        functools.partial(spectra_kernel, n_peers),
        in_specs=[pl.BlockSpec(memory_space=pltpu.HBM)] * 2 + [whole] * len(received),
        out_specs=[whole] * 3,
        out_shape=[
            jax.ShapeDtypeStruct(fwd.shape, BF16),
            jax.ShapeDtypeStruct(bwd.shape, BF16),
            jax.ShapeDtypeStruct((n_peers, 2 * rows, width), F32),
        ],
        scratch_shapes=[pltpu.SemaphoreType.DMA((2,))],
        compiler_params=pltpu.CompilerParams(vmem_limit_bytes=CONV_VMEM),
        cost_estimate=pl.CostEstimate(
            flops=8 * len(received) * rows * rows * width, bytes_accessed=4 * 2**20, transcendentals=0
        ),
    )(*args, *received)


def conv_kernel(fwd_ref, bwd_ref, early_ref, *refs):
    *refs, late, held, turned = refs
    n_blocks, step = early_ref.shape[0], held.shape[2]
    in_refs, out_refs = refs[:-n_blocks], refs[-n_blocks:]
    rows, chans = in_refs[0].shape[0], in_refs[0].shape[1] // 2
    late_slots = slots_of(n_blocks, False)[-2:]
    for slot, in_ref in zip(late_slots, in_refs):
        late[lax.bitwise_and(peer_of(slot), 1)] = block_spectrum(fwd_ref[...], in_ref[...])
    late_pair = lax.div(peer_of(late_slots[0]), 2)

    def spectrum(j, at, lanes):
        return jnp.where(late_pair == j // 2, late[j % 2, at, lanes], early_ref[j, at, lanes])

    def mix(row, sign):
        re, im = pl.ds(row, step), pl.ds(row + rows, step)
        x_at, f_at = slice(0, chans), slice(chans, 2 * chans)
        gains = []
        last_re = last_im = None
        for j in range(n_blocks):
            held[j, 0] = spectrum(j, re, x_at)
            held[j, 1] = spectrum(j, im, x_at)
            f_re, f_im = spectrum(j, re, f_at), spectrum(j, im, f_at)
            if j == 0:
                gains.append((f_re, f_im))
            else:
                gains.append((f_re - sign * last_im, f_im + sign * last_re))
            last_re, last_im = f_re, f_im
        for i in range(n_blocks):
            out_re = out_im = None
            for d in range(i + 1):
                (g_re, g_im), x_re, x_im = gains[d], held[i - d, 0], held[i - d, 1]
                t_re = g_re * x_re - g_im * x_im
                t_im = g_re * x_im + g_im * x_re
                out_re = t_re if d == 0 else out_re + t_re
                out_im = t_im if d == 0 else out_im + t_im
            lanes = slice(i % 2 * chans, (i % 2 + 1) * chans)
            for first, value in ((row, out_re), (row + rows, out_im)):
                high = value.astype(BF16)
                low = (value - high.astype(F32)).astype(BF16)
                for part, piece in enumerate((high, high, low)):
                    turned[i // 2, pl.ds(first + 2 * part * rows, step), lanes] = piece

    half = rows // 2

    @pl.loop(0, half // step)
    def _(t):
        mix(pl.multiple_of(t * step, step), 1.0)

    @pl.loop(half // step, rows // step)
    def _(t):
        mix(pl.multiple_of(t * step, step), -1.0)

    odd = lax.bitwise_and(lax.axis_index("seq"), 1) == 1
    by_slot = dict(zip(slots_of(n_blocks, True), out_refs))
    for slot in range(0, n_blocks, 2):
        pair = lax.div(peer_of(slot), 2)
        both = jnp.dot(bwd_ref[...], turned[pair], preferred_element_type=F32)
        left, right = both[:, :chans], both[:, chans:]
        by_slot[slot][...] = jnp.where(odd, right, left).astype(BF16)
        by_slot[slot + 1][...] = jnp.where(odd, left, right).astype(BF16)


def conv_fast(early, late, fwd, bwd):
    n_blocks = early.shape[0]
    rows, chans = late[0].shape[0], late[0].shape[1] // 2
    step = 16
    whole = pl.BlockSpec(memory_space=pltpu.VMEM)
    return pl.pallas_call(
        conv_kernel,
        in_specs=[whole] * 5,
        out_specs=[whole] * n_blocks,
        out_shape=[jax.ShapeDtypeStruct((rows, chans), BF16)] * n_blocks,
        scratch_shapes=[
            pltpu.VMEM((2, 2 * rows, 2 * chans), F32),
            pltpu.VMEM((n_blocks, 2, step, chans), F32),
            pltpu.VMEM((n_blocks // 2, 6 * rows, 2 * chans), BF16),
        ],
        compiler_params=pltpu.CompilerParams(vmem_limit_bytes=CONV_VMEM),
        cost_estimate=pl.CostEstimate(
            flops=16 * n_blocks * rows * rows * chans, bytes_accessed=4 * 2**20, transcendentals=0
        ),
    )(fwd, bwd, early, *late)


def conv_plain(received, fwd, bwd):
    n_blocks, rows, chans = received.shape[0], received.shape[1], received.shape[2] // 2
    exact = lax.Precision.HIGHEST
    fwd32 = fwd[:, :rows].astype(F32) + fwd[:, rows:].astype(F32)
    bwd32 = bwd[:, : 2 * rows].astype(F32) + bwd[:, 2 * rows : 4 * rows].astype(F32)
    sign = jnp.where(jnp.arange(rows) < rows // 2, 1.0, -1.0).astype(F32)[:, None]

    def spectrum(blocks):
        spec = jnp.einsum("kt,jtc->jkc", fwd32, blocks.astype(F32), precision=exact)
        return spec[:, :rows], spec[:, rows:]

    x_re, x_im = spectrum(received[:, :, :chans])
    f_re, f_im = spectrum(received[:, :, chans:])
    g_re = f_re.at[1:].add(-sign * f_im[:-1])
    g_im = f_im.at[1:].add(sign * f_re[:-1])

    def one(d, total):
        t_re, t_im = total
        later = (jnp.arange(n_blocks) >= d)[:, None, None]
        a_re = jnp.where(later, jnp.roll(x_re, d, axis=0), 0.0)
        a_im = jnp.where(later, jnp.roll(x_im, d, axis=0), 0.0)
        return (
            t_re + g_re[d] * a_re - g_im[d] * a_im,
            t_im + g_re[d] * a_im + g_im[d] * a_re,
        )

    zero = jnp.zeros_like(x_re)
    y_re, y_im = lax.fori_loop(0, n_blocks, one, (zero, zero))
    both = jnp.concatenate([y_re, y_im], axis=1)
    return jnp.einsum("tk,jkc->jtc", bwd32, both, precision=exact).astype(BF16)


def gate_kernel(queries_ref, keys_ref, values_ref, skip_ref, *refs):
    *conv_refs, out_ref = refs
    chans = conv_refs[0].shape[1]
    for slot, conv_ref in zip(slots_of(len(conv_refs), True), conv_refs):
        at = peer_block(slot, chans)
        product = keys_ref[:, at].astype(F32) * values_ref[:, at].astype(F32)
        mixed = conv_ref[...].astype(F32) + skip_ref[:, at] * product
        out_ref[:, at] = (queries_ref[:, at].astype(F32) * mixed).astype(BF16)


def gate(queries, keys, values, skip, conv):
    rows, width = queries.shape
    whole = pl.BlockSpec(memory_space=pltpu.VMEM)
    return pl.pallas_call(
        gate_kernel,
        in_specs=[whole] * (4 + len(conv)),
        out_specs=whole,
        out_shape=jax.ShapeDtypeStruct((rows, width), BF16),
        compiler_params=pltpu.CompilerParams(vmem_limit_bytes=SMALL_VMEM),
        cost_estimate=pl.CostEstimate(
            flops=4 * rows * width, bytes_accessed=10 * rows * width, transcendentals=0
        ),
    )(queries, keys, values, skip, *conv)


def weight_block(weight_ref, other, across, piece, pieces):
    width = weight_ref.shape[1] // 4 // pieces
    place = lax.axis_index("fsdp")
    core, side = lax.rem(place, 2), lax.div(place, 2)
    block = 2 * (1 - side if across else side) + (1 - core if other else core)
    return weight_ref[:, pl.ds(pl.multiple_of((block * pieces + piece) * width, width), width)]


def project_kernel(blocks, gated_ref, weight_ref, *out_refs):
    for block, out_ref in zip(blocks, out_refs):
        columns = weight_block(weight_ref, *block)
        total = jnp.dot(gated_ref[...], columns, preferred_element_type=F32)
        out_ref[...] = total.astype(out_ref.dtype)


def project(gated, weight, blocks, dtypes):
    rows, depth = gated.shape
    widths = [weight.shape[1] // 4 // pieces for *_, pieces in blocks]
    whole = pl.BlockSpec(memory_space=pltpu.VMEM)
    return pl.pallas_call(
        functools.partial(project_kernel, blocks),
        in_specs=[whole] * 2,
        out_specs=[whole] * len(blocks),
        out_shape=[jax.ShapeDtypeStruct((rows, w), t) for w, t in zip(widths, dtypes)],
        compiler_params=pltpu.CompilerParams(vmem_limit_bytes=PROJECT_VMEM),
        cost_estimate=pl.CostEstimate(
            flops=2 * rows * depth * sum(widths), bytes_accessed=2 * depth * sum(widths), transcendentals=0
        ),
    )(gated, weight)


def add_kernel(own_ref, arrived_ref, out_ref):
    total = own_ref[...] + arrived_ref[...].astype(F32)
    out_ref[...] = total.astype(out_ref.dtype)


def add(own, arrived):
    whole = pl.BlockSpec(memory_space=pltpu.VMEM)
    return pl.pallas_call(
        add_kernel,
        in_specs=[whole] * 2,
        out_specs=whole,
        out_shape=jax.ShapeDtypeStruct(arrived.shape, BF16),
        compiler_params=pltpu.CompilerParams(vmem_limit_bytes=SMALL_VMEM),
        cost_estimate=pl.CostEstimate(
            flops=arrived.size, bytes_accessed=8 * arrived.size, transcendentals=0
        ),
    )(own, arrived)


def mark_kernel(*refs):
    refs[-1][...] = jnp.zeros_like(refs[-1])


def mark(arrays):
    return pl.pallas_call(
        mark_kernel,
        in_specs=[pl.BlockSpec(memory_space=pl.ANY)] * len(arrays),
        out_specs=pl.BlockSpec(memory_space=pltpu.VMEM),
        out_shape=jax.ShapeDtypeStruct((8, 128), F32),
        compiler_params=pltpu.CompilerParams(vmem_limit_bytes=SMALL_VMEM),
        cost_estimate=pl.CostEstimate(flops=2 * 10**10, bytes_accessed=2**20, transcendentals=0),
    )(*arrays)


def finish_kernel(own_ref, near_ref, *refs):
    *arrived_refs, _, out_ref = refs
    width = out_ref.shape[1] // len(arrived_refs)
    for c, arrived_ref in enumerate(arrived_refs):
        at = slice(c * width, (c + 1) * width)
        total = own_ref[:, at] + near_ref[:, at].astype(F32) + arrived_ref[...].astype(F32)
        out_ref[:, at] = total.astype(out_ref.dtype)


def finish(own, near, arrived):
    rows, width = own.shape
    whole = pl.BlockSpec(memory_space=pltpu.VMEM)
    return pl.pallas_call(
        finish_kernel,
        in_specs=[whole] * (2 + len(arrived)) + [pl.BlockSpec(memory_space=pl.ANY)],
        out_specs=whole,
        out_shape=jax.ShapeDtypeStruct((rows, width), BF16),
        compiler_params=pltpu.CompilerParams(vmem_limit_bytes=SMALL_VMEM),
        cost_estimate=pl.CostEstimate(
            flops=rows * width, bytes_accessed=8 * rows * width, transcendentals=0
        ),
    )(own, near, *arrived, mark(arrived))


def body(pieces, tables, queries, keys, values, filters, skip_weight, out_weight):
    rows, width = keys.shape
    n_peers = lax.axis_size("seq")
    chans = width // n_peers
    fwd, bwd = (jnp.asarray(t) for t in tables)
    skip = skip_weight[None, :]
    in_chip = [(0, 1), (1, 0), (2, 3), (3, 2)]
    across = [(0, 2), (2, 0), (1, 3), (3, 1)]

    if chans % 128 == 0 and n_peers == 8:
        slots = slots_of(n_peers, False)
        first, rest = slots[1:3], slots[:1] + slots[3:]
        mine = pre(keys, values, filters, first, n_peers)
        own, *others = pre(keys, values, filters, rest, n_peers)
        received = exchange([own, *mine, *others], n_peers, False)
        fwd, bwd, early = spectra(received[:-2], fwd, bwd, n_peers)
        back = exchange(conv_fast(early, received[-2:], fwd, bwd), n_peers, True)
        gated = gate(queries, keys, values, skip, back)
    else:
        product = keys.astype(F32) * values.astype(F32)
        parts = [a.astype(BF16).reshape(rows, n_peers, chans) for a in (product, filters)]
        sent = jnp.concatenate(parts, axis=2).transpose(1, 0, 2)
        received = lax.all_to_all(sent, "seq", split_axis=0, concat_axis=0, tiled=True)
        conv = conv_plain(received, fwd, bwd)
        back = lax.all_to_all(conv, "seq", split_axis=0, concat_axis=0, tiled=True)
        mixed = back.transpose(1, 0, 2).reshape(rows, width).astype(F32) + skip * product
        gated = (queries.astype(F32) * mixed).astype(BF16)

    theirs = []
    for c in range(pieces):
        (sent,) = project(gated, out_weight, [(True, True, c, pieces)], [BF16])
        theirs.append(lax.ppermute(sent, "fsdp", in_chip))
    blocks = [(False, True, c, pieces) for c in range(pieces)]
    ours = project(gated, out_weight, blocks, [F32] * pieces)
    arrived = [lax.ppermute(add(*pair), "fsdp", across) for pair in zip(ours, theirs)]
    blocks = [(True, False, 0, 1), (False, False, 0, 1)]
    sent, own = project(gated, out_weight, blocks, [BF16, F32])
    near = lax.ppermute(sent, "fsdp", in_chip)
    return finish(own, near, arrived)


def solution(mesh):
    in_specs = (
        P("seq", "fsdp"),
        P("seq", "fsdp"),
        P("seq", "fsdp"),
        P("seq", "fsdp"),
        P("fsdp"),
        P("fsdp", None),
    )
    out_specs = P("seq", "fsdp")

    def run(queries, keys, values, filters, skip_weight, out_weight):
        rows = keys.shape[0] // mesh.shape["seq"]
        fn = functools.partial(body, 2, make_tables(rows))
        return jax.shard_map(fn, mesh=mesh, in_specs=in_specs, out_specs=out_specs, check_vma=False)(
            queries, keys, values, filters, skip_weight, out_weight
        )

    return run
```

```python
import functools

import numpy as np

import jax
import jax.numpy as jnp
from jax import lax
from jax.experimental import pallas as pl
from jax.experimental.pallas import tpu as pltpu
from jax.sharding import PartitionSpec as P

BF16 = jnp.bfloat16
F32 = jnp.float32
CONV_VMEM = 24 * 2**20
PROJECT_VMEM = 24 * 2**20
SMALL_VMEM = 12 * 2**20
STEP = 16


def split_bf16(table):
    high = table.astype(BF16)
    return high, (table - high.astype(np.float64)).astype(BF16)


def make_tables(rows):
    order = np.concatenate([np.arange(0, rows, 2), np.arange(1, rows, 2)])
    times = np.arange(rows)
    angle = np.pi * (((2 * order[:, None] + 1) * times[None, :]) % (4 * rows)) / (2 * rows)
    forward = np.concatenate([np.cos(angle), -np.sin(angle)], axis=0)
    high, low = split_bf16(forward)
    back_high, back_low = split_bf16(forward.T / rows)
    return (
        np.concatenate([high, low], axis=1),
        np.concatenate([back_high, back_low, back_high], axis=1),
    )


def peer_of(slot):
    return lax.bitwise_xor(lax.axis_index("seq"), slot)


def peer_block(slot, size):
    return pl.ds(pl.multiple_of(peer_of(slot) * size, size), size)


def pre_kernel(n_peers, keys_hbm, values_hbm, filters_hbm, *refs):
    out_refs = refs[:n_peers]
    keys, values, filters, sem = refs[n_peers:]
    rows, width = keys.shape
    chans = width // n_peers
    steps = sem.shape[0]
    parts = [pl.ds(c * rows // steps, rows // steps) for c in range(steps)]
    pairs = ((keys_hbm, keys), (values_hbm, values), (filters_hbm, filters))
    copies = [
        [
            pltpu.make_async_copy(src.at[part], dst.at[part], sem.at[c, i])
            for i, (src, dst) in enumerate(pairs)
        ]
        for c, part in enumerate(parts)
    ]
    for group in copies:
        for copy in group:
            copy.start()
    for part, group in zip(parts, copies):
        for copy in group:
            copy.wait()
        for slot, out_ref in zip(slots_of(n_peers, False), out_refs):
            at = peer_block(slot, chans)
            product = keys[part, at].astype(F32) * values[part, at].astype(F32)
            out_ref[part, :chans] = product.astype(BF16)
            out_ref[part, chans:] = filters[part, at].astype(BF16)


def pre(keys, values, filters, n_peers):
    rows, width = keys.shape
    chans = width // n_peers
    args = [pltpu.with_memory_space_constraint(a, pltpu.HBM) for a in (keys, values, filters)]
    return pl.pallas_call(
        functools.partial(pre_kernel, n_peers),
        in_specs=[pl.BlockSpec(memory_space=pltpu.HBM)] * 3,
        out_specs=[pl.BlockSpec(memory_space=pltpu.VMEM)] * n_peers,
        out_shape=[jax.ShapeDtypeStruct((rows, 2 * chans), BF16)] * n_peers,
        scratch_shapes=[
            pltpu.VMEM((rows, width), BF16),
            pltpu.VMEM((rows, width), BF16),
            pltpu.VMEM((rows, width), F32),
            pltpu.SemaphoreType.DMA((2, 3)),
        ],
        compiler_params=pltpu.CompilerParams(vmem_limit_bytes=SMALL_VMEM),
        cost_estimate=pl.CostEstimate(
            flops=rows * width, bytes_accessed=12 * rows * width, transcendentals=0
        ),
    )(*args)


def slots_of(n_peers, back):
    half = n_peers // 2
    near, far = list(range(1, half)), list(range(half, n_peers))
    if back:
        return [0, near[0]] + far[:3] + [near[1]] + far[3:] + near[2:]
    return [0, near[0], far[0], near[1], far[1]] + near[2:] + far[2:]


def exchange(blocks, n_peers, back):
    return [
        lax.ppermute(block, "seq", [(i, i ^ slot) for i in range(n_peers)]) if slot else block
        for slot, block in zip(slots_of(n_peers, back), blocks)
    ]


def block_spectrum(table, block):
    return jnp.dot(table, jnp.concatenate([block, block], axis=0), preferred_element_type=F32)


def times(a, b):
    return a[0] * b[0] - a[1] * b[1], a[0] * b[1] + a[1] * b[0]


def plus(a, b):
    return b if a is None else (a[0] + b[0], a[1] + b[1])


def late_place(n_blocks):
    return lax.div(peer_of(slots_of(n_blocks, False)[-1]), 2)


def load(ref, at, row, step, rows, lanes):
    return tuple(ref[(*at, pl.ds(row + part * rows, step), lanes)] for part in range(2))


def mix_early(pair, step, spec_ref, part_ref):
    n_blocks, rows, chans = spec_ref.shape[0], spec_ref.shape[1] // 2, spec_ref.shape[2] // 2
    early = [j for j in range(n_blocks) if j // 2 != pair]

    @pl.loop(0, rows // step)
    def _(t):
        row = pl.multiple_of(t * step, step)
        signal = {j: load(spec_ref, (j,), row, step, rows, slice(0, chans)) for j in early}
        filt = {j: load(spec_ref, (j,), row, step, rows, slice(chans, 2 * chans)) for j in early}
        for i in range(n_blocks):
            total = None
            for d in early:
                if i - d in early:
                    total = plus(total, times(filt[d], signal[i - d]))
            if total is None:
                total = (jnp.zeros((step, chans), F32),) * 2
            for part in range(2):
                part_ref[i, pl.ds(row + part * rows, step)] = total[part]


def spectra_kernel(n_peers, fwd_hbm, bwd_hbm, *refs):
    *in_refs, fwd_ref, bwd_ref, spec_ref, part_ref, sem = refs
    copies = [
        pltpu.make_async_copy(fwd_hbm, fwd_ref, sem.at[0]),
        pltpu.make_async_copy(bwd_hbm, bwd_ref, sem.at[1]),
    ]
    for copy in copies:
        copy.start()
    copies[0].wait()
    for slot, in_ref in zip(slots_of(n_peers, False), in_refs):
        spec_ref[peer_of(slot)] = block_spectrum(fwd_ref[...], in_ref[...])
    for pair in range(n_peers // 2):
        pl.when(late_place(n_peers) == pair)(
            functools.partial(mix_early, pair, STEP, spec_ref, part_ref)
        )
    copies[1].wait()


def spectra(received, fwd, bwd, n_peers):
    rows, width = received[0].shape
    whole = pl.BlockSpec(memory_space=pltpu.VMEM)
    args = [pltpu.with_memory_space_constraint(a, pltpu.HBM) for a in (fwd, bwd)]
    return pl.pallas_call(
        functools.partial(spectra_kernel, n_peers),
        in_specs=[pl.BlockSpec(memory_space=pltpu.HBM)] * 2 + [whole] * len(received),
        out_specs=[whole] * 4,
        out_shape=[
            jax.ShapeDtypeStruct(fwd.shape, BF16),
            jax.ShapeDtypeStruct(bwd.shape, BF16),
            jax.ShapeDtypeStruct((n_peers, 2 * rows, width), F32),
            jax.ShapeDtypeStruct((n_peers, 2 * rows, width // 2), F32),
        ],
        scratch_shapes=[pltpu.SemaphoreType.DMA((2,))],
        compiler_params=pltpu.CompilerParams(vmem_limit_bytes=CONV_VMEM),
        cost_estimate=pl.CostEstimate(
            flops=8 * len(received) * rows * rows * width, bytes_accessed=4 * 2**20, transcendentals=0
        ),
    )(*args, *received)


def mix_late(pair, step, first, last, sign, spec_ref, part_ref, late_ref, turned):
    n_blocks, rows, chans = spec_ref.shape[0], spec_ref.shape[1] // 2, spec_ref.shape[2] // 2
    early = [j for j in range(n_blocks) if j // 2 != pair]
    x_at, f_at = slice(0, chans), slice(chans, 2 * chans)

    @pl.loop(first // step, last // step)
    def _(t):
        row = pl.multiple_of(t * step, step)
        late = [2 * pair, 2 * pair + 1]
        signal = {j: load(late_ref, (j % 2,), row, step, rows, x_at) for j in late}
        filt = {j: load(late_ref, (j % 2,), row, step, rows, f_at) for j in late}
        total = [load(part_ref, (i,), row, step, rows, slice(0, chans)) for i in range(n_blocks)]
        for b in early:
            if b + late[0] >= n_blocks:
                continue
            x_b = load(spec_ref, (b,), row, step, rows, x_at)
            f_b = load(spec_ref, (b,), row, step, rows, f_at)
            for j in late:
                if b + j < n_blocks:
                    total[b + j] = plus(total[b + j], times(filt[j], x_b))
                    total[b + j] = plus(total[b + j], times(f_b, signal[j]))
        for j in late:
            for d in late:
                if j + d < n_blocks:
                    total[j + d] = plus(total[j + d], times(filt[d], signal[j]))
        for i in range(n_blocks):
            value = total[i]
            if i > 0:
                turn_re, turn_im = total[i - 1]
                if sign > 0:
                    value = value[0] - turn_im, value[1] + turn_re
                else:
                    value = value[0] + turn_im, value[1] - turn_re
            lanes = slice(i % 2 * chans, (i % 2 + 1) * chans)
            for part in range(2):
                high = value[part].astype(BF16)
                low = (value[part] - high.astype(F32)).astype(BF16)
                for c, piece in enumerate((high, high, low)):
                    turned[i // 2, pl.ds(row + (2 * c + part) * rows, step), lanes] = piece


def conv_kernel(fwd_ref, bwd_ref, spec_ref, part_ref, *refs):
    *refs, late_ref, turned = refs
    n_blocks = spec_ref.shape[0]
    in_refs, out_refs = refs[:-n_blocks], refs[-n_blocks:]
    rows, chans = in_refs[0].shape[0], in_refs[0].shape[1] // 2
    for slot, in_ref in zip(slots_of(n_blocks, False)[-2:], in_refs):
        late_ref[lax.bitwise_and(peer_of(slot), 1)] = block_spectrum(fwd_ref[...], in_ref[...])

    def mix(pair):
        for first, last, sign in ((0, rows // 2, 1), (rows // 2, rows, -1)):
            mix_late(pair, STEP, first, last, sign, spec_ref, part_ref, late_ref, turned)

    for pair in range(n_blocks // 2):
        pl.when(late_place(n_blocks) == pair)(functools.partial(mix, pair))

    odd = lax.bitwise_and(lax.axis_index("seq"), 1) == 1
    by_slot = dict(zip(slots_of(n_blocks, True), out_refs))
    for slot in range(0, n_blocks, 2):
        pair = lax.div(peer_of(slot), 2)
        both = jnp.dot(bwd_ref[...], turned[pair], preferred_element_type=F32)
        left, right = both[:, :chans], both[:, chans:]
        by_slot[slot][...] = jnp.where(odd, right, left).astype(BF16)
        by_slot[slot + 1][...] = jnp.where(odd, left, right).astype(BF16)


def conv_fast(early, part, late, fwd, bwd):
    n_blocks = early.shape[0]
    rows, chans = late[0].shape[0], late[0].shape[1] // 2
    whole = pl.BlockSpec(memory_space=pltpu.VMEM)
    return pl.pallas_call(
        conv_kernel,
        in_specs=[whole] * 6,
        out_specs=[whole] * n_blocks,
        out_shape=[jax.ShapeDtypeStruct((rows, chans), BF16)] * n_blocks,
        scratch_shapes=[
            pltpu.VMEM((2, 2 * rows, 2 * chans), F32),
            pltpu.VMEM((n_blocks // 2, 6 * rows, 2 * chans), BF16),
        ],
        compiler_params=pltpu.CompilerParams(vmem_limit_bytes=CONV_VMEM),
        cost_estimate=pl.CostEstimate(
            flops=16 * n_blocks * rows * rows * chans, bytes_accessed=4 * 2**20, transcendentals=0
        ),
    )(fwd, bwd, early, part, *late)


def conv_plain(received, fwd, bwd):
    n_blocks, rows, chans = received.shape[0], received.shape[1], received.shape[2] // 2
    exact = lax.Precision.HIGHEST
    fwd32 = fwd[:, :rows].astype(F32) + fwd[:, rows:].astype(F32)
    bwd32 = bwd[:, : 2 * rows].astype(F32) + bwd[:, 2 * rows : 4 * rows].astype(F32)
    sign = jnp.where(jnp.arange(rows) < rows // 2, 1.0, -1.0).astype(F32)[:, None]

    def spectrum(blocks):
        spec = jnp.einsum("kt,jtc->jkc", fwd32, blocks.astype(F32), precision=exact)
        return spec[:, :rows], spec[:, rows:]

    x_re, x_im = spectrum(received[:, :, :chans])
    f_re, f_im = spectrum(received[:, :, chans:])
    g_re = f_re.at[1:].add(-sign * f_im[:-1])
    g_im = f_im.at[1:].add(sign * f_re[:-1])

    def one(d, total):
        t_re, t_im = total
        later = (jnp.arange(n_blocks) >= d)[:, None, None]
        a_re = jnp.where(later, jnp.roll(x_re, d, axis=0), 0.0)
        a_im = jnp.where(later, jnp.roll(x_im, d, axis=0), 0.0)
        return (
            t_re + g_re[d] * a_re - g_im[d] * a_im,
            t_im + g_re[d] * a_im + g_im[d] * a_re,
        )

    zero = jnp.zeros_like(x_re)
    y_re, y_im = lax.fori_loop(0, n_blocks, one, (zero, zero))
    both = jnp.concatenate([y_re, y_im], axis=1)
    return jnp.einsum("tk,jkc->jtc", bwd32, both, precision=exact).astype(BF16)


def columns_of(other, across, piece, pieces, width):
    count = width // 4 // pieces
    place = lax.axis_index("fsdp")
    core, side = lax.rem(place, 2), lax.div(place, 2)
    block = 2 * (1 - side if across else side) + (1 - core if other else core)
    return pl.ds(pl.multiple_of((block * pieces + piece) * count, count), count)


def gate_slot(slot, queries_ref, keys_ref, values_ref, skip_ref, conv_ref):
    at = peer_block(slot, conv_ref.shape[1])
    product = keys_ref[:, at].astype(F32) * values_ref[:, at].astype(F32)
    mixed = conv_ref[...].astype(F32) + skip_ref[:, at] * product
    return (queries_ref[:, at].astype(F32) * mixed).astype(BF16)


def gate_early_kernel(n_peers, queries_ref, keys_ref, values_ref, skip_ref, weight_ref, *refs):
    conv_refs, (gated_ref, *part_refs) = refs[:-3], refs[-3:]
    chans = conv_refs[0].shape[1]
    slots = slots_of(n_peers, True)
    for slot, conv_ref in zip(slots, conv_refs):
        gated = gate_slot(slot, queries_ref, keys_ref, values_ref, skip_ref, conv_ref)
        gated_ref[:, peer_block(slot, chans)] = gated
    for slot in slots[len(conv_refs) :]:
        gated_ref[:, peer_block(slot, chans)] = jnp.zeros((gated_ref.shape[0], chans), BF16)
    for other, part_ref in zip((True, False), part_refs):
        columns = weight_ref[:, columns_of(other, True, 0, 1, weight_ref.shape[1])]
        part_ref[...] = jnp.dot(gated_ref[...], columns, preferred_element_type=F32)


def gate_early(queries, keys, values, skip, weight, conv, n_peers):
    rows, width = queries.shape
    out_width = weight.shape[1] // 4
    whole = pl.BlockSpec(memory_space=pltpu.VMEM)
    return pl.pallas_call(
        functools.partial(gate_early_kernel, n_peers),
        in_specs=[whole] * (5 + len(conv)),
        out_specs=[whole] * 3,
        out_shape=[jax.ShapeDtypeStruct((rows, width), BF16)]
        + [jax.ShapeDtypeStruct((rows, out_width), F32)] * 2,
        compiler_params=pltpu.CompilerParams(vmem_limit_bytes=PROJECT_VMEM),
        cost_estimate=pl.CostEstimate(
            flops=4 * rows * width * out_width, bytes_accessed=10 * rows * width, transcendentals=0
        ),
    )(queries, keys, values, skip, weight, *conv)


def late_product(late, late_slots, block, weight_ref, part_ref):
    chans = late.shape[1] // len(late_slots)
    at = columns_of(*block, weight_ref.shape[1])
    _, _, piece, pieces = block
    count = part_ref.shape[1] // pieces
    columns = jnp.concatenate([weight_ref[peer_block(s, chans), at] for s in late_slots], axis=0)
    part = part_ref[:, piece * count : (piece + 1) * count]
    return part + jnp.dot(late, columns, preferred_element_type=F32)


def gate_late_kernel(late_slots, block, queries_ref, keys_ref, values_ref, skip_ref, weight_ref, part_ref, *refs):
    *conv_refs, late_ref, sent_ref = refs
    chans = conv_refs[0].shape[1]
    for c, (slot, conv_ref) in enumerate(zip(late_slots, conv_refs)):
        gated = gate_slot(slot, queries_ref, keys_ref, values_ref, skip_ref, conv_ref)
        late_ref[:, c * chans : (c + 1) * chans] = gated
    total = late_product(late_ref[...], late_slots, block, weight_ref, part_ref)
    sent_ref[...] = total.astype(BF16)


def gate_late(queries, keys, values, skip, weight, part, conv, late_slots, block):
    rows, chans = conv[0].shape
    whole = pl.BlockSpec(memory_space=pltpu.VMEM)
    return pl.pallas_call(
        functools.partial(gate_late_kernel, late_slots, block),
        in_specs=[whole] * (6 + len(conv)),
        out_specs=[whole] * 2,
        out_shape=[
            jax.ShapeDtypeStruct((rows, chans * len(conv)), BF16),
            jax.ShapeDtypeStruct((rows, weight.shape[1] // 4 // block[-1]), BF16),
        ],
        compiler_params=pltpu.CompilerParams(vmem_limit_bytes=PROJECT_VMEM),
        cost_estimate=pl.CostEstimate(
            flops=rows * chans * weight.shape[1], bytes_accessed=2**20, transcendentals=0
        ),
    )(queries, keys, values, skip, weight, part, *conv)


def late_project_kernel(late_slots, blocks, weight_ref, late_ref, part_ref, *out_refs):
    for block, out_ref in zip(blocks, out_refs):
        total = late_product(late_ref[...], late_slots, block, weight_ref, part_ref)
        out_ref[...] = total.astype(out_ref.dtype)


def late_project(weight, late, part, late_slots, blocks, dtype):
    rows, depth = late.shape
    widths = [weight.shape[1] // 4 // pieces for *_, pieces in blocks]
    whole = pl.BlockSpec(memory_space=pltpu.VMEM)
    return pl.pallas_call(
        functools.partial(late_project_kernel, late_slots, blocks),
        in_specs=[whole] * 3,
        out_specs=[whole] * len(blocks),
        out_shape=[jax.ShapeDtypeStruct((rows, w), dtype) for w in widths],
        compiler_params=pltpu.CompilerParams(vmem_limit_bytes=PROJECT_VMEM),
        cost_estimate=pl.CostEstimate(
            flops=2 * rows * depth * sum(widths), bytes_accessed=2**20, transcendentals=0
        ),
    )(weight, late, part)


def assemble_kernel(late_slots, gated_ref, late_ref, out_ref):
    chans = late_ref.shape[1] // len(late_slots)
    out_ref[...] = gated_ref[...]
    for c, slot in enumerate(late_slots):
        out_ref[:, peer_block(slot, chans)] = late_ref[:, c * chans : (c + 1) * chans]


def assemble(gated, late, late_slots):
    whole = pl.BlockSpec(memory_space=pltpu.VMEM)
    return pl.pallas_call(
        functools.partial(assemble_kernel, late_slots),
        in_specs=[whole] * 2,
        out_specs=whole,
        out_shape=jax.ShapeDtypeStruct(gated.shape, BF16),
        compiler_params=pltpu.CompilerParams(vmem_limit_bytes=SMALL_VMEM),
        cost_estimate=pl.CostEstimate(flops=1000, bytes_accessed=2**20, transcendentals=0),
    )(gated, late)


def project_kernel(blocks, gated_ref, weight_ref, *out_refs):
    for block, out_ref in zip(blocks, out_refs):
        columns = weight_ref[:, columns_of(*block, weight_ref.shape[1])]
        total = jnp.dot(gated_ref[...], columns, preferred_element_type=F32)
        out_ref[...] = total.astype(out_ref.dtype)


def project(gated, weight, blocks, dtypes):
    rows, depth = gated.shape
    widths = [weight.shape[1] // 4 // pieces for *_, pieces in blocks]
    whole = pl.BlockSpec(memory_space=pltpu.VMEM)
    return pl.pallas_call(
        functools.partial(project_kernel, blocks),
        in_specs=[whole] * 2,
        out_specs=[whole] * len(blocks),
        out_shape=[jax.ShapeDtypeStruct((rows, w), t) for w, t in zip(widths, dtypes)],
        compiler_params=pltpu.CompilerParams(vmem_limit_bytes=PROJECT_VMEM),
        cost_estimate=pl.CostEstimate(
            flops=2 * rows * depth * sum(widths), bytes_accessed=2 * depth * sum(widths), transcendentals=0
        ),
    )(gated, weight)


def add_kernel(own_ref, arrived_ref, out_ref):
    total = own_ref[...] + arrived_ref[...].astype(F32)
    out_ref[...] = total.astype(out_ref.dtype)


def add(own, arrived):
    whole = pl.BlockSpec(memory_space=pltpu.VMEM)
    return pl.pallas_call(
        add_kernel,
        in_specs=[whole] * 2,
        out_specs=whole,
        out_shape=jax.ShapeDtypeStruct(arrived.shape, BF16),
        compiler_params=pltpu.CompilerParams(vmem_limit_bytes=SMALL_VMEM),
        cost_estimate=pl.CostEstimate(
            flops=arrived.size, bytes_accessed=8 * arrived.size, transcendentals=0
        ),
    )(own, arrived)


def mark_kernel(*refs):
    refs[-1][...] = jnp.zeros_like(refs[-1])


def mark(arrays):
    return pl.pallas_call(
        mark_kernel,
        in_specs=[pl.BlockSpec(memory_space=pl.ANY)] * len(arrays),
        out_specs=pl.BlockSpec(memory_space=pltpu.VMEM),
        out_shape=jax.ShapeDtypeStruct((8, 128), F32),
        compiler_params=pltpu.CompilerParams(vmem_limit_bytes=SMALL_VMEM),
        cost_estimate=pl.CostEstimate(flops=2 * 10**10, bytes_accessed=2**20, transcendentals=0),
    )(*arrays)


def finish_kernel(own_ref, near_ref, *refs):
    *arrived_refs, _, out_ref, stage, sem = refs
    width = out_ref.shape[1] // len(arrived_refs)
    steps = sem.shape[0]
    rows = out_ref.shape[0] // steps
    copies = []
    for step in range(steps):
        part = pl.ds(step * rows, rows)
        for c, arrived_ref in enumerate(arrived_refs):
            at = slice(c * width, (c + 1) * width)
            total = own_ref[part, at] + near_ref[part, at].astype(F32)
            stage[part, at] = (total + arrived_ref[part].astype(F32)).astype(stage.dtype)
        copies.append(pltpu.make_async_copy(stage.at[part], out_ref.at[part], sem.at[step]))
        copies[-1].start()
    for copy in copies:
        copy.wait()


def finish(own, near, arrived):
    rows, width = own.shape
    whole, anywhere = pl.BlockSpec(memory_space=pltpu.VMEM), pl.BlockSpec(memory_space=pl.ANY)
    return pl.pallas_call(
        finish_kernel,
        in_specs=[whole] * (2 + len(arrived)) + [anywhere],
        out_specs=anywhere,
        out_shape=jax.ShapeDtypeStruct((rows, width), BF16),
        scratch_shapes=[pltpu.VMEM((rows, width), BF16), pltpu.SemaphoreType.DMA((4,))],
        compiler_params=pltpu.CompilerParams(vmem_limit_bytes=SMALL_VMEM),
        cost_estimate=pl.CostEstimate(
            flops=rows * width, bytes_accessed=8 * rows * width, transcendentals=0
        ),
    )(own, near, *arrived, mark(arrived))


def body(pieces, tables, queries, keys, values, filters, skip_weight, out_weight):
    rows, width = keys.shape
    n_peers = lax.axis_size("seq")
    chans = width // n_peers
    fwd, bwd = (jnp.asarray(t) for t in tables)
    skip = skip_weight[None, :]
    in_chip = [(0, 1), (1, 0), (2, 3), (3, 2)]
    across = [(0, 2), (2, 0), (1, 3), (3, 1)]

    sends = [(True, True, c, pieces) for c in range(pieces)]
    keeps = [(False, True, c, pieces) for c in range(pieces)]

    if chans % 128 == 0 and n_peers == 8:
        blocks = pre(keys, values, filters, n_peers)
        received = exchange(blocks, n_peers, False)
        fwd, bwd, early, part = spectra(received[:-2], fwd, bwd, n_peers)
        back = exchange(conv_fast(early, part, received[-2:], fwd, bwd), n_peers, True)
        slots = slots_of(n_peers, True)[-2:]
        gated, send_part, own_part = gate_early(
            queries, keys, values, skip, out_weight, back[:-2], n_peers
        )
        late, last = gate_late(
            queries, keys, values, skip, out_weight, send_part, back[-2:], slots, sends[-1]
        )
        sent = [
            *(late_project(out_weight, late, send_part, slots, [s], BF16)[0] for s in sends[:-1]),
            last,
        ]
        ours = late_project(out_weight, late, own_part, slots, keeps, F32)
        gated = assemble(gated, late, slots)
    else:
        product = keys.astype(F32) * values.astype(F32)
        parts = [a.astype(BF16).reshape(rows, n_peers, chans) for a in (product, filters)]
        sent = jnp.concatenate(parts, axis=2).transpose(1, 0, 2)
        received = lax.all_to_all(sent, "seq", split_axis=0, concat_axis=0, tiled=True)
        conv = conv_plain(received, fwd, bwd)
        back = lax.all_to_all(conv, "seq", split_axis=0, concat_axis=0, tiled=True)
        mixed = back.transpose(1, 0, 2).reshape(rows, width).astype(F32) + skip * product
        gated = (queries.astype(F32) * mixed).astype(BF16)
        sent = project(gated, out_weight, sends, [BF16] * pieces)
        ours = project(gated, out_weight, keeps, [F32] * pieces)

    theirs = [lax.ppermute(piece, "fsdp", in_chip) for piece in sent]
    arrived = [lax.ppermute(add(*pair), "fsdp", across) for pair in zip(ours, theirs)]
    blocks = [(True, False, 0, 1), (False, False, 0, 1)]
    sent, own = project(gated, out_weight, blocks, [BF16, F32])
    near = lax.ppermute(sent, "fsdp", in_chip)
    return finish(own, near, arrived)


def solution(mesh):
    in_specs = (
        P("seq", "fsdp"),
        P("seq", "fsdp"),
        P("seq", "fsdp"),
        P("seq", "fsdp"),
        P("fsdp"),
        P("fsdp", None),
    )
    out_specs = P("seq", "fsdp")

    def run(queries, keys, values, filters, skip_weight, out_weight):
        rows = keys.shape[0] // mesh.shape["seq"]
        fn = functools.partial(body, 2, make_tables(rows))
        return jax.shard_map(fn, mesh=mesh, in_specs=in_specs, out_specs=out_specs, check_vma=False)(
            queries, keys, values, filters, skip_weight, out_weight
        )

    return run
```

```python
import functools

import numpy as np

import jax
import jax.numpy as jnp
from jax import lax
from jax.experimental import pallas as pl
from jax.experimental.pallas import tpu as pltpu
from jax.sharding import PartitionSpec as P

BF16 = jnp.bfloat16
F32 = jnp.float32
CONV_VMEM = 24 * 2**20
PROJECT_VMEM = 24 * 2**20
SMALL_VMEM = 12 * 2**20
STEP = 16


def split_bf16(table):
    high = table.astype(BF16)
    return high, (table - high.astype(np.float64)).astype(BF16)


def make_tables(rows):
    order = np.concatenate([np.arange(0, rows, 2), np.arange(1, rows, 2)])
    times = np.arange(rows)
    angle = np.pi * (((2 * order[:, None] + 1) * times[None, :]) % (4 * rows)) / (2 * rows)
    forward = np.concatenate([np.cos(angle), -np.sin(angle)], axis=0)
    high, low = split_bf16(forward)
    back_high, back_low = split_bf16(forward.T / rows)
    return (
        np.concatenate([high, low], axis=1),
        np.concatenate([back_high, back_low, back_high], axis=1),
    )


def peer_of(slot):
    return lax.bitwise_xor(lax.axis_index("seq"), slot)


def peer_block(slot, size):
    return pl.ds(pl.multiple_of(peer_of(slot) * size, size), size)


def pre_kernel(n_peers, keys_hbm, values_hbm, filters_hbm, *refs):
    out_refs = refs[:n_peers]
    keys, values, filters, sem = refs[n_peers:]
    rows, width = keys.shape
    chans = width // n_peers
    steps = sem.shape[0]
    parts = [pl.ds(c * rows // steps, rows // steps) for c in range(steps)]
    pairs = ((keys_hbm, keys), (values_hbm, values), (filters_hbm, filters))
    copies = [
        [
            pltpu.make_async_copy(src.at[part], dst.at[part], sem.at[c, i])
            for i, (src, dst) in enumerate(pairs)
        ]
        for c, part in enumerate(parts)
    ]
    for group in copies:
        for copy in group:
            copy.start()
    for part, group in zip(parts, copies):
        for copy in group:
            copy.wait()
        for slot, out_ref in zip(slots_of(n_peers, False), out_refs):
            at = peer_block(slot, chans)
            product = keys[part, at].astype(F32) * values[part, at].astype(F32)
            out_ref[part, :chans] = product.astype(BF16)
            out_ref[part, chans:] = filters[part, at].astype(BF16)


def pre(keys, values, filters, n_peers):
    rows, width = keys.shape
    chans = width // n_peers
    args = [pltpu.with_memory_space_constraint(a, pltpu.HBM) for a in (keys, values, filters)]
    return pl.pallas_call(
        functools.partial(pre_kernel, n_peers),
        in_specs=[pl.BlockSpec(memory_space=pltpu.HBM)] * 3,
        out_specs=[pl.BlockSpec(memory_space=pltpu.VMEM)] * n_peers,
        out_shape=[jax.ShapeDtypeStruct((rows, 2 * chans), BF16)] * n_peers,
        scratch_shapes=[
            pltpu.VMEM((rows, width), BF16),
            pltpu.VMEM((rows, width), BF16),
            pltpu.VMEM((rows, width), F32),
            pltpu.SemaphoreType.DMA((2, 3)),
        ],
        compiler_params=pltpu.CompilerParams(vmem_limit_bytes=SMALL_VMEM),
        cost_estimate=pl.CostEstimate(
            flops=rows * width, bytes_accessed=12 * rows * width, transcendentals=0
        ),
    )(*args)


def slots_of(n_peers, back):
    half = n_peers // 2
    near, far = list(range(1, half)), list(range(half, n_peers))
    if back:
        return [0, near[0]] + far[:3] + [near[1]] + far[3:] + near[2:]
    far = far[2:] + far[:2]
    return [0, near[0], far[0], near[1], far[1]] + near[2:] + far[2:]


def exchange(blocks, n_peers, back):
    return [
        lax.ppermute(block, "seq", [(i, i ^ slot) for i in range(n_peers)]) if slot else block
        for slot, block in zip(slots_of(n_peers, back), blocks)
    ]


def block_spectrum(table, block):
    return jnp.dot(table, jnp.concatenate([block, block], axis=0), preferred_element_type=F32)


def times(a, b):
    return a[0] * b[0] - a[1] * b[1], a[0] * b[1] + a[1] * b[0]


def plus(a, b):
    return b if a is None else (a[0] + b[0], a[1] + b[1])


def late_place(n_blocks):
    return lax.div(peer_of(slots_of(n_blocks, False)[-1]), 2)


def load(ref, at, row, step, rows, lanes):
    return tuple(ref[(*at, pl.ds(row + part * rows, step), lanes)] for part in range(2))


def mix_early(pair, step, spec_ref, part_ref):
    n_blocks, rows, chans = spec_ref.shape[0], spec_ref.shape[1] // 2, spec_ref.shape[2] // 2
    early = [j for j in range(n_blocks) if j // 2 != pair]

    @pl.loop(0, rows // step)
    def _(t):
        row = pl.multiple_of(t * step, step)
        signal = {j: load(spec_ref, (j,), row, step, rows, slice(0, chans)) for j in early}
        filt = {j: load(spec_ref, (j,), row, step, rows, slice(chans, 2 * chans)) for j in early}
        for i in range(n_blocks):
            total = None
            for d in early:
                if i - d in early:
                    total = plus(total, times(filt[d], signal[i - d]))
            if total is None:
                total = (jnp.zeros((step, chans), F32),) * 2
            for part in range(2):
                part_ref[i, pl.ds(row + part * rows, step)] = total[part]


def spectra_kernel(n_peers, fwd_hbm, bwd_hbm, *refs):
    *in_refs, fwd_ref, bwd_ref, spec_ref, part_ref, sem = refs
    copies = [
        pltpu.make_async_copy(fwd_hbm, fwd_ref, sem.at[0]),
        pltpu.make_async_copy(bwd_hbm, bwd_ref, sem.at[1]),
    ]
    for copy in copies:
        copy.start()
    copies[0].wait()
    for slot, in_ref in zip(slots_of(n_peers, False), in_refs):
        spec_ref[peer_of(slot)] = block_spectrum(fwd_ref[...], in_ref[...])
    for pair in range(n_peers // 2):
        pl.when(late_place(n_peers) == pair)(
            functools.partial(mix_early, pair, STEP, spec_ref, part_ref)
        )
    copies[1].wait()


def spectra(received, fwd, bwd, n_peers):
    rows, width = received[0].shape
    whole = pl.BlockSpec(memory_space=pltpu.VMEM)
    args = [pltpu.with_memory_space_constraint(a, pltpu.HBM) for a in (fwd, bwd)]
    return pl.pallas_call(
        functools.partial(spectra_kernel, n_peers),
        in_specs=[pl.BlockSpec(memory_space=pltpu.HBM)] * 2 + [whole] * len(received),
        out_specs=[whole] * 4,
        out_shape=[
            jax.ShapeDtypeStruct(fwd.shape, BF16),
            jax.ShapeDtypeStruct(bwd.shape, BF16),
            jax.ShapeDtypeStruct((n_peers, 2 * rows, width), F32),
            jax.ShapeDtypeStruct((n_peers, 2 * rows, width // 2), F32),
        ],
        scratch_shapes=[pltpu.SemaphoreType.DMA((2,))],
        compiler_params=pltpu.CompilerParams(vmem_limit_bytes=CONV_VMEM),
        cost_estimate=pl.CostEstimate(
            flops=8 * len(received) * rows * rows * width, bytes_accessed=4 * 2**20, transcendentals=0
        ),
    )(*args, *received)


def mix_late(pair, step, first, last, sign, spec_ref, part_ref, late_ref, turned):
    n_blocks, rows, chans = spec_ref.shape[0], spec_ref.shape[1] // 2, spec_ref.shape[2] // 2
    early = [j for j in range(n_blocks) if j // 2 != pair]
    x_at, f_at = slice(0, chans), slice(chans, 2 * chans)

    @pl.loop(first // step, last // step)
    def _(t):
        row = pl.multiple_of(t * step, step)
        late = [2 * pair, 2 * pair + 1]
        signal = {j: load(late_ref, (j % 2,), row, step, rows, x_at) for j in late}
        filt = {j: load(late_ref, (j % 2,), row, step, rows, f_at) for j in late}
        total = [load(part_ref, (i,), row, step, rows, slice(0, chans)) for i in range(n_blocks)]
        for b in early:
            if b + late[0] >= n_blocks:
                continue
            x_b = load(spec_ref, (b,), row, step, rows, x_at)
            f_b = load(spec_ref, (b,), row, step, rows, f_at)
            for j in late:
                if b + j < n_blocks:
                    total[b + j] = plus(total[b + j], times(filt[j], x_b))
                    total[b + j] = plus(total[b + j], times(f_b, signal[j]))
        for j in late:
            for d in late:
                if j + d < n_blocks:
                    total[j + d] = plus(total[j + d], times(filt[d], signal[j]))
        for i in range(n_blocks):
            value = total[i]
            if i > 0:
                turn_re, turn_im = total[i - 1]
                if sign > 0:
                    value = value[0] - turn_im, value[1] + turn_re
                else:
                    value = value[0] + turn_im, value[1] - turn_re
            lanes = slice(i % 2 * chans, (i % 2 + 1) * chans)
            for part in range(2):
                high = value[part].astype(BF16)
                low = (value[part] - high.astype(F32)).astype(BF16)
                for c, piece in enumerate((high, high, low)):
                    turned[i // 2, pl.ds(row + (2 * c + part) * rows, step), lanes] = piece


def conv_kernel(fwd_ref, bwd_ref, spec_ref, part_ref, *refs):
    *refs, late_ref, turned = refs
    n_blocks = spec_ref.shape[0]
    in_refs, out_refs = refs[:-n_blocks], refs[-n_blocks:]
    rows, chans = in_refs[0].shape[0], in_refs[0].shape[1] // 2
    for slot, in_ref in zip(slots_of(n_blocks, False)[-2:], in_refs):
        late_ref[lax.bitwise_and(peer_of(slot), 1)] = block_spectrum(fwd_ref[...], in_ref[...])

    def mix(pair):
        for first, last, sign in ((0, rows // 2, 1), (rows // 2, rows, -1)):
            mix_late(pair, STEP, first, last, sign, spec_ref, part_ref, late_ref, turned)

    for pair in range(n_blocks // 2):
        pl.when(late_place(n_blocks) == pair)(functools.partial(mix, pair))

    odd = lax.bitwise_and(lax.axis_index("seq"), 1) == 1
    by_slot = dict(zip(slots_of(n_blocks, True), out_refs))
    for slot in range(0, n_blocks, 2):
        pair = lax.div(peer_of(slot), 2)
        both = jnp.dot(bwd_ref[...], turned[pair], preferred_element_type=F32)
        left, right = both[:, :chans], both[:, chans:]
        by_slot[slot][...] = jnp.where(odd, right, left).astype(BF16)
        by_slot[slot + 1][...] = jnp.where(odd, left, right).astype(BF16)


def conv_fast(early, part, late, fwd, bwd):
    n_blocks = early.shape[0]
    rows, chans = late[0].shape[0], late[0].shape[1] // 2
    whole = pl.BlockSpec(memory_space=pltpu.VMEM)
    return pl.pallas_call(
        conv_kernel,
        in_specs=[whole] * 6,
        out_specs=[whole] * n_blocks,
        out_shape=[jax.ShapeDtypeStruct((rows, chans), BF16)] * n_blocks,
        scratch_shapes=[
            pltpu.VMEM((2, 2 * rows, 2 * chans), F32),
            pltpu.VMEM((n_blocks // 2, 6 * rows, 2 * chans), BF16),
        ],
        compiler_params=pltpu.CompilerParams(vmem_limit_bytes=CONV_VMEM),
        cost_estimate=pl.CostEstimate(
            flops=16 * n_blocks * rows * rows * chans, bytes_accessed=4 * 2**20, transcendentals=0
        ),
    )(fwd, bwd, early, part, *late)


def conv_plain(received, fwd, bwd):
    n_blocks, rows, chans = received.shape[0], received.shape[1], received.shape[2] // 2
    exact = lax.Precision.HIGHEST
    fwd32 = fwd[:, :rows].astype(F32) + fwd[:, rows:].astype(F32)
    bwd32 = bwd[:, : 2 * rows].astype(F32) + bwd[:, 2 * rows : 4 * rows].astype(F32)
    sign = jnp.where(jnp.arange(rows) < rows // 2, 1.0, -1.0).astype(F32)[:, None]

    def spectrum(blocks):
        spec = jnp.einsum("kt,jtc->jkc", fwd32, blocks.astype(F32), precision=exact)
        return spec[:, :rows], spec[:, rows:]

    x_re, x_im = spectrum(received[:, :, :chans])
    f_re, f_im = spectrum(received[:, :, chans:])
    g_re = f_re.at[1:].add(-sign * f_im[:-1])
    g_im = f_im.at[1:].add(sign * f_re[:-1])

    def one(d, total):
        t_re, t_im = total
        later = (jnp.arange(n_blocks) >= d)[:, None, None]
        a_re = jnp.where(later, jnp.roll(x_re, d, axis=0), 0.0)
        a_im = jnp.where(later, jnp.roll(x_im, d, axis=0), 0.0)
        return (
            t_re + g_re[d] * a_re - g_im[d] * a_im,
            t_im + g_re[d] * a_im + g_im[d] * a_re,
        )

    zero = jnp.zeros_like(x_re)
    y_re, y_im = lax.fori_loop(0, n_blocks, one, (zero, zero))
    both = jnp.concatenate([y_re, y_im], axis=1)
    return jnp.einsum("tk,jkc->jtc", bwd32, both, precision=exact).astype(BF16)


def columns_of(other, across, piece, pieces, width):
    count = width // 4 // pieces
    place = lax.axis_index("fsdp")
    core, side = lax.rem(place, 2), lax.div(place, 2)
    block = 2 * (1 - side if across else side) + (1 - core if other else core)
    return pl.ds(pl.multiple_of((block * pieces + piece) * count, count), count)


def gate_slot(slot, queries_ref, keys_ref, values_ref, skip_ref, conv_ref):
    at = peer_block(slot, conv_ref.shape[1])
    product = keys_ref[:, at].astype(F32) * values_ref[:, at].astype(F32)
    mixed = conv_ref[...].astype(F32) + skip_ref[:, at] * product
    return (queries_ref[:, at].astype(F32) * mixed).astype(BF16)


def gate_early_kernel(n_peers, queries_ref, keys_ref, values_ref, skip_ref, weight_ref, *refs):
    conv_refs, (gated_ref, *part_refs) = refs[:-3], refs[-3:]
    chans = conv_refs[0].shape[1]
    slots = slots_of(n_peers, True)
    for slot, conv_ref in zip(slots, conv_refs):
        gated = gate_slot(slot, queries_ref, keys_ref, values_ref, skip_ref, conv_ref)
        gated_ref[:, peer_block(slot, chans)] = gated
    for slot in slots[len(conv_refs) :]:
        gated_ref[:, peer_block(slot, chans)] = jnp.zeros((gated_ref.shape[0], chans), BF16)
    for other, part_ref in zip((True, False), part_refs):
        columns = weight_ref[:, columns_of(other, True, 0, 1, weight_ref.shape[1])]
        part_ref[...] = jnp.dot(gated_ref[...], columns, preferred_element_type=F32)


def gate_early(queries, keys, values, skip, weight, conv, n_peers):
    rows, width = queries.shape
    out_width = weight.shape[1] // 4
    whole = pl.BlockSpec(memory_space=pltpu.VMEM)
    return pl.pallas_call(
        functools.partial(gate_early_kernel, n_peers),
        in_specs=[whole] * (5 + len(conv)),
        out_specs=[whole] * 3,
        out_shape=[jax.ShapeDtypeStruct((rows, width), BF16)]
        + [jax.ShapeDtypeStruct((rows, out_width), F32)] * 2,
        compiler_params=pltpu.CompilerParams(vmem_limit_bytes=PROJECT_VMEM),
        cost_estimate=pl.CostEstimate(
            flops=4 * rows * width * out_width, bytes_accessed=10 * rows * width, transcendentals=0
        ),
    )(queries, keys, values, skip, weight, *conv)


def late_product(late, late_slots, block, weight_ref, part_ref):
    chans = late.shape[1] // len(late_slots)
    at = columns_of(*block, weight_ref.shape[1])
    _, _, piece, pieces = block
    count = part_ref.shape[1] // pieces
    columns = jnp.concatenate([weight_ref[peer_block(s, chans), at] for s in late_slots], axis=0)
    part = part_ref[:, piece * count : (piece + 1) * count]
    return part + jnp.dot(late, columns, preferred_element_type=F32)


def gate_late_kernel(late_slots, block, queries_ref, keys_ref, values_ref, skip_ref, weight_ref, part_ref, *refs):
    *conv_refs, late_ref, sent_ref = refs
    chans = conv_refs[0].shape[1]
    for c, (slot, conv_ref) in enumerate(zip(late_slots, conv_refs)):
        gated = gate_slot(slot, queries_ref, keys_ref, values_ref, skip_ref, conv_ref)
        late_ref[:, c * chans : (c + 1) * chans] = gated
    total = late_product(late_ref[...], late_slots, block, weight_ref, part_ref)
    sent_ref[...] = total.astype(BF16)


def gate_late(queries, keys, values, skip, weight, part, conv, late_slots, block):
    rows, chans = conv[0].shape
    whole = pl.BlockSpec(memory_space=pltpu.VMEM)
    return pl.pallas_call(
        functools.partial(gate_late_kernel, late_slots, block),
        in_specs=[whole] * (6 + len(conv)),
        out_specs=[whole] * 2,
        out_shape=[
            jax.ShapeDtypeStruct((rows, chans * len(conv)), BF16),
            jax.ShapeDtypeStruct((rows, weight.shape[1] // 4 // block[-1]), BF16),
        ],
        compiler_params=pltpu.CompilerParams(vmem_limit_bytes=PROJECT_VMEM),
        cost_estimate=pl.CostEstimate(
            flops=rows * chans * weight.shape[1], bytes_accessed=2**20, transcendentals=0
        ),
    )(queries, keys, values, skip, weight, part, *conv)


def late_project_kernel(late_slots, blocks, weight_ref, late_ref, part_ref, *out_refs):
    for block, out_ref in zip(blocks, out_refs):
        total = late_product(late_ref[...], late_slots, block, weight_ref, part_ref)
        out_ref[...] = total.astype(out_ref.dtype)


def late_project(weight, late, part, late_slots, blocks, dtype):
    rows, depth = late.shape
    widths = [weight.shape[1] // 4 // pieces for *_, pieces in blocks]
    whole = pl.BlockSpec(memory_space=pltpu.VMEM)
    return pl.pallas_call(
        functools.partial(late_project_kernel, late_slots, blocks),
        in_specs=[whole] * 3,
        out_specs=[whole] * len(blocks),
        out_shape=[jax.ShapeDtypeStruct((rows, w), dtype) for w in widths],
        compiler_params=pltpu.CompilerParams(vmem_limit_bytes=PROJECT_VMEM),
        cost_estimate=pl.CostEstimate(
            flops=2 * rows * depth * sum(widths), bytes_accessed=2**20, transcendentals=0
        ),
    )(weight, late, part)


def assemble_kernel(late_slots, gated_ref, late_ref, out_ref):
    chans = late_ref.shape[1] // len(late_slots)
    out_ref[...] = gated_ref[...]
    for c, slot in enumerate(late_slots):
        out_ref[:, peer_block(slot, chans)] = late_ref[:, c * chans : (c + 1) * chans]


def assemble(gated, late, late_slots):
    whole = pl.BlockSpec(memory_space=pltpu.VMEM)
    return pl.pallas_call(
        functools.partial(assemble_kernel, late_slots),
        in_specs=[whole] * 2,
        out_specs=whole,
        out_shape=jax.ShapeDtypeStruct(gated.shape, BF16),
        compiler_params=pltpu.CompilerParams(vmem_limit_bytes=SMALL_VMEM),
        cost_estimate=pl.CostEstimate(flops=1000, bytes_accessed=2**20, transcendentals=0),
    )(gated, late)


def project_kernel(blocks, gated_ref, weight_ref, *out_refs):
    for block, out_ref in zip(blocks, out_refs):
        columns = weight_ref[:, columns_of(*block, weight_ref.shape[1])]
        total = jnp.dot(gated_ref[...], columns, preferred_element_type=F32)
        out_ref[...] = total.astype(out_ref.dtype)


def project(gated, weight, blocks, dtypes):
    rows, depth = gated.shape
    widths = [weight.shape[1] // 4 // pieces for *_, pieces in blocks]
    whole = pl.BlockSpec(memory_space=pltpu.VMEM)
    return pl.pallas_call(
        functools.partial(project_kernel, blocks),
        in_specs=[whole] * 2,
        out_specs=[whole] * len(blocks),
        out_shape=[jax.ShapeDtypeStruct((rows, w), t) for w, t in zip(widths, dtypes)],
        compiler_params=pltpu.CompilerParams(vmem_limit_bytes=PROJECT_VMEM),
        cost_estimate=pl.CostEstimate(
            flops=2 * rows * depth * sum(widths), bytes_accessed=2 * depth * sum(widths), transcendentals=0
        ),
    )(gated, weight)


def add_kernel(own_ref, arrived_ref, out_ref):
    total = own_ref[...] + arrived_ref[...].astype(F32)
    out_ref[...] = total.astype(out_ref.dtype)


def add(own, arrived):
    whole = pl.BlockSpec(memory_space=pltpu.VMEM)
    return pl.pallas_call(
        add_kernel,
        in_specs=[whole] * 2,
        out_specs=whole,
        out_shape=jax.ShapeDtypeStruct(arrived.shape, BF16),
        compiler_params=pltpu.CompilerParams(vmem_limit_bytes=SMALL_VMEM),
        cost_estimate=pl.CostEstimate(
            flops=arrived.size, bytes_accessed=8 * arrived.size, transcendentals=0
        ),
    )(own, arrived)


def mark_kernel(*refs):
    refs[-1][...] = jnp.zeros_like(refs[-1])


def mark(arrays):
    return pl.pallas_call(
        mark_kernel,
        in_specs=[pl.BlockSpec(memory_space=pl.ANY)] * len(arrays),
        out_specs=pl.BlockSpec(memory_space=pltpu.VMEM),
        out_shape=jax.ShapeDtypeStruct((8, 128), F32),
        compiler_params=pltpu.CompilerParams(vmem_limit_bytes=SMALL_VMEM),
        cost_estimate=pl.CostEstimate(flops=2 * 10**10, bytes_accessed=2**20, transcendentals=0),
    )(*arrays)


def finish_kernel(own_ref, near_ref, *refs):
    *arrived_refs, _, out_ref, stage, sem = refs
    width = out_ref.shape[1] // len(arrived_refs)
    steps = sem.shape[0]
    rows = out_ref.shape[0] // steps
    copies = []
    for step in range(steps):
        part = pl.ds(step * rows, rows)
        for c, arrived_ref in enumerate(arrived_refs):
            at = slice(c * width, (c + 1) * width)
            total = own_ref[part, at] + near_ref[part, at].astype(F32)
            stage[part, at] = (total + arrived_ref[part].astype(F32)).astype(stage.dtype)
        copies.append(pltpu.make_async_copy(stage.at[part], out_ref.at[part], sem.at[step]))
        copies[-1].start()
    for copy in copies:
        copy.wait()


def finish(own, near, arrived):
    rows, width = own.shape
    whole, anywhere = pl.BlockSpec(memory_space=pltpu.VMEM), pl.BlockSpec(memory_space=pl.ANY)
    return pl.pallas_call(
        finish_kernel,
        in_specs=[whole] * (2 + len(arrived)) + [anywhere],
        out_specs=anywhere,
        out_shape=jax.ShapeDtypeStruct((rows, width), BF16),
        scratch_shapes=[pltpu.VMEM((rows, width), BF16), pltpu.SemaphoreType.DMA((4,))],
        compiler_params=pltpu.CompilerParams(vmem_limit_bytes=SMALL_VMEM),
        cost_estimate=pl.CostEstimate(
            flops=rows * width, bytes_accessed=8 * rows * width, transcendentals=0
        ),
    )(own, near, *arrived, mark(arrived))


def body(pieces, tables, queries, keys, values, filters, skip_weight, out_weight):
    rows, width = keys.shape
    n_peers = lax.axis_size("seq")
    chans = width // n_peers
    fwd, bwd = (jnp.asarray(t) for t in tables)
    skip = skip_weight[None, :]
    in_chip = [(0, 1), (1, 0), (2, 3), (3, 2)]
    across = [(0, 2), (2, 0), (1, 3), (3, 1)]

    sends = [(True, True, c, pieces) for c in range(pieces)]
    keeps = [(False, True, c, pieces) for c in range(pieces)]

    if chans % 128 == 0 and n_peers == 8:
        blocks = pre(keys, values, filters, n_peers)
        received = exchange(blocks, n_peers, False)
        fwd, bwd, early, part = spectra(received[:-2], fwd, bwd, n_peers)
        back = exchange(conv_fast(early, part, received[-2:], fwd, bwd), n_peers, True)
        slots = slots_of(n_peers, True)[-2:]
        gated, send_part, own_part = gate_early(
            queries, keys, values, skip, out_weight, back[:-2], n_peers
        )
        late, last = gate_late(
            queries, keys, values, skip, out_weight, send_part, back[-2:], slots, sends[-1]
        )
        sent = [
            *(late_project(out_weight, late, send_part, slots, [s], BF16)[0] for s in sends[:-1]),
            last,
        ]
        ours = late_project(out_weight, late, own_part, slots, keeps, F32)
        gated = assemble(gated, late, slots)
    else:
        product = keys.astype(F32) * values.astype(F32)
        parts = [a.astype(BF16).reshape(rows, n_peers, chans) for a in (product, filters)]
        sent = jnp.concatenate(parts, axis=2).transpose(1, 0, 2)
        received = lax.all_to_all(sent, "seq", split_axis=0, concat_axis=0, tiled=True)
        conv = conv_plain(received, fwd, bwd)
        back = lax.all_to_all(conv, "seq", split_axis=0, concat_axis=0, tiled=True)
        mixed = back.transpose(1, 0, 2).reshape(rows, width).astype(F32) + skip * product
        gated = (queries.astype(F32) * mixed).astype(BF16)
        sent = project(gated, out_weight, sends, [BF16] * pieces)
        ours = project(gated, out_weight, keeps, [F32] * pieces)

    theirs = [lax.ppermute(piece, "fsdp", in_chip) for piece in sent]
    arrived = [lax.ppermute(add(*pair), "fsdp", across) for pair in zip(ours, theirs)]
    blocks = [(True, False, 0, 1), (False, False, 0, 1)]
    sent, own = project(gated, out_weight, blocks, [BF16, F32])
    near = lax.ppermute(sent, "fsdp", in_chip)
    return finish(own, near, arrived)


def solution(mesh):
    in_specs = (
        P("seq", "fsdp"),
        P("seq", "fsdp"),
        P("seq", "fsdp"),
        P("seq", "fsdp"),
        P("fsdp"),
        P("fsdp", None),
    )
    out_specs = P("seq", "fsdp")

    def run(queries, keys, values, filters, skip_weight, out_weight):
        rows = keys.shape[0] // mesh.shape["seq"]
        fn = functools.partial(body, 2, make_tables(rows))
        return jax.shard_map(fn, mesh=mesh, in_specs=in_specs, out_specs=out_specs, check_vma=False)(
            queries, keys, values, filters, skip_weight, out_weight
        )

    return run
```

```python
import functools

import numpy as np

import jax
import jax.numpy as jnp
from jax import lax
from jax.experimental import pallas as pl
from jax.experimental.pallas import tpu as pltpu
from jax.sharding import PartitionSpec as P

BF16 = jnp.bfloat16
F32 = jnp.float32
CONV_VMEM = 24 * 2**20
PROJECT_VMEM = 24 * 2**20
SMALL_VMEM = 12 * 2**20
STEP = 16


def split_bf16(table):
    high = table.astype(BF16)
    return high, (table - high.astype(np.float64)).astype(BF16)


def make_tables(rows):
    order = np.concatenate([np.arange(0, rows, 2), np.arange(1, rows, 2)])
    times = np.arange(rows)
    angle = np.pi * (((2 * order[:, None] + 1) * times[None, :]) % (4 * rows)) / (2 * rows)
    forward = np.concatenate([np.cos(angle), -np.sin(angle)], axis=0)
    high, low = split_bf16(forward)
    back_high, back_low = split_bf16(forward.T / rows)
    return (
        np.concatenate([high, low], axis=1),
        np.concatenate([back_high, back_low, back_high], axis=1),
    )


def peer_of(slot):
    return lax.bitwise_xor(lax.axis_index("seq"), slot)


def peer_block(slot, size):
    return pl.ds(pl.multiple_of(peer_of(slot) * size, size), size)


def pre_kernel(n_peers, keys_hbm, values_hbm, filters_hbm, *refs):
    out_refs = refs[:n_peers]
    keys, values, filters, sem = refs[n_peers:]
    rows, width = keys.shape
    chans = width // n_peers
    steps = sem.shape[0]
    parts = [pl.ds(c * rows // steps, rows // steps) for c in range(steps)]
    pairs = ((keys_hbm, keys), (values_hbm, values), (filters_hbm, filters))
    copies = [
        [
            pltpu.make_async_copy(src.at[part], dst.at[part], sem.at[c, i])
            for i, (src, dst) in enumerate(pairs)
        ]
        for c, part in enumerate(parts)
    ]
    for group in copies:
        for copy in group:
            copy.start()
    for part, group in zip(parts, copies):
        for copy in group:
            copy.wait()
        for slot, out_ref in zip(slots_of(n_peers, False), out_refs):
            at = peer_block(slot, chans)
            product = keys[part, at].astype(F32) * values[part, at].astype(F32)
            out_ref[part, :chans] = product.astype(BF16)
            out_ref[part, chans:] = filters[part, at].astype(BF16)


def pre(keys, values, filters, n_peers):
    rows, width = keys.shape
    chans = width // n_peers
    args = [pltpu.with_memory_space_constraint(a, pltpu.HBM) for a in (keys, values, filters)]
    return pl.pallas_call(
        functools.partial(pre_kernel, n_peers),
        in_specs=[pl.BlockSpec(memory_space=pltpu.HBM)] * 3,
        out_specs=[pl.BlockSpec(memory_space=pltpu.VMEM)] * n_peers,
        out_shape=[jax.ShapeDtypeStruct((rows, 2 * chans), BF16)] * n_peers,
        scratch_shapes=[
            pltpu.VMEM((rows, width), BF16),
            pltpu.VMEM((rows, width), BF16),
            pltpu.VMEM((rows, width), F32),
            pltpu.SemaphoreType.DMA((2, 3)),
        ],
        compiler_params=pltpu.CompilerParams(vmem_limit_bytes=SMALL_VMEM),
        cost_estimate=pl.CostEstimate(
            flops=rows * width, bytes_accessed=12 * rows * width, transcendentals=0
        ),
    )(*args)


def slots_of(n_peers, back):
    half = n_peers // 2
    near, far = list(range(1, half)), list(range(half, n_peers))
    if back:
        far = far[2:] + far[:2]
        return [0, near[0]] + far[:3] + [near[1]] + far[3:] + near[2:]
    return [0, near[0], far[0], near[1], far[1]] + near[2:] + far[2:]


def exchange(blocks, n_peers, back):
    return [
        lax.ppermute(block, "seq", [(i, i ^ slot) for i in range(n_peers)]) if slot else block
        for slot, block in zip(slots_of(n_peers, back), blocks)
    ]


def block_spectrum(table, block):
    return jnp.dot(table, jnp.concatenate([block, block], axis=0), preferred_element_type=F32)


def times(a, b):
    return a[0] * b[0] - a[1] * b[1], a[0] * b[1] + a[1] * b[0]


def plus(a, b):
    return b if a is None else (a[0] + b[0], a[1] + b[1])


def late_place(n_blocks):
    return lax.div(peer_of(slots_of(n_blocks, False)[-1]), 2)


def load(ref, at, row, step, rows, lanes):
    return tuple(ref[(*at, pl.ds(row + part * rows, step), lanes)] for part in range(2))


def mix_early(pair, step, spec_ref, part_ref):
    n_blocks, rows, chans = spec_ref.shape[0], spec_ref.shape[1] // 2, spec_ref.shape[2] // 2
    early = [j for j in range(n_blocks) if j // 2 != pair]

    @pl.loop(0, rows // step)
    def _(t):
        row = pl.multiple_of(t * step, step)
        signal = {j: load(spec_ref, (j,), row, step, rows, slice(0, chans)) for j in early}
        filt = {j: load(spec_ref, (j,), row, step, rows, slice(chans, 2 * chans)) for j in early}
        for i in range(n_blocks):
            total = None
            for d in early:
                if i - d in early:
                    total = plus(total, times(filt[d], signal[i - d]))
            if total is None:
                total = (jnp.zeros((step, chans), F32),) * 2
            for part in range(2):
                part_ref[i, pl.ds(row + part * rows, step)] = total[part]


def spectra_kernel(n_peers, fwd_hbm, bwd_hbm, *refs):
    *in_refs, fwd_ref, bwd_ref, spec_ref, part_ref, sem = refs
    copies = [
        pltpu.make_async_copy(fwd_hbm, fwd_ref, sem.at[0]),
        pltpu.make_async_copy(bwd_hbm, bwd_ref, sem.at[1]),
    ]
    for copy in copies:
        copy.start()
    copies[0].wait()
    for slot, in_ref in zip(slots_of(n_peers, False), in_refs):
        spec_ref[peer_of(slot)] = block_spectrum(fwd_ref[...], in_ref[...])
    for pair in range(n_peers // 2):
        pl.when(late_place(n_peers) == pair)(
            functools.partial(mix_early, pair, STEP, spec_ref, part_ref)
        )
    copies[1].wait()


def spectra(received, fwd, bwd, n_peers):
    rows, width = received[0].shape
    whole = pl.BlockSpec(memory_space=pltpu.VMEM)
    args = [pltpu.with_memory_space_constraint(a, pltpu.HBM) for a in (fwd, bwd)]
    return pl.pallas_call(
        functools.partial(spectra_kernel, n_peers),
        in_specs=[pl.BlockSpec(memory_space=pltpu.HBM)] * 2 + [whole] * len(received),
        out_specs=[whole] * 4,
        out_shape=[
            jax.ShapeDtypeStruct(fwd.shape, BF16),
            jax.ShapeDtypeStruct(bwd.shape, BF16),
            jax.ShapeDtypeStruct((n_peers, 2 * rows, width), F32),
            jax.ShapeDtypeStruct((n_peers, 2 * rows, width // 2), F32),
        ],
        scratch_shapes=[pltpu.SemaphoreType.DMA((2,))],
        compiler_params=pltpu.CompilerParams(vmem_limit_bytes=CONV_VMEM),
        cost_estimate=pl.CostEstimate(
            flops=8 * len(received) * rows * rows * width, bytes_accessed=4 * 2**20, transcendentals=0
        ),
    )(*args, *received)


def mix_late(pair, step, first, last, sign, spec_ref, part_ref, late_ref, turned):
    n_blocks, rows, chans = spec_ref.shape[0], spec_ref.shape[1] // 2, spec_ref.shape[2] // 2
    early = [j for j in range(n_blocks) if j // 2 != pair]
    x_at, f_at = slice(0, chans), slice(chans, 2 * chans)

    @pl.loop(first // step, last // step)
    def _(t):
        row = pl.multiple_of(t * step, step)
        late = [2 * pair, 2 * pair + 1]
        signal = {j: load(late_ref, (j % 2,), row, step, rows, x_at) for j in late}
        filt = {j: load(late_ref, (j % 2,), row, step, rows, f_at) for j in late}
        total = [load(part_ref, (i,), row, step, rows, slice(0, chans)) for i in range(n_blocks)]
        for b in early:
            if b + late[0] >= n_blocks:
                continue
            x_b = load(spec_ref, (b,), row, step, rows, x_at)
            f_b = load(spec_ref, (b,), row, step, rows, f_at)
            for j in late:
                if b + j < n_blocks:
                    total[b + j] = plus(total[b + j], times(filt[j], x_b))
                    total[b + j] = plus(total[b + j], times(f_b, signal[j]))
        for j in late:
            for d in late:
                if j + d < n_blocks:
                    total[j + d] = plus(total[j + d], times(filt[d], signal[j]))
        for i in range(n_blocks):
            value = total[i]
            if i > 0:
                turn_re, turn_im = total[i - 1]
                if sign > 0:
                    value = value[0] - turn_im, value[1] + turn_re
                else:
                    value = value[0] + turn_im, value[1] - turn_re
            lanes = slice(i % 2 * chans, (i % 2 + 1) * chans)
            for part in range(2):
                high = value[part].astype(BF16)
                low = (value[part] - high.astype(F32)).astype(BF16)
                for c, piece in enumerate((high, high, low)):
                    turned[i // 2, pl.ds(row + (2 * c + part) * rows, step), lanes] = piece


def conv_kernel(fwd_ref, bwd_ref, spec_ref, part_ref, *refs):
    *refs, late_ref, turned = refs
    n_blocks = spec_ref.shape[0]
    in_refs, out_refs = refs[:-n_blocks], refs[-n_blocks:]
    rows, chans = in_refs[0].shape[0], in_refs[0].shape[1] // 2
    for slot, in_ref in zip(slots_of(n_blocks, False)[-2:], in_refs):
        late_ref[lax.bitwise_and(peer_of(slot), 1)] = block_spectrum(fwd_ref[...], in_ref[...])

    def mix(pair):
        for first, last, sign in ((0, rows // 2, 1), (rows // 2, rows, -1)):
            mix_late(pair, STEP, first, last, sign, spec_ref, part_ref, late_ref, turned)

    for pair in range(n_blocks // 2):
        pl.when(late_place(n_blocks) == pair)(functools.partial(mix, pair))

    odd = lax.bitwise_and(lax.axis_index("seq"), 1) == 1
    by_slot = dict(zip(slots_of(n_blocks, True), out_refs))
    for slot in range(0, n_blocks, 2):
        pair = lax.div(peer_of(slot), 2)
        both = jnp.dot(bwd_ref[...], turned[pair], preferred_element_type=F32)
        left, right = both[:, :chans], both[:, chans:]
        by_slot[slot][...] = jnp.where(odd, right, left).astype(BF16)
        by_slot[slot + 1][...] = jnp.where(odd, left, right).astype(BF16)


def conv_fast(early, part, late, fwd, bwd):
    n_blocks = early.shape[0]
    rows, chans = late[0].shape[0], late[0].shape[1] // 2
    whole = pl.BlockSpec(memory_space=pltpu.VMEM)
    return pl.pallas_call(
        conv_kernel,
        in_specs=[whole] * 6,
        out_specs=[whole] * n_blocks,
        out_shape=[jax.ShapeDtypeStruct((rows, chans), BF16)] * n_blocks,
        scratch_shapes=[
            pltpu.VMEM((2, 2 * rows, 2 * chans), F32),
            pltpu.VMEM((n_blocks // 2, 6 * rows, 2 * chans), BF16),
        ],
        compiler_params=pltpu.CompilerParams(vmem_limit_bytes=CONV_VMEM),
        cost_estimate=pl.CostEstimate(
            flops=16 * n_blocks * rows * rows * chans, bytes_accessed=4 * 2**20, transcendentals=0
        ),
    )(fwd, bwd, early, part, *late)


def conv_plain(received, fwd, bwd):
    n_blocks, rows, chans = received.shape[0], received.shape[1], received.shape[2] // 2
    exact = lax.Precision.HIGHEST
    fwd32 = fwd[:, :rows].astype(F32) + fwd[:, rows:].astype(F32)
    bwd32 = bwd[:, : 2 * rows].astype(F32) + bwd[:, 2 * rows : 4 * rows].astype(F32)
    sign = jnp.where(jnp.arange(rows) < rows // 2, 1.0, -1.0).astype(F32)[:, None]

    def spectrum(blocks):
        spec = jnp.einsum("kt,jtc->jkc", fwd32, blocks.astype(F32), precision=exact)
        return spec[:, :rows], spec[:, rows:]

    x_re, x_im = spectrum(received[:, :, :chans])
    f_re, f_im = spectrum(received[:, :, chans:])
    g_re = f_re.at[1:].add(-sign * f_im[:-1])
    g_im = f_im.at[1:].add(sign * f_re[:-1])

    def one(d, total):
        t_re, t_im = total
        later = (jnp.arange(n_blocks) >= d)[:, None, None]
        a_re = jnp.where(later, jnp.roll(x_re, d, axis=0), 0.0)
        a_im = jnp.where(later, jnp.roll(x_im, d, axis=0), 0.0)
        return (
            t_re + g_re[d] * a_re - g_im[d] * a_im,
            t_im + g_re[d] * a_im + g_im[d] * a_re,
        )

    zero = jnp.zeros_like(x_re)
    y_re, y_im = lax.fori_loop(0, n_blocks, one, (zero, zero))
    both = jnp.concatenate([y_re, y_im], axis=1)
    return jnp.einsum("tk,jkc->jtc", bwd32, both, precision=exact).astype(BF16)


def columns_of(other, across, piece, pieces, width):
    count = width // 4 // pieces
    place = lax.axis_index("fsdp")
    core, side = lax.rem(place, 2), lax.div(place, 2)
    block = 2 * (1 - side if across else side) + (1 - core if other else core)
    return pl.ds(pl.multiple_of((block * pieces + piece) * count, count), count)


def gate_slot(slot, queries_ref, keys_ref, values_ref, skip_ref, conv_ref):
    at = peer_block(slot, conv_ref.shape[1])
    product = keys_ref[:, at].astype(F32) * values_ref[:, at].astype(F32)
    mixed = conv_ref[...].astype(F32) + skip_ref[:, at] * product
    return (queries_ref[:, at].astype(F32) * mixed).astype(BF16)


def gate_early_kernel(n_peers, queries_ref, keys_ref, values_ref, skip_ref, weight_ref, *refs):
    conv_refs, (gated_ref, *part_refs) = refs[:-3], refs[-3:]
    chans = conv_refs[0].shape[1]
    slots = slots_of(n_peers, True)
    for slot, conv_ref in zip(slots, conv_refs):
        gated = gate_slot(slot, queries_ref, keys_ref, values_ref, skip_ref, conv_ref)
        gated_ref[:, peer_block(slot, chans)] = gated
    for slot in slots[len(conv_refs) :]:
        gated_ref[:, peer_block(slot, chans)] = jnp.zeros((gated_ref.shape[0], chans), BF16)
    for other, part_ref in zip((True, False), part_refs):
        columns = weight_ref[:, columns_of(other, True, 0, 1, weight_ref.shape[1])]
        part_ref[...] = jnp.dot(gated_ref[...], columns, preferred_element_type=F32)


def gate_early(queries, keys, values, skip, weight, conv, n_peers):
    rows, width = queries.shape
    out_width = weight.shape[1] // 4
    whole = pl.BlockSpec(memory_space=pltpu.VMEM)
    return pl.pallas_call(
        functools.partial(gate_early_kernel, n_peers),
        in_specs=[whole] * (5 + len(conv)),
        out_specs=[whole] * 3,
        out_shape=[jax.ShapeDtypeStruct((rows, width), BF16)]
        + [jax.ShapeDtypeStruct((rows, out_width), F32)] * 2,
        compiler_params=pltpu.CompilerParams(vmem_limit_bytes=PROJECT_VMEM),
        cost_estimate=pl.CostEstimate(
            flops=4 * rows * width * out_width, bytes_accessed=10 * rows * width, transcendentals=0
        ),
    )(queries, keys, values, skip, weight, *conv)


def late_product(late, late_slots, block, weight_ref, part_ref):
    chans = late.shape[1] // len(late_slots)
    at = columns_of(*block, weight_ref.shape[1])
    _, _, piece, pieces = block
    count = part_ref.shape[1] // pieces
    columns = jnp.concatenate([weight_ref[peer_block(s, chans), at] for s in late_slots], axis=0)
    part = part_ref[:, piece * count : (piece + 1) * count]
    return part + jnp.dot(late, columns, preferred_element_type=F32)


def gate_late_kernel(late_slots, block, queries_ref, keys_ref, values_ref, skip_ref, weight_ref, part_ref, *refs):
    *conv_refs, late_ref, sent_ref = refs
    chans = conv_refs[0].shape[1]
    for c, (slot, conv_ref) in enumerate(zip(late_slots, conv_refs)):
        gated = gate_slot(slot, queries_ref, keys_ref, values_ref, skip_ref, conv_ref)
        late_ref[:, c * chans : (c + 1) * chans] = gated
    total = late_product(late_ref[...], late_slots, block, weight_ref, part_ref)
    sent_ref[...] = total.astype(BF16)


def gate_late(queries, keys, values, skip, weight, part, conv, late_slots, block):
    rows, chans = conv[0].shape
    whole = pl.BlockSpec(memory_space=pltpu.VMEM)
    return pl.pallas_call(
        functools.partial(gate_late_kernel, late_slots, block),
        in_specs=[whole] * (6 + len(conv)),
        out_specs=[whole] * 2,
        out_shape=[
            jax.ShapeDtypeStruct((rows, chans * len(conv)), BF16),
            jax.ShapeDtypeStruct((rows, weight.shape[1] // 4 // block[-1]), BF16),
        ],
        compiler_params=pltpu.CompilerParams(vmem_limit_bytes=PROJECT_VMEM),
        cost_estimate=pl.CostEstimate(
            flops=rows * chans * weight.shape[1], bytes_accessed=2**20, transcendentals=0
        ),
    )(queries, keys, values, skip, weight, part, *conv)


def late_project_kernel(late_slots, blocks, weight_ref, late_ref, part_ref, *out_refs):
    for block, out_ref in zip(blocks, out_refs):
        total = late_product(late_ref[...], late_slots, block, weight_ref, part_ref)
        out_ref[...] = total.astype(out_ref.dtype)


def late_project(weight, late, part, late_slots, blocks, dtype):
    rows, depth = late.shape
    widths = [weight.shape[1] // 4 // pieces for *_, pieces in blocks]
    whole = pl.BlockSpec(memory_space=pltpu.VMEM)
    return pl.pallas_call(
        functools.partial(late_project_kernel, late_slots, blocks),
        in_specs=[whole] * 3,
        out_specs=[whole] * len(blocks),
        out_shape=[jax.ShapeDtypeStruct((rows, w), dtype) for w in widths],
        compiler_params=pltpu.CompilerParams(vmem_limit_bytes=PROJECT_VMEM),
        cost_estimate=pl.CostEstimate(
            flops=2 * rows * depth * sum(widths), bytes_accessed=2**20, transcendentals=0
        ),
    )(weight, late, part)


def assemble_kernel(late_slots, gated_ref, late_ref, out_ref):
    chans = late_ref.shape[1] // len(late_slots)
    out_ref[...] = gated_ref[...]
    for c, slot in enumerate(late_slots):
        out_ref[:, peer_block(slot, chans)] = late_ref[:, c * chans : (c + 1) * chans]


def assemble(gated, late, late_slots):
    whole = pl.BlockSpec(memory_space=pltpu.VMEM)
    return pl.pallas_call(
        functools.partial(assemble_kernel, late_slots),
        in_specs=[whole] * 2,
        out_specs=whole,
        out_shape=jax.ShapeDtypeStruct(gated.shape, BF16),
        compiler_params=pltpu.CompilerParams(vmem_limit_bytes=SMALL_VMEM),
        cost_estimate=pl.CostEstimate(flops=1000, bytes_accessed=2**20, transcendentals=0),
    )(gated, late)


def project_kernel(blocks, gated_ref, weight_ref, *out_refs):
    for block, out_ref in zip(blocks, out_refs):
        columns = weight_ref[:, columns_of(*block, weight_ref.shape[1])]
        total = jnp.dot(gated_ref[...], columns, preferred_element_type=F32)
        out_ref[...] = total.astype(out_ref.dtype)


def project(gated, weight, blocks, dtypes):
    rows, depth = gated.shape
    widths = [weight.shape[1] // 4 // pieces for *_, pieces in blocks]
    whole = pl.BlockSpec(memory_space=pltpu.VMEM)
    return pl.pallas_call(
        functools.partial(project_kernel, blocks),
        in_specs=[whole] * 2,
        out_specs=[whole] * len(blocks),
        out_shape=[jax.ShapeDtypeStruct((rows, w), t) for w, t in zip(widths, dtypes)],
        compiler_params=pltpu.CompilerParams(vmem_limit_bytes=PROJECT_VMEM),
        cost_estimate=pl.CostEstimate(
            flops=2 * rows * depth * sum(widths), bytes_accessed=2 * depth * sum(widths), transcendentals=0
        ),
    )(gated, weight)


def add_kernel(own_ref, arrived_ref, out_ref):
    total = own_ref[...] + arrived_ref[...].astype(F32)
    out_ref[...] = total.astype(out_ref.dtype)


def add(own, arrived):
    whole = pl.BlockSpec(memory_space=pltpu.VMEM)
    return pl.pallas_call(
        add_kernel,
        in_specs=[whole] * 2,
        out_specs=whole,
        out_shape=jax.ShapeDtypeStruct(arrived.shape, BF16),
        compiler_params=pltpu.CompilerParams(vmem_limit_bytes=SMALL_VMEM),
        cost_estimate=pl.CostEstimate(
            flops=arrived.size, bytes_accessed=8 * arrived.size, transcendentals=0
        ),
    )(own, arrived)


def mark_kernel(*refs):
    refs[-1][...] = jnp.zeros_like(refs[-1])


def mark(arrays):
    return pl.pallas_call(
        mark_kernel,
        in_specs=[pl.BlockSpec(memory_space=pl.ANY)] * len(arrays),
        out_specs=pl.BlockSpec(memory_space=pltpu.VMEM),
        out_shape=jax.ShapeDtypeStruct((8, 128), F32),
        compiler_params=pltpu.CompilerParams(vmem_limit_bytes=SMALL_VMEM),
        cost_estimate=pl.CostEstimate(flops=2 * 10**10, bytes_accessed=2**20, transcendentals=0),
    )(*arrays)


def finish_kernel(own_ref, near_ref, *refs):
    *arrived_refs, _, out_ref, stage, sem = refs
    width = out_ref.shape[1] // len(arrived_refs)
    steps = sem.shape[0]
    rows = out_ref.shape[0] // steps
    copies = []
    for step in range(steps):
        part = pl.ds(step * rows, rows)
        for c, arrived_ref in enumerate(arrived_refs):
            at = slice(c * width, (c + 1) * width)
            total = own_ref[part, at] + near_ref[part, at].astype(F32)
            stage[part, at] = (total + arrived_ref[part].astype(F32)).astype(stage.dtype)
        copies.append(pltpu.make_async_copy(stage.at[part], out_ref.at[part], sem.at[step]))
        copies[-1].start()
    for copy in copies:
        copy.wait()


def finish(own, near, arrived):
    rows, width = own.shape
    whole, anywhere = pl.BlockSpec(memory_space=pltpu.VMEM), pl.BlockSpec(memory_space=pl.ANY)
    return pl.pallas_call(
        finish_kernel,
        in_specs=[whole] * (2 + len(arrived)) + [anywhere],
        out_specs=anywhere,
        out_shape=jax.ShapeDtypeStruct((rows, width), BF16),
        scratch_shapes=[pltpu.VMEM((rows, width), BF16), pltpu.SemaphoreType.DMA((4,))],
        compiler_params=pltpu.CompilerParams(vmem_limit_bytes=SMALL_VMEM),
        cost_estimate=pl.CostEstimate(
            flops=rows * width, bytes_accessed=8 * rows * width, transcendentals=0
        ),
    )(own, near, *arrived, mark(arrived))


def body(pieces, tables, queries, keys, values, filters, skip_weight, out_weight):
    rows, width = keys.shape
    n_peers = lax.axis_size("seq")
    chans = width // n_peers
    fwd, bwd = (jnp.asarray(t) for t in tables)
    skip = skip_weight[None, :]
    in_chip = [(0, 1), (1, 0), (2, 3), (3, 2)]
    across = [(0, 2), (2, 0), (1, 3), (3, 1)]

    sends = [(True, True, c, pieces) for c in range(pieces)]
    keeps = [(False, True, c, pieces) for c in range(pieces)]

    if chans % 128 == 0 and n_peers == 8:
        blocks = pre(keys, values, filters, n_peers)
        received = exchange(blocks, n_peers, False)
        fwd, bwd, early, part = spectra(received[:-2], fwd, bwd, n_peers)
        back = exchange(conv_fast(early, part, received[-2:], fwd, bwd), n_peers, True)
        slots = slots_of(n_peers, True)[-2:]
        gated, send_part, own_part = gate_early(
            queries, keys, values, skip, out_weight, back[:-2], n_peers
        )
        late, last = gate_late(
            queries, keys, values, skip, out_weight, send_part, back[-2:], slots, sends[-1]
        )
        sent = [
            *(late_project(out_weight, late, send_part, slots, [s], BF16)[0] for s in sends[:-1]),
            last,
        ]
        ours = late_project(out_weight, late, own_part, slots, keeps, F32)
        gated = assemble(gated, late, slots)
    else:
        product = keys.astype(F32) * values.astype(F32)
        parts = [a.astype(BF16).reshape(rows, n_peers, chans) for a in (product, filters)]
        sent = jnp.concatenate(parts, axis=2).transpose(1, 0, 2)
        received = lax.all_to_all(sent, "seq", split_axis=0, concat_axis=0, tiled=True)
        conv = conv_plain(received, fwd, bwd)
        back = lax.all_to_all(conv, "seq", split_axis=0, concat_axis=0, tiled=True)
        mixed = back.transpose(1, 0, 2).reshape(rows, width).astype(F32) + skip * product
        gated = (queries.astype(F32) * mixed).astype(BF16)
        sent = project(gated, out_weight, sends, [BF16] * pieces)
        ours = project(gated, out_weight, keeps, [F32] * pieces)

    theirs = [lax.ppermute(piece, "fsdp", in_chip) for piece in sent]
    arrived = [lax.ppermute(add(*pair), "fsdp", across) for pair in zip(ours, theirs)]
    blocks = [(True, False, 0, 1), (False, False, 0, 1)]
    sent, own = project(gated, out_weight, blocks, [BF16, F32])
    near = lax.ppermute(sent, "fsdp", in_chip)
    return finish(own, near, arrived)


def solution(mesh):
    in_specs = (
        P("seq", "fsdp"),
        P("seq", "fsdp"),
        P("seq", "fsdp"),
        P("seq", "fsdp"),
        P("fsdp"),
        P("fsdp", None),
    )
    out_specs = P("seq", "fsdp")

    def run(queries, keys, values, filters, skip_weight, out_weight):
        rows = keys.shape[0] // mesh.shape["seq"]
        fn = functools.partial(body, 2, make_tables(rows))
        return jax.shard_map(fn, mesh=mesh, in_specs=in_specs, out_specs=out_specs, check_vma=False)(
            queries, keys, values, filters, skip_weight, out_weight
        )

    return run
```

```python
import functools

import numpy as np

import jax
import jax.numpy as jnp
from jax import lax
from jax.experimental import pallas as pl
from jax.experimental.pallas import tpu as pltpu
from jax.sharding import PartitionSpec as P

BF16 = jnp.bfloat16
F32 = jnp.float32
CONV_VMEM = 24 * 2**20
PROJECT_VMEM = 24 * 2**20
SMALL_VMEM = 12 * 2**20
STEP = 16


def split_bf16(table):
    high = table.astype(BF16)
    return high, (table - high.astype(np.float64)).astype(BF16)


def make_tables(rows):
    order = np.concatenate([np.arange(0, rows, 2), np.arange(1, rows, 2)])
    times = np.arange(rows)
    angle = np.pi * (((2 * order[:, None] + 1) * times[None, :]) % (4 * rows)) / (2 * rows)
    forward = np.concatenate([np.cos(angle), -np.sin(angle)], axis=0)
    high, low = split_bf16(forward)
    back_high, back_low = split_bf16(forward.T / rows)
    return (
        np.concatenate([high, low], axis=1),
        np.concatenate([back_high, back_low, back_high], axis=1),
    )


def peer_of(slot):
    return lax.bitwise_xor(lax.axis_index("seq"), slot)


def peer_block(slot, size):
    return pl.ds(pl.multiple_of(peer_of(slot) * size, size), size)


def pre_kernel(n_peers, keys_hbm, values_hbm, filters_hbm, *refs):
    out_refs = refs[:n_peers]
    keys, values, filters, sem = refs[n_peers:]
    rows, width = keys.shape
    chans = width // n_peers
    steps = sem.shape[0]
    parts = [pl.ds(c * rows // steps, rows // steps) for c in range(steps)]
    pairs = ((keys_hbm, keys), (values_hbm, values), (filters_hbm, filters))
    copies = [
        [
            pltpu.make_async_copy(src.at[part], dst.at[part], sem.at[c, i])
            for i, (src, dst) in enumerate(pairs)
        ]
        for c, part in enumerate(parts)
    ]
    for group in copies:
        for copy in group:
            copy.start()
    for part, group in zip(parts, copies):
        for copy in group:
            copy.wait()
        for slot, out_ref in zip(slots_of(n_peers, False), out_refs):
            at = peer_block(slot, chans)
            product = keys[part, at].astype(F32) * values[part, at].astype(F32)
            out_ref[part, :chans] = product.astype(BF16)
            out_ref[part, chans:] = filters[part, at].astype(BF16)


def pre(keys, values, filters, n_peers):
    rows, width = keys.shape
    chans = width // n_peers
    args = [pltpu.with_memory_space_constraint(a, pltpu.HBM) for a in (keys, values, filters)]
    return pl.pallas_call(
        functools.partial(pre_kernel, n_peers),
        in_specs=[pl.BlockSpec(memory_space=pltpu.HBM)] * 3,
        out_specs=[pl.BlockSpec(memory_space=pltpu.VMEM)] * n_peers,
        out_shape=[jax.ShapeDtypeStruct((rows, 2 * chans), BF16)] * n_peers,
        scratch_shapes=[
            pltpu.VMEM((rows, width), BF16),
            pltpu.VMEM((rows, width), BF16),
            pltpu.VMEM((rows, width), F32),
            pltpu.SemaphoreType.DMA((2, 3)),
        ],
        compiler_params=pltpu.CompilerParams(vmem_limit_bytes=SMALL_VMEM),
        cost_estimate=pl.CostEstimate(
            flops=rows * width, bytes_accessed=12 * rows * width, transcendentals=0
        ),
    )(*args)


def slots_of(n_peers, back):
    half = n_peers // 2
    near, far = list(range(1, half)), list(range(half, n_peers))
    if back:
        return [0, near[0]] + far[2:] + near[1:] + far[:2]
    return [0, near[0], far[0], near[1], far[1]] + near[2:] + far[2:]


def exchange(blocks, n_peers, back):
    return [
        lax.ppermute(block, "seq", [(i, i ^ slot) for i in range(n_peers)]) if slot else block
        for slot, block in zip(slots_of(n_peers, back), blocks)
    ]


def block_spectrum(table, block):
    return jnp.dot(table, jnp.concatenate([block, block], axis=0), preferred_element_type=F32)


def times(a, b):
    return a[0] * b[0] - a[1] * b[1], a[0] * b[1] + a[1] * b[0]


def plus(a, b):
    return b if a is None else (a[0] + b[0], a[1] + b[1])


def late_place(n_blocks):
    return lax.div(peer_of(slots_of(n_blocks, False)[-1]), 2)


def load(ref, at, row, step, rows, lanes):
    return tuple(ref[(*at, pl.ds(row + part * rows, step), lanes)] for part in range(2))


def mix_early(pair, step, spec_ref, part_ref):
    n_blocks, rows, chans = spec_ref.shape[0], spec_ref.shape[1] // 2, spec_ref.shape[2] // 2
    early = [j for j in range(n_blocks) if j // 2 != pair]

    @pl.loop(0, rows // step)
    def _(t):
        row = pl.multiple_of(t * step, step)
        signal = {j: load(spec_ref, (j,), row, step, rows, slice(0, chans)) for j in early}
        filt = {j: load(spec_ref, (j,), row, step, rows, slice(chans, 2 * chans)) for j in early}
        for i in range(n_blocks):
            total = None
            for d in early:
                if i - d in early:
                    total = plus(total, times(filt[d], signal[i - d]))
            if total is None:
                total = (jnp.zeros((step, chans), F32),) * 2
            for part in range(2):
                part_ref[i, pl.ds(row + part * rows, step)] = total[part]


def spectra_kernel(n_peers, fwd_hbm, bwd_hbm, *refs):
    *in_refs, fwd_ref, bwd_ref, spec_ref, part_ref, sem = refs
    copies = [
        pltpu.make_async_copy(fwd_hbm, fwd_ref, sem.at[0]),
        pltpu.make_async_copy(bwd_hbm, bwd_ref, sem.at[1]),
    ]
    for copy in copies:
        copy.start()
    copies[0].wait()
    for slot, in_ref in zip(slots_of(n_peers, False), in_refs):
        spec_ref[peer_of(slot)] = block_spectrum(fwd_ref[...], in_ref[...])
    for pair in range(n_peers // 2):
        pl.when(late_place(n_peers) == pair)(
            functools.partial(mix_early, pair, STEP, spec_ref, part_ref)
        )
    copies[1].wait()


def spectra(received, fwd, bwd, n_peers):
    rows, width = received[0].shape
    whole = pl.BlockSpec(memory_space=pltpu.VMEM)
    args = [pltpu.with_memory_space_constraint(a, pltpu.HBM) for a in (fwd, bwd)]
    return pl.pallas_call(
        functools.partial(spectra_kernel, n_peers),
        in_specs=[pl.BlockSpec(memory_space=pltpu.HBM)] * 2 + [whole] * len(received),
        out_specs=[whole] * 4,
        out_shape=[
            jax.ShapeDtypeStruct(fwd.shape, BF16),
            jax.ShapeDtypeStruct(bwd.shape, BF16),
            jax.ShapeDtypeStruct((n_peers, 2 * rows, width), F32),
            jax.ShapeDtypeStruct((n_peers, 2 * rows, width // 2), F32),
        ],
        scratch_shapes=[pltpu.SemaphoreType.DMA((2,))],
        compiler_params=pltpu.CompilerParams(vmem_limit_bytes=CONV_VMEM),
        cost_estimate=pl.CostEstimate(
            flops=8 * len(received) * rows * rows * width, bytes_accessed=4 * 2**20, transcendentals=0
        ),
    )(*args, *received)


def mix_late(pair, step, first, last, sign, spec_ref, part_ref, late_ref, turned):
    n_blocks, rows, chans = spec_ref.shape[0], spec_ref.shape[1] // 2, spec_ref.shape[2] // 2
    early = [j for j in range(n_blocks) if j // 2 != pair]
    x_at, f_at = slice(0, chans), slice(chans, 2 * chans)

    @pl.loop(first // step, last // step)
    def _(t):
        row = pl.multiple_of(t * step, step)
        late = [2 * pair, 2 * pair + 1]
        signal = {j: load(late_ref, (j % 2,), row, step, rows, x_at) for j in late}
        filt = {j: load(late_ref, (j % 2,), row, step, rows, f_at) for j in late}
        total = [load(part_ref, (i,), row, step, rows, slice(0, chans)) for i in range(n_blocks)]
        for b in early:
            if b + late[0] >= n_blocks:
                continue
            x_b = load(spec_ref, (b,), row, step, rows, x_at)
            f_b = load(spec_ref, (b,), row, step, rows, f_at)
            for j in late:
                if b + j < n_blocks:
                    total[b + j] = plus(total[b + j], times(filt[j], x_b))
                    total[b + j] = plus(total[b + j], times(f_b, signal[j]))
        for j in late:
            for d in late:
                if j + d < n_blocks:
                    total[j + d] = plus(total[j + d], times(filt[d], signal[j]))
        for i in range(n_blocks):
            value = total[i]
            if i > 0:
                turn_re, turn_im = total[i - 1]
                if sign > 0:
                    value = value[0] - turn_im, value[1] + turn_re
                else:
                    value = value[0] + turn_im, value[1] - turn_re
            lanes = slice(i % 2 * chans, (i % 2 + 1) * chans)
            for part in range(2):
                high = value[part].astype(BF16)
                low = (value[part] - high.astype(F32)).astype(BF16)
                for c, piece in enumerate((high, high, low)):
                    turned[i // 2, pl.ds(row + (2 * c + part) * rows, step), lanes] = piece


def conv_kernel(fwd_ref, bwd_ref, spec_ref, part_ref, *refs):
    *refs, late_ref, turned = refs
    n_blocks = spec_ref.shape[0]
    in_refs, out_refs = refs[:-n_blocks], refs[-n_blocks:]
    rows, chans = in_refs[0].shape[0], in_refs[0].shape[1] // 2
    for slot, in_ref in zip(slots_of(n_blocks, False)[-2:], in_refs):
        late_ref[lax.bitwise_and(peer_of(slot), 1)] = block_spectrum(fwd_ref[...], in_ref[...])

    def mix(pair):
        for first, last, sign in ((0, rows // 2, 1), (rows // 2, rows, -1)):
            mix_late(pair, STEP, first, last, sign, spec_ref, part_ref, late_ref, turned)

    for pair in range(n_blocks // 2):
        pl.when(late_place(n_blocks) == pair)(functools.partial(mix, pair))

    odd = lax.bitwise_and(lax.axis_index("seq"), 1) == 1
    by_slot = dict(zip(slots_of(n_blocks, True), out_refs))
    for slot in range(0, n_blocks, 2):
        pair = lax.div(peer_of(slot), 2)
        both = jnp.dot(bwd_ref[...], turned[pair], preferred_element_type=F32)
        left, right = both[:, :chans], both[:, chans:]
        by_slot[slot][...] = jnp.where(odd, right, left).astype(BF16)
        by_slot[slot + 1][...] = jnp.where(odd, left, right).astype(BF16)


def conv_fast(early, part, late, fwd, bwd):
    n_blocks = early.shape[0]
    rows, chans = late[0].shape[0], late[0].shape[1] // 2
    whole = pl.BlockSpec(memory_space=pltpu.VMEM)
    return pl.pallas_call(
        conv_kernel,
        in_specs=[whole] * 6,
        out_specs=[whole] * n_blocks,
        out_shape=[jax.ShapeDtypeStruct((rows, chans), BF16)] * n_blocks,
        scratch_shapes=[
            pltpu.VMEM((2, 2 * rows, 2 * chans), F32),
            pltpu.VMEM((n_blocks // 2, 6 * rows, 2 * chans), BF16),
        ],
        compiler_params=pltpu.CompilerParams(vmem_limit_bytes=CONV_VMEM),
        cost_estimate=pl.CostEstimate(
            flops=16 * n_blocks * rows * rows * chans, bytes_accessed=4 * 2**20, transcendentals=0
        ),
    )(fwd, bwd, early, part, *late)


def conv_plain(received, fwd, bwd):
    n_blocks, rows, chans = received.shape[0], received.shape[1], received.shape[2] // 2
    exact = lax.Precision.HIGHEST
    fwd32 = fwd[:, :rows].astype(F32) + fwd[:, rows:].astype(F32)
    bwd32 = bwd[:, : 2 * rows].astype(F32) + bwd[:, 2 * rows : 4 * rows].astype(F32)
    sign = jnp.where(jnp.arange(rows) < rows // 2, 1.0, -1.0).astype(F32)[:, None]

    def spectrum(blocks):
        spec = jnp.einsum("kt,jtc->jkc", fwd32, blocks.astype(F32), precision=exact)
        return spec[:, :rows], spec[:, rows:]

    x_re, x_im = spectrum(received[:, :, :chans])
    f_re, f_im = spectrum(received[:, :, chans:])
    g_re = f_re.at[1:].add(-sign * f_im[:-1])
    g_im = f_im.at[1:].add(sign * f_re[:-1])

    def one(d, total):
        t_re, t_im = total
        later = (jnp.arange(n_blocks) >= d)[:, None, None]
        a_re = jnp.where(later, jnp.roll(x_re, d, axis=0), 0.0)
        a_im = jnp.where(later, jnp.roll(x_im, d, axis=0), 0.0)
        return (
            t_re + g_re[d] * a_re - g_im[d] * a_im,
            t_im + g_re[d] * a_im + g_im[d] * a_re,
        )

    zero = jnp.zeros_like(x_re)
    y_re, y_im = lax.fori_loop(0, n_blocks, one, (zero, zero))
    both = jnp.concatenate([y_re, y_im], axis=1)
    return jnp.einsum("tk,jkc->jtc", bwd32, both, precision=exact).astype(BF16)


def columns_of(other, across, piece, pieces, width):
    count = width // 4 // pieces
    place = lax.axis_index("fsdp")
    core, side = lax.rem(place, 2), lax.div(place, 2)
    block = 2 * (1 - side if across else side) + (1 - core if other else core)
    return pl.ds(pl.multiple_of((block * pieces + piece) * count, count), count)


def gate_slot(slot, queries_ref, keys_ref, values_ref, skip_ref, conv_ref):
    at = peer_block(slot, conv_ref.shape[1])
    product = keys_ref[:, at].astype(F32) * values_ref[:, at].astype(F32)
    mixed = conv_ref[...].astype(F32) + skip_ref[:, at] * product
    return (queries_ref[:, at].astype(F32) * mixed).astype(BF16)


def gate_early_kernel(n_peers, queries_ref, keys_ref, values_ref, skip_ref, weight_ref, *refs):
    conv_refs, (gated_ref, *part_refs) = refs[:-3], refs[-3:]
    chans = conv_refs[0].shape[1]
    slots = slots_of(n_peers, True)
    for slot, conv_ref in zip(slots, conv_refs):
        gated = gate_slot(slot, queries_ref, keys_ref, values_ref, skip_ref, conv_ref)
        gated_ref[:, peer_block(slot, chans)] = gated
    for slot in slots[len(conv_refs) :]:
        gated_ref[:, peer_block(slot, chans)] = jnp.zeros((gated_ref.shape[0], chans), BF16)
    for other, part_ref in zip((True, False), part_refs):
        columns = weight_ref[:, columns_of(other, True, 0, 1, weight_ref.shape[1])]
        part_ref[...] = jnp.dot(gated_ref[...], columns, preferred_element_type=F32)


def gate_early(queries, keys, values, skip, weight, conv, n_peers):
    rows, width = queries.shape
    out_width = weight.shape[1] // 4
    whole = pl.BlockSpec(memory_space=pltpu.VMEM)
    return pl.pallas_call(
        functools.partial(gate_early_kernel, n_peers),
        in_specs=[whole] * (5 + len(conv)),
        out_specs=[whole] * 3,
        out_shape=[jax.ShapeDtypeStruct((rows, width), BF16)]
        + [jax.ShapeDtypeStruct((rows, out_width), F32)] * 2,
        compiler_params=pltpu.CompilerParams(vmem_limit_bytes=PROJECT_VMEM),
        cost_estimate=pl.CostEstimate(
            flops=4 * rows * width * out_width, bytes_accessed=10 * rows * width, transcendentals=0
        ),
    )(queries, keys, values, skip, weight, *conv)


def late_product(late, late_slots, block, weight_ref, part_ref):
    chans = late.shape[1] // len(late_slots)
    at = columns_of(*block, weight_ref.shape[1])
    _, _, piece, pieces = block
    count = part_ref.shape[1] // pieces
    columns = jnp.concatenate([weight_ref[peer_block(s, chans), at] for s in late_slots], axis=0)
    part = part_ref[:, piece * count : (piece + 1) * count]
    return part + jnp.dot(late, columns, preferred_element_type=F32)


def gate_late_kernel(late_slots, block, queries_ref, keys_ref, values_ref, skip_ref, weight_ref, part_ref, *refs):
    *conv_refs, late_ref, sent_ref = refs
    chans = conv_refs[0].shape[1]
    for c, (slot, conv_ref) in enumerate(zip(late_slots, conv_refs)):
        gated = gate_slot(slot, queries_ref, keys_ref, values_ref, skip_ref, conv_ref)
        late_ref[:, c * chans : (c + 1) * chans] = gated
    total = late_product(late_ref[...], late_slots, block, weight_ref, part_ref)
    sent_ref[...] = total.astype(BF16)


def gate_late(queries, keys, values, skip, weight, part, conv, late_slots, block):
    rows, chans = conv[0].shape
    whole = pl.BlockSpec(memory_space=pltpu.VMEM)
    return pl.pallas_call(
        functools.partial(gate_late_kernel, late_slots, block),
        in_specs=[whole] * (6 + len(conv)),
        out_specs=[whole] * 2,
        out_shape=[
            jax.ShapeDtypeStruct((rows, chans * len(conv)), BF16),
            jax.ShapeDtypeStruct((rows, weight.shape[1] // 4 // block[-1]), BF16),
        ],
        compiler_params=pltpu.CompilerParams(vmem_limit_bytes=PROJECT_VMEM),
        cost_estimate=pl.CostEstimate(
            flops=rows * chans * weight.shape[1], bytes_accessed=2**20, transcendentals=0
        ),
    )(queries, keys, values, skip, weight, part, *conv)


def late_project_kernel(late_slots, blocks, weight_ref, late_ref, part_ref, *out_refs):
    for block, out_ref in zip(blocks, out_refs):
        total = late_product(late_ref[...], late_slots, block, weight_ref, part_ref)
        out_ref[...] = total.astype(out_ref.dtype)


def late_project(weight, late, part, late_slots, blocks, dtype):
    rows, depth = late.shape
    widths = [weight.shape[1] // 4 // pieces for *_, pieces in blocks]
    whole = pl.BlockSpec(memory_space=pltpu.VMEM)
    return pl.pallas_call(
        functools.partial(late_project_kernel, late_slots, blocks),
        in_specs=[whole] * 3,
        out_specs=[whole] * len(blocks),
        out_shape=[jax.ShapeDtypeStruct((rows, w), dtype) for w in widths],
        compiler_params=pltpu.CompilerParams(vmem_limit_bytes=PROJECT_VMEM),
        cost_estimate=pl.CostEstimate(
            flops=2 * rows * depth * sum(widths), bytes_accessed=2**20, transcendentals=0
        ),
    )(weight, late, part)


def assemble_kernel(late_slots, gated_ref, late_ref, out_ref):
    chans = late_ref.shape[1] // len(late_slots)
    out_ref[...] = gated_ref[...]
    for c, slot in enumerate(late_slots):
        out_ref[:, peer_block(slot, chans)] = late_ref[:, c * chans : (c + 1) * chans]


def assemble(gated, late, late_slots):
    whole = pl.BlockSpec(memory_space=pltpu.VMEM)
    return pl.pallas_call(
        functools.partial(assemble_kernel, late_slots),
        in_specs=[whole] * 2,
        out_specs=whole,
        out_shape=jax.ShapeDtypeStruct(gated.shape, BF16),
        compiler_params=pltpu.CompilerParams(vmem_limit_bytes=SMALL_VMEM),
        cost_estimate=pl.CostEstimate(flops=1000, bytes_accessed=2**20, transcendentals=0),
    )(gated, late)


def project_kernel(blocks, gated_ref, weight_ref, *out_refs):
    for block, out_ref in zip(blocks, out_refs):
        columns = weight_ref[:, columns_of(*block, weight_ref.shape[1])]
        total = jnp.dot(gated_ref[...], columns, preferred_element_type=F32)
        out_ref[...] = total.astype(out_ref.dtype)


def project(gated, weight, blocks, dtypes):
    rows, depth = gated.shape
    widths = [weight.shape[1] // 4 // pieces for *_, pieces in blocks]
    whole = pl.BlockSpec(memory_space=pltpu.VMEM)
    return pl.pallas_call(
        functools.partial(project_kernel, blocks),
        in_specs=[whole] * 2,
        out_specs=[whole] * len(blocks),
        out_shape=[jax.ShapeDtypeStruct((rows, w), t) for w, t in zip(widths, dtypes)],
        compiler_params=pltpu.CompilerParams(vmem_limit_bytes=PROJECT_VMEM),
        cost_estimate=pl.CostEstimate(
            flops=2 * rows * depth * sum(widths), bytes_accessed=2 * depth * sum(widths), transcendentals=0
        ),
    )(gated, weight)


def add_kernel(own_ref, arrived_ref, out_ref):
    total = own_ref[...] + arrived_ref[...].astype(F32)
    out_ref[...] = total.astype(out_ref.dtype)


def add(own, arrived):
    whole = pl.BlockSpec(memory_space=pltpu.VMEM)
    return pl.pallas_call(
        add_kernel,
        in_specs=[whole] * 2,
        out_specs=whole,
        out_shape=jax.ShapeDtypeStruct(arrived.shape, BF16),
        compiler_params=pltpu.CompilerParams(vmem_limit_bytes=SMALL_VMEM),
        cost_estimate=pl.CostEstimate(
            flops=arrived.size, bytes_accessed=8 * arrived.size, transcendentals=0
        ),
    )(own, arrived)


def mark_kernel(*refs):
    refs[-1][...] = jnp.zeros_like(refs[-1])


def mark(arrays):
    return pl.pallas_call(
        mark_kernel,
        in_specs=[pl.BlockSpec(memory_space=pl.ANY)] * len(arrays),
        out_specs=pl.BlockSpec(memory_space=pltpu.VMEM),
        out_shape=jax.ShapeDtypeStruct((8, 128), F32),
        compiler_params=pltpu.CompilerParams(vmem_limit_bytes=SMALL_VMEM),
        cost_estimate=pl.CostEstimate(flops=2 * 10**10, bytes_accessed=2**20, transcendentals=0),
    )(*arrays)


def finish_kernel(own_ref, near_ref, *refs):
    *arrived_refs, _, out_ref, stage, sem = refs
    width = out_ref.shape[1] // len(arrived_refs)
    steps = sem.shape[0]
    rows = out_ref.shape[0] // steps
    copies = []
    for step in range(steps):
        part = pl.ds(step * rows, rows)
        for c, arrived_ref in enumerate(arrived_refs):
            at = slice(c * width, (c + 1) * width)
            total = own_ref[part, at] + near_ref[part, at].astype(F32)
            stage[part, at] = (total + arrived_ref[part].astype(F32)).astype(stage.dtype)
        copies.append(pltpu.make_async_copy(stage.at[part], out_ref.at[part], sem.at[step]))
        copies[-1].start()
    for copy in copies:
        copy.wait()


def finish(own, near, arrived):
    rows, width = own.shape
    whole, anywhere = pl.BlockSpec(memory_space=pltpu.VMEM), pl.BlockSpec(memory_space=pl.ANY)
    return pl.pallas_call(
        finish_kernel,
        in_specs=[whole] * (2 + len(arrived)) + [anywhere],
        out_specs=anywhere,
        out_shape=jax.ShapeDtypeStruct((rows, width), BF16),
        scratch_shapes=[pltpu.VMEM((rows, width), BF16), pltpu.SemaphoreType.DMA((4,))],
        compiler_params=pltpu.CompilerParams(vmem_limit_bytes=SMALL_VMEM),
        cost_estimate=pl.CostEstimate(
            flops=rows * width, bytes_accessed=8 * rows * width, transcendentals=0
        ),
    )(own, near, *arrived, mark(arrived))


def body(pieces, tables, queries, keys, values, filters, skip_weight, out_weight):
    rows, width = keys.shape
    n_peers = lax.axis_size("seq")
    chans = width // n_peers
    fwd, bwd = (jnp.asarray(t) for t in tables)
    skip = skip_weight[None, :]
    in_chip = [(0, 1), (1, 0), (2, 3), (3, 2)]
    across = [(0, 2), (2, 0), (1, 3), (3, 1)]

    sends = [(True, True, c, pieces) for c in range(pieces)]
    keeps = [(False, True, c, pieces) for c in range(pieces)]

    if chans % 128 == 0 and n_peers == 8:
        blocks = pre(keys, values, filters, n_peers)
        received = exchange(blocks, n_peers, False)
        fwd, bwd, early, part = spectra(received[:-2], fwd, bwd, n_peers)
        back = exchange(conv_fast(early, part, received[-2:], fwd, bwd), n_peers, True)
        slots = slots_of(n_peers, True)[-2:]
        gated, send_part, own_part = gate_early(
            queries, keys, values, skip, out_weight, back[:-2], n_peers
        )
        late, last = gate_late(
            queries, keys, values, skip, out_weight, send_part, back[-2:], slots, sends[-1]
        )
        sent = [
            *(late_project(out_weight, late, send_part, slots, [s], BF16)[0] for s in sends[:-1]),
            last,
        ]
        ours = late_project(out_weight, late, own_part, slots, keeps, F32)
        gated = assemble(gated, late, slots)
    else:
        product = keys.astype(F32) * values.astype(F32)
        parts = [a.astype(BF16).reshape(rows, n_peers, chans) for a in (product, filters)]
        sent = jnp.concatenate(parts, axis=2).transpose(1, 0, 2)
        received = lax.all_to_all(sent, "seq", split_axis=0, concat_axis=0, tiled=True)
        conv = conv_plain(received, fwd, bwd)
        back = lax.all_to_all(conv, "seq", split_axis=0, concat_axis=0, tiled=True)
        mixed = back.transpose(1, 0, 2).reshape(rows, width).astype(F32) + skip * product
        gated = (queries.astype(F32) * mixed).astype(BF16)
        sent = project(gated, out_weight, sends, [BF16] * pieces)
        ours = project(gated, out_weight, keeps, [F32] * pieces)

    theirs = [lax.ppermute(piece, "fsdp", in_chip) for piece in sent]
    arrived = [lax.ppermute(add(*pair), "fsdp", across) for pair in zip(ours, theirs)]
    blocks = [(True, False, 0, 1), (False, False, 0, 1)]
    sent, own = project(gated, out_weight, blocks, [BF16, F32])
    near = lax.ppermute(sent, "fsdp", in_chip)
    return finish(own, near, arrived)


def solution(mesh):
    in_specs = (
        P("seq", "fsdp"),
        P("seq", "fsdp"),
        P("seq", "fsdp"),
        P("seq", "fsdp"),
        P("fsdp"),
        P("fsdp", None),
    )
    out_specs = P("seq", "fsdp")

    def run(queries, keys, values, filters, skip_weight, out_weight):
        rows = keys.shape[0] // mesh.shape["seq"]
        fn = functools.partial(body, 2, make_tables(rows))
        return jax.shard_map(fn, mesh=mesh, in_specs=in_specs, out_specs=out_specs, check_vma=False)(
            queries, keys, values, filters, skip_weight, out_weight
        )

    return run
```

```python
import functools

import numpy as np

import jax
import jax.numpy as jnp
from jax import lax
from jax.experimental import pallas as pl
from jax.experimental.pallas import tpu as pltpu
from jax.sharding import PartitionSpec as P

BF16 = jnp.bfloat16
F32 = jnp.float32
CONV_VMEM = 24 * 2**20
PROJECT_VMEM = 24 * 2**20
SMALL_VMEM = 12 * 2**20
STEP = 16


def split_bf16(table):
    high = table.astype(BF16)
    return high, (table - high.astype(np.float64)).astype(BF16)


def make_tables(rows):
    order = np.concatenate([np.arange(0, rows, 2), np.arange(1, rows, 2)])
    times = np.arange(rows)
    angle = np.pi * (((2 * order[:, None] + 1) * times[None, :]) % (4 * rows)) / (2 * rows)
    forward = np.concatenate([np.cos(angle), -np.sin(angle)], axis=0)
    high, low = split_bf16(forward)
    back_high, back_low = split_bf16(forward.T / rows)
    return (
        np.concatenate([high, low], axis=1),
        np.concatenate([back_high, back_low, back_high], axis=1),
    )


def peer_of(slot):
    return lax.bitwise_xor(lax.axis_index("seq"), slot)


def peer_block(slot, size):
    return pl.ds(pl.multiple_of(peer_of(slot) * size, size), size)


def pre_kernel(n_peers, keys_hbm, values_hbm, filters_hbm, *refs):
    out_refs = refs[:n_peers]
    keys, values, filters, sem = refs[n_peers:]
    rows, width = keys.shape
    chans = width // n_peers
    steps = sem.shape[0]
    parts = [pl.ds(c * rows // steps, rows // steps) for c in range(steps)]
    pairs = ((keys_hbm, keys), (values_hbm, values), (filters_hbm, filters))
    copies = [
        [
            pltpu.make_async_copy(src.at[part], dst.at[part], sem.at[c, i])
            for i, (src, dst) in enumerate(pairs)
        ]
        for c, part in enumerate(parts)
    ]
    for group in copies:
        for copy in group:
            copy.start()
    for part, group in zip(parts, copies):
        for copy in group:
            copy.wait()
        for slot, out_ref in zip(slots_of(n_peers, False), out_refs):
            at = peer_block(slot, chans)
            product = keys[part, at].astype(F32) * values[part, at].astype(F32)
            out_ref[part, :chans] = product.astype(BF16)
            out_ref[part, chans:] = filters[part, at].astype(BF16)


def pre(keys, values, filters, n_peers):
    rows, width = keys.shape
    chans = width // n_peers
    args = [pltpu.with_memory_space_constraint(a, pltpu.HBM) for a in (keys, values, filters)]
    return pl.pallas_call(
        functools.partial(pre_kernel, n_peers),
        in_specs=[pl.BlockSpec(memory_space=pltpu.HBM)] * 3,
        out_specs=[pl.BlockSpec(memory_space=pltpu.VMEM)] * n_peers,
        out_shape=[jax.ShapeDtypeStruct((rows, 2 * chans), BF16)] * n_peers,
        scratch_shapes=[
            pltpu.VMEM((rows, width), BF16),
            pltpu.VMEM((rows, width), BF16),
            pltpu.VMEM((rows, width), F32),
            pltpu.SemaphoreType.DMA((2, 3)),
        ],
        compiler_params=pltpu.CompilerParams(vmem_limit_bytes=SMALL_VMEM),
        cost_estimate=pl.CostEstimate(
            flops=rows * width, bytes_accessed=12 * rows * width, transcendentals=0
        ),
    )(*args)


def slots_of(n_peers, back):
    half = n_peers // 2
    near, far = list(range(1, half)), list(range(half, n_peers))
    if back:
        return [0, near[0]] + far[2:] + near[1:] + far[:2]
    return [0, far[0], near[0]] + near[:0:-1] + far[1:]


def exchange(blocks, n_peers, back):
    return [
        lax.ppermute(block, "seq", [(i, i ^ slot) for i in range(n_peers)]) if slot else block
        for slot, block in zip(slots_of(n_peers, back), blocks)
    ]


def block_spectrum(table, block):
    return jnp.dot(table, jnp.concatenate([block, block], axis=0), preferred_element_type=F32)


def times(a, b):
    return a[0] * b[0] - a[1] * b[1], a[0] * b[1] + a[1] * b[0]


def plus(a, b):
    return b if a is None else (a[0] + b[0], a[1] + b[1])


def late_place(n_blocks):
    return lax.div(peer_of(slots_of(n_blocks, False)[-1]), 2)


def load(ref, at, row, step, rows, lanes):
    return tuple(ref[(*at, pl.ds(row + part * rows, step), lanes)] for part in range(2))


def mix_early(pair, step, spec_ref, part_ref):
    n_blocks, rows, chans = spec_ref.shape[0], spec_ref.shape[1] // 2, spec_ref.shape[2] // 2
    early = [j for j in range(n_blocks) if j // 2 != pair]

    @pl.loop(0, rows // step)
    def _(t):
        row = pl.multiple_of(t * step, step)
        signal = {j: load(spec_ref, (j,), row, step, rows, slice(0, chans)) for j in early}
        filt = {j: load(spec_ref, (j,), row, step, rows, slice(chans, 2 * chans)) for j in early}
        for i in range(n_blocks):
            total = None
            for d in early:
                if i - d in early:
                    total = plus(total, times(filt[d], signal[i - d]))
            if total is None:
                total = (jnp.zeros((step, chans), F32),) * 2
            for part in range(2):
                part_ref[i, pl.ds(row + part * rows, step)] = total[part]


def spectra_kernel(n_peers, fwd_hbm, bwd_hbm, *refs):
    *in_refs, fwd_ref, bwd_ref, spec_ref, part_ref, sem = refs
    copies = [
        pltpu.make_async_copy(fwd_hbm, fwd_ref, sem.at[0]),
        pltpu.make_async_copy(bwd_hbm, bwd_ref, sem.at[1]),
    ]
    for copy in copies:
        copy.start()
    copies[0].wait()
    for slot, in_ref in zip(slots_of(n_peers, False), in_refs):
        spec_ref[peer_of(slot)] = block_spectrum(fwd_ref[...], in_ref[...])
    for pair in range(n_peers // 2):
        pl.when(late_place(n_peers) == pair)(
            functools.partial(mix_early, pair, STEP, spec_ref, part_ref)
        )
    copies[1].wait()


def spectra(received, fwd, bwd, n_peers):
    rows, width = received[0].shape
    whole = pl.BlockSpec(memory_space=pltpu.VMEM)
    args = [pltpu.with_memory_space_constraint(a, pltpu.HBM) for a in (fwd, bwd)]
    return pl.pallas_call(
        functools.partial(spectra_kernel, n_peers),
        in_specs=[pl.BlockSpec(memory_space=pltpu.HBM)] * 2 + [whole] * len(received),
        out_specs=[whole] * 4,
        out_shape=[
            jax.ShapeDtypeStruct(fwd.shape, BF16),
            jax.ShapeDtypeStruct(bwd.shape, BF16),
            jax.ShapeDtypeStruct((n_peers, 2 * rows, width), F32),
            jax.ShapeDtypeStruct((n_peers, 2 * rows, width // 2), F32),
        ],
        scratch_shapes=[pltpu.SemaphoreType.DMA((2,))],
        compiler_params=pltpu.CompilerParams(vmem_limit_bytes=CONV_VMEM),
        cost_estimate=pl.CostEstimate(
            flops=8 * len(received) * rows * rows * width, bytes_accessed=4 * 2**20, transcendentals=0
        ),
    )(*args, *received)


def mix_late(pair, step, first, last, sign, spec_ref, part_ref, late_ref, turned):
    n_blocks, rows, chans = spec_ref.shape[0], spec_ref.shape[1] // 2, spec_ref.shape[2] // 2
    early = [j for j in range(n_blocks) if j // 2 != pair]
    x_at, f_at = slice(0, chans), slice(chans, 2 * chans)

    @pl.loop(first // step, last // step)
    def _(t):
        row = pl.multiple_of(t * step, step)
        late = [2 * pair, 2 * pair + 1]
        signal = {j: load(late_ref, (j % 2,), row, step, rows, x_at) for j in late}
        filt = {j: load(late_ref, (j % 2,), row, step, rows, f_at) for j in late}
        total = [load(part_ref, (i,), row, step, rows, slice(0, chans)) for i in range(n_blocks)]
        for b in early:
            if b + late[0] >= n_blocks:
                continue
            x_b = load(spec_ref, (b,), row, step, rows, x_at)
            f_b = load(spec_ref, (b,), row, step, rows, f_at)
            for j in late:
                if b + j < n_blocks:
                    total[b + j] = plus(total[b + j], times(filt[j], x_b))
                    total[b + j] = plus(total[b + j], times(f_b, signal[j]))
        for j in late:
            for d in late:
                if j + d < n_blocks:
                    total[j + d] = plus(total[j + d], times(filt[d], signal[j]))
        for i in range(n_blocks):
            value = total[i]
            if i > 0:
                turn_re, turn_im = total[i - 1]
                if sign > 0:
                    value = value[0] - turn_im, value[1] + turn_re
                else:
                    value = value[0] + turn_im, value[1] - turn_re
            lanes = slice(i % 2 * chans, (i % 2 + 1) * chans)
            for part in range(2):
                high = value[part].astype(BF16)
                low = (value[part] - high.astype(F32)).astype(BF16)
                for c, piece in enumerate((high, high, low)):
                    turned[i // 2, pl.ds(row + (2 * c + part) * rows, step), lanes] = piece


def conv_kernel(fwd_ref, bwd_ref, spec_ref, part_ref, *refs):
    *refs, late_ref, turned = refs
    n_blocks = spec_ref.shape[0]
    in_refs, out_refs = refs[:-n_blocks], refs[-n_blocks:]
    rows, chans = in_refs[0].shape[0], in_refs[0].shape[1] // 2
    for slot, in_ref in zip(slots_of(n_blocks, False)[-2:], in_refs):
        late_ref[lax.bitwise_and(peer_of(slot), 1)] = block_spectrum(fwd_ref[...], in_ref[...])

    def mix(pair):
        for first, last, sign in ((0, rows // 2, 1), (rows // 2, rows, -1)):
            mix_late(pair, STEP, first, last, sign, spec_ref, part_ref, late_ref, turned)

    for pair in range(n_blocks // 2):
        pl.when(late_place(n_blocks) == pair)(functools.partial(mix, pair))

    odd = lax.bitwise_and(lax.axis_index("seq"), 1) == 1
    by_slot = dict(zip(slots_of(n_blocks, True), out_refs))
    for slot in range(0, n_blocks, 2):
        pair = lax.div(peer_of(slot), 2)
        both = jnp.dot(bwd_ref[...], turned[pair], preferred_element_type=F32)
        left, right = both[:, :chans], both[:, chans:]
        by_slot[slot][...] = jnp.where(odd, right, left).astype(BF16)
        by_slot[slot + 1][...] = jnp.where(odd, left, right).astype(BF16)


def conv_fast(early, part, late, fwd, bwd):
    n_blocks = early.shape[0]
    rows, chans = late[0].shape[0], late[0].shape[1] // 2
    whole = pl.BlockSpec(memory_space=pltpu.VMEM)
    return pl.pallas_call(
        conv_kernel,
        in_specs=[whole] * 6,
        out_specs=[whole] * n_blocks,
        out_shape=[jax.ShapeDtypeStruct((rows, chans), BF16)] * n_blocks,
        scratch_shapes=[
            pltpu.VMEM((2, 2 * rows, 2 * chans), F32),
            pltpu.VMEM((n_blocks // 2, 6 * rows, 2 * chans), BF16),
        ],
        compiler_params=pltpu.CompilerParams(vmem_limit_bytes=CONV_VMEM),
        cost_estimate=pl.CostEstimate(
            flops=16 * n_blocks * rows * rows * chans, bytes_accessed=4 * 2**20, transcendentals=0
        ),
    )(fwd, bwd, early, part, *late)


def conv_plain(received, fwd, bwd):
    n_blocks, rows, chans = received.shape[0], received.shape[1], received.shape[2] // 2
    exact = lax.Precision.HIGHEST
    fwd32 = fwd[:, :rows].astype(F32) + fwd[:, rows:].astype(F32)
    bwd32 = bwd[:, : 2 * rows].astype(F32) + bwd[:, 2 * rows : 4 * rows].astype(F32)
    sign = jnp.where(jnp.arange(rows) < rows // 2, 1.0, -1.0).astype(F32)[:, None]

    def spectrum(blocks):
        spec = jnp.einsum("kt,jtc->jkc", fwd32, blocks.astype(F32), precision=exact)
        return spec[:, :rows], spec[:, rows:]

    x_re, x_im = spectrum(received[:, :, :chans])
    f_re, f_im = spectrum(received[:, :, chans:])
    g_re = f_re.at[1:].add(-sign * f_im[:-1])
    g_im = f_im.at[1:].add(sign * f_re[:-1])

    def one(d, total):
        t_re, t_im = total
        later = (jnp.arange(n_blocks) >= d)[:, None, None]
        a_re = jnp.where(later, jnp.roll(x_re, d, axis=0), 0.0)
        a_im = jnp.where(later, jnp.roll(x_im, d, axis=0), 0.0)
        return (
            t_re + g_re[d] * a_re - g_im[d] * a_im,
            t_im + g_re[d] * a_im + g_im[d] * a_re,
        )

    zero = jnp.zeros_like(x_re)
    y_re, y_im = lax.fori_loop(0, n_blocks, one, (zero, zero))
    both = jnp.concatenate([y_re, y_im], axis=1)
    return jnp.einsum("tk,jkc->jtc", bwd32, both, precision=exact).astype(BF16)


def columns_of(other, across, piece, pieces, width):
    count = width // 4 // pieces
    place = lax.axis_index("fsdp")
    core, side = lax.rem(place, 2), lax.div(place, 2)
    block = 2 * (1 - side if across else side) + (1 - core if other else core)
    return pl.ds(pl.multiple_of((block * pieces + piece) * count, count), count)


def gate_slot(slot, queries_ref, keys_ref, values_ref, skip_ref, conv_ref):
    at = peer_block(slot, conv_ref.shape[1])
    product = keys_ref[:, at].astype(F32) * values_ref[:, at].astype(F32)
    mixed = conv_ref[...].astype(F32) + skip_ref[:, at] * product
    return (queries_ref[:, at].astype(F32) * mixed).astype(BF16)


def gate_early_kernel(n_peers, queries_ref, keys_ref, values_ref, skip_ref, weight_ref, *refs):
    conv_refs, (gated_ref, *part_refs) = refs[:-3], refs[-3:]
    chans = conv_refs[0].shape[1]
    slots = slots_of(n_peers, True)
    for slot, conv_ref in zip(slots, conv_refs):
        gated = gate_slot(slot, queries_ref, keys_ref, values_ref, skip_ref, conv_ref)
        gated_ref[:, peer_block(slot, chans)] = gated
    for slot in slots[len(conv_refs) :]:
        gated_ref[:, peer_block(slot, chans)] = jnp.zeros((gated_ref.shape[0], chans), BF16)
    for other, part_ref in zip((True, False), part_refs):
        columns = weight_ref[:, columns_of(other, True, 0, 1, weight_ref.shape[1])]
        part_ref[...] = jnp.dot(gated_ref[...], columns, preferred_element_type=F32)


def gate_early(queries, keys, values, skip, weight, conv, n_peers):
    rows, width = queries.shape
    out_width = weight.shape[1] // 4
    whole = pl.BlockSpec(memory_space=pltpu.VMEM)
    return pl.pallas_call(
        functools.partial(gate_early_kernel, n_peers),
        in_specs=[whole] * (5 + len(conv)),
        out_specs=[whole] * 3,
        out_shape=[jax.ShapeDtypeStruct((rows, width), BF16)]
        + [jax.ShapeDtypeStruct((rows, out_width), F32)] * 2,
        compiler_params=pltpu.CompilerParams(vmem_limit_bytes=PROJECT_VMEM),
        cost_estimate=pl.CostEstimate(
            flops=4 * rows * width * out_width, bytes_accessed=10 * rows * width, transcendentals=0
        ),
    )(queries, keys, values, skip, weight, *conv)


def late_product(late, late_slots, block, weight_ref, part_ref):
    chans = late.shape[1] // len(late_slots)
    at = columns_of(*block, weight_ref.shape[1])
    _, _, piece, pieces = block
    count = part_ref.shape[1] // pieces
    columns = jnp.concatenate([weight_ref[peer_block(s, chans), at] for s in late_slots], axis=0)
    part = part_ref[:, piece * count : (piece + 1) * count]
    return part + jnp.dot(late, columns, preferred_element_type=F32)


def gate_late_kernel(late_slots, block, queries_ref, keys_ref, values_ref, skip_ref, weight_ref, part_ref, *refs):
    *conv_refs, late_ref, sent_ref = refs
    chans = conv_refs[0].shape[1]
    for c, (slot, conv_ref) in enumerate(zip(late_slots, conv_refs)):
        gated = gate_slot(slot, queries_ref, keys_ref, values_ref, skip_ref, conv_ref)
        late_ref[:, c * chans : (c + 1) * chans] = gated
    total = late_product(late_ref[...], late_slots, block, weight_ref, part_ref)
    sent_ref[...] = total.astype(BF16)


def gate_late(queries, keys, values, skip, weight, part, conv, late_slots, block):
    rows, chans = conv[0].shape
    whole = pl.BlockSpec(memory_space=pltpu.VMEM)
    return pl.pallas_call(
        functools.partial(gate_late_kernel, late_slots, block),
        in_specs=[whole] * (6 + len(conv)),
        out_specs=[whole] * 2,
        out_shape=[
            jax.ShapeDtypeStruct((rows, chans * len(conv)), BF16),
            jax.ShapeDtypeStruct((rows, weight.shape[1] // 4 // block[-1]), BF16),
        ],
        compiler_params=pltpu.CompilerParams(vmem_limit_bytes=PROJECT_VMEM),
        cost_estimate=pl.CostEstimate(
            flops=rows * chans * weight.shape[1], bytes_accessed=2**20, transcendentals=0
        ),
    )(queries, keys, values, skip, weight, part, *conv)


def late_project_kernel(late_slots, blocks, weight_ref, late_ref, part_ref, *out_refs):
    for block, out_ref in zip(blocks, out_refs):
        total = late_product(late_ref[...], late_slots, block, weight_ref, part_ref)
        out_ref[...] = total.astype(out_ref.dtype)


def late_project(weight, late, part, late_slots, blocks, dtype):
    rows, depth = late.shape
    widths = [weight.shape[1] // 4 // pieces for *_, pieces in blocks]
    whole = pl.BlockSpec(memory_space=pltpu.VMEM)
    return pl.pallas_call(
        functools.partial(late_project_kernel, late_slots, blocks),
        in_specs=[whole] * 3,
        out_specs=[whole] * len(blocks),
        out_shape=[jax.ShapeDtypeStruct((rows, w), dtype) for w in widths],
        compiler_params=pltpu.CompilerParams(vmem_limit_bytes=PROJECT_VMEM),
        cost_estimate=pl.CostEstimate(
            flops=2 * rows * depth * sum(widths), bytes_accessed=2**20, transcendentals=0
        ),
    )(weight, late, part)


def assemble_kernel(late_slots, gated_ref, late_ref, out_ref):
    chans = late_ref.shape[1] // len(late_slots)
    out_ref[...] = gated_ref[...]
    for c, slot in enumerate(late_slots):
        out_ref[:, peer_block(slot, chans)] = late_ref[:, c * chans : (c + 1) * chans]


def assemble(gated, late, late_slots):
    whole = pl.BlockSpec(memory_space=pltpu.VMEM)
    return pl.pallas_call(
        functools.partial(assemble_kernel, late_slots),
        in_specs=[whole] * 2,
        out_specs=whole,
        out_shape=jax.ShapeDtypeStruct(gated.shape, BF16),
        compiler_params=pltpu.CompilerParams(vmem_limit_bytes=SMALL_VMEM),
        cost_estimate=pl.CostEstimate(flops=1000, bytes_accessed=2**20, transcendentals=0),
    )(gated, late)


def project_kernel(blocks, gated_ref, weight_ref, *out_refs):
    for block, out_ref in zip(blocks, out_refs):
        columns = weight_ref[:, columns_of(*block, weight_ref.shape[1])]
        total = jnp.dot(gated_ref[...], columns, preferred_element_type=F32)
        out_ref[...] = total.astype(out_ref.dtype)


def project(gated, weight, blocks, dtypes):
    rows, depth = gated.shape
    widths = [weight.shape[1] // 4 // pieces for *_, pieces in blocks]
    whole = pl.BlockSpec(memory_space=pltpu.VMEM)
    return pl.pallas_call(
        functools.partial(project_kernel, blocks),
        in_specs=[whole] * 2,
        out_specs=[whole] * len(blocks),
        out_shape=[jax.ShapeDtypeStruct((rows, w), t) for w, t in zip(widths, dtypes)],
        compiler_params=pltpu.CompilerParams(vmem_limit_bytes=PROJECT_VMEM),
        cost_estimate=pl.CostEstimate(
            flops=2 * rows * depth * sum(widths), bytes_accessed=2 * depth * sum(widths), transcendentals=0
        ),
    )(gated, weight)


def add_kernel(own_ref, arrived_ref, out_ref):
    total = own_ref[...] + arrived_ref[...].astype(F32)
    out_ref[...] = total.astype(out_ref.dtype)


def add(own, arrived):
    whole = pl.BlockSpec(memory_space=pltpu.VMEM)
    return pl.pallas_call(
        add_kernel,
        in_specs=[whole] * 2,
        out_specs=whole,
        out_shape=jax.ShapeDtypeStruct(arrived.shape, BF16),
        compiler_params=pltpu.CompilerParams(vmem_limit_bytes=SMALL_VMEM),
        cost_estimate=pl.CostEstimate(
            flops=arrived.size, bytes_accessed=8 * arrived.size, transcendentals=0
        ),
    )(own, arrived)


def mark_kernel(*refs):
    refs[-1][...] = jnp.zeros_like(refs[-1])


def mark(arrays):
    return pl.pallas_call(
        mark_kernel,
        in_specs=[pl.BlockSpec(memory_space=pl.ANY)] * len(arrays),
        out_specs=pl.BlockSpec(memory_space=pltpu.VMEM),
        out_shape=jax.ShapeDtypeStruct((8, 128), F32),
        compiler_params=pltpu.CompilerParams(vmem_limit_bytes=SMALL_VMEM),
        cost_estimate=pl.CostEstimate(flops=2 * 10**10, bytes_accessed=2**20, transcendentals=0),
    )(*arrays)


def finish_kernel(own_ref, near_ref, *refs):
    *arrived_refs, _, out_ref, stage, sem = refs
    width = out_ref.shape[1] // len(arrived_refs)
    steps = sem.shape[0]
    rows = out_ref.shape[0] // steps
    copies = []
    for step in range(steps):
        part = pl.ds(step * rows, rows)
        for c, arrived_ref in enumerate(arrived_refs):
            at = slice(c * width, (c + 1) * width)
            total = own_ref[part, at] + near_ref[part, at].astype(F32)
            stage[part, at] = (total + arrived_ref[part].astype(F32)).astype(stage.dtype)
        copies.append(pltpu.make_async_copy(stage.at[part], out_ref.at[part], sem.at[step]))
        copies[-1].start()
    for copy in copies:
        copy.wait()


def finish(own, near, arrived):
    rows, width = own.shape
    whole, anywhere = pl.BlockSpec(memory_space=pltpu.VMEM), pl.BlockSpec(memory_space=pl.ANY)
    return pl.pallas_call(
        finish_kernel,
        in_specs=[whole] * (2 + len(arrived)) + [anywhere],
        out_specs=anywhere,
        out_shape=jax.ShapeDtypeStruct((rows, width), BF16),
        scratch_shapes=[pltpu.VMEM((rows, width), BF16), pltpu.SemaphoreType.DMA((4,))],
        compiler_params=pltpu.CompilerParams(vmem_limit_bytes=SMALL_VMEM),
        cost_estimate=pl.CostEstimate(
            flops=rows * width, bytes_accessed=8 * rows * width, transcendentals=0
        ),
    )(own, near, *arrived, mark(arrived))


def body(pieces, tables, queries, keys, values, filters, skip_weight, out_weight):
    rows, width = keys.shape
    n_peers = lax.axis_size("seq")
    chans = width // n_peers
    fwd, bwd = (jnp.asarray(t) for t in tables)
    skip = skip_weight[None, :]
    in_chip = [(0, 1), (1, 0), (2, 3), (3, 2)]
    across = [(0, 2), (2, 0), (1, 3), (3, 1)]

    sends = [(True, True, c, pieces) for c in range(pieces)]
    keeps = [(False, True, c, pieces) for c in range(pieces)]

    if chans % 128 == 0 and n_peers == 8:
        blocks = pre(keys, values, filters, n_peers)
        received = exchange(blocks, n_peers, False)
        fwd, bwd, early, part = spectra(received[:-2], fwd, bwd, n_peers)
        back = exchange(conv_fast(early, part, received[-2:], fwd, bwd), n_peers, True)
        slots = slots_of(n_peers, True)[-2:]
        gated, send_part, own_part = gate_early(
            queries, keys, values, skip, out_weight, back[:-2], n_peers
        )
        late, last = gate_late(
            queries, keys, values, skip, out_weight, send_part, back[-2:], slots, sends[-1]
        )
        sent = [
            *(late_project(out_weight, late, send_part, slots, [s], BF16)[0] for s in sends[:-1]),
            last,
        ]
        ours = late_project(out_weight, late, own_part, slots, keeps, F32)
        gated = assemble(gated, late, slots)
    else:
        product = keys.astype(F32) * values.astype(F32)
        parts = [a.astype(BF16).reshape(rows, n_peers, chans) for a in (product, filters)]
        sent = jnp.concatenate(parts, axis=2).transpose(1, 0, 2)
        received = lax.all_to_all(sent, "seq", split_axis=0, concat_axis=0, tiled=True)
        conv = conv_plain(received, fwd, bwd)
        back = lax.all_to_all(conv, "seq", split_axis=0, concat_axis=0, tiled=True)
        mixed = back.transpose(1, 0, 2).reshape(rows, width).astype(F32) + skip * product
        gated = (queries.astype(F32) * mixed).astype(BF16)
        sent = project(gated, out_weight, sends, [BF16] * pieces)
        ours = project(gated, out_weight, keeps, [F32] * pieces)

    theirs = [lax.ppermute(piece, "fsdp", in_chip) for piece in sent]
    arrived = [lax.ppermute(add(*pair), "fsdp", across) for pair in zip(ours, theirs)]
    blocks = [(True, False, 0, 1), (False, False, 0, 1)]
    sent, own = project(gated, out_weight, blocks, [BF16, F32])
    near = lax.ppermute(sent, "fsdp", in_chip)
    return finish(own, near, arrived)


def solution(mesh):
    in_specs = (
        P("seq", "fsdp"),
        P("seq", "fsdp"),
        P("seq", "fsdp"),
        P("seq", "fsdp"),
        P("fsdp"),
        P("fsdp", None),
    )
    out_specs = P("seq", "fsdp")

    def run(queries, keys, values, filters, skip_weight, out_weight):
        rows = keys.shape[0] // mesh.shape["seq"]
        fn = functools.partial(body, 2, make_tables(rows))
        return jax.shard_map(fn, mesh=mesh, in_specs=in_specs, out_specs=out_specs, check_vma=False)(
            queries, keys, values, filters, skip_weight, out_weight
        )

    return run
```

```python
import functools

import numpy as np

import jax
import jax.numpy as jnp
from jax import lax
from jax.experimental import pallas as pl
from jax.experimental.pallas import tpu as pltpu
from jax.sharding import PartitionSpec as P

BF16 = jnp.bfloat16
F32 = jnp.float32
CONV_VMEM = 24 * 2**20
PROJECT_VMEM = 24 * 2**20
SMALL_VMEM = 12 * 2**20
STEP = 16


def split_bf16(table):
    high = table.astype(BF16)
    return high, (table - high.astype(np.float64)).astype(BF16)


def make_tables(rows):
    order = np.concatenate([np.arange(0, rows, 2), np.arange(1, rows, 2)])
    times = np.arange(rows)
    angle = np.pi * (((2 * order[:, None] + 1) * times[None, :]) % (4 * rows)) / (2 * rows)
    forward = np.concatenate([np.cos(angle), -np.sin(angle)], axis=0)
    high, low = split_bf16(forward)
    back_high, back_low = split_bf16(forward.T / rows)
    return (
        np.concatenate([high, low], axis=1),
        np.concatenate([back_high, back_low, back_high], axis=1),
    )


def peer_of(slot):
    return lax.bitwise_xor(lax.axis_index("seq"), slot)


def peer_block(slot, size):
    return pl.ds(pl.multiple_of(peer_of(slot) * size, size), size)


def pre_kernel(n_peers, keys_hbm, values_hbm, filters_hbm, *refs):
    out_refs = refs[:n_peers]
    keys, values, filters, sem = refs[n_peers:]
    rows, width = keys.shape
    chans = width // n_peers
    steps = sem.shape[0]
    parts = [pl.ds(c * rows // steps, rows // steps) for c in range(steps)]
    pairs = ((keys_hbm, keys), (values_hbm, values), (filters_hbm, filters))
    copies = [
        [
            pltpu.make_async_copy(src.at[part], dst.at[part], sem.at[c, i])
            for i, (src, dst) in enumerate(pairs)
        ]
        for c, part in enumerate(parts)
    ]
    for group in copies:
        for copy in group:
            copy.start()
    for part, group in zip(parts, copies):
        for copy in group:
            copy.wait()
        for slot, out_ref in zip(slots_of(n_peers, False), out_refs):
            at = peer_block(slot, chans)
            product = keys[part, at].astype(F32) * values[part, at].astype(F32)
            out_ref[part, :chans] = product.astype(BF16)
            out_ref[part, chans:] = filters[part, at].astype(BF16)


def pre(keys, values, filters, n_peers):
    rows, width = keys.shape
    chans = width // n_peers
    args = [pltpu.with_memory_space_constraint(a, pltpu.HBM) for a in (keys, values, filters)]
    return pl.pallas_call(
        functools.partial(pre_kernel, n_peers),
        in_specs=[pl.BlockSpec(memory_space=pltpu.HBM)] * 3,
        out_specs=[pl.BlockSpec(memory_space=pltpu.VMEM)] * n_peers,
        out_shape=[jax.ShapeDtypeStruct((rows, 2 * chans), BF16)] * n_peers,
        scratch_shapes=[
            pltpu.VMEM((rows, width), BF16),
            pltpu.VMEM((rows, width), BF16),
            pltpu.VMEM((rows, width), F32),
            pltpu.SemaphoreType.DMA((2, 3)),
        ],
        compiler_params=pltpu.CompilerParams(vmem_limit_bytes=SMALL_VMEM),
        cost_estimate=pl.CostEstimate(
            flops=rows * width, bytes_accessed=12 * rows * width, transcendentals=0
        ),
    )(*args)


def slots_of(n_peers, back):
    half = n_peers // 2
    near, far = list(range(1, half)), list(range(half, n_peers))
    if back:
        return [0, near[0]] + far[2:] + near[1:] + far[:2]
    return [0, far[0]] + near[::-1] + far[1:]


def exchange(blocks, n_peers, back):
    return [
        lax.ppermute(block, "seq", [(i, i ^ slot) for i in range(n_peers)]) if slot else block
        for slot, block in zip(slots_of(n_peers, back), blocks)
    ]


def block_spectrum(table, block):
    return jnp.dot(table, jnp.concatenate([block, block], axis=0), preferred_element_type=F32)


def times(a, b):
    return a[0] * b[0] - a[1] * b[1], a[0] * b[1] + a[1] * b[0]


def plus(a, b):
    return b if a is None else (a[0] + b[0], a[1] + b[1])


def late_place(n_blocks):
    return lax.div(peer_of(slots_of(n_blocks, False)[-1]), 2)


def load(ref, at, row, step, rows, lanes):
    return tuple(ref[(*at, pl.ds(row + part * rows, step), lanes)] for part in range(2))


def mix_early(pair, step, spec_ref, part_ref):
    n_blocks, rows, chans = spec_ref.shape[0], spec_ref.shape[1] // 2, spec_ref.shape[2] // 2
    early = [j for j in range(n_blocks) if j // 2 != pair]

    @pl.loop(0, rows // step)
    def _(t):
        row = pl.multiple_of(t * step, step)
        signal = {j: load(spec_ref, (j,), row, step, rows, slice(0, chans)) for j in early}
        filt = {j: load(spec_ref, (j,), row, step, rows, slice(chans, 2 * chans)) for j in early}
        for i in range(n_blocks):
            total = None
            for d in early:
                if i - d in early:
                    total = plus(total, times(filt[d], signal[i - d]))
            if total is None:
                total = (jnp.zeros((step, chans), F32),) * 2
            for part in range(2):
                part_ref[i, pl.ds(row + part * rows, step)] = total[part]


def spectra_kernel(n_peers, fwd_hbm, bwd_hbm, *refs):
    *in_refs, fwd_ref, bwd_ref, spec_ref, part_ref, sem = refs
    copies = [
        pltpu.make_async_copy(fwd_hbm, fwd_ref, sem.at[0]),
        pltpu.make_async_copy(bwd_hbm, bwd_ref, sem.at[1]),
    ]
    for copy in copies:
        copy.start()
    copies[0].wait()
    for slot, in_ref in zip(slots_of(n_peers, False), in_refs):
        spec_ref[peer_of(slot)] = block_spectrum(fwd_ref[...], in_ref[...])
    for pair in range(n_peers // 2):
        pl.when(late_place(n_peers) == pair)(
            functools.partial(mix_early, pair, STEP, spec_ref, part_ref)
        )
    copies[1].wait()


def spectra(received, fwd, bwd, n_peers):
    rows, width = received[0].shape
    whole = pl.BlockSpec(memory_space=pltpu.VMEM)
    args = [pltpu.with_memory_space_constraint(a, pltpu.HBM) for a in (fwd, bwd)]
    return pl.pallas_call(
        functools.partial(spectra_kernel, n_peers),
        in_specs=[pl.BlockSpec(memory_space=pltpu.HBM)] * 2 + [whole] * len(received),
        out_specs=[whole] * 4,
        out_shape=[
            jax.ShapeDtypeStruct(fwd.shape, BF16),
            jax.ShapeDtypeStruct(bwd.shape, BF16),
            jax.ShapeDtypeStruct((n_peers, 2 * rows, width), F32),
            jax.ShapeDtypeStruct((n_peers, 2 * rows, width // 2), F32),
        ],
        scratch_shapes=[pltpu.SemaphoreType.DMA((2,))],
        compiler_params=pltpu.CompilerParams(vmem_limit_bytes=CONV_VMEM),
        cost_estimate=pl.CostEstimate(
            flops=8 * len(received) * rows * rows * width, bytes_accessed=4 * 2**20, transcendentals=0
        ),
    )(*args, *received)


def mix_late(pair, step, first, last, sign, spec_ref, part_ref, late_ref, turned):
    n_blocks, rows, chans = spec_ref.shape[0], spec_ref.shape[1] // 2, spec_ref.shape[2] // 2
    early = [j for j in range(n_blocks) if j // 2 != pair]
    x_at, f_at = slice(0, chans), slice(chans, 2 * chans)

    @pl.loop(first // step, last // step)
    def _(t):
        row = pl.multiple_of(t * step, step)
        late = [2 * pair, 2 * pair + 1]
        signal = {j: load(late_ref, (j % 2,), row, step, rows, x_at) for j in late}
        filt = {j: load(late_ref, (j % 2,), row, step, rows, f_at) for j in late}
        total = [load(part_ref, (i,), row, step, rows, slice(0, chans)) for i in range(n_blocks)]
        for b in early:
            if b + late[0] >= n_blocks:
                continue
            x_b = load(spec_ref, (b,), row, step, rows, x_at)
            f_b = load(spec_ref, (b,), row, step, rows, f_at)
            for j in late:
                if b + j < n_blocks:
                    total[b + j] = plus(total[b + j], times(filt[j], x_b))
                    total[b + j] = plus(total[b + j], times(f_b, signal[j]))
        for j in late:
            for d in late:
                if j + d < n_blocks:
                    total[j + d] = plus(total[j + d], times(filt[d], signal[j]))
        for i in range(n_blocks):
            value = total[i]
            if i > 0:
                turn_re, turn_im = total[i - 1]
                if sign > 0:
                    value = value[0] - turn_im, value[1] + turn_re
                else:
                    value = value[0] + turn_im, value[1] - turn_re
            lanes = slice(i % 2 * chans, (i % 2 + 1) * chans)
            for part in range(2):
                high = value[part].astype(BF16)
                low = (value[part] - high.astype(F32)).astype(BF16)
                for c, piece in enumerate((high, high, low)):
                    turned[i // 2, pl.ds(row + (2 * c + part) * rows, step), lanes] = piece


def conv_kernel(fwd_ref, bwd_ref, spec_ref, part_ref, *refs):
    *refs, late_ref, turned = refs
    n_blocks = spec_ref.shape[0]
    in_refs, out_refs = refs[:-n_blocks], refs[-n_blocks:]
    rows, chans = in_refs[0].shape[0], in_refs[0].shape[1] // 2
    for slot, in_ref in zip(slots_of(n_blocks, False)[-2:], in_refs):
        late_ref[lax.bitwise_and(peer_of(slot), 1)] = block_spectrum(fwd_ref[...], in_ref[...])

    def mix(pair):
        for first, last, sign in ((0, rows // 2, 1), (rows // 2, rows, -1)):
            mix_late(pair, STEP, first, last, sign, spec_ref, part_ref, late_ref, turned)

    for pair in range(n_blocks // 2):
        pl.when(late_place(n_blocks) == pair)(functools.partial(mix, pair))

    odd = lax.bitwise_and(lax.axis_index("seq"), 1) == 1
    by_slot = dict(zip(slots_of(n_blocks, True), out_refs))
    for slot in range(0, n_blocks, 2):
        pair = lax.div(peer_of(slot), 2)
        both = jnp.dot(bwd_ref[...], turned[pair], preferred_element_type=F32)
        left, right = both[:, :chans], both[:, chans:]
        by_slot[slot][...] = jnp.where(odd, right, left).astype(BF16)
        by_slot[slot + 1][...] = jnp.where(odd, left, right).astype(BF16)


def conv_fast(early, part, late, fwd, bwd):
    n_blocks = early.shape[0]
    rows, chans = late[0].shape[0], late[0].shape[1] // 2
    whole = pl.BlockSpec(memory_space=pltpu.VMEM)
    return pl.pallas_call(
        conv_kernel,
        in_specs=[whole] * 6,
        out_specs=[whole] * n_blocks,
        out_shape=[jax.ShapeDtypeStruct((rows, chans), BF16)] * n_blocks,
        scratch_shapes=[
            pltpu.VMEM((2, 2 * rows, 2 * chans), F32),
            pltpu.VMEM((n_blocks // 2, 6 * rows, 2 * chans), BF16),
        ],
        compiler_params=pltpu.CompilerParams(vmem_limit_bytes=CONV_VMEM),
        cost_estimate=pl.CostEstimate(
            flops=16 * n_blocks * rows * rows * chans, bytes_accessed=4 * 2**20, transcendentals=0
        ),
    )(fwd, bwd, early, part, *late)


def conv_plain(received, fwd, bwd):
    n_blocks, rows, chans = received.shape[0], received.shape[1], received.shape[2] // 2
    exact = lax.Precision.HIGHEST
    fwd32 = fwd[:, :rows].astype(F32) + fwd[:, rows:].astype(F32)
    bwd32 = bwd[:, : 2 * rows].astype(F32) + bwd[:, 2 * rows : 4 * rows].astype(F32)
    sign = jnp.where(jnp.arange(rows) < rows // 2, 1.0, -1.0).astype(F32)[:, None]

    def spectrum(blocks):
        spec = jnp.einsum("kt,jtc->jkc", fwd32, blocks.astype(F32), precision=exact)
        return spec[:, :rows], spec[:, rows:]

    x_re, x_im = spectrum(received[:, :, :chans])
    f_re, f_im = spectrum(received[:, :, chans:])
    g_re = f_re.at[1:].add(-sign * f_im[:-1])
    g_im = f_im.at[1:].add(sign * f_re[:-1])

    def one(d, total):
        t_re, t_im = total
        later = (jnp.arange(n_blocks) >= d)[:, None, None]
        a_re = jnp.where(later, jnp.roll(x_re, d, axis=0), 0.0)
        a_im = jnp.where(later, jnp.roll(x_im, d, axis=0), 0.0)
        return (
            t_re + g_re[d] * a_re - g_im[d] * a_im,
            t_im + g_re[d] * a_im + g_im[d] * a_re,
        )

    zero = jnp.zeros_like(x_re)
    y_re, y_im = lax.fori_loop(0, n_blocks, one, (zero, zero))
    both = jnp.concatenate([y_re, y_im], axis=1)
    return jnp.einsum("tk,jkc->jtc", bwd32, both, precision=exact).astype(BF16)


def columns_of(other, across, piece, pieces, width):
    count = width // 4 // pieces
    place = lax.axis_index("fsdp")
    core, side = lax.rem(place, 2), lax.div(place, 2)
    block = 2 * (1 - side if across else side) + (1 - core if other else core)
    return pl.ds(pl.multiple_of((block * pieces + piece) * count, count), count)


def gate_slot(slot, queries_ref, keys_ref, values_ref, skip_ref, conv_ref):
    at = peer_block(slot, conv_ref.shape[1])
    product = keys_ref[:, at].astype(F32) * values_ref[:, at].astype(F32)
    mixed = conv_ref[...].astype(F32) + skip_ref[:, at] * product
    return (queries_ref[:, at].astype(F32) * mixed).astype(BF16)


def gate_early_kernel(n_peers, queries_ref, keys_ref, values_ref, skip_ref, weight_ref, *refs):
    conv_refs, (gated_ref, *part_refs) = refs[:-3], refs[-3:]
    chans = conv_refs[0].shape[1]
    slots = slots_of(n_peers, True)
    for slot, conv_ref in zip(slots, conv_refs):
        gated = gate_slot(slot, queries_ref, keys_ref, values_ref, skip_ref, conv_ref)
        gated_ref[:, peer_block(slot, chans)] = gated
    for slot in slots[len(conv_refs) :]:
        gated_ref[:, peer_block(slot, chans)] = jnp.zeros((gated_ref.shape[0], chans), BF16)
    for other, part_ref in zip((True, False), part_refs):
        columns = weight_ref[:, columns_of(other, True, 0, 1, weight_ref.shape[1])]
        part_ref[...] = jnp.dot(gated_ref[...], columns, preferred_element_type=F32)


def gate_early(queries, keys, values, skip, weight, conv, n_peers):
    rows, width = queries.shape
    out_width = weight.shape[1] // 4
    whole = pl.BlockSpec(memory_space=pltpu.VMEM)
    return pl.pallas_call(
        functools.partial(gate_early_kernel, n_peers),
        in_specs=[whole] * (5 + len(conv)),
        out_specs=[whole] * 3,
        out_shape=[jax.ShapeDtypeStruct((rows, width), BF16)]
        + [jax.ShapeDtypeStruct((rows, out_width), F32)] * 2,
        compiler_params=pltpu.CompilerParams(vmem_limit_bytes=PROJECT_VMEM),
        cost_estimate=pl.CostEstimate(
            flops=4 * rows * width * out_width, bytes_accessed=10 * rows * width, transcendentals=0
        ),
    )(queries, keys, values, skip, weight, *conv)


def late_product(late, late_slots, block, weight_ref, part_ref):
    chans = late.shape[1] // len(late_slots)
    at = columns_of(*block, weight_ref.shape[1])
    _, _, piece, pieces = block
    count = part_ref.shape[1] // pieces
    columns = jnp.concatenate([weight_ref[peer_block(s, chans), at] for s in late_slots], axis=0)
    part = part_ref[:, piece * count : (piece + 1) * count]
    return part + jnp.dot(late, columns, preferred_element_type=F32)


def gate_late_kernel(late_slots, block, queries_ref, keys_ref, values_ref, skip_ref, weight_ref, part_ref, *refs):
    *conv_refs, late_ref, sent_ref = refs
    chans = conv_refs[0].shape[1]
    for c, (slot, conv_ref) in enumerate(zip(late_slots, conv_refs)):
        gated = gate_slot(slot, queries_ref, keys_ref, values_ref, skip_ref, conv_ref)
        late_ref[:, c * chans : (c + 1) * chans] = gated
    total = late_product(late_ref[...], late_slots, block, weight_ref, part_ref)
    sent_ref[...] = total.astype(BF16)


def gate_late(queries, keys, values, skip, weight, part, conv, late_slots, block):
    rows, chans = conv[0].shape
    whole = pl.BlockSpec(memory_space=pltpu.VMEM)
    return pl.pallas_call(
        functools.partial(gate_late_kernel, late_slots, block),
        in_specs=[whole] * (6 + len(conv)),
        out_specs=[whole] * 2,
        out_shape=[
            jax.ShapeDtypeStruct((rows, chans * len(conv)), BF16),
            jax.ShapeDtypeStruct((rows, weight.shape[1] // 4 // block[-1]), BF16),
        ],
        compiler_params=pltpu.CompilerParams(vmem_limit_bytes=PROJECT_VMEM),
        cost_estimate=pl.CostEstimate(
            flops=rows * chans * weight.shape[1], bytes_accessed=2**20, transcendentals=0
        ),
    )(queries, keys, values, skip, weight, part, *conv)


def late_project_kernel(late_slots, blocks, weight_ref, late_ref, part_ref, *out_refs):
    for block, out_ref in zip(blocks, out_refs):
        total = late_product(late_ref[...], late_slots, block, weight_ref, part_ref)
        out_ref[...] = total.astype(out_ref.dtype)


def late_project(weight, late, part, late_slots, blocks, dtype):
    rows, depth = late.shape
    widths = [weight.shape[1] // 4 // pieces for *_, pieces in blocks]
    whole = pl.BlockSpec(memory_space=pltpu.VMEM)
    return pl.pallas_call(
        functools.partial(late_project_kernel, late_slots, blocks),
        in_specs=[whole] * 3,
        out_specs=[whole] * len(blocks),
        out_shape=[jax.ShapeDtypeStruct((rows, w), dtype) for w in widths],
        compiler_params=pltpu.CompilerParams(vmem_limit_bytes=PROJECT_VMEM),
        cost_estimate=pl.CostEstimate(
            flops=2 * rows * depth * sum(widths), bytes_accessed=2**20, transcendentals=0
        ),
    )(weight, late, part)


def assemble_kernel(late_slots, gated_ref, late_ref, out_ref):
    chans = late_ref.shape[1] // len(late_slots)
    out_ref[...] = gated_ref[...]
    for c, slot in enumerate(late_slots):
        out_ref[:, peer_block(slot, chans)] = late_ref[:, c * chans : (c + 1) * chans]


def assemble(gated, late, late_slots):
    whole = pl.BlockSpec(memory_space=pltpu.VMEM)
    return pl.pallas_call(
        functools.partial(assemble_kernel, late_slots),
        in_specs=[whole] * 2,
        out_specs=whole,
        out_shape=jax.ShapeDtypeStruct(gated.shape, BF16),
        compiler_params=pltpu.CompilerParams(vmem_limit_bytes=SMALL_VMEM),
        cost_estimate=pl.CostEstimate(flops=1000, bytes_accessed=2**20, transcendentals=0),
    )(gated, late)


def project_kernel(blocks, gated_ref, weight_ref, *out_refs):
    for block, out_ref in zip(blocks, out_refs):
        columns = weight_ref[:, columns_of(*block, weight_ref.shape[1])]
        total = jnp.dot(gated_ref[...], columns, preferred_element_type=F32)
        out_ref[...] = total.astype(out_ref.dtype)


def project(gated, weight, blocks, dtypes):
    rows, depth = gated.shape
    widths = [weight.shape[1] // 4 // pieces for *_, pieces in blocks]
    whole = pl.BlockSpec(memory_space=pltpu.VMEM)
    return pl.pallas_call(
        functools.partial(project_kernel, blocks),
        in_specs=[whole] * 2,
        out_specs=[whole] * len(blocks),
        out_shape=[jax.ShapeDtypeStruct((rows, w), t) for w, t in zip(widths, dtypes)],
        compiler_params=pltpu.CompilerParams(vmem_limit_bytes=PROJECT_VMEM),
        cost_estimate=pl.CostEstimate(
            flops=2 * rows * depth * sum(widths), bytes_accessed=2 * depth * sum(widths), transcendentals=0
        ),
    )(gated, weight)


def add_kernel(own_ref, arrived_ref, out_ref):
    total = own_ref[...] + arrived_ref[...].astype(F32)
    out_ref[...] = total.astype(out_ref.dtype)


def add(own, arrived):
    whole = pl.BlockSpec(memory_space=pltpu.VMEM)
    return pl.pallas_call(
        add_kernel,
        in_specs=[whole] * 2,
        out_specs=whole,
        out_shape=jax.ShapeDtypeStruct(arrived.shape, BF16),
        compiler_params=pltpu.CompilerParams(vmem_limit_bytes=SMALL_VMEM),
        cost_estimate=pl.CostEstimate(
            flops=arrived.size, bytes_accessed=8 * arrived.size, transcendentals=0
        ),
    )(own, arrived)


def mark_kernel(*refs):
    refs[-1][...] = jnp.zeros_like(refs[-1])


def mark(arrays):
    return pl.pallas_call(
        mark_kernel,
        in_specs=[pl.BlockSpec(memory_space=pl.ANY)] * len(arrays),
        out_specs=pl.BlockSpec(memory_space=pltpu.VMEM),
        out_shape=jax.ShapeDtypeStruct((8, 128), F32),
        compiler_params=pltpu.CompilerParams(vmem_limit_bytes=SMALL_VMEM),
        cost_estimate=pl.CostEstimate(flops=2 * 10**10, bytes_accessed=2**20, transcendentals=0),
    )(*arrays)


def finish_kernel(own_ref, near_ref, *refs):
    *arrived_refs, _, out_ref, stage, sem = refs
    width = out_ref.shape[1] // len(arrived_refs)
    steps = sem.shape[0]
    rows = out_ref.shape[0] // steps
    copies = []
    for step in range(steps):
        part = pl.ds(step * rows, rows)
        for c, arrived_ref in enumerate(arrived_refs):
            at = slice(c * width, (c + 1) * width)
            total = own_ref[part, at] + near_ref[part, at].astype(F32)
            stage[part, at] = (total + arrived_ref[part].astype(F32)).astype(stage.dtype)
        copies.append(pltpu.make_async_copy(stage.at[part], out_ref.at[part], sem.at[step]))
        copies[-1].start()
    for copy in copies:
        copy.wait()


def finish(own, near, arrived):
    rows, width = own.shape
    whole, anywhere = pl.BlockSpec(memory_space=pltpu.VMEM), pl.BlockSpec(memory_space=pl.ANY)
    return pl.pallas_call(
        finish_kernel,
        in_specs=[whole] * (2 + len(arrived)) + [anywhere],
        out_specs=anywhere,
        out_shape=jax.ShapeDtypeStruct((rows, width), BF16),
        scratch_shapes=[pltpu.VMEM((rows, width), BF16), pltpu.SemaphoreType.DMA((4,))],
        compiler_params=pltpu.CompilerParams(vmem_limit_bytes=SMALL_VMEM),
        cost_estimate=pl.CostEstimate(
            flops=rows * width, bytes_accessed=8 * rows * width, transcendentals=0
        ),
    )(own, near, *arrived, mark(arrived))


def body(pieces, tables, queries, keys, values, filters, skip_weight, out_weight):
    rows, width = keys.shape
    n_peers = lax.axis_size("seq")
    chans = width // n_peers
    fwd, bwd = (jnp.asarray(t) for t in tables)
    skip = skip_weight[None, :]
    in_chip = [(0, 1), (1, 0), (2, 3), (3, 2)]
    across = [(0, 2), (2, 0), (1, 3), (3, 1)]

    sends = [(True, True, c, pieces) for c in range(pieces)]
    keeps = [(False, True, c, pieces) for c in range(pieces)]

    if chans % 128 == 0 and n_peers == 8:
        blocks = pre(keys, values, filters, n_peers)
        received = exchange(blocks, n_peers, False)
        fwd, bwd, early, part = spectra(received[:-2], fwd, bwd, n_peers)
        back = exchange(conv_fast(early, part, received[-2:], fwd, bwd), n_peers, True)
        slots = slots_of(n_peers, True)[-2:]
        gated, send_part, own_part = gate_early(
            queries, keys, values, skip, out_weight, back[:-2], n_peers
        )
        late, last = gate_late(
            queries, keys, values, skip, out_weight, send_part, back[-2:], slots, sends[-1]
        )
        sent = [
            *(late_project(out_weight, late, send_part, slots, [s], BF16)[0] for s in sends[:-1]),
            last,
        ]
        ours = late_project(out_weight, late, own_part, slots, keeps, F32)
        gated = assemble(gated, late, slots)
    else:
        product = keys.astype(F32) * values.astype(F32)
        parts = [a.astype(BF16).reshape(rows, n_peers, chans) for a in (product, filters)]
        sent = jnp.concatenate(parts, axis=2).transpose(1, 0, 2)
        received = lax.all_to_all(sent, "seq", split_axis=0, concat_axis=0, tiled=True)
        conv = conv_plain(received, fwd, bwd)
        back = lax.all_to_all(conv, "seq", split_axis=0, concat_axis=0, tiled=True)
        mixed = back.transpose(1, 0, 2).reshape(rows, width).astype(F32) + skip * product
        gated = (queries.astype(F32) * mixed).astype(BF16)
        sent = project(gated, out_weight, sends, [BF16] * pieces)
        ours = project(gated, out_weight, keeps, [F32] * pieces)

    theirs = [lax.ppermute(piece, "fsdp", in_chip) for piece in sent]
    arrived = [lax.ppermute(add(*pair), "fsdp", across) for pair in zip(ours, theirs)]
    blocks = [(True, False, 0, 1), (False, False, 0, 1)]
    sent, own = project(gated, out_weight, blocks, [BF16, F32])
    near = lax.ppermute(sent, "fsdp", in_chip)
    return finish(own, near, arrived)


def solution(mesh):
    in_specs = (
        P("seq", "fsdp"),
        P("seq", "fsdp"),
        P("seq", "fsdp"),
        P("seq", "fsdp"),
        P("fsdp"),
        P("fsdp", None),
    )
    out_specs = P("seq", "fsdp")

    def run(queries, keys, values, filters, skip_weight, out_weight):
        rows = keys.shape[0] // mesh.shape["seq"]
        fn = functools.partial(body, 2, make_tables(rows))
        return jax.shard_map(fn, mesh=mesh, in_specs=in_specs, out_specs=out_specs, check_vma=False)(
            queries, keys, values, filters, skip_weight, out_weight
        )

    return run
```

```python
import functools

import numpy as np

import jax
import jax.numpy as jnp
from jax import lax
from jax.experimental import pallas as pl
from jax.experimental.pallas import tpu as pltpu
from jax.sharding import PartitionSpec as P

BF16 = jnp.bfloat16
F32 = jnp.float32
CONV_VMEM = 24 * 2**20
PROJECT_VMEM = 24 * 2**20
SMALL_VMEM = 12 * 2**20
STEP = 16


def split_bf16(table):
    high = table.astype(BF16)
    return high, (table - high.astype(np.float64)).astype(BF16)


def make_tables(rows):
    order = np.concatenate([np.arange(0, rows, 2), np.arange(1, rows, 2)])
    times = np.arange(rows)
    angle = np.pi * (((2 * order[:, None] + 1) * times[None, :]) % (4 * rows)) / (2 * rows)
    forward = np.concatenate([np.cos(angle), -np.sin(angle)], axis=0)
    high, low = split_bf16(forward)
    back_high, back_low = split_bf16(forward.T / rows)
    return (
        np.concatenate([high, low], axis=1),
        np.concatenate([back_high, back_low, back_high], axis=1),
    )


def peer_of(slot):
    return lax.bitwise_xor(lax.axis_index("seq"), slot)


def peer_block(slot, size):
    return pl.ds(pl.multiple_of(peer_of(slot) * size, size), size)


def pre_kernel(n_peers, keys_hbm, values_hbm, filters_hbm, *refs):
    out_refs = refs[:n_peers]
    keys, values, filters, sem = refs[n_peers:]
    rows, width = keys.shape
    chans = width // n_peers
    steps = sem.shape[0]
    parts = [pl.ds(c * rows // steps, rows // steps) for c in range(steps)]
    pairs = ((keys_hbm, keys), (values_hbm, values), (filters_hbm, filters))
    copies = [
        [
            pltpu.make_async_copy(src.at[part], dst.at[part], sem.at[c, i])
            for i, (src, dst) in enumerate(pairs)
        ]
        for c, part in enumerate(parts)
    ]
    for group in copies:
        for copy in group:
            copy.start()
    for part, group in zip(parts, copies):
        for copy in group:
            copy.wait()
        for slot, out_ref in zip(slots_of(n_peers, False), out_refs):
            at = peer_block(slot, chans)
            product = keys[part, at].astype(F32) * values[part, at].astype(F32)
            out_ref[part, :chans] = product.astype(BF16)
            out_ref[part, chans:] = filters[part, at].astype(BF16)


def pre(keys, values, filters, n_peers):
    rows, width = keys.shape
    chans = width // n_peers
    args = [pltpu.with_memory_space_constraint(a, pltpu.HBM) for a in (keys, values, filters)]
    return pl.pallas_call(
        functools.partial(pre_kernel, n_peers),
        in_specs=[pl.BlockSpec(memory_space=pltpu.HBM)] * 3,
        out_specs=[pl.BlockSpec(memory_space=pltpu.VMEM)] * n_peers,
        out_shape=[jax.ShapeDtypeStruct((rows, 2 * chans), BF16)] * n_peers,
        scratch_shapes=[
            pltpu.VMEM((rows, width), BF16),
            pltpu.VMEM((rows, width), BF16),
            pltpu.VMEM((rows, width), F32),
            pltpu.SemaphoreType.DMA((2, 3)),
        ],
        compiler_params=pltpu.CompilerParams(vmem_limit_bytes=SMALL_VMEM),
        cost_estimate=pl.CostEstimate(
            flops=rows * width, bytes_accessed=12 * rows * width, transcendentals=0
        ),
    )(*args)


def slots_of(n_peers, back):
    half = n_peers // 2
    near, far = list(range(1, half)), list(range(half, n_peers))
    if back:
        return [0, near[0]] + far[2:] + near[1:] + far[:2]
    return [0, far[0], near[0]] + near[:0:-1] + far[1:]


def exchange(blocks, n_peers, back):
    return [
        lax.ppermute(block, "seq", [(i, i ^ slot) for i in range(n_peers)]) if slot else block
        for slot, block in zip(slots_of(n_peers, back), blocks)
    ]


def block_spectrum(table, block):
    return jnp.dot(table, jnp.concatenate([block, block], axis=0), preferred_element_type=F32)


def times(a, b):
    return a[0] * b[0] - a[1] * b[1], a[0] * b[1] + a[1] * b[0]


def plus(a, b):
    return b if a is None else (a[0] + b[0], a[1] + b[1])


def late_place(n_blocks):
    return lax.div(peer_of(slots_of(n_blocks, False)[-1]), 2)


def load(ref, at, row, step, rows, lanes):
    return tuple(ref[(*at, pl.ds(row + part * rows, step), lanes)] for part in range(2))


def mix_early(pair, step, spec_ref, part_ref):
    n_blocks, rows, chans = spec_ref.shape[0], spec_ref.shape[1] // 2, spec_ref.shape[2] // 2
    early = [j for j in range(n_blocks) if j // 2 != pair]

    @pl.loop(0, rows // step)
    def _(t):
        row = pl.multiple_of(t * step, step)
        signal = {j: load(spec_ref, (j,), row, step, rows, slice(0, chans)) for j in early}
        filt = {j: load(spec_ref, (j,), row, step, rows, slice(chans, 2 * chans)) for j in early}
        for i in range(n_blocks):
            total = None
            for d in early:
                if i - d in early:
                    total = plus(total, times(filt[d], signal[i - d]))
            if total is None:
                total = (jnp.zeros((step, chans), F32),) * 2
            for part in range(2):
                part_ref[i, pl.ds(row + part * rows, step)] = total[part]


def tables_kernel(fwd_hbm, bwd_hbm, *refs):
    fwd_ref, bwd_ref, sem = refs[-3:]
    copies = [
        pltpu.make_async_copy(fwd_hbm, fwd_ref, sem.at[0]),
        pltpu.make_async_copy(bwd_hbm, bwd_ref, sem.at[1]),
    ]
    for copy in copies:
        copy.start()
    for copy in copies:
        copy.wait()


def load_tables(fwd, bwd, after):
    whole = pl.BlockSpec(memory_space=pltpu.VMEM)
    args = [pltpu.with_memory_space_constraint(a, pltpu.HBM) for a in (fwd, bwd)]
    return pl.pallas_call(
        tables_kernel,
        in_specs=[pl.BlockSpec(memory_space=pltpu.HBM)] * 2
        + [pl.BlockSpec(memory_space=pl.ANY)] * len(after),
        out_specs=[whole] * 2,
        out_shape=[jax.ShapeDtypeStruct(t.shape, BF16) for t in (fwd, bwd)],
        scratch_shapes=[pltpu.SemaphoreType.DMA((2,))],
        compiler_params=pltpu.CompilerParams(vmem_limit_bytes=SMALL_VMEM),
        cost_estimate=pl.CostEstimate(flops=10**6, bytes_accessed=3 * 2**20, transcendentals=0),
    )(*args, *after)


def spectra_kernel(n_peers, fwd_ref, *refs):
    *in_refs, spec_ref, part_ref = refs
    for slot, in_ref in zip(slots_of(n_peers, False), in_refs):
        spec_ref[peer_of(slot)] = block_spectrum(fwd_ref[...], in_ref[...])
    for pair in range(n_peers // 2):
        pl.when(late_place(n_peers) == pair)(
            functools.partial(mix_early, pair, STEP, spec_ref, part_ref)
        )


def spectra(received, fwd, n_peers):
    rows, width = received[0].shape
    whole = pl.BlockSpec(memory_space=pltpu.VMEM)
    return pl.pallas_call(
        functools.partial(spectra_kernel, n_peers),
        in_specs=[whole] * (1 + len(received)),
        out_specs=[whole] * 2,
        out_shape=[
            jax.ShapeDtypeStruct((n_peers, 2 * rows, width), F32),
            jax.ShapeDtypeStruct((n_peers, 2 * rows, width // 2), F32),
        ],
        compiler_params=pltpu.CompilerParams(vmem_limit_bytes=CONV_VMEM),
        cost_estimate=pl.CostEstimate(
            flops=8 * len(received) * rows * rows * width, bytes_accessed=4 * 2**20, transcendentals=0
        ),
    )(fwd, *received)


def mix_late(pair, step, first, last, sign, spec_ref, part_ref, late_ref, turned):
    n_blocks, rows, chans = spec_ref.shape[0], spec_ref.shape[1] // 2, spec_ref.shape[2] // 2
    early = [j for j in range(n_blocks) if j // 2 != pair]
    x_at, f_at = slice(0, chans), slice(chans, 2 * chans)

    @pl.loop(first // step, last // step)
    def _(t):
        row = pl.multiple_of(t * step, step)
        late = [2 * pair, 2 * pair + 1]
        signal = {j: load(late_ref, (j % 2,), row, step, rows, x_at) for j in late}
        filt = {j: load(late_ref, (j % 2,), row, step, rows, f_at) for j in late}
        total = [load(part_ref, (i,), row, step, rows, slice(0, chans)) for i in range(n_blocks)]
        for b in early:
            if b + late[0] >= n_blocks:
                continue
            x_b = load(spec_ref, (b,), row, step, rows, x_at)
            f_b = load(spec_ref, (b,), row, step, rows, f_at)
            for j in late:
                if b + j < n_blocks:
                    total[b + j] = plus(total[b + j], times(filt[j], x_b))
                    total[b + j] = plus(total[b + j], times(f_b, signal[j]))
        for j in late:
            for d in late:
                if j + d < n_blocks:
                    total[j + d] = plus(total[j + d], times(filt[d], signal[j]))
        for i in range(n_blocks):
            value = total[i]
            if i > 0:
                turn_re, turn_im = total[i - 1]
                if sign > 0:
                    value = value[0] - turn_im, value[1] + turn_re
                else:
                    value = value[0] + turn_im, value[1] - turn_re
            lanes = slice(i % 2 * chans, (i % 2 + 1) * chans)
            for part in range(2):
                high = value[part].astype(BF16)
                low = (value[part] - high.astype(F32)).astype(BF16)
                for c, piece in enumerate((high, high, low)):
                    turned[i // 2, pl.ds(row + (2 * c + part) * rows, step), lanes] = piece


def conv_kernel(fwd_ref, bwd_ref, spec_ref, part_ref, *refs):
    *refs, late_ref, turned = refs
    n_blocks = spec_ref.shape[0]
    in_refs, out_refs = refs[:-n_blocks], refs[-n_blocks:]
    rows, chans = in_refs[0].shape[0], in_refs[0].shape[1] // 2
    for slot, in_ref in zip(slots_of(n_blocks, False)[-2:], in_refs):
        late_ref[lax.bitwise_and(peer_of(slot), 1)] = block_spectrum(fwd_ref[...], in_ref[...])

    def mix(pair):
        for first, last, sign in ((0, rows // 2, 1), (rows // 2, rows, -1)):
            mix_late(pair, STEP, first, last, sign, spec_ref, part_ref, late_ref, turned)

    for pair in range(n_blocks // 2):
        pl.when(late_place(n_blocks) == pair)(functools.partial(mix, pair))

    odd = lax.bitwise_and(lax.axis_index("seq"), 1) == 1
    by_slot = dict(zip(slots_of(n_blocks, True), out_refs))
    for slot in range(0, n_blocks, 2):
        pair = lax.div(peer_of(slot), 2)
        both = jnp.dot(bwd_ref[...], turned[pair], preferred_element_type=F32)
        left, right = both[:, :chans], both[:, chans:]
        by_slot[slot][...] = jnp.where(odd, right, left).astype(BF16)
        by_slot[slot + 1][...] = jnp.where(odd, left, right).astype(BF16)


def conv_fast(early, part, late, fwd, bwd):
    n_blocks = early.shape[0]
    rows, chans = late[0].shape[0], late[0].shape[1] // 2
    whole = pl.BlockSpec(memory_space=pltpu.VMEM)
    return pl.pallas_call(
        conv_kernel,
        in_specs=[whole] * 6,
        out_specs=[whole] * n_blocks,
        out_shape=[jax.ShapeDtypeStruct((rows, chans), BF16)] * n_blocks,
        scratch_shapes=[
            pltpu.VMEM((2, 2 * rows, 2 * chans), F32),
            pltpu.VMEM((n_blocks // 2, 6 * rows, 2 * chans), BF16),
        ],
        compiler_params=pltpu.CompilerParams(vmem_limit_bytes=CONV_VMEM),
        cost_estimate=pl.CostEstimate(
            flops=16 * n_blocks * rows * rows * chans, bytes_accessed=4 * 2**20, transcendentals=0
        ),
    )(fwd, bwd, early, part, *late)


def conv_plain(received, fwd, bwd):
    n_blocks, rows, chans = received.shape[0], received.shape[1], received.shape[2] // 2
    exact = lax.Precision.HIGHEST
    fwd32 = fwd[:, :rows].astype(F32) + fwd[:, rows:].astype(F32)
    bwd32 = bwd[:, : 2 * rows].astype(F32) + bwd[:, 2 * rows : 4 * rows].astype(F32)
    sign = jnp.where(jnp.arange(rows) < rows // 2, 1.0, -1.0).astype(F32)[:, None]

    def spectrum(blocks):
        spec = jnp.einsum("kt,jtc->jkc", fwd32, blocks.astype(F32), precision=exact)
        return spec[:, :rows], spec[:, rows:]

    x_re, x_im = spectrum(received[:, :, :chans])
    f_re, f_im = spectrum(received[:, :, chans:])
    g_re = f_re.at[1:].add(-sign * f_im[:-1])
    g_im = f_im.at[1:].add(sign * f_re[:-1])

    def one(d, total):
        t_re, t_im = total
        later = (jnp.arange(n_blocks) >= d)[:, None, None]
        a_re = jnp.where(later, jnp.roll(x_re, d, axis=0), 0.0)
        a_im = jnp.where(later, jnp.roll(x_im, d, axis=0), 0.0)
        return (
            t_re + g_re[d] * a_re - g_im[d] * a_im,
            t_im + g_re[d] * a_im + g_im[d] * a_re,
        )

    zero = jnp.zeros_like(x_re)
    y_re, y_im = lax.fori_loop(0, n_blocks, one, (zero, zero))
    both = jnp.concatenate([y_re, y_im], axis=1)
    return jnp.einsum("tk,jkc->jtc", bwd32, both, precision=exact).astype(BF16)


def columns_of(other, across, piece, pieces, width):
    count = width // 4 // pieces
    place = lax.axis_index("fsdp")
    core, side = lax.rem(place, 2), lax.div(place, 2)
    block = 2 * (1 - side if across else side) + (1 - core if other else core)
    return pl.ds(pl.multiple_of((block * pieces + piece) * count, count), count)


def gate_slot(slot, queries_ref, keys_ref, values_ref, skip_ref, conv_ref):
    at = peer_block(slot, conv_ref.shape[1])
    product = keys_ref[:, at].astype(F32) * values_ref[:, at].astype(F32)
    mixed = conv_ref[...].astype(F32) + skip_ref[:, at] * product
    return (queries_ref[:, at].astype(F32) * mixed).astype(BF16)


def gate_early_kernel(n_peers, queries_ref, keys_ref, values_ref, skip_ref, weight_ref, *refs):
    conv_refs, (gated_ref, *part_refs) = refs[:-3], refs[-3:]
    chans = conv_refs[0].shape[1]
    slots = slots_of(n_peers, True)
    for slot, conv_ref in zip(slots, conv_refs):
        gated = gate_slot(slot, queries_ref, keys_ref, values_ref, skip_ref, conv_ref)
        gated_ref[:, peer_block(slot, chans)] = gated
    for slot in slots[len(conv_refs) :]:
        gated_ref[:, peer_block(slot, chans)] = jnp.zeros((gated_ref.shape[0], chans), BF16)
    for other, part_ref in zip((True, False), part_refs):
        columns = weight_ref[:, columns_of(other, True, 0, 1, weight_ref.shape[1])]
        part_ref[...] = jnp.dot(gated_ref[...], columns, preferred_element_type=F32)


def gate_early(queries, keys, values, skip, weight, conv, n_peers):
    rows, width = queries.shape
    out_width = weight.shape[1] // 4
    whole = pl.BlockSpec(memory_space=pltpu.VMEM)
    return pl.pallas_call(
        functools.partial(gate_early_kernel, n_peers),
        in_specs=[whole] * (5 + len(conv)),
        out_specs=[whole] * 3,
        out_shape=[jax.ShapeDtypeStruct((rows, width), BF16)]
        + [jax.ShapeDtypeStruct((rows, out_width), F32)] * 2,
        compiler_params=pltpu.CompilerParams(vmem_limit_bytes=PROJECT_VMEM),
        cost_estimate=pl.CostEstimate(
            flops=4 * rows * width * out_width, bytes_accessed=10 * rows * width, transcendentals=0
        ),
    )(queries, keys, values, skip, weight, *conv)


def late_product(late, late_slots, block, weight_ref, part_ref):
    chans = late.shape[1] // len(late_slots)
    at = columns_of(*block, weight_ref.shape[1])
    _, _, piece, pieces = block
    count = part_ref.shape[1] // pieces
    columns = jnp.concatenate([weight_ref[peer_block(s, chans), at] for s in late_slots], axis=0)
    part = part_ref[:, piece * count : (piece + 1) * count]
    return part + jnp.dot(late, columns, preferred_element_type=F32)


def gate_late_kernel(late_slots, block, queries_ref, keys_ref, values_ref, skip_ref, weight_ref, part_ref, *refs):
    *conv_refs, late_ref, sent_ref = refs
    chans = conv_refs[0].shape[1]
    for c, (slot, conv_ref) in enumerate(zip(late_slots, conv_refs)):
        gated = gate_slot(slot, queries_ref, keys_ref, values_ref, skip_ref, conv_ref)
        late_ref[:, c * chans : (c + 1) * chans] = gated
    total = late_product(late_ref[...], late_slots, block, weight_ref, part_ref)
    sent_ref[...] = total.astype(BF16)


def gate_late(queries, keys, values, skip, weight, part, conv, late_slots, block):
    rows, chans = conv[0].shape
    whole = pl.BlockSpec(memory_space=pltpu.VMEM)
    return pl.pallas_call(
        functools.partial(gate_late_kernel, late_slots, block),
        in_specs=[whole] * (6 + len(conv)),
        out_specs=[whole] * 2,
        out_shape=[
            jax.ShapeDtypeStruct((rows, chans * len(conv)), BF16),
            jax.ShapeDtypeStruct((rows, weight.shape[1] // 4 // block[-1]), BF16),
        ],
        compiler_params=pltpu.CompilerParams(vmem_limit_bytes=PROJECT_VMEM),
        cost_estimate=pl.CostEstimate(
            flops=rows * chans * weight.shape[1], bytes_accessed=2**20, transcendentals=0
        ),
    )(queries, keys, values, skip, weight, part, *conv)


def late_project_kernel(late_slots, blocks, weight_ref, late_ref, part_ref, *out_refs):
    for block, out_ref in zip(blocks, out_refs):
        total = late_product(late_ref[...], late_slots, block, weight_ref, part_ref)
        out_ref[...] = total.astype(out_ref.dtype)


def late_project(weight, late, part, late_slots, blocks, dtype):
    rows, depth = late.shape
    widths = [weight.shape[1] // 4 // pieces for *_, pieces in blocks]
    whole = pl.BlockSpec(memory_space=pltpu.VMEM)
    return pl.pallas_call(
        functools.partial(late_project_kernel, late_slots, blocks),
        in_specs=[whole] * 3,
        out_specs=[whole] * len(blocks),
        out_shape=[jax.ShapeDtypeStruct((rows, w), dtype) for w in widths],
        compiler_params=pltpu.CompilerParams(vmem_limit_bytes=PROJECT_VMEM),
        cost_estimate=pl.CostEstimate(
            flops=2 * rows * depth * sum(widths), bytes_accessed=2**20, transcendentals=0
        ),
    )(weight, late, part)


def assemble_kernel(late_slots, gated_ref, late_ref, out_ref):
    chans = late_ref.shape[1] // len(late_slots)
    out_ref[...] = gated_ref[...]
    for c, slot in enumerate(late_slots):
        out_ref[:, peer_block(slot, chans)] = late_ref[:, c * chans : (c + 1) * chans]


def assemble(gated, late, late_slots):
    whole = pl.BlockSpec(memory_space=pltpu.VMEM)
    return pl.pallas_call(
        functools.partial(assemble_kernel, late_slots),
        in_specs=[whole] * 2,
        out_specs=whole,
        out_shape=jax.ShapeDtypeStruct(gated.shape, BF16),
        compiler_params=pltpu.CompilerParams(vmem_limit_bytes=SMALL_VMEM),
        cost_estimate=pl.CostEstimate(flops=1000, bytes_accessed=2**20, transcendentals=0),
    )(gated, late)


def project_kernel(blocks, gated_ref, weight_ref, *out_refs):
    for block, out_ref in zip(blocks, out_refs):
        columns = weight_ref[:, columns_of(*block, weight_ref.shape[1])]
        total = jnp.dot(gated_ref[...], columns, preferred_element_type=F32)
        out_ref[...] = total.astype(out_ref.dtype)


def project(gated, weight, blocks, dtypes):
    rows, depth = gated.shape
    widths = [weight.shape[1] // 4 // pieces for *_, pieces in blocks]
    whole = pl.BlockSpec(memory_space=pltpu.VMEM)
    return pl.pallas_call(
        functools.partial(project_kernel, blocks),
        in_specs=[whole] * 2,
        out_specs=[whole] * len(blocks),
        out_shape=[jax.ShapeDtypeStruct((rows, w), t) for w, t in zip(widths, dtypes)],
        compiler_params=pltpu.CompilerParams(vmem_limit_bytes=PROJECT_VMEM),
        cost_estimate=pl.CostEstimate(
            flops=2 * rows * depth * sum(widths), bytes_accessed=2 * depth * sum(widths), transcendentals=0
        ),
    )(gated, weight)


def add_kernel(own_ref, arrived_ref, out_ref):
    total = own_ref[...] + arrived_ref[...].astype(F32)
    out_ref[...] = total.astype(out_ref.dtype)


def add(own, arrived):
    whole = pl.BlockSpec(memory_space=pltpu.VMEM)
    return pl.pallas_call(
        add_kernel,
        in_specs=[whole] * 2,
        out_specs=whole,
        out_shape=jax.ShapeDtypeStruct(arrived.shape, BF16),
        compiler_params=pltpu.CompilerParams(vmem_limit_bytes=SMALL_VMEM),
        cost_estimate=pl.CostEstimate(
            flops=arrived.size, bytes_accessed=8 * arrived.size, transcendentals=0
        ),
    )(own, arrived)


def mark_kernel(*refs):
    refs[-1][...] = jnp.zeros_like(refs[-1])


def mark(arrays):
    return pl.pallas_call(
        mark_kernel,
        in_specs=[pl.BlockSpec(memory_space=pl.ANY)] * len(arrays),
        out_specs=pl.BlockSpec(memory_space=pltpu.VMEM),
        out_shape=jax.ShapeDtypeStruct((8, 128), F32),
        compiler_params=pltpu.CompilerParams(vmem_limit_bytes=SMALL_VMEM),
        cost_estimate=pl.CostEstimate(flops=2 * 10**10, bytes_accessed=2**20, transcendentals=0),
    )(*arrays)


def finish_kernel(own_ref, near_ref, *refs):
    *arrived_refs, _, out_ref, stage, sem = refs
    width = out_ref.shape[1] // len(arrived_refs)
    steps = sem.shape[0]
    rows = out_ref.shape[0] // steps
    copies = []
    for step in range(steps):
        part = pl.ds(step * rows, rows)
        for c, arrived_ref in enumerate(arrived_refs):
            at = slice(c * width, (c + 1) * width)
            total = own_ref[part, at] + near_ref[part, at].astype(F32)
            stage[part, at] = (total + arrived_ref[part].astype(F32)).astype(stage.dtype)
        copies.append(pltpu.make_async_copy(stage.at[part], out_ref.at[part], sem.at[step]))
        copies[-1].start()
    for copy in copies:
        copy.wait()


def finish(own, near, arrived):
    rows, width = own.shape
    whole, anywhere = pl.BlockSpec(memory_space=pltpu.VMEM), pl.BlockSpec(memory_space=pl.ANY)
    return pl.pallas_call(
        finish_kernel,
        in_specs=[whole] * (2 + len(arrived)) + [anywhere],
        out_specs=anywhere,
        out_shape=jax.ShapeDtypeStruct((rows, width), BF16),
        scratch_shapes=[pltpu.VMEM((rows, width), BF16), pltpu.SemaphoreType.DMA((4,))],
        compiler_params=pltpu.CompilerParams(vmem_limit_bytes=SMALL_VMEM),
        cost_estimate=pl.CostEstimate(
            flops=rows * width, bytes_accessed=8 * rows * width, transcendentals=0
        ),
    )(own, near, *arrived, mark(arrived))


def body(pieces, tables, queries, keys, values, filters, skip_weight, out_weight):
    rows, width = keys.shape
    n_peers = lax.axis_size("seq")
    chans = width // n_peers
    fwd, bwd = (jnp.asarray(t) for t in tables)
    skip = skip_weight[None, :]
    in_chip = [(0, 1), (1, 0), (2, 3), (3, 2)]
    across = [(0, 2), (2, 0), (1, 3), (3, 1)]

    sends = [(True, True, c, pieces) for c in range(pieces)]
    keeps = [(False, True, c, pieces) for c in range(pieces)]

    if chans % 128 == 0 and n_peers == 8:
        blocks = pre(keys, values, filters, n_peers)
        received = exchange(blocks, n_peers, False)
        fwd, bwd = load_tables(fwd, bwd, received[1:2])
        early, part = spectra(received[:-2], fwd, n_peers)
        back = exchange(conv_fast(early, part, received[-2:], fwd, bwd), n_peers, True)
        slots = slots_of(n_peers, True)[-2:]
        gated, send_part, own_part = gate_early(
            queries, keys, values, skip, out_weight, back[:-2], n_peers
        )
        late, last = gate_late(
            queries, keys, values, skip, out_weight, send_part, back[-2:], slots, sends[-1]
        )
        sent = [
            *(late_project(out_weight, late, send_part, slots, [s], BF16)[0] for s in sends[:-1]),
            last,
        ]
        ours = late_project(out_weight, late, own_part, slots, keeps, F32)
        gated = assemble(gated, late, slots)
    else:
        product = keys.astype(F32) * values.astype(F32)
        parts = [a.astype(BF16).reshape(rows, n_peers, chans) for a in (product, filters)]
        sent = jnp.concatenate(parts, axis=2).transpose(1, 0, 2)
        received = lax.all_to_all(sent, "seq", split_axis=0, concat_axis=0, tiled=True)
        conv = conv_plain(received, fwd, bwd)
        back = lax.all_to_all(conv, "seq", split_axis=0, concat_axis=0, tiled=True)
        mixed = back.transpose(1, 0, 2).reshape(rows, width).astype(F32) + skip * product
        gated = (queries.astype(F32) * mixed).astype(BF16)
        sent = project(gated, out_weight, sends, [BF16] * pieces)
        ours = project(gated, out_weight, keeps, [F32] * pieces)

    theirs = [lax.ppermute(piece, "fsdp", in_chip) for piece in sent]
    arrived = [lax.ppermute(add(*pair), "fsdp", across) for pair in zip(ours, theirs)]
    blocks = [(True, False, 0, 1), (False, False, 0, 1)]
    sent, own = project(gated, out_weight, blocks, [BF16, F32])
    near = lax.ppermute(sent, "fsdp", in_chip)
    return finish(own, near, arrived)


def solution(mesh):
    in_specs = (
        P("seq", "fsdp"),
        P("seq", "fsdp"),
        P("seq", "fsdp"),
        P("seq", "fsdp"),
        P("fsdp"),
        P("fsdp", None),
    )
    out_specs = P("seq", "fsdp")

    def run(queries, keys, values, filters, skip_weight, out_weight):
        rows = keys.shape[0] // mesh.shape["seq"]
        fn = functools.partial(body, 2, make_tables(rows))
        return jax.shard_map(fn, mesh=mesh, in_specs=in_specs, out_specs=out_specs, check_vma=False)(
            queries, keys, values, filters, skip_weight, out_weight
        )

    return run
```

```python
import functools

import numpy as np

import jax
import jax.numpy as jnp
from jax import lax
from jax.experimental import pallas as pl
from jax.experimental.pallas import tpu as pltpu
from jax.sharding import PartitionSpec as P

BF16 = jnp.bfloat16
F32 = jnp.float32
CONV_VMEM = 24 * 2**20
PROJECT_VMEM = 24 * 2**20
SMALL_VMEM = 12 * 2**20
STEP = 16


def split_bf16(table):
    high = table.astype(BF16)
    return high, (table - high.astype(np.float64)).astype(BF16)


def make_tables(rows):
    order = np.concatenate([np.arange(0, rows, 2), np.arange(1, rows, 2)])
    times = np.arange(rows)
    angle = np.pi * (((2 * order[:, None] + 1) * times[None, :]) % (4 * rows)) / (2 * rows)
    forward = np.concatenate([np.cos(angle), -np.sin(angle)], axis=0)
    high, low = split_bf16(forward)
    back_high, back_low = split_bf16(forward.T / rows)
    return (
        np.concatenate([high, low], axis=1),
        np.concatenate([back_high, back_low, back_high], axis=1),
    )


def peer_of(slot):
    return lax.bitwise_xor(lax.axis_index("seq"), slot)


def peer_block(slot, size):
    return pl.ds(pl.multiple_of(peer_of(slot) * size, size), size)


def pre_kernel(n_peers, keys_hbm, values_hbm, filters_hbm, *refs):
    out_refs = refs[:n_peers]
    keys, values, filters, sem = refs[n_peers:]
    rows, width = keys.shape
    chans = width // n_peers
    steps = sem.shape[0]
    parts = [pl.ds(c * rows // steps, rows // steps) for c in range(steps)]
    pairs = ((keys_hbm, keys), (values_hbm, values), (filters_hbm, filters))
    copies = [
        [
            pltpu.make_async_copy(src.at[part], dst.at[part], sem.at[c, i])
            for i, (src, dst) in enumerate(pairs)
        ]
        for c, part in enumerate(parts)
    ]
    for group in copies:
        for copy in group:
            copy.start()
    for part, group in zip(parts, copies):
        for copy in group:
            copy.wait()
        for slot, out_ref in zip(slots_of(n_peers, False), out_refs):
            at = peer_block(slot, chans)
            product = keys[part, at].astype(F32) * values[part, at].astype(F32)
            out_ref[part, :chans] = product.astype(BF16)
            out_ref[part, chans:] = filters[part, at].astype(BF16)


def pre(keys, values, filters, n_peers):
    rows, width = keys.shape
    chans = width // n_peers
    args = [pltpu.with_memory_space_constraint(a, pltpu.HBM) for a in (keys, values, filters)]
    return pl.pallas_call(
        functools.partial(pre_kernel, n_peers),
        in_specs=[pl.BlockSpec(memory_space=pltpu.HBM)] * 3,
        out_specs=[pl.BlockSpec(memory_space=pltpu.VMEM)] * n_peers,
        out_shape=[jax.ShapeDtypeStruct((rows, 2 * chans), BF16)] * n_peers,
        scratch_shapes=[
            pltpu.VMEM((rows, width), BF16),
            pltpu.VMEM((rows, width), BF16),
            pltpu.VMEM((rows, width), F32),
            pltpu.SemaphoreType.DMA((2, 3)),
        ],
        compiler_params=pltpu.CompilerParams(vmem_limit_bytes=SMALL_VMEM),
        cost_estimate=pl.CostEstimate(
            flops=rows * width, bytes_accessed=12 * rows * width, transcendentals=0
        ),
    )(*args)


def slots_of(n_peers, back):
    half = n_peers // 2
    near, far = list(range(1, half)), list(range(half, n_peers))
    if back:
        return [0, near[0], far[2], far[0], far[1], near[1], far[3]] + near[2:]
    return [0, far[0], near[0]] + near[:0:-1] + far[1:]


def exchange(blocks, n_peers, back):
    return [
        lax.ppermute(block, "seq", [(i, i ^ slot) for i in range(n_peers)]) if slot else block
        for slot, block in zip(slots_of(n_peers, back), blocks)
    ]


def block_spectrum(table, block):
    return jnp.dot(table, jnp.concatenate([block, block], axis=0), preferred_element_type=F32)


def times(a, b):
    return a[0] * b[0] - a[1] * b[1], a[0] * b[1] + a[1] * b[0]


def plus(a, b):
    return b if a is None else (a[0] + b[0], a[1] + b[1])


def late_place(n_blocks):
    return lax.div(peer_of(slots_of(n_blocks, False)[-1]), 2)


def load(ref, at, row, step, rows, lanes):
    return tuple(ref[(*at, pl.ds(row + part * rows, step), lanes)] for part in range(2))


def mix_early(pair, step, spec_ref, part_ref):
    n_blocks, rows, chans = spec_ref.shape[0], spec_ref.shape[1] // 2, spec_ref.shape[2] // 2
    early = [j for j in range(n_blocks) if j // 2 != pair]

    @pl.loop(0, rows // step)
    def _(t):
        row = pl.multiple_of(t * step, step)
        signal = {j: load(spec_ref, (j,), row, step, rows, slice(0, chans)) for j in early}
        filt = {j: load(spec_ref, (j,), row, step, rows, slice(chans, 2 * chans)) for j in early}
        for i in range(n_blocks):
            total = None
            for d in early:
                if i - d in early:
                    total = plus(total, times(filt[d], signal[i - d]))
            if total is None:
                total = (jnp.zeros((step, chans), F32),) * 2
            for part in range(2):
                part_ref[i, pl.ds(row + part * rows, step)] = total[part]


def tables_kernel(fwd_hbm, bwd_hbm, *refs):
    fwd_ref, bwd_ref, sem = refs[-3:]
    copies = [
        pltpu.make_async_copy(fwd_hbm, fwd_ref, sem.at[0]),
        pltpu.make_async_copy(bwd_hbm, bwd_ref, sem.at[1]),
    ]
    for copy in copies:
        copy.start()
    for copy in copies:
        copy.wait()


def load_tables(fwd, bwd, after):
    whole = pl.BlockSpec(memory_space=pltpu.VMEM)
    args = [pltpu.with_memory_space_constraint(a, pltpu.HBM) for a in (fwd, bwd)]
    return pl.pallas_call(
        tables_kernel,
        in_specs=[pl.BlockSpec(memory_space=pltpu.HBM)] * 2
        + [pl.BlockSpec(memory_space=pl.ANY)] * len(after),
        out_specs=[whole] * 2,
        out_shape=[jax.ShapeDtypeStruct(t.shape, BF16) for t in (fwd, bwd)],
        scratch_shapes=[pltpu.SemaphoreType.DMA((2,))],
        compiler_params=pltpu.CompilerParams(vmem_limit_bytes=SMALL_VMEM),
        cost_estimate=pl.CostEstimate(flops=10**6, bytes_accessed=3 * 2**20, transcendentals=0),
    )(*args, *after)


def spectra_kernel(n_peers, fwd_ref, *refs):
    *in_refs, spec_ref, part_ref = refs
    for slot, in_ref in zip(slots_of(n_peers, False), in_refs):
        spec_ref[peer_of(slot)] = block_spectrum(fwd_ref[...], in_ref[...])
    for pair in range(n_peers // 2):
        pl.when(late_place(n_peers) == pair)(
            functools.partial(mix_early, pair, STEP, spec_ref, part_ref)
        )


def spectra(received, fwd, n_peers):
    rows, width = received[0].shape
    whole = pl.BlockSpec(memory_space=pltpu.VMEM)
    return pl.pallas_call(
        functools.partial(spectra_kernel, n_peers),
        in_specs=[whole] * (1 + len(received)),
        out_specs=[whole] * 2,
        out_shape=[
            jax.ShapeDtypeStruct((n_peers, 2 * rows, width), F32),
            jax.ShapeDtypeStruct((n_peers, 2 * rows, width // 2), F32),
        ],
        compiler_params=pltpu.CompilerParams(vmem_limit_bytes=CONV_VMEM),
        cost_estimate=pl.CostEstimate(
            flops=8 * len(received) * rows * rows * width, bytes_accessed=4 * 2**20, transcendentals=0
        ),
    )(fwd, *received)


def mix_late(pair, step, first, last, sign, spec_ref, part_ref, late_ref, turned):
    n_blocks, rows, chans = spec_ref.shape[0], spec_ref.shape[1] // 2, spec_ref.shape[2] // 2
    early = [j for j in range(n_blocks) if j // 2 != pair]
    x_at, f_at = slice(0, chans), slice(chans, 2 * chans)

    @pl.loop(first // step, last // step)
    def _(t):
        row = pl.multiple_of(t * step, step)
        late = [2 * pair, 2 * pair + 1]
        signal = {j: load(late_ref, (j % 2,), row, step, rows, x_at) for j in late}
        filt = {j: load(late_ref, (j % 2,), row, step, rows, f_at) for j in late}
        total = [load(part_ref, (i,), row, step, rows, slice(0, chans)) for i in range(n_blocks)]
        for b in early:
            if b + late[0] >= n_blocks:
                continue
            x_b = load(spec_ref, (b,), row, step, rows, x_at)
            f_b = load(spec_ref, (b,), row, step, rows, f_at)
            for j in late:
                if b + j < n_blocks:
                    total[b + j] = plus(total[b + j], times(filt[j], x_b))
                    total[b + j] = plus(total[b + j], times(f_b, signal[j]))
        for j in late:
            for d in late:
                if j + d < n_blocks:
                    total[j + d] = plus(total[j + d], times(filt[d], signal[j]))
        for i in range(n_blocks):
            value = total[i]
            if i > 0:
                turn_re, turn_im = total[i - 1]
                if sign > 0:
                    value = value[0] - turn_im, value[1] + turn_re
                else:
                    value = value[0] + turn_im, value[1] - turn_re
            lanes = slice(i % 2 * chans, (i % 2 + 1) * chans)
            for part in range(2):
                high = value[part].astype(BF16)
                low = (value[part] - high.astype(F32)).astype(BF16)
                for c, piece in enumerate((high, high, low)):
                    turned[i // 2, pl.ds(row + (2 * c + part) * rows, step), lanes] = piece


def conv_kernel(fwd_ref, bwd_ref, spec_ref, part_ref, *refs):
    *refs, late_ref, turned = refs
    n_blocks = spec_ref.shape[0]
    in_refs, out_refs = refs[:-n_blocks], refs[-n_blocks:]
    rows, chans = in_refs[0].shape[0], in_refs[0].shape[1] // 2
    for slot, in_ref in zip(slots_of(n_blocks, False)[-2:], in_refs):
        late_ref[lax.bitwise_and(peer_of(slot), 1)] = block_spectrum(fwd_ref[...], in_ref[...])

    def mix(pair):
        for first, last, sign in ((0, rows // 2, 1), (rows // 2, rows, -1)):
            mix_late(pair, STEP, first, last, sign, spec_ref, part_ref, late_ref, turned)

    for pair in range(n_blocks // 2):
        pl.when(late_place(n_blocks) == pair)(functools.partial(mix, pair))

    odd = lax.bitwise_and(lax.axis_index("seq"), 1) == 1
    by_slot = dict(zip(slots_of(n_blocks, True), out_refs))
    for slot in range(0, n_blocks, 2):
        pair = lax.div(peer_of(slot), 2)
        both = jnp.dot(bwd_ref[...], turned[pair], preferred_element_type=F32)
        left, right = both[:, :chans], both[:, chans:]
        by_slot[slot][...] = jnp.where(odd, right, left).astype(BF16)
        by_slot[slot + 1][...] = jnp.where(odd, left, right).astype(BF16)


def conv_fast(early, part, late, fwd, bwd):
    n_blocks = early.shape[0]
    rows, chans = late[0].shape[0], late[0].shape[1] // 2
    whole = pl.BlockSpec(memory_space=pltpu.VMEM)
    return pl.pallas_call(
        conv_kernel,
        in_specs=[whole] * 6,
        out_specs=[whole] * n_blocks,
        out_shape=[jax.ShapeDtypeStruct((rows, chans), BF16)] * n_blocks,
        scratch_shapes=[
            pltpu.VMEM((2, 2 * rows, 2 * chans), F32),
            pltpu.VMEM((n_blocks // 2, 6 * rows, 2 * chans), BF16),
        ],
        compiler_params=pltpu.CompilerParams(vmem_limit_bytes=CONV_VMEM),
        cost_estimate=pl.CostEstimate(
            flops=16 * n_blocks * rows * rows * chans, bytes_accessed=4 * 2**20, transcendentals=0
        ),
    )(fwd, bwd, early, part, *late)


def conv_plain(received, fwd, bwd):
    n_blocks, rows, chans = received.shape[0], received.shape[1], received.shape[2] // 2
    exact = lax.Precision.HIGHEST
    fwd32 = fwd[:, :rows].astype(F32) + fwd[:, rows:].astype(F32)
    bwd32 = bwd[:, : 2 * rows].astype(F32) + bwd[:, 2 * rows : 4 * rows].astype(F32)
    sign = jnp.where(jnp.arange(rows) < rows // 2, 1.0, -1.0).astype(F32)[:, None]

    def spectrum(blocks):
        spec = jnp.einsum("kt,jtc->jkc", fwd32, blocks.astype(F32), precision=exact)
        return spec[:, :rows], spec[:, rows:]

    x_re, x_im = spectrum(received[:, :, :chans])
    f_re, f_im = spectrum(received[:, :, chans:])
    g_re = f_re.at[1:].add(-sign * f_im[:-1])
    g_im = f_im.at[1:].add(sign * f_re[:-1])

    def one(d, total):
        t_re, t_im = total
        later = (jnp.arange(n_blocks) >= d)[:, None, None]
        a_re = jnp.where(later, jnp.roll(x_re, d, axis=0), 0.0)
        a_im = jnp.where(later, jnp.roll(x_im, d, axis=0), 0.0)
        return (
            t_re + g_re[d] * a_re - g_im[d] * a_im,
            t_im + g_re[d] * a_im + g_im[d] * a_re,
        )

    zero = jnp.zeros_like(x_re)
    y_re, y_im = lax.fori_loop(0, n_blocks, one, (zero, zero))
    both = jnp.concatenate([y_re, y_im], axis=1)
    return jnp.einsum("tk,jkc->jtc", bwd32, both, precision=exact).astype(BF16)


def columns_of(other, across, piece, pieces, width):
    count = width // 4 // pieces
    place = lax.axis_index("fsdp")
    core, side = lax.rem(place, 2), lax.div(place, 2)
    block = 2 * (1 - side if across else side) + (1 - core if other else core)
    return pl.ds(pl.multiple_of((block * pieces + piece) * count, count), count)


def gate_slot(slot, queries_ref, keys_ref, values_ref, skip_ref, conv_ref):
    at = peer_block(slot, conv_ref.shape[1])
    product = keys_ref[:, at].astype(F32) * values_ref[:, at].astype(F32)
    mixed = conv_ref[...].astype(F32) + skip_ref[:, at] * product
    return (queries_ref[:, at].astype(F32) * mixed).astype(BF16)


def gate_early_kernel(n_peers, queries_ref, keys_ref, values_ref, skip_ref, weight_ref, *refs):
    conv_refs, (gated_ref, *part_refs) = refs[:-3], refs[-3:]
    chans = conv_refs[0].shape[1]
    slots = slots_of(n_peers, True)
    for slot, conv_ref in zip(slots, conv_refs):
        gated = gate_slot(slot, queries_ref, keys_ref, values_ref, skip_ref, conv_ref)
        gated_ref[:, peer_block(slot, chans)] = gated
    for slot in slots[len(conv_refs) :]:
        gated_ref[:, peer_block(slot, chans)] = jnp.zeros((gated_ref.shape[0], chans), BF16)
    for other, part_ref in zip((True, False), part_refs):
        columns = weight_ref[:, columns_of(other, True, 0, 1, weight_ref.shape[1])]
        part_ref[...] = jnp.dot(gated_ref[...], columns, preferred_element_type=F32)


def gate_early(queries, keys, values, skip, weight, conv, n_peers):
    rows, width = queries.shape
    out_width = weight.shape[1] // 4
    whole = pl.BlockSpec(memory_space=pltpu.VMEM)
    return pl.pallas_call(
        functools.partial(gate_early_kernel, n_peers),
        in_specs=[whole] * (5 + len(conv)),
        out_specs=[whole] * 3,
        out_shape=[jax.ShapeDtypeStruct((rows, width), BF16)]
        + [jax.ShapeDtypeStruct((rows, out_width), F32)] * 2,
        compiler_params=pltpu.CompilerParams(vmem_limit_bytes=PROJECT_VMEM),
        cost_estimate=pl.CostEstimate(
            flops=4 * rows * width * out_width, bytes_accessed=10 * rows * width, transcendentals=0
        ),
    )(queries, keys, values, skip, weight, *conv)


def late_product(late, late_slots, block, weight_ref, part_ref):
    chans = late.shape[1] // len(late_slots)
    at = columns_of(*block, weight_ref.shape[1])
    _, _, piece, pieces = block
    count = part_ref.shape[1] // pieces
    columns = jnp.concatenate([weight_ref[peer_block(s, chans), at] for s in late_slots], axis=0)
    part = part_ref[:, piece * count : (piece + 1) * count]
    return part + jnp.dot(late, columns, preferred_element_type=F32)


def gate_late_kernel(late_slots, block, queries_ref, keys_ref, values_ref, skip_ref, weight_ref, part_ref, *refs):
    *conv_refs, late_ref, sent_ref = refs
    chans = conv_refs[0].shape[1]
    for c, (slot, conv_ref) in enumerate(zip(late_slots, conv_refs)):
        gated = gate_slot(slot, queries_ref, keys_ref, values_ref, skip_ref, conv_ref)
        late_ref[:, c * chans : (c + 1) * chans] = gated
    total = late_product(late_ref[...], late_slots, block, weight_ref, part_ref)
    sent_ref[...] = total.astype(BF16)


def gate_late(queries, keys, values, skip, weight, part, conv, late_slots, block):
    rows, chans = conv[0].shape
    whole = pl.BlockSpec(memory_space=pltpu.VMEM)
    return pl.pallas_call(
        functools.partial(gate_late_kernel, late_slots, block),
        in_specs=[whole] * (6 + len(conv)),
        out_specs=[whole] * 2,
        out_shape=[
            jax.ShapeDtypeStruct((rows, chans * len(conv)), BF16),
            jax.ShapeDtypeStruct((rows, weight.shape[1] // 4 // block[-1]), BF16),
        ],
        compiler_params=pltpu.CompilerParams(vmem_limit_bytes=PROJECT_VMEM),
        cost_estimate=pl.CostEstimate(
            flops=rows * chans * weight.shape[1], bytes_accessed=2**20, transcendentals=0
        ),
    )(queries, keys, values, skip, weight, part, *conv)


def late_project_kernel(late_slots, blocks, weight_ref, late_ref, part_ref, *out_refs):
    for block, out_ref in zip(blocks, out_refs):
        total = late_product(late_ref[...], late_slots, block, weight_ref, part_ref)
        out_ref[...] = total.astype(out_ref.dtype)


def late_project(weight, late, part, late_slots, blocks, dtype):
    rows, depth = late.shape
    widths = [weight.shape[1] // 4 // pieces for *_, pieces in blocks]
    whole = pl.BlockSpec(memory_space=pltpu.VMEM)
    return pl.pallas_call(
        functools.partial(late_project_kernel, late_slots, blocks),
        in_specs=[whole] * 3,
        out_specs=[whole] * len(blocks),
        out_shape=[jax.ShapeDtypeStruct((rows, w), dtype) for w in widths],
        compiler_params=pltpu.CompilerParams(vmem_limit_bytes=PROJECT_VMEM),
        cost_estimate=pl.CostEstimate(
            flops=2 * rows * depth * sum(widths), bytes_accessed=2**20, transcendentals=0
        ),
    )(weight, late, part)


def assemble_kernel(late_slots, gated_ref, late_ref, out_ref):
    chans = late_ref.shape[1] // len(late_slots)
    out_ref[...] = gated_ref[...]
    for c, slot in enumerate(late_slots):
        out_ref[:, peer_block(slot, chans)] = late_ref[:, c * chans : (c + 1) * chans]


def assemble(gated, late, late_slots):
    whole = pl.BlockSpec(memory_space=pltpu.VMEM)
    return pl.pallas_call(
        functools.partial(assemble_kernel, late_slots),
        in_specs=[whole] * 2,
        out_specs=whole,
        out_shape=jax.ShapeDtypeStruct(gated.shape, BF16),
        compiler_params=pltpu.CompilerParams(vmem_limit_bytes=SMALL_VMEM),
        cost_estimate=pl.CostEstimate(flops=1000, bytes_accessed=2**20, transcendentals=0),
    )(gated, late)


def project_kernel(blocks, gated_ref, weight_ref, *out_refs):
    for block, out_ref in zip(blocks, out_refs):
        columns = weight_ref[:, columns_of(*block, weight_ref.shape[1])]
        total = jnp.dot(gated_ref[...], columns, preferred_element_type=F32)
        out_ref[...] = total.astype(out_ref.dtype)


def project(gated, weight, blocks, dtypes):
    rows, depth = gated.shape
    widths = [weight.shape[1] // 4 // pieces for *_, pieces in blocks]
    whole = pl.BlockSpec(memory_space=pltpu.VMEM)
    return pl.pallas_call(
        functools.partial(project_kernel, blocks),
        in_specs=[whole] * 2,
        out_specs=[whole] * len(blocks),
        out_shape=[jax.ShapeDtypeStruct((rows, w), t) for w, t in zip(widths, dtypes)],
        compiler_params=pltpu.CompilerParams(vmem_limit_bytes=PROJECT_VMEM),
        cost_estimate=pl.CostEstimate(
            flops=2 * rows * depth * sum(widths), bytes_accessed=2 * depth * sum(widths), transcendentals=0
        ),
    )(gated, weight)


def add_kernel(own_ref, arrived_ref, out_ref):
    total = own_ref[...] + arrived_ref[...].astype(F32)
    out_ref[...] = total.astype(out_ref.dtype)


def add(own, arrived):
    whole = pl.BlockSpec(memory_space=pltpu.VMEM)
    return pl.pallas_call(
        add_kernel,
        in_specs=[whole] * 2,
        out_specs=whole,
        out_shape=jax.ShapeDtypeStruct(arrived.shape, BF16),
        compiler_params=pltpu.CompilerParams(vmem_limit_bytes=SMALL_VMEM),
        cost_estimate=pl.CostEstimate(
            flops=arrived.size, bytes_accessed=8 * arrived.size, transcendentals=0
        ),
    )(own, arrived)


def mark_kernel(*refs):
    refs[-1][...] = jnp.zeros_like(refs[-1])


def mark(arrays):
    return pl.pallas_call(
        mark_kernel,
        in_specs=[pl.BlockSpec(memory_space=pl.ANY)] * len(arrays),
        out_specs=pl.BlockSpec(memory_space=pltpu.VMEM),
        out_shape=jax.ShapeDtypeStruct((8, 128), F32),
        compiler_params=pltpu.CompilerParams(vmem_limit_bytes=SMALL_VMEM),
        cost_estimate=pl.CostEstimate(flops=2 * 10**10, bytes_accessed=2**20, transcendentals=0),
    )(*arrays)


def finish_kernel(own_ref, near_ref, *refs):
    *arrived_refs, _, out_ref, stage, sem = refs
    width = out_ref.shape[1] // len(arrived_refs)
    steps = sem.shape[0]
    rows = out_ref.shape[0] // steps
    copies = []
    for step in range(steps):
        part = pl.ds(step * rows, rows)
        for c, arrived_ref in enumerate(arrived_refs):
            at = slice(c * width, (c + 1) * width)
            total = own_ref[part, at] + near_ref[part, at].astype(F32)
            stage[part, at] = (total + arrived_ref[part].astype(F32)).astype(stage.dtype)
        copies.append(pltpu.make_async_copy(stage.at[part], out_ref.at[part], sem.at[step]))
        copies[-1].start()
    for copy in copies:
        copy.wait()


def finish(own, near, arrived):
    rows, width = own.shape
    whole, anywhere = pl.BlockSpec(memory_space=pltpu.VMEM), pl.BlockSpec(memory_space=pl.ANY)
    return pl.pallas_call(
        finish_kernel,
        in_specs=[whole] * (2 + len(arrived)) + [anywhere],
        out_specs=anywhere,
        out_shape=jax.ShapeDtypeStruct((rows, width), BF16),
        scratch_shapes=[pltpu.VMEM((rows, width), BF16), pltpu.SemaphoreType.DMA((4,))],
        compiler_params=pltpu.CompilerParams(vmem_limit_bytes=SMALL_VMEM),
        cost_estimate=pl.CostEstimate(
            flops=rows * width, bytes_accessed=8 * rows * width, transcendentals=0
        ),
    )(own, near, *arrived, mark(arrived))


def body(pieces, tables, queries, keys, values, filters, skip_weight, out_weight):
    rows, width = keys.shape
    n_peers = lax.axis_size("seq")
    chans = width // n_peers
    fwd, bwd = (jnp.asarray(t) for t in tables)
    skip = skip_weight[None, :]
    in_chip = [(0, 1), (1, 0), (2, 3), (3, 2)]
    across = [(0, 2), (2, 0), (1, 3), (3, 1)]

    sends = [(True, True, c, pieces) for c in range(pieces)]
    keeps = [(False, True, c, pieces) for c in range(pieces)]

    if chans % 128 == 0 and n_peers == 8:
        blocks = pre(keys, values, filters, n_peers)
        received = exchange(blocks, n_peers, False)
        fwd, bwd = load_tables(fwd, bwd, received[1:2])
        early, part = spectra(received[:-2], fwd, n_peers)
        back = exchange(conv_fast(early, part, received[-2:], fwd, bwd), n_peers, True)
        slots = slots_of(n_peers, True)[-2:]
        gated, send_part, own_part = gate_early(
            queries, keys, values, skip, out_weight, back[:-2], n_peers
        )
        late, last = gate_late(
            queries, keys, values, skip, out_weight, send_part, back[-2:], slots, sends[-1]
        )
        sent = [
            *(late_project(out_weight, late, send_part, slots, [s], BF16)[0] for s in sends[:-1]),
            last,
        ]
        ours = late_project(out_weight, late, own_part, slots, keeps, F32)
        gated = assemble(gated, late, slots)
    else:
        product = keys.astype(F32) * values.astype(F32)
        parts = [a.astype(BF16).reshape(rows, n_peers, chans) for a in (product, filters)]
        sent = jnp.concatenate(parts, axis=2).transpose(1, 0, 2)
        received = lax.all_to_all(sent, "seq", split_axis=0, concat_axis=0, tiled=True)
        conv = conv_plain(received, fwd, bwd)
        back = lax.all_to_all(conv, "seq", split_axis=0, concat_axis=0, tiled=True)
        mixed = back.transpose(1, 0, 2).reshape(rows, width).astype(F32) + skip * product
        gated = (queries.astype(F32) * mixed).astype(BF16)
        sent = project(gated, out_weight, sends, [BF16] * pieces)
        ours = project(gated, out_weight, keeps, [F32] * pieces)

    theirs = [lax.ppermute(piece, "fsdp", in_chip) for piece in sent]
    arrived = [lax.ppermute(add(*pair), "fsdp", across) for pair in zip(ours, theirs)]
    blocks = [(True, False, 0, 1), (False, False, 0, 1)]
    sent, own = project(gated, out_weight, blocks, [BF16, F32])
    near = lax.ppermute(sent, "fsdp", in_chip)
    return finish(own, near, arrived)


def solution(mesh):
    in_specs = (
        P("seq", "fsdp"),
        P("seq", "fsdp"),
        P("seq", "fsdp"),
        P("seq", "fsdp"),
        P("fsdp"),
        P("fsdp", None),
    )
    out_specs = P("seq", "fsdp")

    def run(queries, keys, values, filters, skip_weight, out_weight):
        rows = keys.shape[0] // mesh.shape["seq"]
        fn = functools.partial(body, 2, make_tables(rows))
        return jax.shard_map(fn, mesh=mesh, in_specs=in_specs, out_specs=out_specs, check_vma=False)(
            queries, keys, values, filters, skip_weight, out_weight
        )

    return run
```

```python
import functools

import numpy as np

import jax
import jax.numpy as jnp
from jax import lax
from jax.experimental import pallas as pl
from jax.experimental.pallas import tpu as pltpu
from jax.sharding import PartitionSpec as P

BF16 = jnp.bfloat16
F32 = jnp.float32
CONV_VMEM = 24 * 2**20
PROJECT_VMEM = 24 * 2**20
SMALL_VMEM = 12 * 2**20
STEP = 16


def split_bf16(table):
    high = table.astype(BF16)
    return high, (table - high.astype(np.float64)).astype(BF16)


def make_tables(rows):
    order = np.concatenate([np.arange(0, rows, 2), np.arange(1, rows, 2)])
    times = np.arange(rows)
    angle = np.pi * (((2 * order[:, None] + 1) * times[None, :]) % (4 * rows)) / (2 * rows)
    forward = np.concatenate([np.cos(angle), -np.sin(angle)], axis=0)
    high, low = split_bf16(forward)
    back_high, back_low = split_bf16(forward.T / rows)
    return (
        np.concatenate([high, low], axis=1),
        np.concatenate([back_high, back_low, back_high], axis=1),
    )


def peer_of(slot):
    return lax.bitwise_xor(lax.axis_index("seq"), slot)


def peer_block(slot, size):
    return pl.ds(pl.multiple_of(peer_of(slot) * size, size), size)


def pre_kernel(n_peers, keys_hbm, values_hbm, filters_hbm, *refs):
    out_refs = refs[:n_peers]
    keys, values, filters, sem = refs[n_peers:]
    rows, width = keys.shape
    chans = width // n_peers
    steps = sem.shape[0]
    parts = [pl.ds(c * rows // steps, rows // steps) for c in range(steps)]
    pairs = ((keys_hbm, keys), (values_hbm, values), (filters_hbm, filters))
    copies = [
        [
            pltpu.make_async_copy(src.at[part], dst.at[part], sem.at[c, i])
            for i, (src, dst) in enumerate(pairs)
        ]
        for c, part in enumerate(parts)
    ]
    for group in copies:
        for copy in group:
            copy.start()
    for part, group in zip(parts, copies):
        for copy in group:
            copy.wait()
        for slot, out_ref in zip(slots_of(n_peers, False), out_refs):
            at = peer_block(slot, chans)
            product = keys[part, at].astype(F32) * values[part, at].astype(F32)
            out_ref[part, :chans] = product.astype(BF16)
            out_ref[part, chans:] = filters[part, at].astype(BF16)


def pre(keys, values, filters, n_peers):
    rows, width = keys.shape
    chans = width // n_peers
    args = [pltpu.with_memory_space_constraint(a, pltpu.HBM) for a in (keys, values, filters)]
    return pl.pallas_call(
        functools.partial(pre_kernel, n_peers),
        in_specs=[pl.BlockSpec(memory_space=pltpu.HBM)] * 3,
        out_specs=[pl.BlockSpec(memory_space=pltpu.VMEM)] * n_peers,
        out_shape=[jax.ShapeDtypeStruct((rows, 2 * chans), BF16)] * n_peers,
        scratch_shapes=[
            pltpu.VMEM((rows, width), BF16),
            pltpu.VMEM((rows, width), BF16),
            pltpu.VMEM((rows, width), F32),
            pltpu.SemaphoreType.DMA((2, 3)),
        ],
        compiler_params=pltpu.CompilerParams(vmem_limit_bytes=SMALL_VMEM),
        cost_estimate=pl.CostEstimate(
            flops=rows * width, bytes_accessed=12 * rows * width, transcendentals=0
        ),
    )(*args)


def slots_of(n_peers, back):
    half = n_peers // 2
    near, far = list(range(1, half)), list(range(half, n_peers))
    if back:
        return [0, near[0], far[2], far[0], near[1], far[1], far[3]] + near[2:]
    return [0, far[0], near[0]] + near[:0:-1] + far[1:]


def exchange(blocks, n_peers, back):
    return [
        lax.ppermute(block, "seq", [(i, i ^ slot) for i in range(n_peers)]) if slot else block
        for slot, block in zip(slots_of(n_peers, back), blocks)
    ]


def block_spectrum(table, block):
    return jnp.dot(table, jnp.concatenate([block, block], axis=0), preferred_element_type=F32)


def times(a, b):
    return a[0] * b[0] - a[1] * b[1], a[0] * b[1] + a[1] * b[0]


def plus(a, b):
    return b if a is None else (a[0] + b[0], a[1] + b[1])


def late_place(n_blocks):
    return lax.div(peer_of(slots_of(n_blocks, False)[-1]), 2)


def load(ref, at, row, step, rows, lanes):
    return tuple(ref[(*at, pl.ds(row + part * rows, step), lanes)] for part in range(2))


def mix_early(pair, step, spec_ref, part_ref):
    n_blocks, rows, chans = spec_ref.shape[0], spec_ref.shape[1] // 2, spec_ref.shape[2] // 2
    early = [j for j in range(n_blocks) if j // 2 != pair]

    @pl.loop(0, rows // step)
    def _(t):
        row = pl.multiple_of(t * step, step)
        signal = {j: load(spec_ref, (j,), row, step, rows, slice(0, chans)) for j in early}
        filt = {j: load(spec_ref, (j,), row, step, rows, slice(chans, 2 * chans)) for j in early}
        for i in range(n_blocks):
            total = None
            for d in early:
                if i - d in early:
                    total = plus(total, times(filt[d], signal[i - d]))
            if total is None:
                total = (jnp.zeros((step, chans), F32),) * 2
            for part in range(2):
                part_ref[i, pl.ds(row + part * rows, step)] = total[part]


def tables_kernel(fwd_hbm, bwd_hbm, *refs):
    fwd_ref, bwd_ref, sem = refs[-3:]
    copies = [
        pltpu.make_async_copy(fwd_hbm, fwd_ref, sem.at[0]),
        pltpu.make_async_copy(bwd_hbm, bwd_ref, sem.at[1]),
    ]
    for copy in copies:
        copy.start()
    for copy in copies:
        copy.wait()


def load_tables(fwd, bwd, after):
    whole = pl.BlockSpec(memory_space=pltpu.VMEM)
    args = [pltpu.with_memory_space_constraint(a, pltpu.HBM) for a in (fwd, bwd)]
    return pl.pallas_call(
        tables_kernel,
        in_specs=[pl.BlockSpec(memory_space=pltpu.HBM)] * 2
        + [pl.BlockSpec(memory_space=pl.ANY)] * len(after),
        out_specs=[whole] * 2,
        out_shape=[jax.ShapeDtypeStruct(t.shape, BF16) for t in (fwd, bwd)],
        scratch_shapes=[pltpu.SemaphoreType.DMA((2,))],
        compiler_params=pltpu.CompilerParams(vmem_limit_bytes=SMALL_VMEM),
        cost_estimate=pl.CostEstimate(flops=10**6, bytes_accessed=3 * 2**20, transcendentals=0),
    )(*args, *after)


def spectra_kernel(n_peers, fwd_ref, *refs):
    *in_refs, spec_ref, part_ref = refs
    for slot, in_ref in zip(slots_of(n_peers, False), in_refs):
        spec_ref[peer_of(slot)] = block_spectrum(fwd_ref[...], in_ref[...])
    for pair in range(n_peers // 2):
        pl.when(late_place(n_peers) == pair)(
            functools.partial(mix_early, pair, STEP, spec_ref, part_ref)
        )


def spectra(received, fwd, n_peers):
    rows, width = received[0].shape
    whole = pl.BlockSpec(memory_space=pltpu.VMEM)
    return pl.pallas_call(
        functools.partial(spectra_kernel, n_peers),
        in_specs=[whole] * (1 + len(received)),
        out_specs=[whole] * 2,
        out_shape=[
            jax.ShapeDtypeStruct((n_peers, 2 * rows, width), F32),
            jax.ShapeDtypeStruct((n_peers, 2 * rows, width // 2), F32),
        ],
        compiler_params=pltpu.CompilerParams(vmem_limit_bytes=CONV_VMEM),
        cost_estimate=pl.CostEstimate(
            flops=8 * len(received) * rows * rows * width, bytes_accessed=4 * 2**20, transcendentals=0
        ),
    )(fwd, *received)


def mix_late(pair, step, first, last, sign, spec_ref, part_ref, late_ref, turned):
    n_blocks, rows, chans = spec_ref.shape[0], spec_ref.shape[1] // 2, spec_ref.shape[2] // 2
    early = [j for j in range(n_blocks) if j // 2 != pair]
    x_at, f_at = slice(0, chans), slice(chans, 2 * chans)

    @pl.loop(first // step, last // step)
    def _(t):
        row = pl.multiple_of(t * step, step)
        late = [2 * pair, 2 * pair + 1]
        signal = {j: load(late_ref, (j % 2,), row, step, rows, x_at) for j in late}
        filt = {j: load(late_ref, (j % 2,), row, step, rows, f_at) for j in late}
        total = [load(part_ref, (i,), row, step, rows, slice(0, chans)) for i in range(n_blocks)]
        for b in early:
            if b + late[0] >= n_blocks:
                continue
            x_b = load(spec_ref, (b,), row, step, rows, x_at)
            f_b = load(spec_ref, (b,), row, step, rows, f_at)
            for j in late:
                if b + j < n_blocks:
                    total[b + j] = plus(total[b + j], times(filt[j], x_b))
                    total[b + j] = plus(total[b + j], times(f_b, signal[j]))
        for j in late:
            for d in late:
                if j + d < n_blocks:
                    total[j + d] = plus(total[j + d], times(filt[d], signal[j]))
        for i in range(n_blocks):
            value = total[i]
            if i > 0:
                turn_re, turn_im = total[i - 1]
                if sign > 0:
                    value = value[0] - turn_im, value[1] + turn_re
                else:
                    value = value[0] + turn_im, value[1] - turn_re
            lanes = slice(i % 2 * chans, (i % 2 + 1) * chans)
            for part in range(2):
                high = value[part].astype(BF16)
                low = (value[part] - high.astype(F32)).astype(BF16)
                for c, piece in enumerate((high, high, low)):
                    turned[i // 2, pl.ds(row + (2 * c + part) * rows, step), lanes] = piece


def conv_kernel(fwd_ref, bwd_ref, spec_ref, part_ref, *refs):
    *refs, late_ref, turned = refs
    n_blocks = spec_ref.shape[0]
    in_refs, out_refs = refs[:-n_blocks], refs[-n_blocks:]
    rows, chans = in_refs[0].shape[0], in_refs[0].shape[1] // 2
    for slot, in_ref in zip(slots_of(n_blocks, False)[-2:], in_refs):
        late_ref[lax.bitwise_and(peer_of(slot), 1)] = block_spectrum(fwd_ref[...], in_ref[...])

    def mix(pair):
        for first, last, sign in ((0, rows // 2, 1), (rows // 2, rows, -1)):
            mix_late(pair, STEP, first, last, sign, spec_ref, part_ref, late_ref, turned)

    for pair in range(n_blocks // 2):
        pl.when(late_place(n_blocks) == pair)(functools.partial(mix, pair))

    odd = lax.bitwise_and(lax.axis_index("seq"), 1) == 1
    by_slot = dict(zip(slots_of(n_blocks, True), out_refs))
    for slot in range(0, n_blocks, 2):
        pair = lax.div(peer_of(slot), 2)
        both = jnp.dot(bwd_ref[...], turned[pair], preferred_element_type=F32)
        left, right = both[:, :chans], both[:, chans:]
        by_slot[slot][...] = jnp.where(odd, right, left).astype(BF16)
        by_slot[slot + 1][...] = jnp.where(odd, left, right).astype(BF16)


def conv_fast(early, part, late, fwd, bwd):
    n_blocks = early.shape[0]
    rows, chans = late[0].shape[0], late[0].shape[1] // 2
    whole = pl.BlockSpec(memory_space=pltpu.VMEM)
    return pl.pallas_call(
        conv_kernel,
        in_specs=[whole] * 6,
        out_specs=[whole] * n_blocks,
        out_shape=[jax.ShapeDtypeStruct((rows, chans), BF16)] * n_blocks,
        scratch_shapes=[
            pltpu.VMEM((2, 2 * rows, 2 * chans), F32),
            pltpu.VMEM((n_blocks // 2, 6 * rows, 2 * chans), BF16),
        ],
        compiler_params=pltpu.CompilerParams(vmem_limit_bytes=CONV_VMEM),
        cost_estimate=pl.CostEstimate(
            flops=16 * n_blocks * rows * rows * chans, bytes_accessed=4 * 2**20, transcendentals=0
        ),
    )(fwd, bwd, early, part, *late)


def conv_plain(received, fwd, bwd):
    n_blocks, rows, chans = received.shape[0], received.shape[1], received.shape[2] // 2
    exact = lax.Precision.HIGHEST
    fwd32 = fwd[:, :rows].astype(F32) + fwd[:, rows:].astype(F32)
    bwd32 = bwd[:, : 2 * rows].astype(F32) + bwd[:, 2 * rows : 4 * rows].astype(F32)
    sign = jnp.where(jnp.arange(rows) < rows // 2, 1.0, -1.0).astype(F32)[:, None]

    def spectrum(blocks):
        spec = jnp.einsum("kt,jtc->jkc", fwd32, blocks.astype(F32), precision=exact)
        return spec[:, :rows], spec[:, rows:]

    x_re, x_im = spectrum(received[:, :, :chans])
    f_re, f_im = spectrum(received[:, :, chans:])
    g_re = f_re.at[1:].add(-sign * f_im[:-1])
    g_im = f_im.at[1:].add(sign * f_re[:-1])

    def one(d, total):
        t_re, t_im = total
        later = (jnp.arange(n_blocks) >= d)[:, None, None]
        a_re = jnp.where(later, jnp.roll(x_re, d, axis=0), 0.0)
        a_im = jnp.where(later, jnp.roll(x_im, d, axis=0), 0.0)
        return (
            t_re + g_re[d] * a_re - g_im[d] * a_im,
            t_im + g_re[d] * a_im + g_im[d] * a_re,
        )

    zero = jnp.zeros_like(x_re)
    y_re, y_im = lax.fori_loop(0, n_blocks, one, (zero, zero))
    both = jnp.concatenate([y_re, y_im], axis=1)
    return jnp.einsum("tk,jkc->jtc", bwd32, both, precision=exact).astype(BF16)


def columns_of(other, across, piece, pieces, width):
    count = width // 4 // pieces
    place = lax.axis_index("fsdp")
    core, side = lax.rem(place, 2), lax.div(place, 2)
    block = 2 * (1 - side if across else side) + (1 - core if other else core)
    return pl.ds(pl.multiple_of((block * pieces + piece) * count, count), count)


def gate_slot(slot, queries_ref, keys_ref, values_ref, skip_ref, conv_ref):
    at = peer_block(slot, conv_ref.shape[1])
    product = keys_ref[:, at].astype(F32) * values_ref[:, at].astype(F32)
    mixed = conv_ref[...].astype(F32) + skip_ref[:, at] * product
    return (queries_ref[:, at].astype(F32) * mixed).astype(BF16)


def gate_early_kernel(n_peers, queries_ref, keys_ref, values_ref, skip_ref, weight_ref, *refs):
    conv_refs, (gated_ref, *part_refs) = refs[:-3], refs[-3:]
    chans = conv_refs[0].shape[1]
    slots = slots_of(n_peers, True)
    for slot, conv_ref in zip(slots, conv_refs):
        gated = gate_slot(slot, queries_ref, keys_ref, values_ref, skip_ref, conv_ref)
        gated_ref[:, peer_block(slot, chans)] = gated
    for slot in slots[len(conv_refs) :]:
        gated_ref[:, peer_block(slot, chans)] = jnp.zeros((gated_ref.shape[0], chans), BF16)
    for other, part_ref in zip((True, False), part_refs):
        columns = weight_ref[:, columns_of(other, True, 0, 1, weight_ref.shape[1])]
        part_ref[...] = jnp.dot(gated_ref[...], columns, preferred_element_type=F32)


def gate_early(queries, keys, values, skip, weight, conv, n_peers):
    rows, width = queries.shape
    out_width = weight.shape[1] // 4
    whole = pl.BlockSpec(memory_space=pltpu.VMEM)
    return pl.pallas_call(
        functools.partial(gate_early_kernel, n_peers),
        in_specs=[whole] * (5 + len(conv)),
        out_specs=[whole] * 3,
        out_shape=[jax.ShapeDtypeStruct((rows, width), BF16)]
        + [jax.ShapeDtypeStruct((rows, out_width), F32)] * 2,
        compiler_params=pltpu.CompilerParams(vmem_limit_bytes=PROJECT_VMEM),
        cost_estimate=pl.CostEstimate(
            flops=4 * rows * width * out_width, bytes_accessed=10 * rows * width, transcendentals=0
        ),
    )(queries, keys, values, skip, weight, *conv)


def late_product(late, late_slots, block, weight_ref, part_ref):
    chans = late.shape[1] // len(late_slots)
    at = columns_of(*block, weight_ref.shape[1])
    _, _, piece, pieces = block
    count = part_ref.shape[1] // pieces
    columns = jnp.concatenate([weight_ref[peer_block(s, chans), at] for s in late_slots], axis=0)
    part = part_ref[:, piece * count : (piece + 1) * count]
    return part + jnp.dot(late, columns, preferred_element_type=F32)


def gate_late_kernel(late_slots, block, queries_ref, keys_ref, values_ref, skip_ref, weight_ref, part_ref, *refs):
    *conv_refs, late_ref, sent_ref = refs
    chans = conv_refs[0].shape[1]
    for c, (slot, conv_ref) in enumerate(zip(late_slots, conv_refs)):
        gated = gate_slot(slot, queries_ref, keys_ref, values_ref, skip_ref, conv_ref)
        late_ref[:, c * chans : (c + 1) * chans] = gated
    total = late_product(late_ref[...], late_slots, block, weight_ref, part_ref)
    sent_ref[...] = total.astype(BF16)


def gate_late(queries, keys, values, skip, weight, part, conv, late_slots, block):
    rows, chans = conv[0].shape
    whole = pl.BlockSpec(memory_space=pltpu.VMEM)
    return pl.pallas_call(
        functools.partial(gate_late_kernel, late_slots, block),
        in_specs=[whole] * (6 + len(conv)),
        out_specs=[whole] * 2,
        out_shape=[
            jax.ShapeDtypeStruct((rows, chans * len(conv)), BF16),
            jax.ShapeDtypeStruct((rows, weight.shape[1] // 4 // block[-1]), BF16),
        ],
        compiler_params=pltpu.CompilerParams(vmem_limit_bytes=PROJECT_VMEM),
        cost_estimate=pl.CostEstimate(
            flops=rows * chans * weight.shape[1], bytes_accessed=2**20, transcendentals=0
        ),
    )(queries, keys, values, skip, weight, part, *conv)


def late_project_kernel(late_slots, blocks, weight_ref, late_ref, part_ref, *out_refs):
    for block, out_ref in zip(blocks, out_refs):
        total = late_product(late_ref[...], late_slots, block, weight_ref, part_ref)
        out_ref[...] = total.astype(out_ref.dtype)


def late_project(weight, late, part, late_slots, blocks, dtype):
    rows, depth = late.shape
    widths = [weight.shape[1] // 4 // pieces for *_, pieces in blocks]
    whole = pl.BlockSpec(memory_space=pltpu.VMEM)
    return pl.pallas_call(
        functools.partial(late_project_kernel, late_slots, blocks),
        in_specs=[whole] * 3,
        out_specs=[whole] * len(blocks),
        out_shape=[jax.ShapeDtypeStruct((rows, w), dtype) for w in widths],
        compiler_params=pltpu.CompilerParams(vmem_limit_bytes=PROJECT_VMEM),
        cost_estimate=pl.CostEstimate(
            flops=2 * rows * depth * sum(widths), bytes_accessed=2**20, transcendentals=0
        ),
    )(weight, late, part)


def assemble_kernel(late_slots, gated_ref, late_ref, out_ref):
    chans = late_ref.shape[1] // len(late_slots)
    out_ref[...] = gated_ref[...]
    for c, slot in enumerate(late_slots):
        out_ref[:, peer_block(slot, chans)] = late_ref[:, c * chans : (c + 1) * chans]


def assemble(gated, late, late_slots):
    whole = pl.BlockSpec(memory_space=pltpu.VMEM)
    return pl.pallas_call(
        functools.partial(assemble_kernel, late_slots),
        in_specs=[whole] * 2,
        out_specs=whole,
        out_shape=jax.ShapeDtypeStruct(gated.shape, BF16),
        compiler_params=pltpu.CompilerParams(vmem_limit_bytes=SMALL_VMEM),
        cost_estimate=pl.CostEstimate(flops=1000, bytes_accessed=2**20, transcendentals=0),
    )(gated, late)


def project_kernel(blocks, gated_ref, weight_ref, *out_refs):
    for block, out_ref in zip(blocks, out_refs):
        columns = weight_ref[:, columns_of(*block, weight_ref.shape[1])]
        total = jnp.dot(gated_ref[...], columns, preferred_element_type=F32)
        out_ref[...] = total.astype(out_ref.dtype)


def project(gated, weight, blocks, dtypes):
    rows, depth = gated.shape
    widths = [weight.shape[1] // 4 // pieces for *_, pieces in blocks]
    whole = pl.BlockSpec(memory_space=pltpu.VMEM)
    return pl.pallas_call(
        functools.partial(project_kernel, blocks),
        in_specs=[whole] * 2,
        out_specs=[whole] * len(blocks),
        out_shape=[jax.ShapeDtypeStruct((rows, w), t) for w, t in zip(widths, dtypes)],
        compiler_params=pltpu.CompilerParams(vmem_limit_bytes=PROJECT_VMEM),
        cost_estimate=pl.CostEstimate(
            flops=2 * rows * depth * sum(widths), bytes_accessed=2 * depth * sum(widths), transcendentals=0
        ),
    )(gated, weight)


def add_kernel(own_ref, arrived_ref, out_ref):
    total = own_ref[...] + arrived_ref[...].astype(F32)
    out_ref[...] = total.astype(out_ref.dtype)


def add(own, arrived):
    whole = pl.BlockSpec(memory_space=pltpu.VMEM)
    return pl.pallas_call(
        add_kernel,
        in_specs=[whole] * 2,
        out_specs=whole,
        out_shape=jax.ShapeDtypeStruct(arrived.shape, BF16),
        compiler_params=pltpu.CompilerParams(vmem_limit_bytes=SMALL_VMEM),
        cost_estimate=pl.CostEstimate(
            flops=arrived.size, bytes_accessed=8 * arrived.size, transcendentals=0
        ),
    )(own, arrived)


def mark_kernel(*refs):
    refs[-1][...] = jnp.zeros_like(refs[-1])


def mark(arrays):
    return pl.pallas_call(
        mark_kernel,
        in_specs=[pl.BlockSpec(memory_space=pl.ANY)] * len(arrays),
        out_specs=pl.BlockSpec(memory_space=pltpu.VMEM),
        out_shape=jax.ShapeDtypeStruct((8, 128), F32),
        compiler_params=pltpu.CompilerParams(vmem_limit_bytes=SMALL_VMEM),
        cost_estimate=pl.CostEstimate(flops=2 * 10**10, bytes_accessed=2**20, transcendentals=0),
    )(*arrays)


def finish_kernel(own_ref, near_ref, *refs):
    *arrived_refs, _, out_ref, stage, sem = refs
    width = out_ref.shape[1] // len(arrived_refs)
    steps = sem.shape[0]
    rows = out_ref.shape[0] // steps
    copies = []
    for step in range(steps):
        part = pl.ds(step * rows, rows)
        for c, arrived_ref in enumerate(arrived_refs):
            at = slice(c * width, (c + 1) * width)
            total = own_ref[part, at] + near_ref[part, at].astype(F32)
            stage[part, at] = (total + arrived_ref[part].astype(F32)).astype(stage.dtype)
        copies.append(pltpu.make_async_copy(stage.at[part], out_ref.at[part], sem.at[step]))
        copies[-1].start()
    for copy in copies:
        copy.wait()


def finish(own, near, arrived):
    rows, width = own.shape
    whole, anywhere = pl.BlockSpec(memory_space=pltpu.VMEM), pl.BlockSpec(memory_space=pl.ANY)
    return pl.pallas_call(
        finish_kernel,
        in_specs=[whole] * (2 + len(arrived)) + [anywhere],
        out_specs=anywhere,
        out_shape=jax.ShapeDtypeStruct((rows, width), BF16),
        scratch_shapes=[pltpu.VMEM((rows, width), BF16), pltpu.SemaphoreType.DMA((4,))],
        compiler_params=pltpu.CompilerParams(vmem_limit_bytes=SMALL_VMEM),
        cost_estimate=pl.CostEstimate(
            flops=rows * width, bytes_accessed=8 * rows * width, transcendentals=0
        ),
    )(own, near, *arrived, mark(arrived))


def body(pieces, tables, queries, keys, values, filters, skip_weight, out_weight):
    rows, width = keys.shape
    n_peers = lax.axis_size("seq")
    chans = width // n_peers
    fwd, bwd = (jnp.asarray(t) for t in tables)
    skip = skip_weight[None, :]
    in_chip = [(0, 1), (1, 0), (2, 3), (3, 2)]
    across = [(0, 2), (2, 0), (1, 3), (3, 1)]

    sends = [(True, True, c, pieces) for c in range(pieces)]
    keeps = [(False, True, c, pieces) for c in range(pieces)]

    if chans % 128 == 0 and n_peers == 8:
        blocks = pre(keys, values, filters, n_peers)
        received = exchange(blocks, n_peers, False)
        fwd, bwd = load_tables(fwd, bwd, received[1:2])
        early, part = spectra(received[:-2], fwd, n_peers)
        back = exchange(conv_fast(early, part, received[-2:], fwd, bwd), n_peers, True)
        slots = slots_of(n_peers, True)[-3:]
        gated, send_part, own_part = gate_early(
            queries, keys, values, skip, out_weight, back[:-3], n_peers
        )
        late, last = gate_late(
            queries, keys, values, skip, out_weight, send_part, back[-3:], slots, sends[-1]
        )
        sent = [
            *(late_project(out_weight, late, send_part, slots, [s], BF16)[0] for s in sends[:-1]),
            last,
        ]
        ours = late_project(out_weight, late, own_part, slots, keeps, F32)
        gated = assemble(gated, late, slots)
    else:
        product = keys.astype(F32) * values.astype(F32)
        parts = [a.astype(BF16).reshape(rows, n_peers, chans) for a in (product, filters)]
        sent = jnp.concatenate(parts, axis=2).transpose(1, 0, 2)
        received = lax.all_to_all(sent, "seq", split_axis=0, concat_axis=0, tiled=True)
        conv = conv_plain(received, fwd, bwd)
        back = lax.all_to_all(conv, "seq", split_axis=0, concat_axis=0, tiled=True)
        mixed = back.transpose(1, 0, 2).reshape(rows, width).astype(F32) + skip * product
        gated = (queries.astype(F32) * mixed).astype(BF16)
        sent = project(gated, out_weight, sends, [BF16] * pieces)
        ours = project(gated, out_weight, keeps, [F32] * pieces)

    theirs = [lax.ppermute(piece, "fsdp", in_chip) for piece in sent]
    arrived = [lax.ppermute(add(*pair), "fsdp", across) for pair in zip(ours, theirs)]
    blocks = [(True, False, 0, 1), (False, False, 0, 1)]
    sent, own = project(gated, out_weight, blocks, [BF16, F32])
    near = lax.ppermute(sent, "fsdp", in_chip)
    return finish(own, near, arrived)


def solution(mesh):
    in_specs = (
        P("seq", "fsdp"),
        P("seq", "fsdp"),
        P("seq", "fsdp"),
        P("seq", "fsdp"),
        P("fsdp"),
        P("fsdp", None),
    )
    out_specs = P("seq", "fsdp")

    def run(queries, keys, values, filters, skip_weight, out_weight):
        rows = keys.shape[0] // mesh.shape["seq"]
        fn = functools.partial(body, 2, make_tables(rows))
        return jax.shard_map(fn, mesh=mesh, in_specs=in_specs, out_specs=out_specs, check_vma=False)(
            queries, keys, values, filters, skip_weight, out_weight
        )

    return run
```

```python
import functools

import numpy as np

import jax
import jax.numpy as jnp
from jax import lax
from jax.experimental import pallas as pl
from jax.experimental.pallas import tpu as pltpu
from jax.sharding import PartitionSpec as P

BF16 = jnp.bfloat16
F32 = jnp.float32
CONV_VMEM = 24 * 2**20
PROJECT_VMEM = 24 * 2**20
SMALL_VMEM = 12 * 2**20
STEP = 16


def split_bf16(table):
    high = table.astype(BF16)
    return high, (table - high.astype(np.float64)).astype(BF16)


def make_tables(rows):
    order = np.concatenate([np.arange(0, rows, 2), np.arange(1, rows, 2)])
    times = np.arange(rows)
    angle = np.pi * (((2 * order[:, None] + 1) * times[None, :]) % (4 * rows)) / (2 * rows)
    forward = np.concatenate([np.cos(angle), -np.sin(angle)], axis=0)
    high, low = split_bf16(forward)
    back_high, back_low = split_bf16(forward.T / rows)
    return (
        np.concatenate([high, low], axis=1),
        np.concatenate([back_high, back_low, back_high], axis=1),
    )


def peer_of(slot):
    return lax.bitwise_xor(lax.axis_index("seq"), slot)


def peer_block(slot, size):
    return pl.ds(pl.multiple_of(peer_of(slot) * size, size), size)


def pre_kernel(n_peers, keys_hbm, values_hbm, filters_hbm, *refs):
    out_refs = refs[:n_peers]
    keys, values, filters, sem = refs[n_peers:]
    rows, width = keys.shape
    chans = width // n_peers
    steps = sem.shape[0]
    parts = [pl.ds(c * rows // steps, rows // steps) for c in range(steps)]
    pairs = ((keys_hbm, keys), (values_hbm, values), (filters_hbm, filters))
    copies = [
        [
            pltpu.make_async_copy(src.at[part], dst.at[part], sem.at[c, i])
            for i, (src, dst) in enumerate(pairs)
        ]
        for c, part in enumerate(parts)
    ]
    for group in copies:
        for copy in group:
            copy.start()
    for part, group in zip(parts, copies):
        for copy in group:
            copy.wait()
        for slot, out_ref in zip(slots_of(n_peers, False), out_refs):
            at = peer_block(slot, chans)
            product = keys[part, at].astype(F32) * values[part, at].astype(F32)
            out_ref[part, :chans] = product.astype(BF16)
            out_ref[part, chans:] = filters[part, at].astype(BF16)


def pre(keys, values, filters, n_peers):
    rows, width = keys.shape
    chans = width // n_peers
    args = [pltpu.with_memory_space_constraint(a, pltpu.HBM) for a in (keys, values, filters)]
    return pl.pallas_call(
        functools.partial(pre_kernel, n_peers),
        in_specs=[pl.BlockSpec(memory_space=pltpu.HBM)] * 3,
        out_specs=[pl.BlockSpec(memory_space=pltpu.VMEM)] * n_peers,
        out_shape=[jax.ShapeDtypeStruct((rows, 2 * chans), BF16)] * n_peers,
        scratch_shapes=[
            pltpu.VMEM((rows, width), BF16),
            pltpu.VMEM((rows, width), BF16),
            pltpu.VMEM((rows, width), F32),
            pltpu.SemaphoreType.DMA((2, 3)),
        ],
        compiler_params=pltpu.CompilerParams(vmem_limit_bytes=SMALL_VMEM),
        cost_estimate=pl.CostEstimate(
            flops=rows * width, bytes_accessed=12 * rows * width, transcendentals=0
        ),
    )(*args)


def slots_of(n_peers, back):
    half = n_peers // 2
    near, far = list(range(1, half)), list(range(half, n_peers))
    if back:
        return [0, near[0], far[2], far[0], far[1], near[1], far[3]] + near[2:]
    return [0, far[0], near[0]] + near[:0:-1] + far[1:]


def exchange(blocks, n_peers, back):
    return [
        lax.ppermute(block, "seq", [(i, i ^ slot) for i in range(n_peers)]) if slot else block
        for slot, block in zip(slots_of(n_peers, back), blocks)
    ]


def block_spectrum(table, block):
    return jnp.dot(table, jnp.concatenate([block, block], axis=0), preferred_element_type=F32)


def times(a, b):
    return a[0] * b[0] - a[1] * b[1], a[0] * b[1] + a[1] * b[0]


def plus(a, b):
    return b if a is None else (a[0] + b[0], a[1] + b[1])


def late_place(n_blocks):
    return lax.div(peer_of(slots_of(n_blocks, False)[-1]), 2)


def load(ref, at, row, step, rows, lanes):
    return tuple(ref[(*at, pl.ds(row + part * rows, step), lanes)] for part in range(2))


def mix_early(pair, step, spec_ref, part_ref):
    n_blocks, rows, chans = spec_ref.shape[0], spec_ref.shape[1] // 2, spec_ref.shape[2] // 2
    early = [j for j in range(n_blocks) if j // 2 != pair]

    @pl.loop(0, rows // step)
    def _(t):
        row = pl.multiple_of(t * step, step)
        signal = {j: load(spec_ref, (j,), row, step, rows, slice(0, chans)) for j in early}
        filt = {j: load(spec_ref, (j,), row, step, rows, slice(chans, 2 * chans)) for j in early}
        for i in range(n_blocks):
            total = None
            for d in early:
                if i - d in early:
                    total = plus(total, times(filt[d], signal[i - d]))
            if total is None:
                total = (jnp.zeros((step, chans), F32),) * 2
            for part in range(2):
                part_ref[i, pl.ds(row + part * rows, step)] = total[part]


def tables_kernel(fwd_hbm, bwd_hbm, *refs):
    fwd_ref, bwd_ref, sem = refs[-3:]
    copies = [
        pltpu.make_async_copy(fwd_hbm, fwd_ref, sem.at[0]),
        pltpu.make_async_copy(bwd_hbm, bwd_ref, sem.at[1]),
    ]
    for copy in copies:
        copy.start()
    for copy in copies:
        copy.wait()


def load_tables(fwd, bwd, after):
    whole = pl.BlockSpec(memory_space=pltpu.VMEM)
    args = [pltpu.with_memory_space_constraint(a, pltpu.HBM) for a in (fwd, bwd)]
    return pl.pallas_call(
        tables_kernel,
        in_specs=[pl.BlockSpec(memory_space=pltpu.HBM)] * 2
        + [pl.BlockSpec(memory_space=pl.ANY)] * len(after),
        out_specs=[whole] * 2,
        out_shape=[jax.ShapeDtypeStruct(t.shape, BF16) for t in (fwd, bwd)],
        scratch_shapes=[pltpu.SemaphoreType.DMA((2,))],
        compiler_params=pltpu.CompilerParams(vmem_limit_bytes=SMALL_VMEM),
        cost_estimate=pl.CostEstimate(flops=10**6, bytes_accessed=3 * 2**20, transcendentals=0),
    )(*args, *after)


def spectra_kernel(n_peers, fwd_ref, *refs):
    *in_refs, spec_ref, part_ref = refs
    for slot, in_ref in zip(slots_of(n_peers, False), in_refs):
        spec_ref[peer_of(slot)] = block_spectrum(fwd_ref[...], in_ref[...])
    for pair in range(n_peers // 2):
        pl.when(late_place(n_peers) == pair)(
            functools.partial(mix_early, pair, STEP, spec_ref, part_ref)
        )


def spectra(received, fwd, n_peers):
    rows, width = received[0].shape
    whole = pl.BlockSpec(memory_space=pltpu.VMEM)
    return pl.pallas_call(
        functools.partial(spectra_kernel, n_peers),
        in_specs=[whole] * (1 + len(received)),
        out_specs=[whole] * 2,
        out_shape=[
            jax.ShapeDtypeStruct((n_peers, 2 * rows, width), F32),
            jax.ShapeDtypeStruct((n_peers, 2 * rows, width // 2), F32),
        ],
        compiler_params=pltpu.CompilerParams(vmem_limit_bytes=CONV_VMEM),
        cost_estimate=pl.CostEstimate(
            flops=8 * len(received) * rows * rows * width, bytes_accessed=4 * 2**20, transcendentals=0
        ),
    )(fwd, *received)


def add_block(total, place, new, others, row, step, rows, chans):
    n_blocks = len(total)
    x_at, f_at = slice(0, chans), slice(chans, 2 * chans)
    x_new, f_new = load(new, (), row, step, rows, x_at), load(new, (), row, step, rows, f_at)
    for j, (ref, at) in others.items():
        if j + place < n_blocks:
            x_j = load(ref, at, row, step, rows, x_at)
            f_j = load(ref, at, row, step, rows, f_at)
            total[j + place] = plus(total[j + place], times(f_new, x_j))
            total[j + place] = plus(total[j + place], times(f_j, x_new))
    if 2 * place < n_blocks:
        total[2 * place] = plus(total[2 * place], times(f_new, x_new))


def early_blocks(place, n_blocks, spec_ref):
    return {j: (spec_ref, (j,)) for j in range(n_blocks) if j // 2 != place // 2}


def mix_middle(place, step, spec_ref, part_ref, new_ref, out_ref):
    n_blocks, rows, chans = spec_ref.shape[0], spec_ref.shape[1] // 2, spec_ref.shape[2] // 2
    others = early_blocks(place, n_blocks, spec_ref)

    @pl.loop(0, rows // step)
    def _(t):
        row = pl.multiple_of(t * step, step)
        total = [load(part_ref, (i,), row, step, rows, slice(0, chans)) for i in range(n_blocks)]
        add_block(total, place, new_ref, others, row, step, rows, chans)
        for i in range(n_blocks):
            for part in range(2):
                out_ref[i, pl.ds(row + part * rows, step)] = total[i][part]


def middle_kernel(fwd_ref, spec_ref, part_ref, in_ref, new_ref, out_ref):
    n_blocks = spec_ref.shape[0]
    new_ref[...] = block_spectrum(fwd_ref[...], in_ref[...])
    mine = peer_of(slots_of(n_blocks, False)[-2])
    for place in range(n_blocks):
        pl.when(mine == place)(
            functools.partial(mix_middle, place, STEP, spec_ref, part_ref, new_ref, out_ref)
        )


def middle(early, part, block, fwd):
    whole = pl.BlockSpec(memory_space=pltpu.VMEM)
    return pl.pallas_call(
        middle_kernel,
        in_specs=[whole] * 4,
        out_specs=[whole] * 2,
        out_shape=[jax.ShapeDtypeStruct(a.shape, F32) for a in (early[0], part)],
        compiler_params=pltpu.CompilerParams(vmem_limit_bytes=CONV_VMEM),
        cost_estimate=pl.CostEstimate(flops=10**9, bytes_accessed=4 * 2**20, transcendentals=0),
    )(fwd, early, part, block)


def mix_last(place, step, first, last, sign, spec_ref, part_ref, next_ref, new_ref, turned):
    n_blocks, rows, chans = spec_ref.shape[0], spec_ref.shape[1] // 2, spec_ref.shape[2] // 2
    others = early_blocks(place, n_blocks, spec_ref)
    others[place ^ 1] = (next_ref, ())

    @pl.loop(first // step, last // step)
    def _(t):
        row = pl.multiple_of(t * step, step)
        total = [load(part_ref, (i,), row, step, rows, slice(0, chans)) for i in range(n_blocks)]
        add_block(total, place, new_ref, others, row, step, rows, chans)
        for i in range(n_blocks):
            value = total[i]
            if i > 0:
                turn_re, turn_im = total[i - 1]
                if sign > 0:
                    value = value[0] - turn_im, value[1] + turn_re
                else:
                    value = value[0] + turn_im, value[1] - turn_re
            lanes = slice(i % 2 * chans, (i % 2 + 1) * chans)
            for part in range(2):
                high = value[part].astype(BF16)
                low = (value[part] - high.astype(F32)).astype(BF16)
                for c, piece in enumerate((high, high, low)):
                    turned[i // 2, pl.ds(row + (2 * c + part) * rows, step), lanes] = piece


def conv_kernel(fwd_ref, bwd_ref, spec_ref, part_ref, next_ref, in_ref, *refs):
    *out_refs, new_ref, turned = refs
    n_blocks, rows, chans = spec_ref.shape[0], in_ref.shape[0], in_ref.shape[1] // 2
    new_ref[...] = block_spectrum(fwd_ref[...], in_ref[...])

    def mix(place):
        for first, last, sign in ((0, rows // 2, 1), (rows // 2, rows, -1)):
            mix_last(place, STEP, first, last, sign, spec_ref, part_ref, next_ref, new_ref, turned)

    mine = peer_of(slots_of(n_blocks, False)[-1])
    for place in range(n_blocks):
        pl.when(mine == place)(functools.partial(mix, place))

    odd = lax.bitwise_and(lax.axis_index("seq"), 1) == 1
    by_slot = dict(zip(slots_of(n_blocks, True), out_refs))
    for slot in range(0, n_blocks, 2):
        pair = lax.div(peer_of(slot), 2)
        both = jnp.dot(bwd_ref[...], turned[pair], preferred_element_type=F32)
        left, right = both[:, :chans], both[:, chans:]
        by_slot[slot][...] = jnp.where(odd, right, left).astype(BF16)
        by_slot[slot + 1][...] = jnp.where(odd, left, right).astype(BF16)


def conv_fast(early, part, late, fwd, bwd):
    n_blocks = early.shape[0]
    rows, chans = late[0].shape[0], late[0].shape[1] // 2
    late_spec, part = middle(early, part, late[0], fwd)
    whole = pl.BlockSpec(memory_space=pltpu.VMEM)
    return pl.pallas_call(
        conv_kernel,
        in_specs=[whole] * 6,
        out_specs=[whole] * n_blocks,
        out_shape=[jax.ShapeDtypeStruct((rows, chans), BF16)] * n_blocks,
        scratch_shapes=[
            pltpu.VMEM((2 * rows, 2 * chans), F32),
            pltpu.VMEM((n_blocks // 2, 6 * rows, 2 * chans), BF16),
        ],
        compiler_params=pltpu.CompilerParams(vmem_limit_bytes=CONV_VMEM),
        cost_estimate=pl.CostEstimate(
            flops=16 * n_blocks * rows * rows * chans, bytes_accessed=4 * 2**20, transcendentals=0
        ),
    )(fwd, bwd, early, part, late_spec, late[1])


def conv_plain(received, fwd, bwd):
    n_blocks, rows, chans = received.shape[0], received.shape[1], received.shape[2] // 2
    exact = lax.Precision.HIGHEST
    fwd32 = fwd[:, :rows].astype(F32) + fwd[:, rows:].astype(F32)
    bwd32 = bwd[:, : 2 * rows].astype(F32) + bwd[:, 2 * rows : 4 * rows].astype(F32)
    sign = jnp.where(jnp.arange(rows) < rows // 2, 1.0, -1.0).astype(F32)[:, None]

    def spectrum(blocks):
        spec = jnp.einsum("kt,jtc->jkc", fwd32, blocks.astype(F32), precision=exact)
        return spec[:, :rows], spec[:, rows:]

    x_re, x_im = spectrum(received[:, :, :chans])
    f_re, f_im = spectrum(received[:, :, chans:])
    g_re = f_re.at[1:].add(-sign * f_im[:-1])
    g_im = f_im.at[1:].add(sign * f_re[:-1])

    def one(d, total):
        t_re, t_im = total
        later = (jnp.arange(n_blocks) >= d)[:, None, None]
        a_re = jnp.where(later, jnp.roll(x_re, d, axis=0), 0.0)
        a_im = jnp.where(later, jnp.roll(x_im, d, axis=0), 0.0)
        return (
            t_re + g_re[d] * a_re - g_im[d] * a_im,
            t_im + g_re[d] * a_im + g_im[d] * a_re,
        )

    zero = jnp.zeros_like(x_re)
    y_re, y_im = lax.fori_loop(0, n_blocks, one, (zero, zero))
    both = jnp.concatenate([y_re, y_im], axis=1)
    return jnp.einsum("tk,jkc->jtc", bwd32, both, precision=exact).astype(BF16)


def columns_of(other, across, piece, pieces, width):
    count = width // 4 // pieces
    place = lax.axis_index("fsdp")
    core, side = lax.rem(place, 2), lax.div(place, 2)
    block = 2 * (1 - side if across else side) + (1 - core if other else core)
    return pl.ds(pl.multiple_of((block * pieces + piece) * count, count), count)


def gate_slot(slot, queries_ref, keys_ref, values_ref, skip_ref, conv_ref):
    at = peer_block(slot, conv_ref.shape[1])
    product = keys_ref[:, at].astype(F32) * values_ref[:, at].astype(F32)
    mixed = conv_ref[...].astype(F32) + skip_ref[:, at] * product
    return (queries_ref[:, at].astype(F32) * mixed).astype(BF16)


def gate_early_kernel(n_peers, queries_ref, keys_ref, values_ref, skip_ref, weight_ref, *refs):
    conv_refs, (gated_ref, *part_refs) = refs[:-3], refs[-3:]
    chans = conv_refs[0].shape[1]
    slots = slots_of(n_peers, True)
    for slot, conv_ref in zip(slots, conv_refs):
        gated = gate_slot(slot, queries_ref, keys_ref, values_ref, skip_ref, conv_ref)
        gated_ref[:, peer_block(slot, chans)] = gated
    for slot in slots[len(conv_refs) :]:
        gated_ref[:, peer_block(slot, chans)] = jnp.zeros((gated_ref.shape[0], chans), BF16)
    for other, part_ref in zip((True, False), part_refs):
        columns = weight_ref[:, columns_of(other, True, 0, 1, weight_ref.shape[1])]
        part_ref[...] = jnp.dot(gated_ref[...], columns, preferred_element_type=F32)


def gate_early(queries, keys, values, skip, weight, conv, n_peers):
    rows, width = queries.shape
    out_width = weight.shape[1] // 4
    whole = pl.BlockSpec(memory_space=pltpu.VMEM)
    return pl.pallas_call(
        functools.partial(gate_early_kernel, n_peers),
        in_specs=[whole] * (5 + len(conv)),
        out_specs=[whole] * 3,
        out_shape=[jax.ShapeDtypeStruct((rows, width), BF16)]
        + [jax.ShapeDtypeStruct((rows, out_width), F32)] * 2,
        compiler_params=pltpu.CompilerParams(vmem_limit_bytes=PROJECT_VMEM),
        cost_estimate=pl.CostEstimate(
            flops=4 * rows * width * out_width, bytes_accessed=10 * rows * width, transcendentals=0
        ),
    )(queries, keys, values, skip, weight, *conv)


def late_product(late, late_slots, block, weight_ref, part_ref):
    chans = late.shape[1] // len(late_slots)
    at = columns_of(*block, weight_ref.shape[1])
    _, _, piece, pieces = block
    count = part_ref.shape[1] // pieces
    columns = jnp.concatenate([weight_ref[peer_block(s, chans), at] for s in late_slots], axis=0)
    part = part_ref[:, piece * count : (piece + 1) * count]
    return part + jnp.dot(late, columns, preferred_element_type=F32)


def gate_late_kernel(late_slots, block, queries_ref, keys_ref, values_ref, skip_ref, weight_ref, part_ref, *refs):
    *conv_refs, late_ref, sent_ref = refs
    chans = conv_refs[0].shape[1]
    for c, (slot, conv_ref) in enumerate(zip(late_slots, conv_refs)):
        gated = gate_slot(slot, queries_ref, keys_ref, values_ref, skip_ref, conv_ref)
        late_ref[:, c * chans : (c + 1) * chans] = gated
    total = late_product(late_ref[...], late_slots, block, weight_ref, part_ref)
    sent_ref[...] = total.astype(BF16)


def gate_late(queries, keys, values, skip, weight, part, conv, late_slots, block):
    rows, chans = conv[0].shape
    whole = pl.BlockSpec(memory_space=pltpu.VMEM)
    return pl.pallas_call(
        functools.partial(gate_late_kernel, late_slots, block),
        in_specs=[whole] * (6 + len(conv)),
        out_specs=[whole] * 2,
        out_shape=[
            jax.ShapeDtypeStruct((rows, chans * len(conv)), BF16),
            jax.ShapeDtypeStruct((rows, weight.shape[1] // 4 // block[-1]), BF16),
        ],
        compiler_params=pltpu.CompilerParams(vmem_limit_bytes=PROJECT_VMEM),
        cost_estimate=pl.CostEstimate(
            flops=rows * chans * weight.shape[1], bytes_accessed=2**20, transcendentals=0
        ),
    )(queries, keys, values, skip, weight, part, *conv)


def late_project_kernel(late_slots, blocks, weight_ref, late_ref, part_ref, *out_refs):
    for block, out_ref in zip(blocks, out_refs):
        total = late_product(late_ref[...], late_slots, block, weight_ref, part_ref)
        out_ref[...] = total.astype(out_ref.dtype)


def late_project(weight, late, part, late_slots, blocks, dtype):
    rows, depth = late.shape
    widths = [weight.shape[1] // 4 // pieces for *_, pieces in blocks]
    whole = pl.BlockSpec(memory_space=pltpu.VMEM)
    return pl.pallas_call(
        functools.partial(late_project_kernel, late_slots, blocks),
        in_specs=[whole] * 3,
        out_specs=[whole] * len(blocks),
        out_shape=[jax.ShapeDtypeStruct((rows, w), dtype) for w in widths],
        compiler_params=pltpu.CompilerParams(vmem_limit_bytes=PROJECT_VMEM),
        cost_estimate=pl.CostEstimate(
            flops=2 * rows * depth * sum(widths), bytes_accessed=2**20, transcendentals=0
        ),
    )(weight, late, part)


def assemble_kernel(late_slots, gated_ref, late_ref, out_ref):
    chans = late_ref.shape[1] // len(late_slots)
    out_ref[...] = gated_ref[...]
    for c, slot in enumerate(late_slots):
        out_ref[:, peer_block(slot, chans)] = late_ref[:, c * chans : (c + 1) * chans]


def assemble(gated, late, late_slots):
    whole = pl.BlockSpec(memory_space=pltpu.VMEM)
    return pl.pallas_call(
        functools.partial(assemble_kernel, late_slots),
        in_specs=[whole] * 2,
        out_specs=whole,
        out_shape=jax.ShapeDtypeStruct(gated.shape, BF16),
        compiler_params=pltpu.CompilerParams(vmem_limit_bytes=SMALL_VMEM),
        cost_estimate=pl.CostEstimate(flops=1000, bytes_accessed=2**20, transcendentals=0),
    )(gated, late)


def project_kernel(blocks, gated_ref, weight_ref, *out_refs):
    for block, out_ref in zip(blocks, out_refs):
        columns = weight_ref[:, columns_of(*block, weight_ref.shape[1])]
        total = jnp.dot(gated_ref[...], columns, preferred_element_type=F32)
        out_ref[...] = total.astype(out_ref.dtype)


def project(gated, weight, blocks, dtypes):
    rows, depth = gated.shape
    widths = [weight.shape[1] // 4 // pieces for *_, pieces in blocks]
    whole = pl.BlockSpec(memory_space=pltpu.VMEM)
    return pl.pallas_call(
        functools.partial(project_kernel, blocks),
        in_specs=[whole] * 2,
        out_specs=[whole] * len(blocks),
        out_shape=[jax.ShapeDtypeStruct((rows, w), t) for w, t in zip(widths, dtypes)],
        compiler_params=pltpu.CompilerParams(vmem_limit_bytes=PROJECT_VMEM),
        cost_estimate=pl.CostEstimate(
            flops=2 * rows * depth * sum(widths), bytes_accessed=2 * depth * sum(widths), transcendentals=0
        ),
    )(gated, weight)


def add_kernel(own_ref, arrived_ref, out_ref):
    total = own_ref[...] + arrived_ref[...].astype(F32)
    out_ref[...] = total.astype(out_ref.dtype)


def add(own, arrived):
    whole = pl.BlockSpec(memory_space=pltpu.VMEM)
    return pl.pallas_call(
        add_kernel,
        in_specs=[whole] * 2,
        out_specs=whole,
        out_shape=jax.ShapeDtypeStruct(arrived.shape, BF16),
        compiler_params=pltpu.CompilerParams(vmem_limit_bytes=SMALL_VMEM),
        cost_estimate=pl.CostEstimate(
            flops=arrived.size, bytes_accessed=8 * arrived.size, transcendentals=0
        ),
    )(own, arrived)


def mark_kernel(*refs):
    refs[-1][...] = jnp.zeros_like(refs[-1])


def mark(arrays):
    return pl.pallas_call(
        mark_kernel,
        in_specs=[pl.BlockSpec(memory_space=pl.ANY)] * len(arrays),
        out_specs=pl.BlockSpec(memory_space=pltpu.VMEM),
        out_shape=jax.ShapeDtypeStruct((8, 128), F32),
        compiler_params=pltpu.CompilerParams(vmem_limit_bytes=SMALL_VMEM),
        cost_estimate=pl.CostEstimate(flops=2 * 10**10, bytes_accessed=2**20, transcendentals=0),
    )(*arrays)


def finish_kernel(own_ref, near_ref, *refs):
    *arrived_refs, _, out_ref, stage, sem = refs
    width = out_ref.shape[1] // len(arrived_refs)
    steps = sem.shape[0]
    rows = out_ref.shape[0] // steps
    copies = []
    for step in range(steps):
        part = pl.ds(step * rows, rows)
        for c, arrived_ref in enumerate(arrived_refs):
            at = slice(c * width, (c + 1) * width)
            total = own_ref[part, at] + near_ref[part, at].astype(F32)
            stage[part, at] = (total + arrived_ref[part].astype(F32)).astype(stage.dtype)
        copies.append(pltpu.make_async_copy(stage.at[part], out_ref.at[part], sem.at[step]))
        copies[-1].start()
    for copy in copies:
        copy.wait()


def finish(own, near, arrived):
    rows, width = own.shape
    whole, anywhere = pl.BlockSpec(memory_space=pltpu.VMEM), pl.BlockSpec(memory_space=pl.ANY)
    return pl.pallas_call(
        finish_kernel,
        in_specs=[whole] * (2 + len(arrived)) + [anywhere],
        out_specs=anywhere,
        out_shape=jax.ShapeDtypeStruct((rows, width), BF16),
        scratch_shapes=[pltpu.VMEM((rows, width), BF16), pltpu.SemaphoreType.DMA((4,))],
        compiler_params=pltpu.CompilerParams(vmem_limit_bytes=SMALL_VMEM),
        cost_estimate=pl.CostEstimate(
            flops=rows * width, bytes_accessed=8 * rows * width, transcendentals=0
        ),
    )(own, near, *arrived, mark(arrived))


def body(pieces, tables, queries, keys, values, filters, skip_weight, out_weight):
    rows, width = keys.shape
    n_peers = lax.axis_size("seq")
    chans = width // n_peers
    fwd, bwd = (jnp.asarray(t) for t in tables)
    skip = skip_weight[None, :]
    in_chip = [(0, 1), (1, 0), (2, 3), (3, 2)]
    across = [(0, 2), (2, 0), (1, 3), (3, 1)]

    sends = [(True, True, c, pieces) for c in range(pieces)]
    keeps = [(False, True, c, pieces) for c in range(pieces)]

    if chans % 128 == 0 and n_peers == 8:
        blocks = pre(keys, values, filters, n_peers)
        received = exchange(blocks, n_peers, False)
        fwd, bwd = load_tables(fwd, bwd, received[3:4])
        early, part = spectra(received[:-2], fwd, n_peers)
        back = exchange(conv_fast(early, part, received[-2:], fwd, bwd), n_peers, True)
        slots = slots_of(n_peers, True)[-2:]
        gated, send_part, own_part = gate_early(
            queries, keys, values, skip, out_weight, back[:-2], n_peers
        )
        late, last = gate_late(
            queries, keys, values, skip, out_weight, send_part, back[-2:], slots, sends[-1]
        )
        sent = [
            *(late_project(out_weight, late, send_part, slots, [s], BF16)[0] for s in sends[:-1]),
            last,
        ]
        ours = late_project(out_weight, late, own_part, slots, keeps, F32)
        gated = assemble(gated, late, slots)
    else:
        product = keys.astype(F32) * values.astype(F32)
        parts = [a.astype(BF16).reshape(rows, n_peers, chans) for a in (product, filters)]
        sent = jnp.concatenate(parts, axis=2).transpose(1, 0, 2)
        received = lax.all_to_all(sent, "seq", split_axis=0, concat_axis=0, tiled=True)
        conv = conv_plain(received, fwd, bwd)
        back = lax.all_to_all(conv, "seq", split_axis=0, concat_axis=0, tiled=True)
        mixed = back.transpose(1, 0, 2).reshape(rows, width).astype(F32) + skip * product
        gated = (queries.astype(F32) * mixed).astype(BF16)
        sent = project(gated, out_weight, sends, [BF16] * pieces)
        ours = project(gated, out_weight, keeps, [F32] * pieces)

    theirs = [lax.ppermute(piece, "fsdp", in_chip) for piece in sent]
    arrived = [lax.ppermute(add(*pair), "fsdp", across) for pair in zip(ours, theirs)]
    blocks = [(True, False, 0, 1), (False, False, 0, 1)]
    sent, own = project(gated, out_weight, blocks, [BF16, F32])
    near = lax.ppermute(sent, "fsdp", in_chip)
    return finish(own, near, arrived)


def solution(mesh):
    in_specs = (
        P("seq", "fsdp"),
        P("seq", "fsdp"),
        P("seq", "fsdp"),
        P("seq", "fsdp"),
        P("fsdp"),
        P("fsdp", None),
    )
    out_specs = P("seq", "fsdp")

    def run(queries, keys, values, filters, skip_weight, out_weight):
        rows = keys.shape[0] // mesh.shape["seq"]
        fn = functools.partial(body, 2, make_tables(rows))
        return jax.shard_map(fn, mesh=mesh, in_specs=in_specs, out_specs=out_specs, check_vma=False)(
            queries, keys, values, filters, skip_weight, out_weight
        )

    return run
```

```python
import functools

import numpy as np

import jax
import jax.numpy as jnp
from jax import lax
from jax.experimental import pallas as pl
from jax.experimental.pallas import tpu as pltpu
from jax.sharding import PartitionSpec as P

BF16 = jnp.bfloat16
F32 = jnp.float32
CONV_VMEM = 24 * 2**20
PROJECT_VMEM = 24 * 2**20
SMALL_VMEM = 12 * 2**20
STEP = 16


def split_bf16(table):
    high = table.astype(BF16)
    return high, (table - high.astype(np.float64)).astype(BF16)


def make_tables(rows):
    order = np.concatenate([np.arange(0, rows, 2), np.arange(1, rows, 2)])
    times = np.arange(rows)
    angle = np.pi * (((2 * order[:, None] + 1) * times[None, :]) % (4 * rows)) / (2 * rows)
    forward = np.concatenate([np.cos(angle), -np.sin(angle)], axis=0)
    high, low = split_bf16(forward)
    back_high, back_low = split_bf16(forward.T / rows)
    return (
        np.concatenate([high, low], axis=1),
        np.concatenate([back_high, back_low, back_high], axis=1),
    )


def peer_of(slot):
    return lax.bitwise_xor(lax.axis_index("seq"), slot)


def peer_block(slot, size):
    return pl.ds(pl.multiple_of(peer_of(slot) * size, size), size)


def pre_kernel(n_peers, keys_hbm, values_hbm, filters_hbm, *refs):
    out_refs = refs[:n_peers]
    keys, values, filters, sem = refs[n_peers:]
    rows, width = keys.shape
    chans = width // n_peers
    steps = sem.shape[0]
    parts = [pl.ds(c * rows // steps, rows // steps) for c in range(steps)]
    pairs = ((keys_hbm, keys), (values_hbm, values), (filters_hbm, filters))
    copies = [
        [
            pltpu.make_async_copy(src.at[part], dst.at[part], sem.at[c, i])
            for i, (src, dst) in enumerate(pairs)
        ]
        for c, part in enumerate(parts)
    ]
    for group in copies:
        for copy in group:
            copy.start()
    for part, group in zip(parts, copies):
        for copy in group:
            copy.wait()
        for slot, out_ref in zip(slots_of(n_peers, False), out_refs):
            at = peer_block(slot, chans)
            product = keys[part, at].astype(F32) * values[part, at].astype(F32)
            out_ref[part, :chans] = product.astype(BF16)
            out_ref[part, chans:] = filters[part, at].astype(BF16)


def pre(keys, values, filters, n_peers):
    rows, width = keys.shape
    chans = width // n_peers
    args = [pltpu.with_memory_space_constraint(a, pltpu.HBM) for a in (keys, values, filters)]
    return pl.pallas_call(
        functools.partial(pre_kernel, n_peers),
        in_specs=[pl.BlockSpec(memory_space=pltpu.HBM)] * 3,
        out_specs=[pl.BlockSpec(memory_space=pltpu.VMEM)] * n_peers,
        out_shape=[jax.ShapeDtypeStruct((rows, 2 * chans), BF16)] * n_peers,
        scratch_shapes=[
            pltpu.VMEM((rows, width), BF16),
            pltpu.VMEM((rows, width), BF16),
            pltpu.VMEM((rows, width), F32),
            pltpu.SemaphoreType.DMA((2, 3)),
        ],
        compiler_params=pltpu.CompilerParams(vmem_limit_bytes=SMALL_VMEM),
        cost_estimate=pl.CostEstimate(
            flops=rows * width, bytes_accessed=12 * rows * width, transcendentals=0
        ),
    )(*args)


def slots_of(n_peers, back):
    half = n_peers // 2
    near, far = list(range(1, half)), list(range(half, n_peers))
    if back:
        return [0, near[0], far[2], far[0], far[1], near[1], far[3]] + near[2:]
    return [0, far[0], near[0]] + near[:0:-1] + far[1:]


def exchange(blocks, n_peers, back):
    return [
        lax.ppermute(block, "seq", [(i, i ^ slot) for i in range(n_peers)]) if slot else block
        for slot, block in zip(slots_of(n_peers, back), blocks)
    ]


def block_spectrum(table, block):
    return jnp.dot(table, jnp.concatenate([block, block], axis=0), preferred_element_type=F32)


def times(a, b):
    return a[0] * b[0] - a[1] * b[1], a[0] * b[1] + a[1] * b[0]


def plus(a, b):
    return b if a is None else (a[0] + b[0], a[1] + b[1])


def late_place(n_blocks):
    return lax.div(peer_of(slots_of(n_blocks, False)[-1]), 2)


def load(ref, at, row, step, rows, lanes):
    return tuple(ref[(*at, pl.ds(row + part * rows, step), lanes)] for part in range(2))


def mix_early(pair, step, spec_ref, part_ref):
    n_blocks, rows, chans = spec_ref.shape[0], spec_ref.shape[1] // 2, spec_ref.shape[2] // 2
    early = [j for j in range(n_blocks) if j // 2 != pair]

    @pl.loop(0, rows // step)
    def _(t):
        row = pl.multiple_of(t * step, step)
        signal = {j: load(spec_ref, (j,), row, step, rows, slice(0, chans)) for j in early}
        filt = {j: load(spec_ref, (j,), row, step, rows, slice(chans, 2 * chans)) for j in early}
        for i in range(n_blocks):
            total = None
            for d in early:
                if i - d in early:
                    total = plus(total, times(filt[d], signal[i - d]))
            if total is None:
                total = (jnp.zeros((step, chans), F32),) * 2
            for part in range(2):
                part_ref[i, pl.ds(row + part * rows, step)] = total[part]


def tables_kernel(fwd_hbm, bwd_hbm, *refs):
    fwd_ref, bwd_ref, sem = refs[-3:]
    copies = [
        pltpu.make_async_copy(fwd_hbm, fwd_ref, sem.at[0]),
        pltpu.make_async_copy(bwd_hbm, bwd_ref, sem.at[1]),
    ]
    for copy in copies:
        copy.start()
    for copy in copies:
        copy.wait()


def load_tables(fwd, bwd, after):
    whole = pl.BlockSpec(memory_space=pltpu.VMEM)
    args = [pltpu.with_memory_space_constraint(a, pltpu.HBM) for a in (fwd, bwd)]
    return pl.pallas_call(
        tables_kernel,
        in_specs=[pl.BlockSpec(memory_space=pltpu.HBM)] * 2
        + [pl.BlockSpec(memory_space=pl.ANY)] * len(after),
        out_specs=[whole] * 2,
        out_shape=[jax.ShapeDtypeStruct(t.shape, BF16) for t in (fwd, bwd)],
        scratch_shapes=[pltpu.SemaphoreType.DMA((2,))],
        compiler_params=pltpu.CompilerParams(vmem_limit_bytes=SMALL_VMEM),
        cost_estimate=pl.CostEstimate(flops=10**6, bytes_accessed=3 * 2**20, transcendentals=0),
    )(*args, *after)


def spectra_kernel(n_peers, fwd_ref, *refs):
    *in_refs, spec_ref, part_ref = refs
    for slot, in_ref in zip(slots_of(n_peers, False), in_refs):
        spec_ref[peer_of(slot)] = block_spectrum(fwd_ref[...], in_ref[...])
    for pair in range(n_peers // 2):
        pl.when(late_place(n_peers) == pair)(
            functools.partial(mix_early, pair, STEP, spec_ref, part_ref)
        )


def spectra(received, fwd, n_peers):
    rows, width = received[0].shape
    whole = pl.BlockSpec(memory_space=pltpu.VMEM)
    return pl.pallas_call(
        functools.partial(spectra_kernel, n_peers),
        in_specs=[whole] * (1 + len(received)),
        out_specs=[whole] * 2,
        out_shape=[
            jax.ShapeDtypeStruct((n_peers, 2 * rows, width), F32),
            jax.ShapeDtypeStruct((n_peers, 2 * rows, width // 2), F32),
        ],
        compiler_params=pltpu.CompilerParams(vmem_limit_bytes=CONV_VMEM),
        cost_estimate=pl.CostEstimate(
            flops=8 * len(received) * rows * rows * width, bytes_accessed=4 * 2**20, transcendentals=0
        ),
    )(fwd, *received)


def add_block(total, place, new, others, row, step, rows, chans):
    n_blocks = len(total)
    x_at, f_at = slice(0, chans), slice(chans, 2 * chans)
    x_new, f_new = load(new, (), row, step, rows, x_at), load(new, (), row, step, rows, f_at)
    for j, (ref, at) in others.items():
        if j + place < n_blocks:
            x_j = load(ref, at, row, step, rows, x_at)
            f_j = load(ref, at, row, step, rows, f_at)
            total[j + place] = plus(total[j + place], times(f_new, x_j))
            total[j + place] = plus(total[j + place], times(f_j, x_new))
    if 2 * place < n_blocks:
        total[2 * place] = plus(total[2 * place], times(f_new, x_new))


def early_blocks(place, n_blocks, spec_ref):
    return {j: (spec_ref, (j,)) for j in range(n_blocks) if j // 2 != place // 2}


def mix_middle(place, step, spec_ref, part_ref, new_ref, out_ref):
    n_blocks, rows, chans = spec_ref.shape[0], spec_ref.shape[1] // 2, spec_ref.shape[2] // 2
    others = early_blocks(place, n_blocks, spec_ref)

    @pl.loop(0, rows // step)
    def _(t):
        row = pl.multiple_of(t * step, step)
        total = [load(part_ref, (i,), row, step, rows, slice(0, chans)) for i in range(n_blocks)]
        add_block(total, place, new_ref, others, row, step, rows, chans)
        for i in range(n_blocks):
            for part in range(2):
                out_ref[i, pl.ds(row + part * rows, step)] = total[i][part]


def middle_kernel(fwd_ref, spec_ref, part_ref, in_ref, new_ref, out_ref):
    n_blocks = spec_ref.shape[0]
    new_ref[...] = block_spectrum(fwd_ref[...], in_ref[...])
    mine = peer_of(slots_of(n_blocks, False)[-2])
    for place in range(n_blocks):
        pl.when(mine == place)(
            functools.partial(mix_middle, place, STEP, spec_ref, part_ref, new_ref, out_ref)
        )


def middle(early, part, block, fwd):
    whole = pl.BlockSpec(memory_space=pltpu.VMEM)
    return pl.pallas_call(
        middle_kernel,
        in_specs=[whole] * 4,
        out_specs=[whole] * 2,
        out_shape=[jax.ShapeDtypeStruct(a.shape, F32) for a in (early[0], part)],
        compiler_params=pltpu.CompilerParams(vmem_limit_bytes=CONV_VMEM),
        cost_estimate=pl.CostEstimate(flops=10**9, bytes_accessed=4 * 2**20, transcendentals=0),
    )(fwd, early, part, block)


def mix_last(place, step, first, last, sign, spec_ref, part_ref, next_ref, new_ref, turned):
    n_blocks, rows, chans = spec_ref.shape[0], spec_ref.shape[1] // 2, spec_ref.shape[2] // 2
    others = early_blocks(place, n_blocks, spec_ref)
    others[place ^ 1] = (next_ref, ())

    @pl.loop(first // step, last // step)
    def _(t):
        row = pl.multiple_of(t * step, step)
        total = [load(part_ref, (i,), row, step, rows, slice(0, chans)) for i in range(n_blocks)]
        add_block(total, place, new_ref, others, row, step, rows, chans)
        for i in range(n_blocks):
            value = total[i]
            if i > 0:
                turn_re, turn_im = total[i - 1]
                if sign > 0:
                    value = value[0] - turn_im, value[1] + turn_re
                else:
                    value = value[0] + turn_im, value[1] - turn_re
            lanes = slice(i % 2 * chans, (i % 2 + 1) * chans)
            for part in range(2):
                high = value[part].astype(BF16)
                low = (value[part] - high.astype(F32)).astype(BF16)
                for c, piece in enumerate((high, high, low)):
                    turned[i // 2, pl.ds(row + (2 * c + part) * rows, step), lanes] = piece


def conv_kernel(fwd_ref, bwd_ref, spec_ref, part_ref, next_ref, in_ref, *refs):
    *out_refs, new_ref, turned = refs
    n_blocks, rows, chans = spec_ref.shape[0], in_ref.shape[0], in_ref.shape[1] // 2
    new_ref[...] = block_spectrum(fwd_ref[...], in_ref[...])

    def mix(place):
        for first, last, sign in ((0, rows // 2, 1), (rows // 2, rows, -1)):
            mix_last(place, STEP, first, last, sign, spec_ref, part_ref, next_ref, new_ref, turned)

    mine = peer_of(slots_of(n_blocks, False)[-1])
    for place in range(n_blocks):
        pl.when(mine == place)(functools.partial(mix, place))

    odd = lax.bitwise_and(lax.axis_index("seq"), 1) == 1
    by_slot = dict(zip(slots_of(n_blocks, True), out_refs))
    for slot in range(0, n_blocks, 2):
        pair = lax.div(peer_of(slot), 2)
        both = jnp.dot(bwd_ref[...], turned[pair], preferred_element_type=F32)
        left, right = both[:, :chans], both[:, chans:]
        by_slot[slot][...] = jnp.where(odd, right, left).astype(BF16)
        by_slot[slot + 1][...] = jnp.where(odd, left, right).astype(BF16)


def conv_fast(early, part, late, fwd, bwd):
    n_blocks = early.shape[0]
    rows, chans = late[0].shape[0], late[0].shape[1] // 2
    late_spec, part = middle(early, part, late[0], fwd)
    whole = pl.BlockSpec(memory_space=pltpu.VMEM)
    return pl.pallas_call(
        conv_kernel,
        in_specs=[whole] * 6,
        out_specs=[whole] * n_blocks,
        out_shape=[jax.ShapeDtypeStruct((rows, chans), BF16)] * n_blocks,
        scratch_shapes=[
            pltpu.VMEM((2 * rows, 2 * chans), F32),
            pltpu.VMEM((n_blocks // 2, 6 * rows, 2 * chans), BF16),
        ],
        compiler_params=pltpu.CompilerParams(vmem_limit_bytes=CONV_VMEM),
        cost_estimate=pl.CostEstimate(
            flops=16 * n_blocks * rows * rows * chans, bytes_accessed=4 * 2**20, transcendentals=0
        ),
    )(fwd, bwd, early, part, late_spec, late[1])


def conv_plain(received, fwd, bwd):
    n_blocks, rows, chans = received.shape[0], received.shape[1], received.shape[2] // 2
    exact = lax.Precision.HIGHEST
    fwd32 = fwd[:, :rows].astype(F32) + fwd[:, rows:].astype(F32)
    bwd32 = bwd[:, : 2 * rows].astype(F32) + bwd[:, 2 * rows : 4 * rows].astype(F32)
    sign = jnp.where(jnp.arange(rows) < rows // 2, 1.0, -1.0).astype(F32)[:, None]

    def spectrum(blocks):
        spec = jnp.einsum("kt,jtc->jkc", fwd32, blocks.astype(F32), precision=exact)
        return spec[:, :rows], spec[:, rows:]

    x_re, x_im = spectrum(received[:, :, :chans])
    f_re, f_im = spectrum(received[:, :, chans:])
    g_re = f_re.at[1:].add(-sign * f_im[:-1])
    g_im = f_im.at[1:].add(sign * f_re[:-1])

    def one(d, total):
        t_re, t_im = total
        later = (jnp.arange(n_blocks) >= d)[:, None, None]
        a_re = jnp.where(later, jnp.roll(x_re, d, axis=0), 0.0)
        a_im = jnp.where(later, jnp.roll(x_im, d, axis=0), 0.0)
        return (
            t_re + g_re[d] * a_re - g_im[d] * a_im,
            t_im + g_re[d] * a_im + g_im[d] * a_re,
        )

    zero = jnp.zeros_like(x_re)
    y_re, y_im = lax.fori_loop(0, n_blocks, one, (zero, zero))
    both = jnp.concatenate([y_re, y_im], axis=1)
    return jnp.einsum("tk,jkc->jtc", bwd32, both, precision=exact).astype(BF16)


def columns_of(other, across, piece, pieces, width):
    count = width // 4 // pieces
    place = lax.axis_index("fsdp")
    core, side = lax.rem(place, 2), lax.div(place, 2)
    block = 2 * (1 - side if across else side) + (1 - core if other else core)
    return pl.ds(pl.multiple_of((block * pieces + piece) * count, count), count)


def gate_slot(slot, queries_ref, keys_ref, values_ref, skip_ref, conv_ref):
    at = peer_block(slot, conv_ref.shape[1])
    product = keys_ref[:, at].astype(F32) * values_ref[:, at].astype(F32)
    mixed = conv_ref[...].astype(F32) + skip_ref[:, at] * product
    return (queries_ref[:, at].astype(F32) * mixed).astype(BF16)


def gate_early_kernel(n_peers, queries_ref, keys_ref, values_ref, skip_ref, weight_ref, *refs):
    conv_refs, (gated_ref, *part_refs) = refs[:-3], refs[-3:]
    chans = conv_refs[0].shape[1]
    slots = slots_of(n_peers, True)
    for slot, conv_ref in zip(slots, conv_refs):
        gated = gate_slot(slot, queries_ref, keys_ref, values_ref, skip_ref, conv_ref)
        gated_ref[:, peer_block(slot, chans)] = gated
    for slot in slots[len(conv_refs) :]:
        gated_ref[:, peer_block(slot, chans)] = jnp.zeros((gated_ref.shape[0], chans), BF16)
    for other, part_ref in zip((True, False), part_refs):
        columns = weight_ref[:, columns_of(other, True, 0, 1, weight_ref.shape[1])]
        part_ref[...] = jnp.dot(gated_ref[...], columns, preferred_element_type=F32)


def gate_early(queries, keys, values, skip, weight, conv, n_peers):
    rows, width = queries.shape
    out_width = weight.shape[1] // 4
    whole = pl.BlockSpec(memory_space=pltpu.VMEM)
    return pl.pallas_call(
        functools.partial(gate_early_kernel, n_peers),
        in_specs=[whole] * (5 + len(conv)),
        out_specs=[whole] * 3,
        out_shape=[jax.ShapeDtypeStruct((rows, width), BF16)]
        + [jax.ShapeDtypeStruct((rows, out_width), F32)] * 2,
        compiler_params=pltpu.CompilerParams(vmem_limit_bytes=PROJECT_VMEM),
        cost_estimate=pl.CostEstimate(
            flops=4 * rows * width * out_width, bytes_accessed=10 * rows * width, transcendentals=0
        ),
    )(queries, keys, values, skip, weight, *conv)


def late_product(late, late_slots, block, weight_ref, part_ref):
    chans = late.shape[1] // len(late_slots)
    at = columns_of(*block, weight_ref.shape[1])
    _, _, piece, pieces = block
    count = part_ref.shape[1] // pieces
    columns = jnp.concatenate([weight_ref[peer_block(s, chans), at] for s in late_slots], axis=0)
    part = part_ref[:, piece * count : (piece + 1) * count]
    return part + jnp.dot(late, columns, preferred_element_type=F32)


def gate_late_kernel(late_slots, block, queries_ref, keys_ref, values_ref, skip_ref, weight_ref, part_ref, *refs):
    *conv_refs, late_ref, sent_ref = refs
    chans = conv_refs[0].shape[1]
    for c, (slot, conv_ref) in enumerate(zip(late_slots, conv_refs)):
        gated = gate_slot(slot, queries_ref, keys_ref, values_ref, skip_ref, conv_ref)
        late_ref[:, c * chans : (c + 1) * chans] = gated
    total = late_product(late_ref[...], late_slots, block, weight_ref, part_ref)
    sent_ref[...] = total.astype(BF16)


def gate_late(queries, keys, values, skip, weight, part, conv, late_slots, block):
    rows, chans = conv[0].shape
    whole = pl.BlockSpec(memory_space=pltpu.VMEM)
    return pl.pallas_call(
        functools.partial(gate_late_kernel, late_slots, block),
        in_specs=[whole] * (6 + len(conv)),
        out_specs=[whole] * 2,
        out_shape=[
            jax.ShapeDtypeStruct((rows, chans * len(conv)), BF16),
            jax.ShapeDtypeStruct((rows, weight.shape[1] // 4 // block[-1]), BF16),
        ],
        compiler_params=pltpu.CompilerParams(vmem_limit_bytes=PROJECT_VMEM),
        cost_estimate=pl.CostEstimate(
            flops=rows * chans * weight.shape[1], bytes_accessed=2**20, transcendentals=0
        ),
    )(queries, keys, values, skip, weight, part, *conv)


def late_project_kernel(late_slots, blocks, weight_ref, late_ref, part_ref, *out_refs):
    for block, out_ref in zip(blocks, out_refs):
        total = late_product(late_ref[...], late_slots, block, weight_ref, part_ref)
        out_ref[...] = total.astype(out_ref.dtype)


def late_project(weight, late, part, late_slots, blocks, dtype):
    rows, depth = late.shape
    widths = [weight.shape[1] // 4 // pieces for *_, pieces in blocks]
    whole = pl.BlockSpec(memory_space=pltpu.VMEM)
    return pl.pallas_call(
        functools.partial(late_project_kernel, late_slots, blocks),
        in_specs=[whole] * 3,
        out_specs=[whole] * len(blocks),
        out_shape=[jax.ShapeDtypeStruct((rows, w), dtype) for w in widths],
        compiler_params=pltpu.CompilerParams(vmem_limit_bytes=PROJECT_VMEM),
        cost_estimate=pl.CostEstimate(
            flops=2 * rows * depth * sum(widths), bytes_accessed=2**20, transcendentals=0
        ),
    )(weight, late, part)


def assemble_kernel(late_slots, gated_ref, late_ref, out_ref):
    chans = late_ref.shape[1] // len(late_slots)
    out_ref[...] = gated_ref[...]
    for c, slot in enumerate(late_slots):
        out_ref[:, peer_block(slot, chans)] = late_ref[:, c * chans : (c + 1) * chans]


def assemble(gated, late, late_slots):
    whole = pl.BlockSpec(memory_space=pltpu.VMEM)
    return pl.pallas_call(
        functools.partial(assemble_kernel, late_slots),
        in_specs=[whole] * 2,
        out_specs=whole,
        out_shape=jax.ShapeDtypeStruct(gated.shape, BF16),
        compiler_params=pltpu.CompilerParams(vmem_limit_bytes=SMALL_VMEM),
        cost_estimate=pl.CostEstimate(flops=1000, bytes_accessed=2**20, transcendentals=0),
    )(gated, late)


def project_kernel(blocks, gated_ref, weight_ref, *out_refs):
    for block, out_ref in zip(blocks, out_refs):
        columns = weight_ref[:, columns_of(*block, weight_ref.shape[1])]
        total = jnp.dot(gated_ref[...], columns, preferred_element_type=F32)
        out_ref[...] = total.astype(out_ref.dtype)


def project(gated, weight, blocks, dtypes):
    rows, depth = gated.shape
    widths = [weight.shape[1] // 4 // pieces for *_, pieces in blocks]
    whole = pl.BlockSpec(memory_space=pltpu.VMEM)
    return pl.pallas_call(
        functools.partial(project_kernel, blocks),
        in_specs=[whole] * 2,
        out_specs=[whole] * len(blocks),
        out_shape=[jax.ShapeDtypeStruct((rows, w), t) for w, t in zip(widths, dtypes)],
        compiler_params=pltpu.CompilerParams(vmem_limit_bytes=PROJECT_VMEM),
        cost_estimate=pl.CostEstimate(
            flops=2 * rows * depth * sum(widths), bytes_accessed=2 * depth * sum(widths), transcendentals=0
        ),
    )(gated, weight)


def add_kernel(own_ref, arrived_ref, out_ref):
    total = own_ref[...] + arrived_ref[...].astype(F32)
    out_ref[...] = total.astype(out_ref.dtype)


def add(own, arrived):
    whole = pl.BlockSpec(memory_space=pltpu.VMEM)
    return pl.pallas_call(
        add_kernel,
        in_specs=[whole] * 2,
        out_specs=whole,
        out_shape=jax.ShapeDtypeStruct(arrived.shape, BF16),
        compiler_params=pltpu.CompilerParams(vmem_limit_bytes=SMALL_VMEM),
        cost_estimate=pl.CostEstimate(
            flops=arrived.size, bytes_accessed=8 * arrived.size, transcendentals=0
        ),
    )(own, arrived)


def mark_kernel(*refs):
    refs[-1][...] = jnp.zeros_like(refs[-1])


def mark(arrays):
    return pl.pallas_call(
        mark_kernel,
        in_specs=[pl.BlockSpec(memory_space=pl.ANY)] * len(arrays),
        out_specs=pl.BlockSpec(memory_space=pltpu.VMEM),
        out_shape=jax.ShapeDtypeStruct((8, 128), F32),
        compiler_params=pltpu.CompilerParams(vmem_limit_bytes=SMALL_VMEM),
        cost_estimate=pl.CostEstimate(flops=2 * 10**10, bytes_accessed=2**20, transcendentals=0),
    )(*arrays)


def finish_kernel(own_ref, near_ref, *refs):
    *arrived_refs, _, out_ref, stage, sem = refs
    width = out_ref.shape[1] // len(arrived_refs)
    steps = sem.shape[0]
    rows = out_ref.shape[0] // steps
    copies = []
    for step in range(steps):
        part = pl.ds(step * rows, rows)
        for c, arrived_ref in enumerate(arrived_refs):
            at = slice(c * width, (c + 1) * width)
            total = own_ref[part, at] + near_ref[part, at].astype(F32)
            stage[part, at] = (total + arrived_ref[part].astype(F32)).astype(stage.dtype)
        copies.append(pltpu.make_async_copy(stage.at[part], out_ref.at[part], sem.at[step]))
        copies[-1].start()
    for copy in copies:
        copy.wait()


def finish(own, near, arrived):
    rows, width = own.shape
    whole, anywhere = pl.BlockSpec(memory_space=pltpu.VMEM), pl.BlockSpec(memory_space=pl.ANY)
    return pl.pallas_call(
        finish_kernel,
        in_specs=[whole] * (2 + len(arrived)) + [anywhere],
        out_specs=anywhere,
        out_shape=jax.ShapeDtypeStruct((rows, width), BF16),
        scratch_shapes=[pltpu.VMEM((rows, width), BF16), pltpu.SemaphoreType.DMA((4,))],
        compiler_params=pltpu.CompilerParams(vmem_limit_bytes=SMALL_VMEM),
        cost_estimate=pl.CostEstimate(
            flops=rows * width, bytes_accessed=8 * rows * width, transcendentals=0
        ),
    )(own, near, *arrived, mark(arrived))


def body(pieces, tables, queries, keys, values, filters, skip_weight, out_weight):
    rows, width = keys.shape
    n_peers = lax.axis_size("seq")
    chans = width // n_peers
    fwd, bwd = (jnp.asarray(t) for t in tables)
    skip = skip_weight[None, :]
    in_chip = [(0, 1), (1, 0), (2, 3), (3, 2)]
    across = [(0, 2), (2, 0), (1, 3), (3, 1)]

    sends = [(True, True, c, pieces) for c in range(pieces)]
    keeps = [(False, True, c, pieces) for c in range(pieces)]

    if chans % 128 == 0 and n_peers == 8:
        blocks = pre(keys, values, filters, n_peers)
        received = exchange(blocks, n_peers, False)
        fwd, bwd = load_tables(fwd, bwd, received[1:2])
        early, part = spectra(received[:-2], fwd, n_peers)
        back = exchange(conv_fast(early, part, received[-2:], fwd, bwd), n_peers, True)
        slots = slots_of(n_peers, True)[-2:]
        gated, send_part, own_part = gate_early(
            queries, keys, values, skip, out_weight, back[:-2], n_peers
        )
        late, last = gate_late(
            queries, keys, values, skip, out_weight, send_part, back[-2:], slots, sends[-1]
        )
        sent = [
            *(late_project(out_weight, late, send_part, slots, [s], BF16)[0] for s in sends[:-1]),
            last,
        ]
        ours = late_project(out_weight, late, own_part, slots, keeps, F32)
        gated = assemble(gated, late, slots)
    else:
        product = keys.astype(F32) * values.astype(F32)
        parts = [a.astype(BF16).reshape(rows, n_peers, chans) for a in (product, filters)]
        sent = jnp.concatenate(parts, axis=2).transpose(1, 0, 2)
        received = lax.all_to_all(sent, "seq", split_axis=0, concat_axis=0, tiled=True)
        conv = conv_plain(received, fwd, bwd)
        back = lax.all_to_all(conv, "seq", split_axis=0, concat_axis=0, tiled=True)
        mixed = back.transpose(1, 0, 2).reshape(rows, width).astype(F32) + skip * product
        gated = (queries.astype(F32) * mixed).astype(BF16)
        sent = project(gated, out_weight, sends, [BF16] * pieces)
        ours = project(gated, out_weight, keeps, [F32] * pieces)

    theirs = [lax.ppermute(piece, "fsdp", in_chip) for piece in sent]
    arrived = [lax.ppermute(add(*pair), "fsdp", across) for pair in zip(ours, theirs)]
    blocks = [(True, False, 0, 1), (False, False, 0, 1)]
    sent, own = project(gated, out_weight, blocks, [BF16, F32])
    near = lax.ppermute(sent, "fsdp", in_chip)
    return finish(own, near, arrived)


def solution(mesh):
    in_specs = (
        P("seq", "fsdp"),
        P("seq", "fsdp"),
        P("seq", "fsdp"),
        P("seq", "fsdp"),
        P("fsdp"),
        P("fsdp", None),
    )
    out_specs = P("seq", "fsdp")

    def run(queries, keys, values, filters, skip_weight, out_weight):
        rows = keys.shape[0] // mesh.shape["seq"]
        fn = functools.partial(body, 2, make_tables(rows))
        return jax.shard_map(fn, mesh=mesh, in_specs=in_specs, out_specs=out_specs, check_vma=False)(
            queries, keys, values, filters, skip_weight, out_weight
        )

    return run
```

```python
import functools

import numpy as np

import jax
import jax.numpy as jnp
from jax import lax
from jax.experimental import pallas as pl
from jax.experimental.pallas import tpu as pltpu
from jax.sharding import PartitionSpec as P

BF16 = jnp.bfloat16
F32 = jnp.float32
CONV_VMEM = 24 * 2**20
PROJECT_VMEM = 24 * 2**20
SMALL_VMEM = 12 * 2**20
STEP = 16


def split_bf16(table):
    high = table.astype(BF16)
    return high, (table - high.astype(np.float64)).astype(BF16)


def make_tables(rows):
    order = np.concatenate([np.arange(0, rows, 2), np.arange(1, rows, 2)])
    times = np.arange(rows)
    angle = np.pi * (((2 * order[:, None] + 1) * times[None, :]) % (4 * rows)) / (2 * rows)
    forward = np.concatenate([np.cos(angle), -np.sin(angle)], axis=0)
    high, low = split_bf16(forward)
    back_high, back_low = split_bf16(forward.T / rows)
    return (
        np.concatenate([high, low], axis=1),
        np.concatenate([back_high, back_low, back_high], axis=1),
    )


def peer_of(slot):
    return lax.bitwise_xor(lax.axis_index("seq"), slot)


def peer_block(slot, size):
    return pl.ds(pl.multiple_of(peer_of(slot) * size, size), size)


def pre_kernel(n_peers, keys_hbm, values_hbm, filters_hbm, *refs):
    out_refs = refs[:n_peers]
    keys, values, filters, sem = refs[n_peers:]
    rows, width = keys.shape
    chans = width // n_peers
    steps = sem.shape[0]
    parts = [pl.ds(c * rows // steps, rows // steps) for c in range(steps)]
    pairs = ((keys_hbm, keys), (values_hbm, values), (filters_hbm, filters))
    copies = [
        [
            pltpu.make_async_copy(src.at[part], dst.at[part], sem.at[c, i])
            for i, (src, dst) in enumerate(pairs)
        ]
        for c, part in enumerate(parts)
    ]
    for group in copies:
        for copy in group:
            copy.start()
    for part, group in zip(parts, copies):
        for copy in group:
            copy.wait()
        for slot, out_ref in zip(slots_of(n_peers, False), out_refs):
            at = peer_block(slot, chans)
            product = keys[part, at].astype(F32) * values[part, at].astype(F32)
            out_ref[part, :chans] = product.astype(BF16)
            out_ref[part, chans:] = filters[part, at].astype(BF16)


def pre(keys, values, filters, n_peers):
    rows, width = keys.shape
    chans = width // n_peers
    args = [pltpu.with_memory_space_constraint(a, pltpu.HBM) for a in (keys, values, filters)]
    return pl.pallas_call(
        functools.partial(pre_kernel, n_peers),
        in_specs=[pl.BlockSpec(memory_space=pltpu.HBM)] * 3,
        out_specs=[pl.BlockSpec(memory_space=pltpu.VMEM)] * n_peers,
        out_shape=[jax.ShapeDtypeStruct((rows, 2 * chans), BF16)] * n_peers,
        scratch_shapes=[
            pltpu.VMEM((rows, width), BF16),
            pltpu.VMEM((rows, width), BF16),
            pltpu.VMEM((rows, width), F32),
            pltpu.SemaphoreType.DMA((2, 3)),
        ],
        compiler_params=pltpu.CompilerParams(vmem_limit_bytes=SMALL_VMEM),
        cost_estimate=pl.CostEstimate(
            flops=rows * width, bytes_accessed=12 * rows * width, transcendentals=0
        ),
    )(*args)


def slots_of(n_peers, back):
    half = n_peers // 2
    near, far = list(range(1, half)), list(range(half, n_peers))
    if back:
        return [0, near[0], far[2], far[0], near[1], far[1], far[3]] + near[2:]
    return [0, far[0], near[0]] + near[:0:-1] + far[1:]


def exchange(blocks, n_peers, back):
    return [
        lax.ppermute(block, "seq", [(i, i ^ slot) for i in range(n_peers)]) if slot else block
        for slot, block in zip(slots_of(n_peers, back), blocks)
    ]


def block_spectrum(table, block):
    return jnp.dot(table, jnp.concatenate([block, block], axis=0), preferred_element_type=F32)


def times(a, b):
    return a[0] * b[0] - a[1] * b[1], a[0] * b[1] + a[1] * b[0]


def plus(a, b):
    return b if a is None else (a[0] + b[0], a[1] + b[1])


def late_place(n_blocks):
    return lax.div(peer_of(slots_of(n_blocks, False)[-1]), 2)


def load(ref, at, row, step, rows, lanes):
    return tuple(ref[(*at, pl.ds(row + part * rows, step), lanes)] for part in range(2))


def mix_early(pair, step, spec_ref, part_ref):
    n_blocks, rows, chans = spec_ref.shape[0], spec_ref.shape[1] // 2, spec_ref.shape[2] // 2
    early = [j for j in range(n_blocks) if j // 2 != pair]

    @pl.loop(0, rows // step)
    def _(t):
        row = pl.multiple_of(t * step, step)
        signal = {j: load(spec_ref, (j,), row, step, rows, slice(0, chans)) for j in early}
        filt = {j: load(spec_ref, (j,), row, step, rows, slice(chans, 2 * chans)) for j in early}
        for i in range(n_blocks):
            total = None
            for d in early:
                if i - d in early:
                    total = plus(total, times(filt[d], signal[i - d]))
            if total is None:
                total = (jnp.zeros((step, chans), F32),) * 2
            for part in range(2):
                part_ref[i, pl.ds(row + part * rows, step)] = total[part]


def tables_kernel(fwd_hbm, bwd_hbm, *refs):
    fwd_ref, bwd_ref, sem = refs[-3:]
    copies = [
        pltpu.make_async_copy(fwd_hbm, fwd_ref, sem.at[0]),
        pltpu.make_async_copy(bwd_hbm, bwd_ref, sem.at[1]),
    ]
    for copy in copies:
        copy.start()
    for copy in copies:
        copy.wait()


def load_tables(fwd, bwd, after):
    whole = pl.BlockSpec(memory_space=pltpu.VMEM)
    args = [pltpu.with_memory_space_constraint(a, pltpu.HBM) for a in (fwd, bwd)]
    return pl.pallas_call(
        tables_kernel,
        in_specs=[pl.BlockSpec(memory_space=pltpu.HBM)] * 2
        + [pl.BlockSpec(memory_space=pl.ANY)] * len(after),
        out_specs=[whole] * 2,
        out_shape=[jax.ShapeDtypeStruct(t.shape, BF16) for t in (fwd, bwd)],
        scratch_shapes=[pltpu.SemaphoreType.DMA((2,))],
        compiler_params=pltpu.CompilerParams(vmem_limit_bytes=SMALL_VMEM),
        cost_estimate=pl.CostEstimate(flops=10**6, bytes_accessed=3 * 2**20, transcendentals=0),
    )(*args, *after)


def spectra_kernel(n_peers, fwd_ref, *refs):
    *in_refs, spec_ref, part_ref = refs
    for slot, in_ref in zip(slots_of(n_peers, False), in_refs):
        spec_ref[peer_of(slot)] = block_spectrum(fwd_ref[...], in_ref[...])
    for pair in range(n_peers // 2):
        pl.when(late_place(n_peers) == pair)(
            functools.partial(mix_early, pair, STEP, spec_ref, part_ref)
        )


def spectra(received, fwd, n_peers):
    rows, width = received[0].shape
    whole = pl.BlockSpec(memory_space=pltpu.VMEM)
    return pl.pallas_call(
        functools.partial(spectra_kernel, n_peers),
        in_specs=[whole] * (1 + len(received)),
        out_specs=[whole] * 2,
        out_shape=[
            jax.ShapeDtypeStruct((n_peers, 2 * rows, width), F32),
            jax.ShapeDtypeStruct((n_peers, 2 * rows, width // 2), F32),
        ],
        compiler_params=pltpu.CompilerParams(vmem_limit_bytes=CONV_VMEM),
        cost_estimate=pl.CostEstimate(
            flops=8 * len(received) * rows * rows * width, bytes_accessed=4 * 2**20, transcendentals=0
        ),
    )(fwd, *received)


def add_block(total, place, new, others, row, step, rows, chans):
    n_blocks = len(total)
    x_at, f_at = slice(0, chans), slice(chans, 2 * chans)
    x_new, f_new = load(new, (), row, step, rows, x_at), load(new, (), row, step, rows, f_at)
    for j, (ref, at) in others.items():
        if j + place < n_blocks:
            x_j = load(ref, at, row, step, rows, x_at)
            f_j = load(ref, at, row, step, rows, f_at)
            total[j + place] = plus(total[j + place], times(f_new, x_j))
            total[j + place] = plus(total[j + place], times(f_j, x_new))
    if 2 * place < n_blocks:
        total[2 * place] = plus(total[2 * place], times(f_new, x_new))


def early_blocks(place, n_blocks, spec_ref):
    return {j: (spec_ref, (j,)) for j in range(n_blocks) if j // 2 != place // 2}


def mix_middle(place, step, spec_ref, part_ref, new_ref, out_ref):
    n_blocks, rows, chans = spec_ref.shape[0], spec_ref.shape[1] // 2, spec_ref.shape[2] // 2
    others = early_blocks(place, n_blocks, spec_ref)

    @pl.loop(0, rows // step)
    def _(t):
        row = pl.multiple_of(t * step, step)
        total = [load(part_ref, (i,), row, step, rows, slice(0, chans)) for i in range(n_blocks)]
        add_block(total, place, new_ref, others, row, step, rows, chans)
        for i in range(n_blocks):
            for part in range(2):
                out_ref[i, pl.ds(row + part * rows, step)] = total[i][part]


def middle_kernel(fwd_ref, spec_ref, part_ref, in_ref, new_ref, out_ref):
    n_blocks = spec_ref.shape[0]
    new_ref[...] = block_spectrum(fwd_ref[...], in_ref[...])
    mine = peer_of(slots_of(n_blocks, False)[-2])
    for place in range(n_blocks):
        pl.when(mine == place)(
            functools.partial(mix_middle, place, STEP, spec_ref, part_ref, new_ref, out_ref)
        )


def middle(early, part, block, fwd):
    whole = pl.BlockSpec(memory_space=pltpu.VMEM)
    return pl.pallas_call(
        middle_kernel,
        in_specs=[whole] * 4,
        out_specs=[whole] * 2,
        out_shape=[jax.ShapeDtypeStruct(a.shape, F32) for a in (early[0], part)],
        compiler_params=pltpu.CompilerParams(vmem_limit_bytes=CONV_VMEM),
        cost_estimate=pl.CostEstimate(flops=10**9, bytes_accessed=4 * 2**20, transcendentals=0),
    )(fwd, early, part, block)


def mix_last(place, step, first, last, sign, spec_ref, part_ref, next_ref, new_ref, turned):
    n_blocks, rows, chans = spec_ref.shape[0], spec_ref.shape[1] // 2, spec_ref.shape[2] // 2
    others = early_blocks(place, n_blocks, spec_ref)
    others[place ^ 1] = (next_ref, ())

    @pl.loop(first // step, last // step)
    def _(t):
        row = pl.multiple_of(t * step, step)
        total = [load(part_ref, (i,), row, step, rows, slice(0, chans)) for i in range(n_blocks)]
        add_block(total, place, new_ref, others, row, step, rows, chans)
        for i in range(n_blocks):
            value = total[i]
            if i > 0:
                turn_re, turn_im = total[i - 1]
                if sign > 0:
                    value = value[0] - turn_im, value[1] + turn_re
                else:
                    value = value[0] + turn_im, value[1] - turn_re
            lanes = slice(i % 2 * chans, (i % 2 + 1) * chans)
            for part in range(2):
                high = value[part].astype(BF16)
                low = (value[part] - high.astype(F32)).astype(BF16)
                for c, piece in enumerate((high, high, low)):
                    turned[i // 2, pl.ds(row + (2 * c + part) * rows, step), lanes] = piece


def conv_kernel(fwd_ref, bwd_ref, spec_ref, part_ref, next_ref, in_ref, *refs):
    *out_refs, new_ref, turned = refs
    n_blocks, rows, chans = spec_ref.shape[0], in_ref.shape[0], in_ref.shape[1] // 2
    new_ref[...] = block_spectrum(fwd_ref[...], in_ref[...])

    def mix(place):
        for first, last, sign in ((0, rows // 2, 1), (rows // 2, rows, -1)):
            mix_last(place, STEP, first, last, sign, spec_ref, part_ref, next_ref, new_ref, turned)

    mine = peer_of(slots_of(n_blocks, False)[-1])
    for place in range(n_blocks):
        pl.when(mine == place)(functools.partial(mix, place))

    odd = lax.bitwise_and(lax.axis_index("seq"), 1) == 1
    by_slot = dict(zip(slots_of(n_blocks, True), out_refs))
    for slot in range(0, n_blocks, 2):
        pair = lax.div(peer_of(slot), 2)
        both = jnp.dot(bwd_ref[...], turned[pair], preferred_element_type=F32)
        left, right = both[:, :chans], both[:, chans:]
        by_slot[slot][...] = jnp.where(odd, right, left).astype(BF16)
        by_slot[slot + 1][...] = jnp.where(odd, left, right).astype(BF16)


def conv_fast(early, part, late, fwd, bwd):
    n_blocks = early.shape[0]
    rows, chans = late[0].shape[0], late[0].shape[1] // 2
    late_spec, part = middle(early, part, late[0], fwd)
    whole = pl.BlockSpec(memory_space=pltpu.VMEM)
    return pl.pallas_call(
        conv_kernel,
        in_specs=[whole] * 6,
        out_specs=[whole] * n_blocks,
        out_shape=[jax.ShapeDtypeStruct((rows, chans), BF16)] * n_blocks,
        scratch_shapes=[
            pltpu.VMEM((2 * rows, 2 * chans), F32),
            pltpu.VMEM((n_blocks // 2, 6 * rows, 2 * chans), BF16),
        ],
        compiler_params=pltpu.CompilerParams(vmem_limit_bytes=CONV_VMEM),
        cost_estimate=pl.CostEstimate(
            flops=16 * n_blocks * rows * rows * chans, bytes_accessed=4 * 2**20, transcendentals=0
        ),
    )(fwd, bwd, early, part, late_spec, late[1])


def conv_plain(received, fwd, bwd):
    n_blocks, rows, chans = received.shape[0], received.shape[1], received.shape[2] // 2
    exact = lax.Precision.HIGHEST
    fwd32 = fwd[:, :rows].astype(F32) + fwd[:, rows:].astype(F32)
    bwd32 = bwd[:, : 2 * rows].astype(F32) + bwd[:, 2 * rows : 4 * rows].astype(F32)
    sign = jnp.where(jnp.arange(rows) < rows // 2, 1.0, -1.0).astype(F32)[:, None]

    def spectrum(blocks):
        spec = jnp.einsum("kt,jtc->jkc", fwd32, blocks.astype(F32), precision=exact)
        return spec[:, :rows], spec[:, rows:]

    x_re, x_im = spectrum(received[:, :, :chans])
    f_re, f_im = spectrum(received[:, :, chans:])
    g_re = f_re.at[1:].add(-sign * f_im[:-1])
    g_im = f_im.at[1:].add(sign * f_re[:-1])

    def one(d, total):
        t_re, t_im = total
        later = (jnp.arange(n_blocks) >= d)[:, None, None]
        a_re = jnp.where(later, jnp.roll(x_re, d, axis=0), 0.0)
        a_im = jnp.where(later, jnp.roll(x_im, d, axis=0), 0.0)
        return (
            t_re + g_re[d] * a_re - g_im[d] * a_im,
            t_im + g_re[d] * a_im + g_im[d] * a_re,
        )

    zero = jnp.zeros_like(x_re)
    y_re, y_im = lax.fori_loop(0, n_blocks, one, (zero, zero))
    both = jnp.concatenate([y_re, y_im], axis=1)
    return jnp.einsum("tk,jkc->jtc", bwd32, both, precision=exact).astype(BF16)


def columns_of(other, across, piece, pieces, width):
    count = width // 4 // pieces
    place = lax.axis_index("fsdp")
    core, side = lax.rem(place, 2), lax.div(place, 2)
    block = 2 * (1 - side if across else side) + (1 - core if other else core)
    return pl.ds(pl.multiple_of((block * pieces + piece) * count, count), count)


def gate_slot(slot, queries_ref, keys_ref, values_ref, skip_ref, conv_ref):
    at = peer_block(slot, conv_ref.shape[1])
    product = keys_ref[:, at].astype(F32) * values_ref[:, at].astype(F32)
    mixed = conv_ref[...].astype(F32) + skip_ref[:, at] * product
    return (queries_ref[:, at].astype(F32) * mixed).astype(BF16)


def gate_early_kernel(n_peers, queries_ref, keys_ref, values_ref, skip_ref, weight_ref, *refs):
    conv_refs, (gated_ref, *part_refs) = refs[:-3], refs[-3:]
    chans = conv_refs[0].shape[1]
    slots = slots_of(n_peers, True)
    for slot, conv_ref in zip(slots, conv_refs):
        gated = gate_slot(slot, queries_ref, keys_ref, values_ref, skip_ref, conv_ref)
        gated_ref[:, peer_block(slot, chans)] = gated
    for slot in slots[len(conv_refs) :]:
        gated_ref[:, peer_block(slot, chans)] = jnp.zeros((gated_ref.shape[0], chans), BF16)
    for other, part_ref in zip((True, False), part_refs):
        columns = weight_ref[:, columns_of(other, True, 0, 1, weight_ref.shape[1])]
        part_ref[...] = jnp.dot(gated_ref[...], columns, preferred_element_type=F32)


def gate_early(queries, keys, values, skip, weight, conv, n_peers):
    rows, width = queries.shape
    out_width = weight.shape[1] // 4
    whole = pl.BlockSpec(memory_space=pltpu.VMEM)
    return pl.pallas_call(
        functools.partial(gate_early_kernel, n_peers),
        in_specs=[whole] * (5 + len(conv)),
        out_specs=[whole] * 3,
        out_shape=[jax.ShapeDtypeStruct((rows, width), BF16)]
        + [jax.ShapeDtypeStruct((rows, out_width), F32)] * 2,
        compiler_params=pltpu.CompilerParams(vmem_limit_bytes=PROJECT_VMEM),
        cost_estimate=pl.CostEstimate(
            flops=4 * rows * width * out_width, bytes_accessed=10 * rows * width, transcendentals=0
        ),
    )(queries, keys, values, skip, weight, *conv)


def late_product(late, late_slots, block, weight_ref, part_ref):
    chans = late.shape[1] // len(late_slots)
    at = columns_of(*block, weight_ref.shape[1])
    _, _, piece, pieces = block
    count = part_ref.shape[1] // pieces
    columns = jnp.concatenate([weight_ref[peer_block(s, chans), at] for s in late_slots], axis=0)
    part = part_ref[:, piece * count : (piece + 1) * count]
    return part + jnp.dot(late, columns, preferred_element_type=F32)


def gate_late_kernel(late_slots, block, queries_ref, keys_ref, values_ref, skip_ref, weight_ref, part_ref, *refs):
    *conv_refs, late_ref, sent_ref = refs
    chans = conv_refs[0].shape[1]
    for c, (slot, conv_ref) in enumerate(zip(late_slots, conv_refs)):
        gated = gate_slot(slot, queries_ref, keys_ref, values_ref, skip_ref, conv_ref)
        late_ref[:, c * chans : (c + 1) * chans] = gated
    total = late_product(late_ref[...], late_slots, block, weight_ref, part_ref)
    sent_ref[...] = total.astype(BF16)


def gate_late(queries, keys, values, skip, weight, part, conv, late_slots, block):
    rows, chans = conv[0].shape
    whole = pl.BlockSpec(memory_space=pltpu.VMEM)
    return pl.pallas_call(
        functools.partial(gate_late_kernel, late_slots, block),
        in_specs=[whole] * (6 + len(conv)),
        out_specs=[whole] * 2,
        out_shape=[
            jax.ShapeDtypeStruct((rows, chans * len(conv)), BF16),
            jax.ShapeDtypeStruct((rows, weight.shape[1] // 4 // block[-1]), BF16),
        ],
        compiler_params=pltpu.CompilerParams(vmem_limit_bytes=PROJECT_VMEM),
        cost_estimate=pl.CostEstimate(
            flops=rows * chans * weight.shape[1], bytes_accessed=2**20, transcendentals=0
        ),
    )(queries, keys, values, skip, weight, part, *conv)


def late_project_kernel(late_slots, blocks, weight_ref, late_ref, part_ref, *out_refs):
    for block, out_ref in zip(blocks, out_refs):
        total = late_product(late_ref[...], late_slots, block, weight_ref, part_ref)
        out_ref[...] = total.astype(out_ref.dtype)


def late_project(weight, late, part, late_slots, blocks, dtype):
    rows, depth = late.shape
    widths = [weight.shape[1] // 4 // pieces for *_, pieces in blocks]
    whole = pl.BlockSpec(memory_space=pltpu.VMEM)
    return pl.pallas_call(
        functools.partial(late_project_kernel, late_slots, blocks),
        in_specs=[whole] * 3,
        out_specs=[whole] * len(blocks),
        out_shape=[jax.ShapeDtypeStruct((rows, w), dtype) for w in widths],
        compiler_params=pltpu.CompilerParams(vmem_limit_bytes=PROJECT_VMEM),
        cost_estimate=pl.CostEstimate(
            flops=2 * rows * depth * sum(widths), bytes_accessed=2**20, transcendentals=0
        ),
    )(weight, late, part)


def assemble_kernel(late_slots, gated_ref, late_ref, out_ref):
    chans = late_ref.shape[1] // len(late_slots)
    out_ref[...] = gated_ref[...]
    for c, slot in enumerate(late_slots):
        out_ref[:, peer_block(slot, chans)] = late_ref[:, c * chans : (c + 1) * chans]


def assemble(gated, late, late_slots):
    whole = pl.BlockSpec(memory_space=pltpu.VMEM)
    return pl.pallas_call(
        functools.partial(assemble_kernel, late_slots),
        in_specs=[whole] * 2,
        out_specs=whole,
        out_shape=jax.ShapeDtypeStruct(gated.shape, BF16),
        compiler_params=pltpu.CompilerParams(vmem_limit_bytes=SMALL_VMEM),
        cost_estimate=pl.CostEstimate(flops=1000, bytes_accessed=2**20, transcendentals=0),
    )(gated, late)


def project_kernel(blocks, gated_ref, weight_ref, *out_refs):
    for block, out_ref in zip(blocks, out_refs):
        columns = weight_ref[:, columns_of(*block, weight_ref.shape[1])]
        total = jnp.dot(gated_ref[...], columns, preferred_element_type=F32)
        out_ref[...] = total.astype(out_ref.dtype)


def project(gated, weight, blocks, dtypes):
    rows, depth = gated.shape
    widths = [weight.shape[1] // 4 // pieces for *_, pieces in blocks]
    whole = pl.BlockSpec(memory_space=pltpu.VMEM)
    return pl.pallas_call(
        functools.partial(project_kernel, blocks),
        in_specs=[whole] * 2,
        out_specs=[whole] * len(blocks),
        out_shape=[jax.ShapeDtypeStruct((rows, w), t) for w, t in zip(widths, dtypes)],
        compiler_params=pltpu.CompilerParams(vmem_limit_bytes=PROJECT_VMEM),
        cost_estimate=pl.CostEstimate(
            flops=2 * rows * depth * sum(widths), bytes_accessed=2 * depth * sum(widths), transcendentals=0
        ),
    )(gated, weight)


def add_kernel(own_ref, arrived_ref, out_ref):
    total = own_ref[...] + arrived_ref[...].astype(F32)
    out_ref[...] = total.astype(out_ref.dtype)


def add(own, arrived):
    whole = pl.BlockSpec(memory_space=pltpu.VMEM)
    return pl.pallas_call(
        add_kernel,
        in_specs=[whole] * 2,
        out_specs=whole,
        out_shape=jax.ShapeDtypeStruct(arrived.shape, BF16),
        compiler_params=pltpu.CompilerParams(vmem_limit_bytes=SMALL_VMEM),
        cost_estimate=pl.CostEstimate(
            flops=arrived.size, bytes_accessed=8 * arrived.size, transcendentals=0
        ),
    )(own, arrived)


def mark_kernel(*refs):
    refs[-1][...] = jnp.zeros_like(refs[-1])


def mark(arrays):
    return pl.pallas_call(
        mark_kernel,
        in_specs=[pl.BlockSpec(memory_space=pl.ANY)] * len(arrays),
        out_specs=pl.BlockSpec(memory_space=pltpu.VMEM),
        out_shape=jax.ShapeDtypeStruct((8, 128), F32),
        compiler_params=pltpu.CompilerParams(vmem_limit_bytes=SMALL_VMEM),
        cost_estimate=pl.CostEstimate(flops=2 * 10**10, bytes_accessed=2**20, transcendentals=0),
    )(*arrays)


def finish_kernel(own_ref, near_ref, *refs):
    *arrived_refs, _, out_ref, stage, sem = refs
    width = out_ref.shape[1] // len(arrived_refs)
    steps = sem.shape[0]
    rows = out_ref.shape[0] // steps
    copies = []
    for step in range(steps):
        part = pl.ds(step * rows, rows)
        for c, arrived_ref in enumerate(arrived_refs):
            at = slice(c * width, (c + 1) * width)
            total = own_ref[part, at] + near_ref[part, at].astype(F32)
            stage[part, at] = (total + arrived_ref[part].astype(F32)).astype(stage.dtype)
        copies.append(pltpu.make_async_copy(stage.at[part], out_ref.at[part], sem.at[step]))
        copies[-1].start()
    for copy in copies:
        copy.wait()


def finish(own, near, arrived):
    rows, width = own.shape
    whole, anywhere = pl.BlockSpec(memory_space=pltpu.VMEM), pl.BlockSpec(memory_space=pl.ANY)
    return pl.pallas_call(
        finish_kernel,
        in_specs=[whole] * (2 + len(arrived)) + [anywhere],
        out_specs=anywhere,
        out_shape=jax.ShapeDtypeStruct((rows, width), BF16),
        scratch_shapes=[pltpu.VMEM((rows, width), BF16), pltpu.SemaphoreType.DMA((4,))],
        compiler_params=pltpu.CompilerParams(vmem_limit_bytes=SMALL_VMEM),
        cost_estimate=pl.CostEstimate(
            flops=rows * width, bytes_accessed=8 * rows * width, transcendentals=0
        ),
    )(own, near, *arrived, mark(arrived))


def body(pieces, tables, queries, keys, values, filters, skip_weight, out_weight):
    rows, width = keys.shape
    n_peers = lax.axis_size("seq")
    chans = width // n_peers
    fwd, bwd = (jnp.asarray(t) for t in tables)
    skip = skip_weight[None, :]
    in_chip = [(0, 1), (1, 0), (2, 3), (3, 2)]
    across = [(0, 2), (2, 0), (1, 3), (3, 1)]

    sends = [(True, True, c, pieces) for c in range(pieces)]
    keeps = [(False, True, c, pieces) for c in range(pieces)]

    if chans % 128 == 0 and n_peers == 8:
        blocks = pre(keys, values, filters, n_peers)
        received = exchange(blocks, n_peers, False)
        fwd, bwd = load_tables(fwd, bwd, received[1:2])
        early, part = spectra(received[:-2], fwd, n_peers)
        back = exchange(conv_fast(early, part, received[-2:], fwd, bwd), n_peers, True)
        slots = slots_of(n_peers, True)[-3:]
        gated, send_part, own_part = gate_early(
            queries, keys, values, skip, out_weight, back[:-3], n_peers
        )
        late, last = gate_late(
            queries, keys, values, skip, out_weight, send_part, back[-3:], slots, sends[-1]
        )
        sent = [
            *(late_project(out_weight, late, send_part, slots, [s], BF16)[0] for s in sends[:-1]),
            last,
        ]
        ours = late_project(out_weight, late, own_part, slots, keeps, F32)
        gated = assemble(gated, late, slots)
    else:
        product = keys.astype(F32) * values.astype(F32)
        parts = [a.astype(BF16).reshape(rows, n_peers, chans) for a in (product, filters)]
        sent = jnp.concatenate(parts, axis=2).transpose(1, 0, 2)
        received = lax.all_to_all(sent, "seq", split_axis=0, concat_axis=0, tiled=True)
        conv = conv_plain(received, fwd, bwd)
        back = lax.all_to_all(conv, "seq", split_axis=0, concat_axis=0, tiled=True)
        mixed = back.transpose(1, 0, 2).reshape(rows, width).astype(F32) + skip * product
        gated = (queries.astype(F32) * mixed).astype(BF16)
        sent = project(gated, out_weight, sends, [BF16] * pieces)
        ours = project(gated, out_weight, keeps, [F32] * pieces)

    theirs = [lax.ppermute(piece, "fsdp", in_chip) for piece in sent]
    arrived = [lax.ppermute(add(*pair), "fsdp", across) for pair in zip(ours, theirs)]
    blocks = [(True, False, 0, 1), (False, False, 0, 1)]
    sent, own = project(gated, out_weight, blocks, [BF16, F32])
    near = lax.ppermute(sent, "fsdp", in_chip)
    return finish(own, near, arrived)


def solution(mesh):
    in_specs = (
        P("seq", "fsdp"),
        P("seq", "fsdp"),
        P("seq", "fsdp"),
        P("seq", "fsdp"),
        P("fsdp"),
        P("fsdp", None),
    )
    out_specs = P("seq", "fsdp")

    def run(queries, keys, values, filters, skip_weight, out_weight):
        rows = keys.shape[0] // mesh.shape["seq"]
        fn = functools.partial(body, 2, make_tables(rows))
        return jax.shard_map(fn, mesh=mesh, in_specs=in_specs, out_specs=out_specs, check_vma=False)(
            queries, keys, values, filters, skip_weight, out_weight
        )

    return run
```

```python
import functools

import numpy as np

import jax
import jax.numpy as jnp
from jax import lax
from jax.experimental import pallas as pl
from jax.experimental.pallas import tpu as pltpu
from jax.sharding import PartitionSpec as P

BF16 = jnp.bfloat16
F32 = jnp.float32
CONV_VMEM = 24 * 2**20
PROJECT_VMEM = 24 * 2**20
SMALL_VMEM = 12 * 2**20
STEP = 16


def split_bf16(table):
    high = table.astype(BF16)
    return high, (table - high.astype(np.float64)).astype(BF16)


def make_tables(rows):
    order = np.concatenate([np.arange(0, rows, 2), np.arange(1, rows, 2)])
    times = np.arange(rows)
    angle = np.pi * (((2 * order[:, None] + 1) * times[None, :]) % (4 * rows)) / (2 * rows)
    forward = np.concatenate([np.cos(angle), -np.sin(angle)], axis=0)
    high, low = split_bf16(forward)
    back_high, back_low = split_bf16(forward.T / rows)
    return (
        np.concatenate([high, low], axis=1),
        np.concatenate([back_high, back_low, back_high], axis=1),
    )


def peer_of(slot):
    return lax.bitwise_xor(lax.axis_index("seq"), slot)


def peer_block(slot, size):
    return pl.ds(pl.multiple_of(peer_of(slot) * size, size), size)


def pre_kernel(n_peers, keys_hbm, values_hbm, filters_hbm, *refs):
    out_refs = refs[:n_peers]
    keys, values, filters, sem = refs[n_peers:]
    rows, width = keys.shape
    chans = width // n_peers
    steps = sem.shape[0]
    parts = [pl.ds(c * rows // steps, rows // steps) for c in range(steps)]
    pairs = ((keys_hbm, keys), (values_hbm, values), (filters_hbm, filters))
    copies = [
        [
            pltpu.make_async_copy(src.at[part], dst.at[part], sem.at[c, i])
            for i, (src, dst) in enumerate(pairs)
        ]
        for c, part in enumerate(parts)
    ]
    for group in copies:
        for copy in group:
            copy.start()
    for part, group in zip(parts, copies):
        for copy in group:
            copy.wait()
        for slot, out_ref in zip(slots_of(n_peers, False), out_refs):
            at = peer_block(slot, chans)
            product = keys[part, at].astype(F32) * values[part, at].astype(F32)
            out_ref[part, :chans] = product.astype(BF16)
            out_ref[part, chans:] = filters[part, at].astype(BF16)


def pre(keys, values, filters, n_peers):
    rows, width = keys.shape
    chans = width // n_peers
    args = [pltpu.with_memory_space_constraint(a, pltpu.HBM) for a in (keys, values, filters)]
    return pl.pallas_call(
        functools.partial(pre_kernel, n_peers),
        in_specs=[pl.BlockSpec(memory_space=pltpu.HBM)] * 3,
        out_specs=[pl.BlockSpec(memory_space=pltpu.VMEM)] * n_peers,
        out_shape=[jax.ShapeDtypeStruct((rows, 2 * chans), BF16)] * n_peers,
        scratch_shapes=[
            pltpu.VMEM((rows, width), BF16),
            pltpu.VMEM((rows, width), BF16),
            pltpu.VMEM((rows, width), F32),
            pltpu.SemaphoreType.DMA((2, 3)),
        ],
        compiler_params=pltpu.CompilerParams(vmem_limit_bytes=SMALL_VMEM),
        cost_estimate=pl.CostEstimate(
            flops=rows * width, bytes_accessed=12 * rows * width, transcendentals=0
        ),
    )(*args)


def slots_of(n_peers, back):
    half = n_peers // 2
    near, far = list(range(1, half)), list(range(half, n_peers))
    if back:
        return [0, near[0], far[2], far[0], near[1], far[1], far[3]] + near[2:]
    return [0, far[0], near[0]] + near[:0:-1] + [far[1], far[3], far[2]]


def exchange(blocks, n_peers, back):
    return [
        lax.ppermute(block, "seq", [(i, i ^ slot) for i in range(n_peers)]) if slot else block
        for slot, block in zip(slots_of(n_peers, back), blocks)
    ]


def block_spectrum(table, block):
    return jnp.dot(table, jnp.concatenate([block, block], axis=0), preferred_element_type=F32)


def times(a, b):
    return a[0] * b[0] - a[1] * b[1], a[0] * b[1] + a[1] * b[0]


def plus(a, b):
    return b if a is None else (a[0] + b[0], a[1] + b[1])


def late_place(n_blocks):
    return lax.div(peer_of(slots_of(n_blocks, False)[-1]), 2)


def load(ref, at, row, step, rows, lanes):
    return tuple(ref[(*at, pl.ds(row + part * rows, step), lanes)] for part in range(2))


def mix_early(pair, step, spec_ref, part_ref):
    n_blocks, rows, chans = spec_ref.shape[0], spec_ref.shape[1] // 2, spec_ref.shape[2] // 2
    early = [j for j in range(n_blocks) if j // 2 != pair]

    @pl.loop(0, rows // step)
    def _(t):
        row = pl.multiple_of(t * step, step)
        signal = {j: load(spec_ref, (j,), row, step, rows, slice(0, chans)) for j in early}
        filt = {j: load(spec_ref, (j,), row, step, rows, slice(chans, 2 * chans)) for j in early}
        for i in range(n_blocks):
            total = None
            for d in early:
                if i - d in early:
                    total = plus(total, times(filt[d], signal[i - d]))
            if total is None:
                total = (jnp.zeros((step, chans), F32),) * 2
            for part in range(2):
                part_ref[i, pl.ds(row + part * rows, step)] = total[part]


def tables_kernel(fwd_hbm, bwd_hbm, *refs):
    fwd_ref, bwd_ref, sem = refs[-3:]
    copies = [
        pltpu.make_async_copy(fwd_hbm, fwd_ref, sem.at[0]),
        pltpu.make_async_copy(bwd_hbm, bwd_ref, sem.at[1]),
    ]
    for copy in copies:
        copy.start()
    for copy in copies:
        copy.wait()


def load_tables(fwd, bwd, after):
    whole = pl.BlockSpec(memory_space=pltpu.VMEM)
    args = [pltpu.with_memory_space_constraint(a, pltpu.HBM) for a in (fwd, bwd)]
    return pl.pallas_call(
        tables_kernel,
        in_specs=[pl.BlockSpec(memory_space=pltpu.HBM)] * 2
        + [pl.BlockSpec(memory_space=pl.ANY)] * len(after),
        out_specs=[whole] * 2,
        out_shape=[jax.ShapeDtypeStruct(t.shape, BF16) for t in (fwd, bwd)],
        scratch_shapes=[pltpu.SemaphoreType.DMA((2,))],
        compiler_params=pltpu.CompilerParams(vmem_limit_bytes=SMALL_VMEM),
        cost_estimate=pl.CostEstimate(flops=10**6, bytes_accessed=3 * 2**20, transcendentals=0),
    )(*args, *after)


def spectra_kernel(n_peers, fwd_ref, *refs):
    *in_refs, spec_ref, part_ref = refs
    for slot, in_ref in zip(slots_of(n_peers, False), in_refs):
        spec_ref[peer_of(slot)] = block_spectrum(fwd_ref[...], in_ref[...])
    for pair in range(n_peers // 2):
        pl.when(late_place(n_peers) == pair)(
            functools.partial(mix_early, pair, STEP, spec_ref, part_ref)
        )


def spectra(received, fwd, n_peers):
    rows, width = received[0].shape
    whole = pl.BlockSpec(memory_space=pltpu.VMEM)
    return pl.pallas_call(
        functools.partial(spectra_kernel, n_peers),
        in_specs=[whole] * (1 + len(received)),
        out_specs=[whole] * 2,
        out_shape=[
            jax.ShapeDtypeStruct((n_peers, 2 * rows, width), F32),
            jax.ShapeDtypeStruct((n_peers, 2 * rows, width // 2), F32),
        ],
        compiler_params=pltpu.CompilerParams(vmem_limit_bytes=CONV_VMEM),
        cost_estimate=pl.CostEstimate(
            flops=8 * len(received) * rows * rows * width, bytes_accessed=4 * 2**20, transcendentals=0
        ),
    )(fwd, *received)


def add_block(total, place, new, others, row, step, rows, chans):
    n_blocks = len(total)
    x_at, f_at = slice(0, chans), slice(chans, 2 * chans)
    x_new, f_new = load(new, (), row, step, rows, x_at), load(new, (), row, step, rows, f_at)
    for j, (ref, at) in others.items():
        if j + place < n_blocks:
            x_j = load(ref, at, row, step, rows, x_at)
            f_j = load(ref, at, row, step, rows, f_at)
            total[j + place] = plus(total[j + place], times(f_new, x_j))
            total[j + place] = plus(total[j + place], times(f_j, x_new))
    if 2 * place < n_blocks:
        total[2 * place] = plus(total[2 * place], times(f_new, x_new))


def early_blocks(place, n_blocks, spec_ref):
    return {j: (spec_ref, (j,)) for j in range(n_blocks) if j // 2 != place // 2}


def mix_middle(place, step, spec_ref, part_ref, new_ref, out_ref):
    n_blocks, rows, chans = spec_ref.shape[0], spec_ref.shape[1] // 2, spec_ref.shape[2] // 2
    others = early_blocks(place, n_blocks, spec_ref)

    @pl.loop(0, rows // step)
    def _(t):
        row = pl.multiple_of(t * step, step)
        total = [load(part_ref, (i,), row, step, rows, slice(0, chans)) for i in range(n_blocks)]
        add_block(total, place, new_ref, others, row, step, rows, chans)
        for i in range(n_blocks):
            for part in range(2):
                out_ref[i, pl.ds(row + part * rows, step)] = total[i][part]


def middle_kernel(fwd_ref, spec_ref, part_ref, in_ref, new_ref, out_ref):
    n_blocks = spec_ref.shape[0]
    new_ref[...] = block_spectrum(fwd_ref[...], in_ref[...])
    mine = peer_of(slots_of(n_blocks, False)[-2])
    for place in range(n_blocks):
        pl.when(mine == place)(
            functools.partial(mix_middle, place, STEP, spec_ref, part_ref, new_ref, out_ref)
        )


def middle(early, part, block, fwd):
    whole = pl.BlockSpec(memory_space=pltpu.VMEM)
    return pl.pallas_call(
        middle_kernel,
        in_specs=[whole] * 4,
        out_specs=[whole] * 2,
        out_shape=[jax.ShapeDtypeStruct(a.shape, F32) for a in (early[0], part)],
        compiler_params=pltpu.CompilerParams(vmem_limit_bytes=CONV_VMEM),
        cost_estimate=pl.CostEstimate(flops=10**9, bytes_accessed=4 * 2**20, transcendentals=0),
    )(fwd, early, part, block)


def mix_last(place, step, first, last, sign, spec_ref, part_ref, next_ref, new_ref, turned):
    n_blocks, rows, chans = spec_ref.shape[0], spec_ref.shape[1] // 2, spec_ref.shape[2] // 2
    others = early_blocks(place, n_blocks, spec_ref)
    others[place ^ 1] = (next_ref, ())

    @pl.loop(first // step, last // step)
    def _(t):
        row = pl.multiple_of(t * step, step)
        total = [load(part_ref, (i,), row, step, rows, slice(0, chans)) for i in range(n_blocks)]
        add_block(total, place, new_ref, others, row, step, rows, chans)
        for i in range(n_blocks):
            value = total[i]
            if i > 0:
                turn_re, turn_im = total[i - 1]
                if sign > 0:
                    value = value[0] - turn_im, value[1] + turn_re
                else:
                    value = value[0] + turn_im, value[1] - turn_re
            lanes = slice(i % 2 * chans, (i % 2 + 1) * chans)
            for part in range(2):
                high = value[part].astype(BF16)
                low = (value[part] - high.astype(F32)).astype(BF16)
                for c, piece in enumerate((high, high, low)):
                    turned[i // 2, pl.ds(row + (2 * c + part) * rows, step), lanes] = piece


def conv_kernel(fwd_ref, bwd_ref, spec_ref, part_ref, next_ref, in_ref, *refs):
    *out_refs, new_ref, turned = refs
    n_blocks, rows, chans = spec_ref.shape[0], in_ref.shape[0], in_ref.shape[1] // 2
    new_ref[...] = block_spectrum(fwd_ref[...], in_ref[...])

    def mix(place):
        for first, last, sign in ((0, rows // 2, 1), (rows // 2, rows, -1)):
            mix_last(place, STEP, first, last, sign, spec_ref, part_ref, next_ref, new_ref, turned)

    mine = peer_of(slots_of(n_blocks, False)[-1])
    for place in range(n_blocks):
        pl.when(mine == place)(functools.partial(mix, place))

    odd = lax.bitwise_and(lax.axis_index("seq"), 1) == 1
    by_slot = dict(zip(slots_of(n_blocks, True), out_refs))
    for slot in range(0, n_blocks, 2):
        pair = lax.div(peer_of(slot), 2)
        both = jnp.dot(bwd_ref[...], turned[pair], preferred_element_type=F32)
        left, right = both[:, :chans], both[:, chans:]
        by_slot[slot][...] = jnp.where(odd, right, left).astype(BF16)
        by_slot[slot + 1][...] = jnp.where(odd, left, right).astype(BF16)


def conv_fast(early, part, late, fwd, bwd):
    n_blocks = early.shape[0]
    rows, chans = late[0].shape[0], late[0].shape[1] // 2
    late_spec, part = middle(early, part, late[0], fwd)
    whole = pl.BlockSpec(memory_space=pltpu.VMEM)
    return pl.pallas_call(
        conv_kernel,
        in_specs=[whole] * 6,
        out_specs=[whole] * n_blocks,
        out_shape=[jax.ShapeDtypeStruct((rows, chans), BF16)] * n_blocks,
        scratch_shapes=[
            pltpu.VMEM((2 * rows, 2 * chans), F32),
            pltpu.VMEM((n_blocks // 2, 6 * rows, 2 * chans), BF16),
        ],
        compiler_params=pltpu.CompilerParams(vmem_limit_bytes=CONV_VMEM),
        cost_estimate=pl.CostEstimate(
            flops=16 * n_blocks * rows * rows * chans, bytes_accessed=4 * 2**20, transcendentals=0
        ),
    )(fwd, bwd, early, part, late_spec, late[1])


def conv_plain(received, fwd, bwd):
    n_blocks, rows, chans = received.shape[0], received.shape[1], received.shape[2] // 2
    exact = lax.Precision.HIGHEST
    fwd32 = fwd[:, :rows].astype(F32) + fwd[:, rows:].astype(F32)
    bwd32 = bwd[:, : 2 * rows].astype(F32) + bwd[:, 2 * rows : 4 * rows].astype(F32)
    sign = jnp.where(jnp.arange(rows) < rows // 2, 1.0, -1.0).astype(F32)[:, None]

    def spectrum(blocks):
        spec = jnp.einsum("kt,jtc->jkc", fwd32, blocks.astype(F32), precision=exact)
        return spec[:, :rows], spec[:, rows:]

    x_re, x_im = spectrum(received[:, :, :chans])
    f_re, f_im = spectrum(received[:, :, chans:])
    g_re = f_re.at[1:].add(-sign * f_im[:-1])
    g_im = f_im.at[1:].add(sign * f_re[:-1])

    def one(d, total):
        t_re, t_im = total
        later = (jnp.arange(n_blocks) >= d)[:, None, None]
        a_re = jnp.where(later, jnp.roll(x_re, d, axis=0), 0.0)
        a_im = jnp.where(later, jnp.roll(x_im, d, axis=0), 0.0)
        return (
            t_re + g_re[d] * a_re - g_im[d] * a_im,
            t_im + g_re[d] * a_im + g_im[d] * a_re,
        )

    zero = jnp.zeros_like(x_re)
    y_re, y_im = lax.fori_loop(0, n_blocks, one, (zero, zero))
    both = jnp.concatenate([y_re, y_im], axis=1)
    return jnp.einsum("tk,jkc->jtc", bwd32, both, precision=exact).astype(BF16)


def columns_of(other, across, piece, pieces, width):
    count = width // 4 // pieces
    place = lax.axis_index("fsdp")
    core, side = lax.rem(place, 2), lax.div(place, 2)
    block = 2 * (1 - side if across else side) + (1 - core if other else core)
    return pl.ds(pl.multiple_of((block * pieces + piece) * count, count), count)


def gate_slot(slot, queries_ref, keys_ref, values_ref, skip_ref, conv_ref):
    at = peer_block(slot, conv_ref.shape[1])
    product = keys_ref[:, at].astype(F32) * values_ref[:, at].astype(F32)
    mixed = conv_ref[...].astype(F32) + skip_ref[:, at] * product
    return (queries_ref[:, at].astype(F32) * mixed).astype(BF16)


def gate_early_kernel(n_peers, queries_ref, keys_ref, values_ref, skip_ref, weight_ref, *refs):
    conv_refs, (gated_ref, *part_refs) = refs[:-3], refs[-3:]
    chans = conv_refs[0].shape[1]
    slots = slots_of(n_peers, True)
    for slot, conv_ref in zip(slots, conv_refs):
        gated = gate_slot(slot, queries_ref, keys_ref, values_ref, skip_ref, conv_ref)
        gated_ref[:, peer_block(slot, chans)] = gated
    for slot in slots[len(conv_refs) :]:
        gated_ref[:, peer_block(slot, chans)] = jnp.zeros((gated_ref.shape[0], chans), BF16)
    for other, part_ref in zip((True, False), part_refs):
        columns = weight_ref[:, columns_of(other, True, 0, 1, weight_ref.shape[1])]
        part_ref[...] = jnp.dot(gated_ref[...], columns, preferred_element_type=F32)


def gate_early(queries, keys, values, skip, weight, conv, n_peers):
    rows, width = queries.shape
    out_width = weight.shape[1] // 4
    whole = pl.BlockSpec(memory_space=pltpu.VMEM)
    return pl.pallas_call(
        functools.partial(gate_early_kernel, n_peers),
        in_specs=[whole] * (5 + len(conv)),
        out_specs=[whole] * 3,
        out_shape=[jax.ShapeDtypeStruct((rows, width), BF16)]
        + [jax.ShapeDtypeStruct((rows, out_width), F32)] * 2,
        compiler_params=pltpu.CompilerParams(vmem_limit_bytes=PROJECT_VMEM),
        cost_estimate=pl.CostEstimate(
            flops=4 * rows * width * out_width, bytes_accessed=10 * rows * width, transcendentals=0
        ),
    )(queries, keys, values, skip, weight, *conv)


def late_product(late, late_slots, block, weight_ref, part_ref):
    chans = late.shape[1] // len(late_slots)
    at = columns_of(*block, weight_ref.shape[1])
    _, _, piece, pieces = block
    count = part_ref.shape[1] // pieces
    columns = jnp.concatenate([weight_ref[peer_block(s, chans), at] for s in late_slots], axis=0)
    part = part_ref[:, piece * count : (piece + 1) * count]
    return part + jnp.dot(late, columns, preferred_element_type=F32)


def gate_late_kernel(late_slots, block, queries_ref, keys_ref, values_ref, skip_ref, weight_ref, part_ref, *refs):
    *conv_refs, late_ref, sent_ref = refs
    chans = conv_refs[0].shape[1]
    for c, (slot, conv_ref) in enumerate(zip(late_slots, conv_refs)):
        gated = gate_slot(slot, queries_ref, keys_ref, values_ref, skip_ref, conv_ref)
        late_ref[:, c * chans : (c + 1) * chans] = gated
    total = late_product(late_ref[...], late_slots, block, weight_ref, part_ref)
    sent_ref[...] = total.astype(BF16)


def gate_late(queries, keys, values, skip, weight, part, conv, late_slots, block):
    rows, chans = conv[0].shape
    whole = pl.BlockSpec(memory_space=pltpu.VMEM)
    return pl.pallas_call(
        functools.partial(gate_late_kernel, late_slots, block),
        in_specs=[whole] * (6 + len(conv)),
        out_specs=[whole] * 2,
        out_shape=[
            jax.ShapeDtypeStruct((rows, chans * len(conv)), BF16),
            jax.ShapeDtypeStruct((rows, weight.shape[1] // 4 // block[-1]), BF16),
        ],
        compiler_params=pltpu.CompilerParams(vmem_limit_bytes=PROJECT_VMEM),
        cost_estimate=pl.CostEstimate(
            flops=rows * chans * weight.shape[1], bytes_accessed=2**20, transcendentals=0
        ),
    )(queries, keys, values, skip, weight, part, *conv)


def late_project_kernel(late_slots, blocks, weight_ref, late_ref, part_ref, *out_refs):
    for block, out_ref in zip(blocks, out_refs):
        total = late_product(late_ref[...], late_slots, block, weight_ref, part_ref)
        out_ref[...] = total.astype(out_ref.dtype)


def late_project(weight, late, part, late_slots, blocks, dtype):
    rows, depth = late.shape
    widths = [weight.shape[1] // 4 // pieces for *_, pieces in blocks]
    whole = pl.BlockSpec(memory_space=pltpu.VMEM)
    return pl.pallas_call(
        functools.partial(late_project_kernel, late_slots, blocks),
        in_specs=[whole] * 3,
        out_specs=[whole] * len(blocks),
        out_shape=[jax.ShapeDtypeStruct((rows, w), dtype) for w in widths],
        compiler_params=pltpu.CompilerParams(vmem_limit_bytes=PROJECT_VMEM),
        cost_estimate=pl.CostEstimate(
            flops=2 * rows * depth * sum(widths), bytes_accessed=2**20, transcendentals=0
        ),
    )(weight, late, part)


def assemble_kernel(late_slots, gated_ref, late_ref, out_ref):
    chans = late_ref.shape[1] // len(late_slots)
    out_ref[...] = gated_ref[...]
    for c, slot in enumerate(late_slots):
        out_ref[:, peer_block(slot, chans)] = late_ref[:, c * chans : (c + 1) * chans]


def assemble(gated, late, late_slots):
    whole = pl.BlockSpec(memory_space=pltpu.VMEM)
    return pl.pallas_call(
        functools.partial(assemble_kernel, late_slots),
        in_specs=[whole] * 2,
        out_specs=whole,
        out_shape=jax.ShapeDtypeStruct(gated.shape, BF16),
        compiler_params=pltpu.CompilerParams(vmem_limit_bytes=SMALL_VMEM),
        cost_estimate=pl.CostEstimate(flops=1000, bytes_accessed=2**20, transcendentals=0),
    )(gated, late)


def project_kernel(blocks, gated_ref, weight_ref, *out_refs):
    for block, out_ref in zip(blocks, out_refs):
        columns = weight_ref[:, columns_of(*block, weight_ref.shape[1])]
        total = jnp.dot(gated_ref[...], columns, preferred_element_type=F32)
        out_ref[...] = total.astype(out_ref.dtype)


def project(gated, weight, blocks, dtypes):
    rows, depth = gated.shape
    widths = [weight.shape[1] // 4 // pieces for *_, pieces in blocks]
    whole = pl.BlockSpec(memory_space=pltpu.VMEM)
    return pl.pallas_call(
        functools.partial(project_kernel, blocks),
        in_specs=[whole] * 2,
        out_specs=[whole] * len(blocks),
        out_shape=[jax.ShapeDtypeStruct((rows, w), t) for w, t in zip(widths, dtypes)],
        compiler_params=pltpu.CompilerParams(vmem_limit_bytes=PROJECT_VMEM),
        cost_estimate=pl.CostEstimate(
            flops=2 * rows * depth * sum(widths), bytes_accessed=2 * depth * sum(widths), transcendentals=0
        ),
    )(gated, weight)


def add_kernel(own_ref, arrived_ref, out_ref):
    total = own_ref[...] + arrived_ref[...].astype(F32)
    out_ref[...] = total.astype(out_ref.dtype)


def add(own, arrived):
    whole = pl.BlockSpec(memory_space=pltpu.VMEM)
    return pl.pallas_call(
        add_kernel,
        in_specs=[whole] * 2,
        out_specs=whole,
        out_shape=jax.ShapeDtypeStruct(arrived.shape, BF16),
        compiler_params=pltpu.CompilerParams(vmem_limit_bytes=SMALL_VMEM),
        cost_estimate=pl.CostEstimate(
            flops=arrived.size, bytes_accessed=8 * arrived.size, transcendentals=0
        ),
    )(own, arrived)


def mark_kernel(*refs):
    refs[-1][...] = jnp.zeros_like(refs[-1])


def mark(arrays):
    return pl.pallas_call(
        mark_kernel,
        in_specs=[pl.BlockSpec(memory_space=pl.ANY)] * len(arrays),
        out_specs=pl.BlockSpec(memory_space=pltpu.VMEM),
        out_shape=jax.ShapeDtypeStruct((8, 128), F32),
        compiler_params=pltpu.CompilerParams(vmem_limit_bytes=SMALL_VMEM),
        cost_estimate=pl.CostEstimate(flops=2 * 10**10, bytes_accessed=2**20, transcendentals=0),
    )(*arrays)


def finish_kernel(own_ref, near_ref, *refs):
    *arrived_refs, _, out_ref, stage, sem = refs
    width = out_ref.shape[1] // len(arrived_refs)
    steps = sem.shape[0]
    rows = out_ref.shape[0] // steps
    copies = []
    for step in range(steps):
        part = pl.ds(step * rows, rows)
        for c, arrived_ref in enumerate(arrived_refs):
            at = slice(c * width, (c + 1) * width)
            total = own_ref[part, at] + near_ref[part, at].astype(F32)
            stage[part, at] = (total + arrived_ref[part].astype(F32)).astype(stage.dtype)
        copies.append(pltpu.make_async_copy(stage.at[part], out_ref.at[part], sem.at[step]))
        copies[-1].start()
    for copy in copies:
        copy.wait()


def finish(own, near, arrived):
    rows, width = own.shape
    whole, anywhere = pl.BlockSpec(memory_space=pltpu.VMEM), pl.BlockSpec(memory_space=pl.ANY)
    return pl.pallas_call(
        finish_kernel,
        in_specs=[whole] * (2 + len(arrived)) + [anywhere],
        out_specs=anywhere,
        out_shape=jax.ShapeDtypeStruct((rows, width), BF16),
        scratch_shapes=[pltpu.VMEM((rows, width), BF16), pltpu.SemaphoreType.DMA((4,))],
        compiler_params=pltpu.CompilerParams(vmem_limit_bytes=SMALL_VMEM),
        cost_estimate=pl.CostEstimate(
            flops=rows * width, bytes_accessed=8 * rows * width, transcendentals=0
        ),
    )(own, near, *arrived, mark(arrived))


def body(pieces, tables, queries, keys, values, filters, skip_weight, out_weight):
    rows, width = keys.shape
    n_peers = lax.axis_size("seq")
    chans = width // n_peers
    fwd, bwd = (jnp.asarray(t) for t in tables)
    skip = skip_weight[None, :]
    in_chip = [(0, 1), (1, 0), (2, 3), (3, 2)]
    across = [(0, 2), (2, 0), (1, 3), (3, 1)]

    sends = [(True, True, c, pieces) for c in range(pieces)]
    keeps = [(False, True, c, pieces) for c in range(pieces)]

    if chans % 128 == 0 and n_peers == 8:
        blocks = pre(keys, values, filters, n_peers)
        received = exchange(blocks, n_peers, False)
        fwd, bwd = load_tables(fwd, bwd, received[1:2])
        early, part = spectra(received[:-2], fwd, n_peers)
        back = exchange(conv_fast(early, part, received[-2:], fwd, bwd), n_peers, True)
        slots = slots_of(n_peers, True)[-3:]
        gated, send_part, own_part = gate_early(
            queries, keys, values, skip, out_weight, back[:-3], n_peers
        )
        late, last = gate_late(
            queries, keys, values, skip, out_weight, send_part, back[-3:], slots, sends[-1]
        )
        sent = [
            *(late_project(out_weight, late, send_part, slots, [s], BF16)[0] for s in sends[:-1]),
            last,
        ]
        ours = late_project(out_weight, late, own_part, slots, keeps, F32)
        gated = assemble(gated, late, slots)
    else:
        product = keys.astype(F32) * values.astype(F32)
        parts = [a.astype(BF16).reshape(rows, n_peers, chans) for a in (product, filters)]
        sent = jnp.concatenate(parts, axis=2).transpose(1, 0, 2)
        received = lax.all_to_all(sent, "seq", split_axis=0, concat_axis=0, tiled=True)
        conv = conv_plain(received, fwd, bwd)
        back = lax.all_to_all(conv, "seq", split_axis=0, concat_axis=0, tiled=True)
        mixed = back.transpose(1, 0, 2).reshape(rows, width).astype(F32) + skip * product
        gated = (queries.astype(F32) * mixed).astype(BF16)
        sent = project(gated, out_weight, sends, [BF16] * pieces)
        ours = project(gated, out_weight, keeps, [F32] * pieces)

    theirs = [lax.ppermute(piece, "fsdp", in_chip) for piece in sent]
    arrived = [lax.ppermute(add(*pair), "fsdp", across) for pair in zip(ours, theirs)]
    blocks = [(True, False, 0, 1), (False, False, 0, 1)]
    sent, own = project(gated, out_weight, blocks, [BF16, F32])
    near = lax.ppermute(sent, "fsdp", in_chip)
    return finish(own, near, arrived)


def solution(mesh):
    in_specs = (
        P("seq", "fsdp"),
        P("seq", "fsdp"),
        P("seq", "fsdp"),
        P("seq", "fsdp"),
        P("fsdp"),
        P("fsdp", None),
    )
    out_specs = P("seq", "fsdp")

    def run(queries, keys, values, filters, skip_weight, out_weight):
        rows = keys.shape[0] // mesh.shape["seq"]
        fn = functools.partial(body, 2, make_tables(rows))
        return jax.shard_map(fn, mesh=mesh, in_specs=in_specs, out_specs=out_specs, check_vma=False)(
            queries, keys, values, filters, skip_weight, out_weight
        )

    return run
```

```python
import functools

import numpy as np

import jax
import jax.numpy as jnp
from jax import lax
from jax.experimental import pallas as pl
from jax.experimental.pallas import tpu as pltpu
from jax.sharding import PartitionSpec as P

BF16 = jnp.bfloat16
F32 = jnp.float32
CONV_VMEM = 24 * 2**20
PROJECT_VMEM = 24 * 2**20
SMALL_VMEM = 12 * 2**20
STEP = 16


def split_bf16(table):
    high = table.astype(BF16)
    return high, (table - high.astype(np.float64)).astype(BF16)


def make_tables(rows):
    order = np.concatenate([np.arange(0, rows, 2), np.arange(1, rows, 2)])
    times = np.arange(rows)
    angle = np.pi * (((2 * order[:, None] + 1) * times[None, :]) % (4 * rows)) / (2 * rows)
    forward = np.concatenate([np.cos(angle), -np.sin(angle)], axis=0)
    high, low = split_bf16(forward)
    back_high, back_low = split_bf16(forward.T / rows)
    return (
        np.concatenate([high, low], axis=1),
        np.concatenate([back_high, back_low, back_high], axis=1),
    )


def peer_of(slot):
    return lax.bitwise_xor(lax.axis_index("seq"), slot)


def peer_block(slot, size):
    return pl.ds(pl.multiple_of(peer_of(slot) * size, size), size)


def pre_kernel(n_peers, keys_hbm, values_hbm, filters_hbm, *refs):
    out_refs = refs[:n_peers]
    keys, values, filters, sem = refs[n_peers:]
    rows, width = keys.shape
    chans = width // n_peers
    steps = sem.shape[0]
    parts = [pl.ds(c * rows // steps, rows // steps) for c in range(steps)]
    pairs = ((keys_hbm, keys), (values_hbm, values), (filters_hbm, filters))
    copies = [
        [
            pltpu.make_async_copy(src.at[part], dst.at[part], sem.at[c, i])
            for i, (src, dst) in enumerate(pairs)
        ]
        for c, part in enumerate(parts)
    ]
    for group in copies:
        for copy in group:
            copy.start()
    for part, group in zip(parts, copies):
        for copy in group:
            copy.wait()
        for slot, out_ref in zip(slots_of(n_peers, False), out_refs):
            at = peer_block(slot, chans)
            product = keys[part, at].astype(F32) * values[part, at].astype(F32)
            out_ref[part, :chans] = product.astype(BF16)
            out_ref[part, chans:] = filters[part, at].astype(BF16)


def pre(keys, values, filters, n_peers):
    rows, width = keys.shape
    chans = width // n_peers
    args = [pltpu.with_memory_space_constraint(a, pltpu.HBM) for a in (keys, values, filters)]
    return pl.pallas_call(
        functools.partial(pre_kernel, n_peers),
        in_specs=[pl.BlockSpec(memory_space=pltpu.HBM)] * 3,
        out_specs=[pl.BlockSpec(memory_space=pltpu.VMEM)] * n_peers,
        out_shape=[jax.ShapeDtypeStruct((rows, 2 * chans), BF16)] * n_peers,
        scratch_shapes=[
            pltpu.VMEM((rows, width), BF16),
            pltpu.VMEM((rows, width), BF16),
            pltpu.VMEM((rows, width), F32),
            pltpu.SemaphoreType.DMA((2, 3)),
        ],
        compiler_params=pltpu.CompilerParams(vmem_limit_bytes=SMALL_VMEM),
        cost_estimate=pl.CostEstimate(
            flops=rows * width, bytes_accessed=12 * rows * width, transcendentals=0
        ),
    )(*args)


def slots_of(n_peers, back):
    half = n_peers // 2
    near, far = list(range(1, half)), list(range(half, n_peers))
    if back:
        return [0, near[0], far[3], far[0], near[1], far[1], far[2]] + near[2:]
    return [0, far[0], near[0]] + near[:0:-1] + [far[1], far[3], far[2]]


def exchange(blocks, n_peers, back):
    return [
        lax.ppermute(block, "seq", [(i, i ^ slot) for i in range(n_peers)]) if slot else block
        for slot, block in zip(slots_of(n_peers, back), blocks)
    ]


def block_spectrum(table, block):
    return jnp.dot(table, jnp.concatenate([block, block], axis=0), preferred_element_type=F32)


def times(a, b):
    return a[0] * b[0] - a[1] * b[1], a[0] * b[1] + a[1] * b[0]


def plus(a, b):
    return b if a is None else (a[0] + b[0], a[1] + b[1])


def late_place(n_blocks):
    return lax.div(peer_of(slots_of(n_blocks, False)[-1]), 2)


def load(ref, at, row, step, rows, lanes):
    return tuple(ref[(*at, pl.ds(row + part * rows, step), lanes)] for part in range(2))


def mix_early(pair, step, spec_ref, part_ref):
    n_blocks, rows, chans = spec_ref.shape[0], spec_ref.shape[1] // 2, spec_ref.shape[2] // 2
    early = [j for j in range(n_blocks) if j // 2 != pair]

    @pl.loop(0, rows // step)
    def _(t):
        row = pl.multiple_of(t * step, step)
        signal = {j: load(spec_ref, (j,), row, step, rows, slice(0, chans)) for j in early}
        filt = {j: load(spec_ref, (j,), row, step, rows, slice(chans, 2 * chans)) for j in early}
        for i in range(n_blocks):
            total = None
            for d in early:
                if i - d in early:
                    total = plus(total, times(filt[d], signal[i - d]))
            if total is None:
                total = (jnp.zeros((step, chans), F32),) * 2
            for part in range(2):
                part_ref[i, pl.ds(row + part * rows, step)] = total[part]


def tables_kernel(fwd_hbm, bwd_hbm, *refs):
    fwd_ref, bwd_ref, sem = refs[-3:]
    copies = [
        pltpu.make_async_copy(fwd_hbm, fwd_ref, sem.at[0]),
        pltpu.make_async_copy(bwd_hbm, bwd_ref, sem.at[1]),
    ]
    for copy in copies:
        copy.start()
    for copy in copies:
        copy.wait()


def load_tables(fwd, bwd, after):
    whole = pl.BlockSpec(memory_space=pltpu.VMEM)
    args = [pltpu.with_memory_space_constraint(a, pltpu.HBM) for a in (fwd, bwd)]
    return pl.pallas_call(
        tables_kernel,
        in_specs=[pl.BlockSpec(memory_space=pltpu.HBM)] * 2
        + [pl.BlockSpec(memory_space=pl.ANY)] * len(after),
        out_specs=[whole] * 2,
        out_shape=[jax.ShapeDtypeStruct(t.shape, BF16) for t in (fwd, bwd)],
        scratch_shapes=[pltpu.SemaphoreType.DMA((2,))],
        compiler_params=pltpu.CompilerParams(vmem_limit_bytes=SMALL_VMEM),
        cost_estimate=pl.CostEstimate(flops=10**6, bytes_accessed=3 * 2**20, transcendentals=0),
    )(*args, *after)


def spectra_kernel(n_peers, fwd_ref, *refs):
    *in_refs, spec_ref, part_ref = refs
    for slot, in_ref in zip(slots_of(n_peers, False), in_refs):
        spec_ref[peer_of(slot)] = block_spectrum(fwd_ref[...], in_ref[...])
    for pair in range(n_peers // 2):
        pl.when(late_place(n_peers) == pair)(
            functools.partial(mix_early, pair, STEP, spec_ref, part_ref)
        )


def spectra(received, fwd, n_peers):
    rows, width = received[0].shape
    whole = pl.BlockSpec(memory_space=pltpu.VMEM)
    return pl.pallas_call(
        functools.partial(spectra_kernel, n_peers),
        in_specs=[whole] * (1 + len(received)),
        out_specs=[whole] * 2,
        out_shape=[
            jax.ShapeDtypeStruct((n_peers, 2 * rows, width), F32),
            jax.ShapeDtypeStruct((n_peers, 2 * rows, width // 2), F32),
        ],
        compiler_params=pltpu.CompilerParams(vmem_limit_bytes=CONV_VMEM),
        cost_estimate=pl.CostEstimate(
            flops=8 * len(received) * rows * rows * width, bytes_accessed=4 * 2**20, transcendentals=0
        ),
    )(fwd, *received)


def add_block(total, place, new, others, row, step, rows, chans):
    n_blocks = len(total)
    x_at, f_at = slice(0, chans), slice(chans, 2 * chans)
    x_new, f_new = load(new, (), row, step, rows, x_at), load(new, (), row, step, rows, f_at)
    for j, (ref, at) in others.items():
        if j + place < n_blocks:
            x_j = load(ref, at, row, step, rows, x_at)
            f_j = load(ref, at, row, step, rows, f_at)
            total[j + place] = plus(total[j + place], times(f_new, x_j))
            total[j + place] = plus(total[j + place], times(f_j, x_new))
    if 2 * place < n_blocks:
        total[2 * place] = plus(total[2 * place], times(f_new, x_new))


def early_blocks(place, n_blocks, spec_ref):
    return {j: (spec_ref, (j,)) for j in range(n_blocks) if j // 2 != place // 2}


def mix_middle(place, step, spec_ref, part_ref, new_ref, out_ref):
    n_blocks, rows, chans = spec_ref.shape[0], spec_ref.shape[1] // 2, spec_ref.shape[2] // 2
    others = early_blocks(place, n_blocks, spec_ref)

    @pl.loop(0, rows // step)
    def _(t):
        row = pl.multiple_of(t * step, step)
        total = [load(part_ref, (i,), row, step, rows, slice(0, chans)) for i in range(n_blocks)]
        add_block(total, place, new_ref, others, row, step, rows, chans)
        for i in range(n_blocks):
            for part in range(2):
                out_ref[i, pl.ds(row + part * rows, step)] = total[i][part]


def middle_kernel(fwd_ref, spec_ref, part_ref, in_ref, new_ref, out_ref):
    n_blocks = spec_ref.shape[0]
    new_ref[...] = block_spectrum(fwd_ref[...], in_ref[...])
    mine = peer_of(slots_of(n_blocks, False)[-2])
    for place in range(n_blocks):
        pl.when(mine == place)(
            functools.partial(mix_middle, place, STEP, spec_ref, part_ref, new_ref, out_ref)
        )


def middle(early, part, block, fwd):
    whole = pl.BlockSpec(memory_space=pltpu.VMEM)
    return pl.pallas_call(
        middle_kernel,
        in_specs=[whole] * 4,
        out_specs=[whole] * 2,
        out_shape=[jax.ShapeDtypeStruct(a.shape, F32) for a in (early[0], part)],
        compiler_params=pltpu.CompilerParams(vmem_limit_bytes=CONV_VMEM),
        cost_estimate=pl.CostEstimate(flops=10**9, bytes_accessed=4 * 2**20, transcendentals=0),
    )(fwd, early, part, block)


def mix_last(place, step, first, last, sign, spec_ref, part_ref, next_ref, new_ref, turned):
    n_blocks, rows, chans = spec_ref.shape[0], spec_ref.shape[1] // 2, spec_ref.shape[2] // 2
    others = early_blocks(place, n_blocks, spec_ref)
    others[place ^ 1] = (next_ref, ())

    @pl.loop(first // step, last // step)
    def _(t):
        row = pl.multiple_of(t * step, step)
        total = [load(part_ref, (i,), row, step, rows, slice(0, chans)) for i in range(n_blocks)]
        add_block(total, place, new_ref, others, row, step, rows, chans)
        for i in range(n_blocks):
            value = total[i]
            if i > 0:
                turn_re, turn_im = total[i - 1]
                if sign > 0:
                    value = value[0] - turn_im, value[1] + turn_re
                else:
                    value = value[0] + turn_im, value[1] - turn_re
            lanes = slice(i % 2 * chans, (i % 2 + 1) * chans)
            for part in range(2):
                high = value[part].astype(BF16)
                low = (value[part] - high.astype(F32)).astype(BF16)
                for c, piece in enumerate((high, high, low)):
                    turned[i // 2, pl.ds(row + (2 * c + part) * rows, step), lanes] = piece


def conv_kernel(fwd_ref, bwd_ref, spec_ref, part_ref, next_ref, in_ref, *refs):
    *out_refs, new_ref, turned = refs
    n_blocks, rows, chans = spec_ref.shape[0], in_ref.shape[0], in_ref.shape[1] // 2
    new_ref[...] = block_spectrum(fwd_ref[...], in_ref[...])

    def mix(place):
        for first, last, sign in ((0, rows // 2, 1), (rows // 2, rows, -1)):
            mix_last(place, STEP, first, last, sign, spec_ref, part_ref, next_ref, new_ref, turned)

    mine = peer_of(slots_of(n_blocks, False)[-1])
    for place in range(n_blocks):
        pl.when(mine == place)(functools.partial(mix, place))

    odd = lax.bitwise_and(lax.axis_index("seq"), 1) == 1
    by_slot = dict(zip(slots_of(n_blocks, True), out_refs))
    for slot in range(0, n_blocks, 2):
        pair = lax.div(peer_of(slot), 2)
        both = jnp.dot(bwd_ref[...], turned[pair], preferred_element_type=F32)
        left, right = both[:, :chans], both[:, chans:]
        by_slot[slot][...] = jnp.where(odd, right, left).astype(BF16)
        by_slot[slot + 1][...] = jnp.where(odd, left, right).astype(BF16)


def conv_fast(early, part, late, fwd, bwd):
    n_blocks = early.shape[0]
    rows, chans = late[0].shape[0], late[0].shape[1] // 2
    late_spec, part = middle(early, part, late[0], fwd)
    whole = pl.BlockSpec(memory_space=pltpu.VMEM)
    return pl.pallas_call(
        conv_kernel,
        in_specs=[whole] * 6,
        out_specs=[whole] * n_blocks,
        out_shape=[jax.ShapeDtypeStruct((rows, chans), BF16)] * n_blocks,
        scratch_shapes=[
            pltpu.VMEM((2 * rows, 2 * chans), F32),
            pltpu.VMEM((n_blocks // 2, 6 * rows, 2 * chans), BF16),
        ],
        compiler_params=pltpu.CompilerParams(vmem_limit_bytes=CONV_VMEM),
        cost_estimate=pl.CostEstimate(
            flops=16 * n_blocks * rows * rows * chans, bytes_accessed=4 * 2**20, transcendentals=0
        ),
    )(fwd, bwd, early, part, late_spec, late[1])


def conv_plain(received, fwd, bwd):
    n_blocks, rows, chans = received.shape[0], received.shape[1], received.shape[2] // 2
    exact = lax.Precision.HIGHEST
    fwd32 = fwd[:, :rows].astype(F32) + fwd[:, rows:].astype(F32)
    bwd32 = bwd[:, : 2 * rows].astype(F32) + bwd[:, 2 * rows : 4 * rows].astype(F32)
    sign = jnp.where(jnp.arange(rows) < rows // 2, 1.0, -1.0).astype(F32)[:, None]

    def spectrum(blocks):
        spec = jnp.einsum("kt,jtc->jkc", fwd32, blocks.astype(F32), precision=exact)
        return spec[:, :rows], spec[:, rows:]

    x_re, x_im = spectrum(received[:, :, :chans])
    f_re, f_im = spectrum(received[:, :, chans:])
    g_re = f_re.at[1:].add(-sign * f_im[:-1])
    g_im = f_im.at[1:].add(sign * f_re[:-1])

    def one(d, total):
        t_re, t_im = total
        later = (jnp.arange(n_blocks) >= d)[:, None, None]
        a_re = jnp.where(later, jnp.roll(x_re, d, axis=0), 0.0)
        a_im = jnp.where(later, jnp.roll(x_im, d, axis=0), 0.0)
        return (
            t_re + g_re[d] * a_re - g_im[d] * a_im,
            t_im + g_re[d] * a_im + g_im[d] * a_re,
        )

    zero = jnp.zeros_like(x_re)
    y_re, y_im = lax.fori_loop(0, n_blocks, one, (zero, zero))
    both = jnp.concatenate([y_re, y_im], axis=1)
    return jnp.einsum("tk,jkc->jtc", bwd32, both, precision=exact).astype(BF16)


def columns_of(other, across, piece, pieces, width):
    count = width // 4 // pieces
    place = lax.axis_index("fsdp")
    core, side = lax.rem(place, 2), lax.div(place, 2)
    block = 2 * (1 - side if across else side) + (1 - core if other else core)
    return pl.ds(pl.multiple_of((block * pieces + piece) * count, count), count)


def gate_slot(slot, queries_ref, keys_ref, values_ref, skip_ref, conv_ref):
    at = peer_block(slot, conv_ref.shape[1])
    product = keys_ref[:, at].astype(F32) * values_ref[:, at].astype(F32)
    mixed = conv_ref[...].astype(F32) + skip_ref[:, at] * product
    return (queries_ref[:, at].astype(F32) * mixed).astype(BF16)


def gate_early_kernel(n_peers, queries_ref, keys_ref, values_ref, skip_ref, weight_ref, *refs):
    conv_refs, (gated_ref, *part_refs) = refs[:-3], refs[-3:]
    chans = conv_refs[0].shape[1]
    slots = slots_of(n_peers, True)
    for slot, conv_ref in zip(slots, conv_refs):
        gated = gate_slot(slot, queries_ref, keys_ref, values_ref, skip_ref, conv_ref)
        gated_ref[:, peer_block(slot, chans)] = gated
    for slot in slots[len(conv_refs) :]:
        gated_ref[:, peer_block(slot, chans)] = jnp.zeros((gated_ref.shape[0], chans), BF16)
    for other, part_ref in zip((True, False), part_refs):
        columns = weight_ref[:, columns_of(other, True, 0, 1, weight_ref.shape[1])]
        part_ref[...] = jnp.dot(gated_ref[...], columns, preferred_element_type=F32)


def gate_early(queries, keys, values, skip, weight, conv, n_peers):
    rows, width = queries.shape
    out_width = weight.shape[1] // 4
    whole = pl.BlockSpec(memory_space=pltpu.VMEM)
    return pl.pallas_call(
        functools.partial(gate_early_kernel, n_peers),
        in_specs=[whole] * (5 + len(conv)),
        out_specs=[whole] * 3,
        out_shape=[jax.ShapeDtypeStruct((rows, width), BF16)]
        + [jax.ShapeDtypeStruct((rows, out_width), F32)] * 2,
        compiler_params=pltpu.CompilerParams(vmem_limit_bytes=PROJECT_VMEM),
        cost_estimate=pl.CostEstimate(
            flops=4 * rows * width * out_width, bytes_accessed=10 * rows * width, transcendentals=0
        ),
    )(queries, keys, values, skip, weight, *conv)


def late_product(late, late_slots, block, weight_ref, part_ref):
    chans = late.shape[1] // len(late_slots)
    at = columns_of(*block, weight_ref.shape[1])
    _, _, piece, pieces = block
    count = part_ref.shape[1] // pieces
    columns = jnp.concatenate([weight_ref[peer_block(s, chans), at] for s in late_slots], axis=0)
    part = part_ref[:, piece * count : (piece + 1) * count]
    return part + jnp.dot(late, columns, preferred_element_type=F32)


def gate_late_kernel(late_slots, block, queries_ref, keys_ref, values_ref, skip_ref, weight_ref, part_ref, *refs):
    *conv_refs, late_ref, sent_ref = refs
    chans = conv_refs[0].shape[1]
    for c, (slot, conv_ref) in enumerate(zip(late_slots, conv_refs)):
        gated = gate_slot(slot, queries_ref, keys_ref, values_ref, skip_ref, conv_ref)
        late_ref[:, c * chans : (c + 1) * chans] = gated
    total = late_product(late_ref[...], late_slots, block, weight_ref, part_ref)
    sent_ref[...] = total.astype(BF16)


def gate_late(queries, keys, values, skip, weight, part, conv, late_slots, block):
    rows, chans = conv[0].shape
    whole = pl.BlockSpec(memory_space=pltpu.VMEM)
    return pl.pallas_call(
        functools.partial(gate_late_kernel, late_slots, block),
        in_specs=[whole] * (6 + len(conv)),
        out_specs=[whole] * 2,
        out_shape=[
            jax.ShapeDtypeStruct((rows, chans * len(conv)), BF16),
            jax.ShapeDtypeStruct((rows, weight.shape[1] // 4 // block[-1]), BF16),
        ],
        compiler_params=pltpu.CompilerParams(vmem_limit_bytes=PROJECT_VMEM),
        cost_estimate=pl.CostEstimate(
            flops=rows * chans * weight.shape[1], bytes_accessed=2**20, transcendentals=0
        ),
    )(queries, keys, values, skip, weight, part, *conv)


def late_project_kernel(late_slots, blocks, weight_ref, late_ref, part_ref, *out_refs):
    for block, out_ref in zip(blocks, out_refs):
        total = late_product(late_ref[...], late_slots, block, weight_ref, part_ref)
        out_ref[...] = total.astype(out_ref.dtype)


def late_project(weight, late, part, late_slots, blocks, dtype):
    rows, depth = late.shape
    widths = [weight.shape[1] // 4 // pieces for *_, pieces in blocks]
    whole = pl.BlockSpec(memory_space=pltpu.VMEM)
    return pl.pallas_call(
        functools.partial(late_project_kernel, late_slots, blocks),
        in_specs=[whole] * 3,
        out_specs=[whole] * len(blocks),
        out_shape=[jax.ShapeDtypeStruct((rows, w), dtype) for w in widths],
        compiler_params=pltpu.CompilerParams(vmem_limit_bytes=PROJECT_VMEM),
        cost_estimate=pl.CostEstimate(
            flops=2 * rows * depth * sum(widths), bytes_accessed=2**20, transcendentals=0
        ),
    )(weight, late, part)


def assemble_kernel(late_slots, gated_ref, late_ref, out_ref):
    chans = late_ref.shape[1] // len(late_slots)
    out_ref[...] = gated_ref[...]
    for c, slot in enumerate(late_slots):
        out_ref[:, peer_block(slot, chans)] = late_ref[:, c * chans : (c + 1) * chans]


def assemble(gated, late, late_slots):
    whole = pl.BlockSpec(memory_space=pltpu.VMEM)
    return pl.pallas_call(
        functools.partial(assemble_kernel, late_slots),
        in_specs=[whole] * 2,
        out_specs=whole,
        out_shape=jax.ShapeDtypeStruct(gated.shape, BF16),
        compiler_params=pltpu.CompilerParams(vmem_limit_bytes=SMALL_VMEM),
        cost_estimate=pl.CostEstimate(flops=1000, bytes_accessed=2**20, transcendentals=0),
    )(gated, late)


def project_kernel(blocks, gated_ref, weight_ref, *out_refs):
    for block, out_ref in zip(blocks, out_refs):
        columns = weight_ref[:, columns_of(*block, weight_ref.shape[1])]
        total = jnp.dot(gated_ref[...], columns, preferred_element_type=F32)
        out_ref[...] = total.astype(out_ref.dtype)


def project(gated, weight, blocks, dtypes):
    rows, depth = gated.shape
    widths = [weight.shape[1] // 4 // pieces for *_, pieces in blocks]
    whole = pl.BlockSpec(memory_space=pltpu.VMEM)
    return pl.pallas_call(
        functools.partial(project_kernel, blocks),
        in_specs=[whole] * 2,
        out_specs=[whole] * len(blocks),
        out_shape=[jax.ShapeDtypeStruct((rows, w), t) for w, t in zip(widths, dtypes)],
        compiler_params=pltpu.CompilerParams(vmem_limit_bytes=PROJECT_VMEM),
        cost_estimate=pl.CostEstimate(
            flops=2 * rows * depth * sum(widths), bytes_accessed=2 * depth * sum(widths), transcendentals=0
        ),
    )(gated, weight)


def add_kernel(own_ref, arrived_ref, out_ref):
    total = own_ref[...] + arrived_ref[...].astype(F32)
    out_ref[...] = total.astype(out_ref.dtype)


def add(own, arrived):
    whole = pl.BlockSpec(memory_space=pltpu.VMEM)
    return pl.pallas_call(
        add_kernel,
        in_specs=[whole] * 2,
        out_specs=whole,
        out_shape=jax.ShapeDtypeStruct(arrived.shape, BF16),
        compiler_params=pltpu.CompilerParams(vmem_limit_bytes=SMALL_VMEM),
        cost_estimate=pl.CostEstimate(
            flops=arrived.size, bytes_accessed=8 * arrived.size, transcendentals=0
        ),
    )(own, arrived)


def mark_kernel(*refs):
    refs[-1][...] = jnp.zeros_like(refs[-1])


def mark(arrays):
    return pl.pallas_call(
        mark_kernel,
        in_specs=[pl.BlockSpec(memory_space=pl.ANY)] * len(arrays),
        out_specs=pl.BlockSpec(memory_space=pltpu.VMEM),
        out_shape=jax.ShapeDtypeStruct((8, 128), F32),
        compiler_params=pltpu.CompilerParams(vmem_limit_bytes=SMALL_VMEM),
        cost_estimate=pl.CostEstimate(flops=2 * 10**10, bytes_accessed=2**20, transcendentals=0),
    )(*arrays)


def finish_kernel(own_ref, near_ref, *refs):
    *arrived_refs, _, out_ref, stage, sem = refs
    width = out_ref.shape[1] // len(arrived_refs)
    steps = sem.shape[0]
    rows = out_ref.shape[0] // steps
    copies = []
    for step in range(steps):
        part = pl.ds(step * rows, rows)
        for c, arrived_ref in enumerate(arrived_refs):
            at = slice(c * width, (c + 1) * width)
            total = own_ref[part, at] + near_ref[part, at].astype(F32)
            stage[part, at] = (total + arrived_ref[part].astype(F32)).astype(stage.dtype)
        copies.append(pltpu.make_async_copy(stage.at[part], out_ref.at[part], sem.at[step]))
        copies[-1].start()
    for copy in copies:
        copy.wait()


def finish(own, near, arrived):
    rows, width = own.shape
    whole, anywhere = pl.BlockSpec(memory_space=pltpu.VMEM), pl.BlockSpec(memory_space=pl.ANY)
    return pl.pallas_call(
        finish_kernel,
        in_specs=[whole] * (2 + len(arrived)) + [anywhere],
        out_specs=anywhere,
        out_shape=jax.ShapeDtypeStruct((rows, width), BF16),
        scratch_shapes=[pltpu.VMEM((rows, width), BF16), pltpu.SemaphoreType.DMA((4,))],
        compiler_params=pltpu.CompilerParams(vmem_limit_bytes=SMALL_VMEM),
        cost_estimate=pl.CostEstimate(
            flops=rows * width, bytes_accessed=8 * rows * width, transcendentals=0
        ),
    )(own, near, *arrived, mark(arrived))


def body(pieces, tables, queries, keys, values, filters, skip_weight, out_weight):
    rows, width = keys.shape
    n_peers = lax.axis_size("seq")
    chans = width // n_peers
    fwd, bwd = (jnp.asarray(t) for t in tables)
    skip = skip_weight[None, :]
    in_chip = [(0, 1), (1, 0), (2, 3), (3, 2)]
    across = [(0, 2), (2, 0), (1, 3), (3, 1)]

    sends = [(True, True, c, pieces) for c in range(pieces)]
    keeps = [(False, True, c, pieces) for c in range(pieces)]

    if chans % 128 == 0 and n_peers == 8:
        blocks = pre(keys, values, filters, n_peers)
        received = exchange(blocks, n_peers, False)
        fwd, bwd = load_tables(fwd, bwd, received[1:2])
        early, part = spectra(received[:-2], fwd, n_peers)
        back = exchange(conv_fast(early, part, received[-2:], fwd, bwd), n_peers, True)
        slots = slots_of(n_peers, True)[-3:]
        gated, send_part, own_part = gate_early(
            queries, keys, values, skip, out_weight, back[:-3], n_peers
        )
        late, last = gate_late(
            queries, keys, values, skip, out_weight, send_part, back[-3:], slots, sends[-1]
        )
        sent = [
            *(late_project(out_weight, late, send_part, slots, [s], BF16)[0] for s in sends[:-1]),
            last,
        ]
        ours = late_project(out_weight, late, own_part, slots, keeps, F32)
        gated = assemble(gated, late, slots)
    else:
        product = keys.astype(F32) * values.astype(F32)
        parts = [a.astype(BF16).reshape(rows, n_peers, chans) for a in (product, filters)]
        sent = jnp.concatenate(parts, axis=2).transpose(1, 0, 2)
        received = lax.all_to_all(sent, "seq", split_axis=0, concat_axis=0, tiled=True)
        conv = conv_plain(received, fwd, bwd)
        back = lax.all_to_all(conv, "seq", split_axis=0, concat_axis=0, tiled=True)
        mixed = back.transpose(1, 0, 2).reshape(rows, width).astype(F32) + skip * product
        gated = (queries.astype(F32) * mixed).astype(BF16)
        sent = project(gated, out_weight, sends, [BF16] * pieces)
        ours = project(gated, out_weight, keeps, [F32] * pieces)

    theirs = [lax.ppermute(piece, "fsdp", in_chip) for piece in sent]
    arrived = [lax.ppermute(add(*pair), "fsdp", across) for pair in zip(ours, theirs)]
    blocks = [(True, False, 0, 1), (False, False, 0, 1)]
    sent, own = project(gated, out_weight, blocks, [BF16, F32])
    near = lax.ppermute(sent, "fsdp", in_chip)
    return finish(own, near, arrived)


def solution(mesh):
    in_specs = (
        P("seq", "fsdp"),
        P("seq", "fsdp"),
        P("seq", "fsdp"),
        P("seq", "fsdp"),
        P("fsdp"),
        P("fsdp", None),
    )
    out_specs = P("seq", "fsdp")

    def run(queries, keys, values, filters, skip_weight, out_weight):
        rows = keys.shape[0] // mesh.shape["seq"]
        fn = functools.partial(body, 2, make_tables(rows))
        return jax.shard_map(fn, mesh=mesh, in_specs=in_specs, out_specs=out_specs, check_vma=False)(
            queries, keys, values, filters, skip_weight, out_weight
        )

    return run
```
